32 devices in a mesh: dp: 32 (over z, y, x, core).
Axes of the slice: x: 2, y: 2, z: 4, core: 2. Of those that a mesh axis runs over, the one named last changes fastest.
Arguments:
- tokens: bfloat16 [65536, 512], P('dp'), may hold values from -6 to 6
- segment: int32 [65536], P('dp'), may hold values from 0 to 2, as said below
- counts: int32 [32], P('dp'), may hold values from 1024 to 2048, as said below
- memory: bfloat16 [20, 512], P(None, 'dp'), may hold values from -6 to 6
- w_query: bfloat16 [512, 512], P('dp'), may hold values from -0.375 to 0.375
- b_query: bfloat16 [512], P('dp'), may hold values from -3 to 3
- w_key: bfloat16 [512, 512], P('dp'), may hold values from -0.25 to 0.25
- w_value: bfloat16 [512, 512], P('dp'), may hold values from -0.25 to 0.25
- b_value: bfloat16 [512], P('dp'), may hold values from -3 to 3
- w_out: bfloat16 [512, 512], P('dp'), may hold values from -1 to 1
- b_out: bfloat16 [512], P('dp'), may hold values from -3 to 3
- gain_attn: bfloat16 [512], P('dp'), may hold values from 0.5 to 1.5
- shift_attn: bfloat16 [512], P('dp'), may hold values from -3 to 3
- w_up: bfloat16 [512, 2048], P('dp'), may hold values from -0.25 to 0.25
- b_up: bfloat16 [2048], P('dp'), may hold values from -3 to 3
- w_down: bfloat16 [2048, 512], P('dp'), may hold values from -0.125 to 0.125
- b_down: bfloat16 [512], P('dp'), may hold values from -3 to 3
- gain_ffn: bfloat16 [512], P('dp'), may hold values from 0.5 to 1.5
- shift_ffn: bfloat16 [512], P('dp'), may hold values from -3 to 3
- cotangent: bfloat16 [65536, 512], P('dp'), may hold values from -6 to 6
Outputs:
- output: bfloat16 [65536, 512], P('dp')
- grad_tokens: float32 [65536, 512], P('dp')
- grad_memory: float32 [20, 512], P(None, 'dp')
- grad_w_query: float32 [512, 512], P('dp')
- grad_b_query: float32 [512], P('dp')
- grad_w_key: float32 [512, 512], P('dp')
- grad_w_value: float32 [512, 512], P('dp')
- grad_b_value: float32 [512], P('dp')
- grad_w_out: float32 [512, 512], P('dp')
- grad_b_out: float32 [512], P('dp')
- grad_gain_attn: float32 [512], P('dp')
- grad_shift_attn: float32 [512], P('dp')
- grad_w_up: float32 [512, 2048], P('dp')
- grad_b_up: float32 [2048], P('dp')
- grad_w_down: float32 [2048, 512], P('dp')
- grad_b_down: float32 [512], P('dp')
- grad_gain_ffn: float32 [512], P('dp')
- grad_shift_ffn: float32 [512], P('dp')
The draws below stay inside these ranges and needn't reach their ends.
Inputs may be any that keep to these rules, and one draw needn't show every extreme that they name: `segment`: within each device's 2048 slots the ids never fall and each id marks one sequence; every used sequence has 128 to 1024 slots; in every draw some device holds a used sequence of exactly 1024 tokens. Ids past a device's used count carry no meaning. `counts`: slots are used from the start of each device and end where a sequence ends; in every draw some device uses all 2048 and some device uses 1024.
All inputs are finite; a program needn't handle non-finite values.
Results may differ from the reference program's by a relative error of at most 0.015.
The reference program's roundings to bfloat16 on the way count: a program that leaves them out, or rounds other values in their place, can miss the bound.
Values may be sent and summed in bfloat16 or wider, within the bound.
A program may use at most 320 MiB of HBM per device.

```python
import jax
import jax.numpy as jnp
from jax import lax

D = 512
H = 8
HD = 64
FF = 2048
MEM = 20
CAP = 2048
QB = 512
TOKENS = 65536
N_DP = 32


def layout(key):
    key_count, key_pick, key_offset = jax.random.split(key, 3)
    half = CAP // 2
    least = half // 8
    rank = jnp.arange(N_DP)
    chosen = jax.random.randint(key_pick, (), 0, N_DP)
    offsets = jax.random.randint(key_offset, (N_DP,), least, half - least + 1)
    offsets = jnp.where(rank == (chosen + 1) % N_DP, 0, offsets)
    whole = jax.random.randint(key_count, (N_DP,), 0, 2)
    used = jnp.where(whole == 1, CAP, 2 * half - offsets)
    used = jnp.where(rank == chosen, CAP, used)
    used = jnp.where(rank == (chosen + 1) % N_DP, half, used)
    return (used.astype(jnp.int32), offsets.astype(jnp.int32))


def draw_segment(key, part):
    used, offsets = layout(key)
    place = jnp.arange(CAP, dtype=jnp.int32)
    ids = (place[None, :] + offsets[:, None]) // (CAP // 2)
    return ids.reshape(N_DP * CAP).astype(jnp.int32)


def draw_counts(key, part):
    used, offsets = layout(key)
    return used


def levels(key, extent, cuts, low, top_value):
    level, own = 1.0, jax.random.fold_in(key, 6)
    for position, parts in cuts:
        draws = jnp.exp(jax.random.uniform(jax.random.fold_in(own, position), (parts,), jnp.float32, low / len(cuts), top_value / len(cuts)))
        level = level * jnp.repeat(draws, extent[position] // parts).reshape([-1 if axis == position else 1 for axis in range(len(extent))])
    return level


def normal_values(rng, extent, scale, bound, cuts=(), kind=jnp.bfloat16):
    values = jax.random.normal(rng, extent, jnp.float32) * scale
    if len(cuts) > 0:
        values = levels(rng, extent, cuts, -0.22, 0.18) * values
    return jnp.clip(values, min=-bound, max=bound).astype(kind)


def setup_inputs(seed: int = 0) -> dict:
    streams_of = jax.random.split(jax.random.key(seed), 21)
    tokens = normal_values(streams_of[0], (TOKENS, D), 1.0, 6.0, ((0, 32),))
    segment = draw_segment(jax.random.fold_in(streams_of[20], 71), 0)
    counts = draw_counts(jax.random.fold_in(streams_of[20], 71), 0)
    memory = normal_values(streams_of[3], (MEM, D), 1.0, 6.0, ((1, 32),))
    w_query = normal_values(streams_of[4], (D, D), (D // 2) ** -0.5, 0.375, ((0, 32),))
    b_query = normal_values(streams_of[5], (D,), 0.5, 3.0, ((0, 32),))
    w_key = normal_values(streams_of[6], (D, D), D ** -0.5, 0.25, ((0, 32),))
    w_value = normal_values(streams_of[7], (D, D), D ** -0.5, 0.25, ((0, 32),))
    b_value = normal_values(streams_of[8], (D,), 0.5, 3.0, ((0, 32),))
    w_out = normal_values(streams_of[9], (D, D), (D // 16) ** -0.5, 1.0, ((0, 32),))
    b_out = normal_values(streams_of[10], (D,), 0.5, 3.0, ((0, 32),))
    gain_attn = jnp.clip(1.0 + 0.1 * jax.random.normal(streams_of[11], (D,), jnp.float32), 0.5, 1.5).astype(jnp.bfloat16)
    shift_attn = normal_values(streams_of[12], (D,), 0.5, 3.0, ((0, 32),))
    w_up = normal_values(streams_of[13], (D, FF), D ** -0.5, 0.25, ((0, 32),))
    b_up = normal_values(streams_of[14], (FF,), 0.5, 3.0, ((0, 32),))
    w_down = normal_values(streams_of[15], (FF, D), FF ** -0.5, 0.125, ((0, 32),))
    b_down = normal_values(streams_of[16], (D,), 0.5, 3.0, ((0, 32),))
    gain_ffn = jnp.clip(1.0 + 0.1 * jax.random.normal(streams_of[17], (D,), jnp.float32), 0.5, 1.5).astype(jnp.bfloat16)
    shift_ffn = normal_values(streams_of[18], (D,), 0.5, 3.0, ((0, 32),))
    cotangent = normal_values(streams_of[19], (TOKENS, D), 1.0, 6.0, ((0, 32),))
    return dict(tokens=tokens, segment=segment, counts=counts, memory=memory, w_query=w_query, b_query=b_query, w_key=w_key, w_value=w_value, b_value=b_value, w_out=w_out, b_out=b_out, gain_attn=gain_attn, shift_attn=shift_attn, w_up=w_up, b_up=b_up, w_down=w_down, b_down=b_down, gain_ffn=gain_ffn, shift_ffn=shift_ffn, cotangent=cotangent)


EPS = 1e-05
NEG = -1e+30
HIGH = lax.Precision.HIGHEST

@jax.custom_vjp
def low(v):
    return lax.optimization_barrier(v.astype(jnp.bfloat16)).astype(jnp.float32)

@jax.custom_vjp
def low_back(v):
    return v

def low_keep(v):
    return (low(v), None)

def low_pass(kept, grad):
    return (grad,)

def back_keep(v):
    return (v, None)

def back_low(kept, grad):
    return (low(grad),)
low.defvjp(low_keep, low_pass)
low_back.defvjp(back_keep, back_low)

def rounded_both(value):
    return low(low_back(value))

def layer_norm(value, gain, shift):
    mean = lax.optimization_barrier(jnp.mean(value, axis=-1, keepdims=True))
    centred = value - mean
    spread = lax.optimization_barrier(jnp.mean(centred * centred, axis=-1, keepdims=True))
    return centred * lax.rsqrt(spread + EPS) * gain + shift

def project(left, right):
    return jnp.dot(left, right, precision=HIGH)

def attend_block(query_block, seg_block, keys, values, key_seg):
    query_heads = query_block.reshape(QB, H, HD)
    key_heads = keys.reshape(MEM + CAP, H, HD)
    value_heads = values.reshape(MEM + CAP, H, HD)
    scores = jnp.einsum('qhd,khd->hqk', query_heads, key_heads, precision=HIGH) * HD ** (-0.5)
    scores = low_back(scores)
    memory_slot = jnp.arange(MEM + CAP) < MEM
    allowed = (key_seg[None, :] == seg_block[:, None]) | memory_slot[None, :]
    scores = jnp.where(allowed[None], scores, NEG)
    weights = low(jax.nn.softmax(scores, axis=-1))
    mixed = jnp.einsum('hqk,khd->qhd', weights, value_heads, precision=HIGH)
    return mixed.reshape(QB, D)

def pack_layer(params, inputs):
    memory, w_query, b_query, w_key, w_value, b_value, w_out, b_out, gain_attn, shift_attn, w_up, b_up, w_down, b_down, gain_ffn, shift_ffn = params
    tokens, segment, count = inputs
    valid = jnp.arange(CAP) < count
    key_seg = jnp.concatenate([jnp.full((MEM,), -1, jnp.int32), jnp.where(valid, segment, -1).astype(jnp.int32)])
    queries = rounded_both(project(tokens, w_query) + b_query)
    sources = jnp.concatenate([memory, tokens], axis=0)
    keys = rounded_both(project(sources, w_key))
    values = rounded_both(project(sources, w_value) + b_value)

    def one_block(item):
        return attend_block(item[0], item[1], keys, values, key_seg)
    blocks = lax.map(jax.checkpoint(one_block), (queries.reshape(CAP // QB, QB, D), segment.reshape(CAP // QB, QB)))
    mixed = rounded_both(blocks.reshape(CAP, D))
    attention = low_back(project(mixed, w_out) + b_out)
    first = layer_norm(tokens + attention, gain_attn, shift_attn)
    hidden = low_back(project(low(first), w_up) + b_up)
    active = low(jax.nn.gelu(hidden, approximate=False))
    branch = low_back(project(active, w_down) + b_down)
    result = layer_norm(first + branch, gain_ffn, shift_ffn)
    return jnp.where(valid[:, None], result, 0.0)

def reference(tokens, segment, counts, memory, w_query, b_query, w_key, w_value, b_value, w_out, b_out, gain_attn, shift_attn, w_up, b_up, w_down, b_down, gain_ffn, shift_ffn, cotangent):
    params = tuple((p.astype(jnp.float32) for p in (memory, w_query, b_query, w_key, w_value, b_value, w_out, b_out, gain_attn, shift_attn, w_up, b_up, w_down, b_down, gain_ffn, shift_ffn)))

    def whole(token_values, *weights):
        packs = (token_values.reshape(N_DP, CAP, D), segment.reshape(N_DP, CAP), counts)

        def one_pack(item):
            return pack_layer(weights, item)
        outs = lax.map(jax.checkpoint(one_pack), packs)
        return outs.reshape(N_DP * CAP, D)
    result, pullback = jax.vjp(whole, tokens.astype(jnp.float32), *params)
    grads = pullback(cotangent.astype(jnp.float32))
    return (result.astype(jnp.bfloat16), grads[0], grads[1], grads[2], grads[3], grads[4], grads[5], grads[6], grads[7], grads[8], grads[9], grads[10], grads[11], grads[12], grads[13], grads[14], grads[15], grads[16])
```

```python
import functools
import jax
import jax.numpy as jnp
from jax import lax
from jax.experimental import pallas as pl
from jax.experimental.pallas import tpu as pltpu
from jax.sharding import PartitionSpec as P

H = 8
HD = 64
HA = 80
EPS = 1e-05
BIG = 1e30
PARTS = 32
ROWS = 208
BQ = 256
BK = 256
MP = 32
F32 = jnp.float32
BF16 = jnp.bfloat16
VMEM_LIMIT = 60 << 20

V_BQ, V_BV, V_BO, V_GA, V_SA, V_BD, V_GF, V_SF = range(8)


def dot(left, right, lc, rc):
    return lax.dot_general(left, right, (((lc,), (rc,)), ((), ())), preferred_element_type=F32)


def params(**kw):
    return pltpu.CompilerParams(vmem_limit_bytes=VMEM_LIMIT, **kw)


def qkv_kernel(mem_rows, g_ref, tok_ref, seg_ref, cnt_ref, qa_ref, ka_ref, va_ref, km_ref, vm_ref, wt_ref):
    step = pl.program_id(0)
    rows = tok_ref.shape[0]
    small = g_ref[:, 48:64, :].reshape(512, 512)
    bq = small[:, 128 + V_BQ : 129 + V_BQ].astype(F32)
    bv = small[:, 128 + V_BV : 129 + V_BV].astype(F32)

    @pl.when(step == 0)
    def _():
        for j in range(3):
            wt_ref[512 * j : 512 * j + 512, :] = g_ref[:, 16 * j : 16 * j + 16, :].reshape(512, 512).T
        memt = small[:, 0:128]
        km = dot(wt_ref[512:1024, :], memt, 1, 0).astype(BF16)
        vm = (dot(wt_ref[1024:1536, :], memt, 1, 0) + bv).astype(BF16)
        frow = lax.broadcasted_iota(jnp.int32, (16, 128), 0)
        lane = lax.broadcasted_iota(jnp.int32, (16, 128), 1)
        kf = jnp.where(frow < 3, jnp.where(lane < mem_rows, 0.0, 1.0), jnp.where(frow < 6, 1.0, 0.0)).astype(BF16)
        vf = jnp.where(frow < 3, 1.0, 0.0).astype(BF16)
        for h in range(H):
            km_ref[h, 0:64, :] = km[64 * h : 64 * h + 64, :]
            km_ref[h, 64:80, :] = kf
            vm_ref[h, 0:64, :] = vm[64 * h : 64 * h + 64, :]
            vm_ref[h, 64:80, :] = vf

    tok = tok_ref[...]
    q = ((dot(wt_ref[0:512, :], tok, 1, 1) + bq).astype(BF16) * jnp.asarray(HD ** -0.5, BF16))
    k = dot(wt_ref[512:1024, :], tok, 1, 1).astype(BF16)
    v = (dot(wt_ref[1024:1536, :], tok, 1, 1) + bv).astype(BF16)
    frow = lax.broadcasted_iota(jnp.int32, (16, rows), 0)
    seg = jnp.broadcast_to(seg_ref[...], (16, rows))
    pos = lax.broadcasted_iota(jnp.int32, (16, rows), 1) + step * rows
    valid = pos < cnt_ref[0]
    qf = jnp.where((frow < 3) & (frow != seg), -BIG, 0.0).astype(BF16)
    kf = jnp.where(frow < 3, jnp.where(valid & (frow != seg), 0.0, 1.0), jnp.where(frow < 6, 1.0, 0.0)).astype(BF16)
    vf = jnp.where(frow < 3, 1.0, 0.0).astype(BF16)
    for h in range(H):
        s = slice(64 * h, 64 * h + 64)
        qa_ref[h, 0:64, :] = q[s]
        qa_ref[h, 64:80, :] = qf
        ka_ref[h, 0:64, :] = k[s]
        ka_ref[h, 64:80, :] = kf
        va_ref[h, 0:64, :] = v[s]
        va_ref[h, 64:80, :] = vf


def qkv(g, tokens, segment, counts, mem_rows):
    slots = tokens.shape[0]
    rb = 512
    out = [jax.ShapeDtypeStruct((H, HA, slots), BF16)] * 3 + [jax.ShapeDtypeStruct((H, HA, 128), BF16)] * 2
    blk = pl.BlockSpec((H, HA, rb), lambda i: (0, 0, i))
    mblk = pl.BlockSpec((H, HA, 128), lambda i: (0, 0, 0))
    return pl.pallas_call(
        functools.partial(qkv_kernel, mem_rows),
        grid=(slots // rb,),
        in_specs=[
            pl.BlockSpec((PARTS, 64, 512), lambda i: (0, 0, 0)),
            pl.BlockSpec((rb, 512), lambda i: (i, 0)),
            pl.BlockSpec((1, rb), lambda i: (0, i)),
            pl.BlockSpec(memory_space=pltpu.SMEM),
        ],
        out_specs=[blk, blk, blk, mblk, mblk],
        out_shape=out,
        scratch_shapes=[pltpu.VMEM((1536, 512), BF16)],
        compiler_params=params(),
        name="qkv",
    )(g, tokens, segment.reshape(1, slots), counts)


def key_range(seg, count, first, slots):
    r, c = seg.shape
    pos = lax.broadcasted_iota(jnp.int32, (r, c), 0) * c + lax.broadcasted_iota(jnp.int32, (r, c), 1)
    valid = pos < count
    last = jnp.minimum(first + BQ, count)
    low, high, start = jnp.int32(slots), jnp.int32(0), jnp.int32(0)
    for s in range(3):
        end = jnp.sum(jnp.where(valid & (seg <= s), 1.0, 0.0)).astype(jnp.int32)
        hit = (end > first) & (start < last) & (end > start)
        low = jnp.where(hit, jnp.minimum(low, start), low)
        high = jnp.where(hit, jnp.maximum(high, end), high)
        start = end
    begin = low // 128
    blocks = jnp.where(high > low, (high - begin * 128 + BK - 1) // BK, 0)
    begin = jnp.minimum(begin, slots // 128 - blocks * (BK // 128))
    return begin, blocks


def fwd_kernel(slots, seg_ref, cnt_ref, qa_ref, ka_ref, va_ref, km_ref, vm_ref, mix_ref, lse_ref, acc_ref, m_ref):
    begin, blocks = key_range(seg_ref[...], cnt_ref[0], pl.program_id(0) * BQ, slots)
    for h in range(H):
        s = dot(km_ref[h, :, 0:MP], qa_ref[h], 0, 0)
        top = jnp.max(s, axis=0, keepdims=True)
        p = jnp.exp(s - top).astype(BF16)
        acc_ref[h] = dot(vm_ref[h, :, 0:MP], p, 1, 0)
        m_ref[h : h + 1, :] = top

    @pl.loop(0, blocks)
    def _(j):
        ks = pl.ds(pl.multiple_of((begin + j * (BK // 128)) * 128, 128), BK)
        for h in range(H):
            s = dot(ka_ref[h, :, ks], qa_ref[h], 0, 0)
            old = m_ref[h : h + 1, :]
            top = jnp.maximum(old, jnp.max(s, axis=0, keepdims=True))
            p = jnp.exp(s - top).astype(BF16)
            acc_ref[h] = acc_ref[h] * jnp.exp(old - top) + dot(va_ref[h, :, ks], p, 1, 0)
            m_ref[h : h + 1, :] = top

    for h in range(H):
        total = acc_ref[h, 64:65, :]
        mix_ref[64 * h : 64 * h + 64, :] = (acc_ref[h, 0:64, :] / total).astype(BF16)
        lse_ref[h : h + 1, :] = m_ref[h : h + 1, :] + jnp.log(total)


def attend_forward(seg2, counts, qa, ka, va, km, vm):
    slots = qa.shape[2]
    full = pl.BlockSpec((H, HA, slots), lambda i: (0, 0, 0))
    mfull = pl.BlockSpec((H, HA, 128), lambda i: (0, 0, 0))
    return pl.pallas_call(
        functools.partial(fwd_kernel, slots),
        grid=(slots // BQ,),
        in_specs=[
            pl.BlockSpec(seg2.shape, lambda i: (0, 0)),
            pl.BlockSpec(memory_space=pltpu.SMEM),
            pl.BlockSpec((H, HA, BQ), lambda i: (0, 0, i)),
            full, full, mfull, mfull,
        ],
        out_specs=[pl.BlockSpec((512, BQ), lambda i: (0, i)), pl.BlockSpec((H, BQ), lambda i: (0, i))],
        out_shape=[jax.ShapeDtypeStruct((512, slots), BF16), jax.ShapeDtypeStruct((H, slots), F32)],
        scratch_shapes=[pltpu.VMEM((H, HA, BQ), F32), pltpu.VMEM((H, BQ), F32)],
        compiler_params=params(),
        name="attend_forward",
    )(seg2, counts, qa, ka, va, km, vm)


def norm_parts(value):
    mean = jnp.mean(value, axis=-1, keepdims=True)
    centred = value - mean
    rstd = lax.rsqrt(jnp.mean(centred * centred, axis=-1, keepdims=True) + EPS)
    return centred * rstd, rstd


def norm_grad(grad_hat, hat, rstd):
    return rstd * (
        grad_hat
        - jnp.mean(grad_hat, axis=-1, keepdims=True)
        - hat * jnp.mean(grad_hat * hat, axis=-1, keepdims=True)
    )


def colsum(value):
    return jnp.sum(value, axis=0, keepdims=True)


def mid_kernel(
    rb, cnt_ref, gs_ref, up_ref, dn_ref, wo_ref, mix_ref, tok_ref, cot_ref,
    out_ref, gfirst_ref, mgrad_ref, delta_ref, gw_ref, vec_ref, bup_ref,
    row_ref, rbup_ref, wup_ref, wdn_ref, aup_ref, adn_ref, ao_ref,
):
    step = pl.program_id(0)

    @pl.when(step == 0)
    def _():
        small = gs_ref[...].reshape(512, 512)
        row_ref[...] = small[:, 128:256].astype(F32).T
        bup = jnp.sum(gs_ref[:, 0:8, 256:512].astype(F32), axis=0)
        for v in range(8):
            rbup_ref[0:1, 256 * v : 256 * v + 256] = bup[v : v + 1, :]
        for c in range(4):
            wup_ref[:, 512 * c : 512 * c + 512] = up_ref[:, 16 * c : 16 * c + 16, :].reshape(512, 512)
        wdn_ref[...] = dn_ref[...].reshape(2048, 512)
        aup_ref[...] = jnp.zeros_like(aup_ref)
        adn_ref[...] = jnp.zeros_like(adn_ref)
        ao_ref[...] = jnp.zeros_like(ao_ref)
        vec_ref[...] = jnp.zeros_like(vec_ref)
        bup_ref[...] = jnp.zeros_like(bup_ref)

    wo = wo_ref[...].reshape(512, 512)

    def row(v):
        return row_ref[v : v + 1, :]

    mixt = mix_ref[...]
    attention = dot(mixt, wo, 0, 0) + row(V_BO)
    hat1, rstd1 = norm_parts(tok_ref[...].astype(F32) + attention)
    first = hat1 * row(V_GA) + row(V_SA)
    first_low = first.astype(BF16)
    hidden = dot(first_low, wup_ref[...], 1, 0) + rbup_ref[...]
    cdf = 0.5 + 0.5 * lax.erf(hidden * (2.0 ** -0.5))
    active = (hidden * cdf).astype(BF16)
    slope = cdf + hidden * jnp.exp(hidden * hidden * -0.5) * 0.3989422804014327
    branch = dot(active, wdn_ref[...], 1, 0) + row(V_BD)
    hat2, rstd2 = norm_parts(first + branch)
    valid = lax.broadcasted_iota(jnp.int32, (rb, 1), 0) + step * rb < cnt_ref[0]
    out_ref[...] = jnp.where(valid, hat2 * row(V_GF) + row(V_SF), 0.0).astype(BF16)

    seed = jnp.where(valid, cot_ref[...].astype(F32), 0.0)
    vec_ref[V_GF : V_GF + 1, :] += colsum(seed * hat2)
    vec_ref[V_SF : V_SF + 1, :] += colsum(seed)
    grad_second = norm_grad(seed * row(V_GF), hat2, rstd2)
    branch_grad = grad_second.astype(BF16)
    adn_ref[...] += dot(active, branch_grad, 0, 0)
    vec_ref[V_BD : V_BD + 1, :] += colsum(branch_grad.astype(F32))
    hidden_grad = (dot(branch_grad, wdn_ref[...], 1, 1) * slope).astype(BF16)
    aup_ref[...] += dot(first_low, hidden_grad, 0, 0)
    bup_ref[...] += colsum(hidden_grad.astype(F32))
    first_grad = grad_second + dot(hidden_grad, wup_ref[...], 1, 1)
    vec_ref[V_GA : V_GA + 1, :] += colsum(first_grad * hat1)
    vec_ref[V_SA : V_SA + 1, :] += colsum(first_grad)
    grad_first = norm_grad(first_grad * row(V_GA), hat1, rstd1)
    gfirst_ref[...] = grad_first
    attention_grad = grad_first.astype(BF16)
    vec_ref[V_BO : V_BO + 1, :] += colsum(attention_grad.astype(F32))
    ao_ref[...] += dot(mixt, attention_grad, 1, 0)
    mgrad = dot(wo, attention_grad, 1, 1).astype(BF16)
    mgrad_ref[...] = mgrad
    prod = mgrad.astype(F32) * mixt.astype(F32)
    for h in range(H):
        delta_ref[h : h + 1, :] = jnp.sum(prod[64 * h : 64 * h + 64, :], axis=0, keepdims=True)

    @pl.when(step == pl.num_programs(0) - 1)
    def _():
        gw_ref[:, 0:16, :] = ao_ref[...].astype(gw_ref.dtype).reshape(PARTS, 16, 512)
        for c in range(4):
            gw_ref[:, 16 + 16 * c : 32 + 16 * c, :] = (
                aup_ref[:, 512 * c : 512 * c + 512].astype(gw_ref.dtype).reshape(PARTS, 16, 512)
            )
        gw_ref[:, 80:144, :] = adn_ref[...].astype(gw_ref.dtype).reshape(PARTS, 64, 512)


def middle(g, counts, mixt, tokens, cotangent, rb=256):
    slots = tokens.shape[0]
    rows = pl.BlockSpec((rb, 512), lambda i: (i, 0))
    cols = pl.BlockSpec((512, rb), lambda i: (0, i))
    once = pl.Buffered(1)
    return pl.pallas_call(
        functools.partial(mid_kernel, rb),
        grid=(slots // rb,),
        in_specs=[
            pl.BlockSpec(memory_space=pltpu.SMEM),
            pl.BlockSpec((PARTS, 16, 512), lambda i: (0, 3, 0), pipeline_mode=once),
            pl.BlockSpec((PARTS, 64, 512), lambda i: (0, 1, 0), pipeline_mode=once),
            pl.BlockSpec((PARTS, 64, 512), lambda i: (0, 2, 0), pipeline_mode=once),
            pl.BlockSpec((PARTS, 16, 512), lambda i: (0, 12, 0), pipeline_mode=once),
            cols, rows, rows,
        ],
        out_specs=[
            rows, rows, cols,
            pl.BlockSpec((H, rb), lambda i: (0, i)),
            pl.BlockSpec((PARTS, 144, 512), lambda i: (0, 0, 0), pipeline_mode=once),
            pl.BlockSpec((8, 512), lambda i: (0, 0)),
            pl.BlockSpec((1, 2048), lambda i: (0, 0)),
        ],
        out_shape=[
            jax.ShapeDtypeStruct((slots, 512), BF16),
            jax.ShapeDtypeStruct((slots, 512), F32),
            jax.ShapeDtypeStruct((512, slots), BF16),
            jax.ShapeDtypeStruct((H, slots), F32),
            jax.ShapeDtypeStruct((PARTS, 144, 512), BF16),
            jax.ShapeDtypeStruct((8, 512), F32),
            jax.ShapeDtypeStruct((1, 2048), F32),
        ],
        scratch_shapes=[
            pltpu.VMEM((128, 512), F32),
            pltpu.VMEM((1, 2048), F32),
            pltpu.VMEM((512, 2048), BF16),
            pltpu.VMEM((2048, 512), BF16),
            pltpu.VMEM((512, 2048), F32),
            pltpu.VMEM((2048, 512), F32),
            pltpu.VMEM((512, 512), F32),
        ],
        compiler_params=params(),
        name="middle",
    )(counts, g, g, g, g, mixt, tokens, cotangent)


def split3(value):
    high = value.astype(BF16)
    rest = value - high.astype(F32)
    mid = rest.astype(BF16)
    return high, mid, (rest - mid.astype(F32)).astype(BF16)


def bwd_kernel(
    slots, seg_ref, cnt_ref, qa_ref, ka_ref, va_ref, km_ref, vm_ref, do_ref, lse_ref, delta_ref,
    dq_ref, dk_ref, dv_ref, dkm_ref, dvm_ref, q2_ref, do2_ref, dqa_ref, dka_ref, dva_ref, dkma_ref, dvma_ref,
):
    step = pl.program_id(0)
    begin, blocks = key_range(seg_ref[...], cnt_ref[0], step * BQ, slots)

    @pl.when(step == 0)
    def _():
        dka_ref[...] = jnp.zeros_like(dka_ref)
        dva_ref[...] = jnp.zeros_like(dva_ref)
        dkma_ref[...] = jnp.zeros_like(dkma_ref)
        dvma_ref[...] = jnp.zeros_like(dvma_ref)

    frow = lax.broadcasted_iota(jnp.int32, (16, BQ), 0)

    def feature(value, at):
        high, mid, low = (jnp.broadcast_to(v.astype(F32), (16, BQ)) for v in split3(value))
        return jnp.where(frow == at, high, jnp.where(frow == at + 1, mid, jnp.where(frow == at + 2, low, 0.0)))

    for h in range(H):
        q2_ref[h, 0:64, :] = qa_ref[h, 0:64, :]
        q2_ref[h, 64:80, :] = (qa_ref[h, 64:80, :].astype(F32) + feature(-lse_ref[h : h + 1, :], 3)).astype(BF16)
        do2_ref[h, 0:64, :] = do_ref[64 * h : 64 * h + 64, :]
        do2_ref[h, 64:80, :] = feature(-delta_ref[h : h + 1, :], 0).astype(BF16)

    for h in range(H):
        p = jnp.exp(dot(km_ref[h, :, 0:MP], q2_ref[h], 0, 0))
        ds = (p * dot(vm_ref[h, :, 0:MP], do2_ref[h], 0, 0)).astype(BF16)
        dvma_ref[h, :, 0:MP] += dot(do2_ref[h, 0:64, :], p.astype(BF16), 1, 1)
        dkma_ref[h, :, 0:MP] += dot(q2_ref[h, 0:64, :], ds, 1, 1)
        dqa_ref[h] = dot(km_ref[h, 0:64, 0:MP], ds, 1, 0)

    @pl.loop(0, blocks)
    def _(j):
        ks = pl.ds(pl.multiple_of((begin + j * (BK // 128)) * 128, 128), BK)
        for h in range(H):
            p = jnp.exp(dot(ka_ref[h, :, ks], q2_ref[h], 0, 0))
            ds = (p * dot(va_ref[h, :, ks], do2_ref[h], 0, 0)).astype(BF16)
            dva_ref[h, :, ks] += dot(do2_ref[h, 0:64, :], p.astype(BF16), 1, 1)
            dka_ref[h, :, ks] += dot(q2_ref[h, 0:64, :], ds, 1, 1)
            dqa_ref[h] += dot(ka_ref[h, 0:64, ks], ds, 1, 0)

    for h in range(H):
        dq_ref[64 * h : 64 * h + 64, :] = (dqa_ref[h] * HD ** -0.5).astype(BF16)

    @pl.when(step == pl.num_programs(0) - 1)
    def _():
        for h in range(H):
            s = slice(64 * h, 64 * h + 64)
            dk_ref[s, :] = dka_ref[h].astype(BF16)
            dv_ref[s, :] = dva_ref[h].astype(BF16)
            dkm_ref[s, :] = dkma_ref[h].astype(BF16)
            dvm_ref[s, :] = dvma_ref[h].astype(BF16)


def attend_backward(seg2, counts, qa, ka, va, km, vm, mgrad, lse, delta):
    slots = qa.shape[2]
    once = pl.Buffered(1)
    full = pl.BlockSpec((H, HA, slots), lambda i: (0, 0, 0), pipeline_mode=once)
    mfull = pl.BlockSpec((H, HA, 128), lambda i: (0, 0, 0))
    cols = pl.BlockSpec((512, BQ), lambda i: (0, i))
    stat = pl.BlockSpec((H, BQ), lambda i: (0, i))
    whole = pl.BlockSpec((512, slots), lambda i: (0, 0), pipeline_mode=once)
    mwhole = pl.BlockSpec((512, 128), lambda i: (0, 0))
    return pl.pallas_call(
        functools.partial(bwd_kernel, slots),
        grid=(slots // BQ,),
        in_specs=[
            pl.BlockSpec(seg2.shape, lambda i: (0, 0)),
            pl.BlockSpec(memory_space=pltpu.SMEM),
            pl.BlockSpec((H, HA, BQ), lambda i: (0, 0, i)),
            full, full, mfull, mfull, cols, stat, stat,
        ],
        out_specs=[cols, whole, whole, mwhole, mwhole],
        out_shape=[jax.ShapeDtypeStruct((512, slots), BF16)] * 3 + [jax.ShapeDtypeStruct((512, 128), BF16)] * 2,
        scratch_shapes=[
            pltpu.VMEM((H, HA, BQ), BF16),
            pltpu.VMEM((H, HA, BQ), BF16),
            pltpu.VMEM((H, HD, BQ), F32),
            pltpu.VMEM((H, HD, slots), F32),
            pltpu.VMEM((H, HD, slots), F32),
            pltpu.VMEM((H, HD, 128), F32),
            pltpu.VMEM((H, HD, 128), F32),
        ],
        compiler_params=params(),
        name="attend_backward",
    )(seg2, counts, qa, ka, va, km, vm, mgrad, lse, delta)


def tail_kernel(
    g_ref, tok_ref, dq_ref, dk_ref, dv_ref, dkm_ref, dvm_ref, gfirst_ref, vec_ref, bup_ref,
    gtok_ref, gw_ref, wt_ref, acc_ref, sum_ref,
):
    step = pl.program_id(0)

    @pl.when(step == 0)
    def _():
        for j in range(3):
            wt_ref[512 * j : 512 * j + 512, :] = g_ref[:, 16 * j : 16 * j + 16, :].reshape(512, 512).T
        memt = g_ref[:, 48:64, 0:128].reshape(512, 128)
        acc_ref[0:512, :] = jnp.zeros((512, 512), F32)
        acc_ref[512:1024, :] = dot(dkm_ref[...], memt, 1, 1)
        acc_ref[1024:1536, :] = dot(dvm_ref[...], memt, 1, 1)
        sum_ref[...] = jnp.zeros_like(sum_ref)
        sum_ref[:, 1:2] = jnp.sum(dvm_ref[...].astype(F32), axis=1, keepdims=True)

    tok = tok_ref[...]
    dq, dk, dv = dq_ref[...], dk_ref[...], dv_ref[...]
    acc_ref[0:512, :] += dot(dq, tok, 1, 0)
    acc_ref[512:1024, :] += dot(dk, tok, 1, 0)
    acc_ref[1024:1536, :] += dot(dv, tok, 1, 0)
    sum_ref[:, 0:1] += jnp.sum(dq.astype(F32), axis=1, keepdims=True)
    sum_ref[:, 1:2] += jnp.sum(dv.astype(F32), axis=1, keepdims=True)
    gtok_ref[...] = (
        gfirst_ref[...]
        + dot(dq, wt_ref[0:512, :], 0, 0)
        + dot(dk, wt_ref[512:1024, :], 0, 0)
        + dot(dv, wt_ref[1024:1536, :], 0, 0)
    )

    @pl.when(step == pl.num_programs(0) - 1)
    def _():
        for j in range(3):
            gw_ref[:, 16 * j : 16 * j + 16, :] = (
                acc_ref[512 * j : 512 * j + 512, :].T.astype(gw_ref.dtype).reshape(PARTS, 16, 512)
            )
        gmem = dot(wt_ref[512:1024, :], dkm_ref[...], 0, 0) + dot(wt_ref[1024:1536, :], dvm_ref[...], 0, 0)
        gw_ref[:, 48:64, 0:128] = gmem.astype(gw_ref.dtype).reshape(PARTS, 16, 128)
        lane = lax.broadcasted_iota(jnp.int32, (512, 128), 1)
        vecs = jnp.concatenate([vec_ref[...], jnp.zeros((120, 512), F32)], axis=0).T
        vecs = jnp.where(lane < 2, sum_ref[...], vecs)
        gw_ref[:, 48:64, 128:256] = vecs.astype(gw_ref.dtype).reshape(PARTS, 16, 128)
        rows = jnp.concatenate([bup_ref[0:1, 256 * v : 256 * v + 256] for v in range(8)] + [jnp.zeros((8, 256), F32)], axis=0)
        gw_ref[:, 48:64, 256:512] = jnp.broadcast_to(rows[None].astype(gw_ref.dtype), (PARTS, 16, 256))


def tail(g, tokens, dq, dk, dv, dkm, dvm, gfirst, vec, bup, rb=512):
    slots = tokens.shape[0]
    rows = pl.BlockSpec((rb, 512), lambda i: (i, 0))
    cols = pl.BlockSpec((512, rb), lambda i: (0, i))
    mwhole = pl.BlockSpec((512, 128), lambda i: (0, 0))
    once = pl.Buffered(1)
    return pl.pallas_call(
        tail_kernel,
        grid=(slots // rb,),
        in_specs=[
            pl.BlockSpec((PARTS, 64, 512), lambda i: (0, 0, 0), pipeline_mode=once),
            rows, cols, cols, cols, mwhole, mwhole, rows,
            pl.BlockSpec((8, 512), lambda i: (0, 0)),
            pl.BlockSpec((1, 2048), lambda i: (0, 0)),
        ],
        out_specs=[rows, pl.BlockSpec((PARTS, 64, 512), lambda i: (0, 0, 0), pipeline_mode=once)],
        out_shape=[jax.ShapeDtypeStruct((slots, 512), F32), jax.ShapeDtypeStruct((PARTS, 64, 512), BF16)],
        scratch_shapes=[
            pltpu.VMEM((1536, 512), BF16),
            pltpu.VMEM((1536, 512), F32),
            pltpu.VMEM((512, 128), F32),
        ],
        compiler_params=params(),
        name="tail",
    )(g, tokens, dq, dk, dv, dkm, dvm, gfirst, vec, bup)


NAMES = (
    "memory", "w_query", "b_query", "w_key", "w_value", "b_value", "w_out", "b_out", "gain_attn",
    "shift_attn", "w_up", "b_up", "w_down", "b_down", "gain_ffn", "shift_ffn",
)
VECTORS = ("b_query", "b_value", "b_out", "gain_attn", "shift_attn", "b_down", "gain_ffn", "shift_ffn")


def pad_lanes(value, lanes):
    return jnp.pad(value, ((0, 0), (0, lanes - value.shape[1])))


def pack_part(p, me):
    up = p["w_up"].reshape(16, 4, 512).transpose(1, 0, 2).reshape(64, 512)
    memory = pad_lanes(p["memory"].T, 128)
    vectors = pad_lanes(jnp.stack([p[name] for name in VECTORS], axis=1), 128)
    own = jnp.arange(2048) // 64 == me
    b_up = jnp.where(own, jnp.tile(p["b_up"], PARTS), 0).astype(BF16).reshape(8, 256)
    b_up = jnp.pad(b_up, ((0, 8), (0, 0)))
    small = jnp.concatenate([memory, vectors, b_up], axis=1)
    return jnp.concatenate([p["w_query"], p["w_key"], p["w_value"], small, up, p["w_down"], p["w_out"]], axis=0)


def pack_whole(p):
    parts = []
    for d in range(PARTS):
        mine = {}
        for name in NAMES:
            axis = 1 if name == "memory" else 0
            size = p[name].shape[axis] // PARTS
            mine[name] = lax.slice_in_dim(p[name], d * size, d * size + size, axis=axis)
        parts.append(pack_part(mine, d))
    return jnp.stack(parts)


def unpack_part(early, late, mem_rows, me):
    small = late[48:64]
    vectors = small[:, 128:256]
    b_up = small[0:8, 256:512].reshape(2048)
    out = {
        "memory": small[:, 0:mem_rows].T,
        "w_query": late[0:16],
        "w_key": late[16:32],
        "w_value": late[32:48],
        "w_out": early[0:16],
        "w_up": early[16:80].reshape(4, 16, 512).transpose(1, 0, 2).reshape(16, 2048),
        "w_down": early[80:144],
        "b_up": lax.dynamic_slice_in_dim(b_up, me * 64, 64),
    }
    for index, name in enumerate(VECTORS):
        out[name] = vectors[:, index]
    return out


def shards(n, tokens, segment, counts, *rest):
    p = dict(zip(NAMES, rest[:-1]))
    cotangent = rest[-1]
    slots = tokens.shape[0]
    mem_rows = p["memory"].shape[0]
    me = lax.axis_index("dp")
    if n == PARTS:
        g = lax.all_gather(pack_part(p, me), "dp", axis=0, tiled=False)
    else:
        g = pack_whole(
            {k: lax.all_gather(v, "dp", axis=1 if k == "memory" else 0, tiled=True) for k, v in p.items()}
        )
    seg2 = segment.reshape(slots // 128, 128)
    qa, ka, va, km, vm = qkv(g, tokens, segment, counts, mem_rows)
    mixt, lse = attend_forward(seg2, counts, qa, ka, va, km, vm)
    output, gfirst, mgrad, delta, early, vec, bup = middle(g, counts, mixt, tokens, cotangent)
    dq, dk, dv, dkm, dvm = attend_backward(seg2, counts, qa, ka, va, km, vm, mgrad, lse, delta)
    gtok, late = tail(g, tokens, dq, dk, dv, dkm, dvm, gfirst, vec, bup)
    if n == PARTS:
        early = lax.psum_scatter(early.astype(F32), "dp", scatter_dimension=0)
        late = lax.psum_scatter(late.astype(F32), "dp", scatter_dimension=0)
        grads = unpack_part(early, late, mem_rows, me)
    else:
        parts = [unpack_part(early[d].astype(F32), late[d].astype(F32), mem_rows, d) for d in range(PARTS)]
        grads = {}
        for name in NAMES:
            axis = 1 if name == "memory" else 0
            whole = jnp.concatenate([part[name] for part in parts], axis=axis)
            grads[name] = lax.psum_scatter(whole, "dp", scatter_dimension=axis, tiled=True)
    return (output, gtok) + tuple(grads[name] for name in NAMES)


def solution(mesh):
    n = mesh.shape["dp"]
    row, mat, mem = P("dp"), P("dp", None), P(None, "dp")
    spec = {name: mat if name.startswith("w_") else row for name in NAMES}
    spec["memory"] = mem
    weights = tuple(spec[name] for name in NAMES)
    return jax.shard_map(
        functools.partial(shards, n),
        mesh=mesh,
        in_specs=(mat, row, row) + weights + (mat,),
        out_specs=(mat, mat) + weights,
        check_vma=False,
    )
```

```python
import functools
import jax
import jax.numpy as jnp
from jax import lax
from jax.experimental import pallas as pl
from jax.experimental.pallas import tpu as pltpu
from jax.sharding import PartitionSpec as P

H = 8
HD = 64
HA = 80
EPS = 1e-05
BIG = 1e30
PARTS = 32
ROWS = 208
BQ = 256
BK = 256
MP = 32
F32 = jnp.float32
BF16 = jnp.bfloat16
VMEM_LIMIT = 60 << 20

V_BQ, V_BV, V_BO, V_GA, V_SA, V_BD, V_GF, V_SF = range(8)


def dot(left, right, lc, rc):
    return lax.dot_general(left, right, (((lc,), (rc,)), ((), ())), preferred_element_type=F32)


def params(**kw):
    return pltpu.CompilerParams(vmem_limit_bytes=VMEM_LIMIT, **kw)


def qkv_kernel(mem_rows, g_ref, tok_ref, seg_ref, cnt_ref, qa_ref, ka_ref, va_ref, km_ref, vm_ref, wt_ref):
    step = pl.program_id(0)
    rows = tok_ref.shape[0]
    small = g_ref[:, 48:64, :].reshape(512, 512)
    bq = small[:, 128 + V_BQ : 129 + V_BQ].astype(F32)
    bv = small[:, 128 + V_BV : 129 + V_BV].astype(F32)

    @pl.when(step == 0)
    def _():
        for j in range(3):
            wt_ref[512 * j : 512 * j + 512, :] = g_ref[:, 16 * j : 16 * j + 16, :].reshape(512, 512).T
        memt = small[:, 0:128]
        km = dot(wt_ref[512:1024, :], memt, 1, 0).astype(BF16)
        vm = (dot(wt_ref[1024:1536, :], memt, 1, 0) + bv).astype(BF16)
        frow = lax.broadcasted_iota(jnp.int32, (16, 128), 0)
        lane = lax.broadcasted_iota(jnp.int32, (16, 128), 1)
        kf = jnp.where(frow < 3, jnp.where(lane < mem_rows, 0.0, 1.0), jnp.where(frow < 6, 1.0, 0.0)).astype(BF16)
        vf = jnp.where(frow < 3, 1.0, 0.0).astype(BF16)
        for h in range(H):
            km_ref[h, 0:64, :] = km[64 * h : 64 * h + 64, :]
            km_ref[h, 64:80, :] = kf
            vm_ref[h, 0:64, :] = vm[64 * h : 64 * h + 64, :]
            vm_ref[h, 64:80, :] = vf

    tok = tok_ref[...]
    q = ((dot(wt_ref[0:512, :], tok, 1, 1) + bq).astype(BF16) * jnp.asarray(HD ** -0.5, BF16))
    k = dot(wt_ref[512:1024, :], tok, 1, 1).astype(BF16)
    v = (dot(wt_ref[1024:1536, :], tok, 1, 1) + bv).astype(BF16)
    frow = lax.broadcasted_iota(jnp.int32, (16, rows), 0)
    seg = jnp.broadcast_to(seg_ref[...], (16, rows))
    pos = lax.broadcasted_iota(jnp.int32, (16, rows), 1) + step * rows
    valid = pos < cnt_ref[0]
    qf = jnp.where((frow < 3) & (frow != seg), -BIG, 0.0).astype(BF16)
    kf = jnp.where(frow < 3, jnp.where(valid & (frow != seg), 0.0, 1.0), jnp.where(frow < 6, 1.0, 0.0)).astype(BF16)
    vf = jnp.where(frow < 3, 1.0, 0.0).astype(BF16)
    for h in range(H):
        s = slice(64 * h, 64 * h + 64)
        qa_ref[h, 0:64, :] = q[s]
        qa_ref[h, 64:80, :] = qf
        ka_ref[h, 0:64, :] = k[s]
        ka_ref[h, 64:80, :] = kf
        va_ref[h, 0:64, :] = v[s]
        va_ref[h, 64:80, :] = vf


def qkv(g, tokens, segment, counts, mem_rows):
    slots = tokens.shape[0]
    rb = 512
    out = [jax.ShapeDtypeStruct((H, HA, slots), BF16)] * 3 + [jax.ShapeDtypeStruct((H, HA, 128), BF16)] * 2
    blk = pl.BlockSpec((H, HA, rb), lambda i: (0, 0, i))
    mblk = pl.BlockSpec((H, HA, 128), lambda i: (0, 0, 0))
    return pl.pallas_call(
        functools.partial(qkv_kernel, mem_rows),
        grid=(slots // rb,),
        in_specs=[
            pl.BlockSpec((PARTS, 64, 512), lambda i: (0, 0, 0)),
            pl.BlockSpec((rb, 512), lambda i: (i, 0)),
            pl.BlockSpec((1, rb), lambda i: (0, i)),
            pl.BlockSpec(memory_space=pltpu.SMEM),
        ],
        out_specs=[blk, blk, blk, mblk, mblk],
        out_shape=out,
        scratch_shapes=[pltpu.VMEM((1536, 512), BF16)],
        compiler_params=params(),
        name="qkv",
    )(g, tokens, segment.reshape(1, slots), counts)


def key_range(seg, count, first, slots):
    r, c = seg.shape
    pos = lax.broadcasted_iota(jnp.int32, (r, c), 0) * c + lax.broadcasted_iota(jnp.int32, (r, c), 1)
    valid = pos < count
    last = jnp.minimum(first + BQ, count)
    low, high, start = jnp.int32(slots), jnp.int32(0), jnp.int32(0)
    for s in range(3):
        end = jnp.sum(jnp.where(valid & (seg <= s), 1.0, 0.0)).astype(jnp.int32)
        hit = (end > first) & (start < last) & (end > start)
        low = jnp.where(hit, jnp.minimum(low, start), low)
        high = jnp.where(hit, jnp.maximum(high, end), high)
        start = end
    begin = low // 128
    blocks = jnp.where(high > low, (high - begin * 128 + BK - 1) // BK, 0)
    begin = jnp.minimum(begin, slots // 128 - blocks * (BK // 128))
    return begin, blocks


def fwd_kernel(slots, seg_ref, cnt_ref, qa_ref, ka_ref, va_ref, km_ref, vm_ref, mix_ref, lse_ref, acc_ref, m_ref):
    begin, blocks = key_range(seg_ref[...], cnt_ref[0], pl.program_id(0) * BQ, slots)
    for h in range(H):
        s = dot(km_ref[h, :, 0:MP], qa_ref[h], 0, 0)
        top = jnp.max(s, axis=0, keepdims=True)
        p = jnp.exp(s - top).astype(BF16)
        acc_ref[h] = dot(vm_ref[h, :, 0:MP], p, 1, 0)
        m_ref[h : h + 1, :] = top

    @pl.loop(0, blocks)
    def _(j):
        ks = pl.ds(pl.multiple_of((begin + j * (BK // 128)) * 128, 128), BK)
        for h in range(H):
            s = dot(ka_ref[h, :, ks], qa_ref[h], 0, 0)
            old = m_ref[h : h + 1, :]
            top = jnp.maximum(old, jnp.max(s, axis=0, keepdims=True))
            p = jnp.exp(s - top).astype(BF16)
            acc_ref[h] = acc_ref[h] * jnp.exp(old - top) + dot(va_ref[h, :, ks], p, 1, 0)
            m_ref[h : h + 1, :] = top

    for h in range(H):
        total = acc_ref[h, 64:65, :]
        mix_ref[64 * h : 64 * h + 64, :] = (acc_ref[h, 0:64, :] / total).astype(BF16)
        lse_ref[h : h + 1, :] = m_ref[h : h + 1, :] + jnp.log(total)


def attend_forward(seg2, counts, qa, ka, va, km, vm):
    slots = qa.shape[2]
    full = pl.BlockSpec((H, HA, slots), lambda i: (0, 0, 0))
    mfull = pl.BlockSpec((H, HA, 128), lambda i: (0, 0, 0))
    return pl.pallas_call(
        functools.partial(fwd_kernel, slots),
        grid=(slots // BQ,),
        in_specs=[
            pl.BlockSpec(seg2.shape, lambda i: (0, 0)),
            pl.BlockSpec(memory_space=pltpu.SMEM),
            pl.BlockSpec((H, HA, BQ), lambda i: (0, 0, i)),
            full, full, mfull, mfull,
        ],
        out_specs=[pl.BlockSpec((512, BQ), lambda i: (0, i)), pl.BlockSpec((H, BQ), lambda i: (0, i))],
        out_shape=[jax.ShapeDtypeStruct((512, slots), BF16), jax.ShapeDtypeStruct((H, slots), F32)],
        scratch_shapes=[pltpu.VMEM((H, HA, BQ), F32), pltpu.VMEM((H, BQ), F32)],
        compiler_params=params(),
        name="attend_forward",
    )(seg2, counts, qa, ka, va, km, vm)


def norm_parts(value):
    mean = jnp.mean(value, axis=-1, keepdims=True)
    centred = value - mean
    rstd = lax.rsqrt(jnp.mean(centred * centred, axis=-1, keepdims=True) + EPS)
    return centred * rstd, rstd


def norm_grad(grad_hat, hat, rstd):
    return rstd * (
        grad_hat
        - jnp.mean(grad_hat, axis=-1, keepdims=True)
        - hat * jnp.mean(grad_hat * hat, axis=-1, keepdims=True)
    )


def colsum(value):
    return jnp.sum(value, axis=0, keepdims=True)


def mid_kernel(
    rb, cnt_ref, gs_ref, up_ref, dn_ref, wo_ref, mix_ref, tok_ref, cot_ref,
    out_ref, gfirst_ref, mgrad_ref, delta_ref, gw_ref, vec_ref, bup_ref,
    row_ref, rbup_ref, wup_ref, wdn_ref, aup_ref, adn_ref, ao_ref,
):
    step = pl.program_id(0)

    @pl.when(step == 0)
    def _():
        small = gs_ref[...].reshape(512, 512)
        row_ref[...] = small[:, 128:256].astype(F32).T
        bup = jnp.sum(gs_ref[:, 0:8, 256:512].astype(F32), axis=0)
        for v in range(8):
            rbup_ref[0:1, 256 * v : 256 * v + 256] = bup[v : v + 1, :]
        for c in range(4):
            wup_ref[:, 512 * c : 512 * c + 512] = up_ref[:, 16 * c : 16 * c + 16, :].reshape(512, 512)
        wdn_ref[...] = dn_ref[...].reshape(2048, 512)
        aup_ref[...] = jnp.zeros_like(aup_ref)
        adn_ref[...] = jnp.zeros_like(adn_ref)
        ao_ref[...] = jnp.zeros_like(ao_ref)
        vec_ref[...] = jnp.zeros_like(vec_ref)
        bup_ref[...] = jnp.zeros_like(bup_ref)

    wo = wo_ref[...].reshape(512, 512)

    def row(v):
        return row_ref[v : v + 1, :]

    mixt = mix_ref[...]
    attention = dot(mixt, wo, 0, 0) + row(V_BO)
    hat1, rstd1 = norm_parts(tok_ref[...].astype(F32) + attention)
    first = hat1 * row(V_GA) + row(V_SA)
    first_low = first.astype(BF16)
    hidden = dot(first_low, wup_ref[...], 1, 0) + rbup_ref[...]
    cdf = 0.5 + 0.5 * lax.erf(hidden * (2.0 ** -0.5))
    active = (hidden * cdf).astype(BF16)
    slope = cdf + hidden * jnp.exp(hidden * hidden * -0.5) * 0.3989422804014327
    branch = dot(active, wdn_ref[...], 1, 0) + row(V_BD)
    hat2, rstd2 = norm_parts(first + branch)
    valid = lax.broadcasted_iota(jnp.int32, (rb, 1), 0) + step * rb < cnt_ref[0]
    out_ref[...] = jnp.where(valid, hat2 * row(V_GF) + row(V_SF), 0.0).astype(BF16)

    seed = jnp.where(valid, cot_ref[...].astype(F32), 0.0)
    vec_ref[V_GF : V_GF + 1, :] += colsum(seed * hat2)
    vec_ref[V_SF : V_SF + 1, :] += colsum(seed)
    grad_second = norm_grad(seed * row(V_GF), hat2, rstd2)
    branch_grad = grad_second.astype(BF16)
    adn_ref[...] += dot(active, branch_grad, 0, 0)
    vec_ref[V_BD : V_BD + 1, :] += colsum(branch_grad.astype(F32))
    hidden_grad = (dot(branch_grad, wdn_ref[...], 1, 1) * slope).astype(BF16)
    aup_ref[...] += dot(first_low, hidden_grad, 0, 0)
    bup_ref[...] += colsum(hidden_grad.astype(F32))
    first_grad = grad_second + dot(hidden_grad, wup_ref[...], 1, 1)
    vec_ref[V_GA : V_GA + 1, :] += colsum(first_grad * hat1)
    vec_ref[V_SA : V_SA + 1, :] += colsum(first_grad)
    grad_first = norm_grad(first_grad * row(V_GA), hat1, rstd1)
    gfirst_ref[...] = grad_first
    attention_grad = grad_first.astype(BF16)
    vec_ref[V_BO : V_BO + 1, :] += colsum(attention_grad.astype(F32))
    ao_ref[...] += dot(mixt, attention_grad, 1, 0)
    mgrad = dot(wo, attention_grad, 1, 1).astype(BF16)
    mgrad_ref[...] = mgrad
    prod = mgrad.astype(F32) * mixt.astype(F32)
    for h in range(H):
        delta_ref[h : h + 1, :] = jnp.sum(prod[64 * h : 64 * h + 64, :], axis=0, keepdims=True)

    @pl.when(step == pl.num_programs(0) - 1)
    def _():
        gw_ref[:, 0:16, :] = ao_ref[...].astype(gw_ref.dtype).reshape(PARTS, 16, 512)
        for c in range(4):
            gw_ref[:, 16 + 16 * c : 32 + 16 * c, :] = (
                aup_ref[:, 512 * c : 512 * c + 512].astype(gw_ref.dtype).reshape(PARTS, 16, 512)
            )
        gw_ref[:, 80:144, :] = adn_ref[...].astype(gw_ref.dtype).reshape(PARTS, 64, 512)


def middle(g, counts, mixt, tokens, cotangent, rb=256):
    slots = tokens.shape[0]
    rows = pl.BlockSpec((rb, 512), lambda i: (i, 0))
    cols = pl.BlockSpec((512, rb), lambda i: (0, i))
    once = pl.Buffered(1)
    return pl.pallas_call(
        functools.partial(mid_kernel, rb),
        grid=(slots // rb,),
        in_specs=[
            pl.BlockSpec(memory_space=pltpu.SMEM),
            pl.BlockSpec((PARTS, 16, 512), lambda i: (0, 3, 0), pipeline_mode=once),
            pl.BlockSpec((PARTS, 64, 512), lambda i: (0, 1, 0), pipeline_mode=once),
            pl.BlockSpec((PARTS, 64, 512), lambda i: (0, 2, 0), pipeline_mode=once),
            pl.BlockSpec((PARTS, 16, 512), lambda i: (0, 12, 0), pipeline_mode=once),
            cols, rows, rows,
        ],
        out_specs=[
            rows, rows, cols,
            pl.BlockSpec((H, rb), lambda i: (0, i)),
            pl.BlockSpec((PARTS, 144, 512), lambda i: (0, 0, 0), pipeline_mode=once),
            pl.BlockSpec((8, 512), lambda i: (0, 0)),
            pl.BlockSpec((1, 2048), lambda i: (0, 0)),
        ],
        out_shape=[
            jax.ShapeDtypeStruct((slots, 512), BF16),
            jax.ShapeDtypeStruct((slots, 512), F32),
            jax.ShapeDtypeStruct((512, slots), BF16),
            jax.ShapeDtypeStruct((H, slots), F32),
            jax.ShapeDtypeStruct((PARTS, 144, 512), BF16),
            jax.ShapeDtypeStruct((8, 512), F32),
            jax.ShapeDtypeStruct((1, 2048), F32),
        ],
        scratch_shapes=[
            pltpu.VMEM((128, 512), F32),
            pltpu.VMEM((1, 2048), F32),
            pltpu.VMEM((512, 2048), BF16),
            pltpu.VMEM((2048, 512), BF16),
            pltpu.VMEM((512, 2048), F32),
            pltpu.VMEM((2048, 512), F32),
            pltpu.VMEM((512, 512), F32),
        ],
        compiler_params=params(),
        name="middle",
    )(counts, g, g, g, g, mixt, tokens, cotangent)


def split3(value):
    high = value.astype(BF16)
    rest = value - high.astype(F32)
    mid = rest.astype(BF16)
    return high, mid, (rest - mid.astype(F32)).astype(BF16)


def bwd_kernel(
    slots, seg_ref, cnt_ref, qa_ref, ka_ref, va_ref, km_ref, vm_ref, do_ref, lse_ref, delta_ref,
    dq_ref, dk_ref, dv_ref, dkm_ref, dvm_ref, q2_ref, do2_ref, dqa_ref, dka_ref, dva_ref, dkma_ref, dvma_ref,
):
    step = pl.program_id(0)
    begin, blocks = key_range(seg_ref[...], cnt_ref[0], step * BQ, slots)

    @pl.when(step == 0)
    def _():
        dka_ref[...] = jnp.zeros_like(dka_ref)
        dva_ref[...] = jnp.zeros_like(dva_ref)
        dkma_ref[...] = jnp.zeros_like(dkma_ref)
        dvma_ref[...] = jnp.zeros_like(dvma_ref)

    frow = lax.broadcasted_iota(jnp.int32, (16, BQ), 0)

    def feature(value, at):
        high, mid, low = (jnp.broadcast_to(v.astype(F32), (16, BQ)) for v in split3(value))
        return jnp.where(frow == at, high, jnp.where(frow == at + 1, mid, jnp.where(frow == at + 2, low, 0.0)))

    for h in range(H):
        q2_ref[h, 0:64, :] = qa_ref[h, 0:64, :]
        q2_ref[h, 64:80, :] = (qa_ref[h, 64:80, :].astype(F32) + feature(-lse_ref[h : h + 1, :], 3)).astype(BF16)
        do2_ref[h, 0:64, :] = do_ref[64 * h : 64 * h + 64, :]
        do2_ref[h, 64:80, :] = feature(-delta_ref[h : h + 1, :], 0).astype(BF16)

    for h in range(H):
        p = jnp.exp(dot(km_ref[h, :, 0:MP], q2_ref[h], 0, 0))
        ds = (p * dot(vm_ref[h, :, 0:MP], do2_ref[h], 0, 0)).astype(BF16)
        dvma_ref[h, :, 0:MP] += dot(do2_ref[h, 0:64, :], p.astype(BF16), 1, 1)
        dkma_ref[h, :, 0:MP] += dot(q2_ref[h, 0:64, :], ds, 1, 1)
        dqa_ref[h] = dot(km_ref[h, 0:64, 0:MP], ds, 1, 0)

    @pl.loop(0, blocks)
    def _(j):
        ks = pl.ds(pl.multiple_of((begin + j * (BK // 128)) * 128, 128), BK)
        for h in range(H):
            p = jnp.exp(dot(ka_ref[h, :, ks], q2_ref[h], 0, 0))
            ds = (p * dot(va_ref[h, :, ks], do2_ref[h], 0, 0)).astype(BF16)
            dva_ref[h, :, ks] += dot(do2_ref[h, 0:64, :], p.astype(BF16), 1, 1)
            dka_ref[h, :, ks] += dot(q2_ref[h, 0:64, :], ds, 1, 1)
            dqa_ref[h] += dot(ka_ref[h, 0:64, ks], ds, 1, 0)

    for h in range(H):
        dq_ref[64 * h : 64 * h + 64, :] = (dqa_ref[h] * HD ** -0.5).astype(BF16)

    @pl.when(step == pl.num_programs(0) - 1)
    def _():
        for h in range(H):
            s = slice(64 * h, 64 * h + 64)
            dk_ref[s, :] = dka_ref[h].astype(BF16)
            dv_ref[s, :] = dva_ref[h].astype(BF16)
            dkm_ref[s, :] = dkma_ref[h].astype(BF16)
            dvm_ref[s, :] = dvma_ref[h].astype(BF16)


def attend_backward(seg2, counts, qa, ka, va, km, vm, mgrad, lse, delta):
    slots = qa.shape[2]
    once = pl.Buffered(1)
    full = pl.BlockSpec((H, HA, slots), lambda i: (0, 0, 0), pipeline_mode=once)
    mfull = pl.BlockSpec((H, HA, 128), lambda i: (0, 0, 0))
    cols = pl.BlockSpec((512, BQ), lambda i: (0, i))
    stat = pl.BlockSpec((H, BQ), lambda i: (0, i))
    whole = pl.BlockSpec((512, slots), lambda i: (0, 0), pipeline_mode=once)
    mwhole = pl.BlockSpec((512, 128), lambda i: (0, 0))
    return pl.pallas_call(
        functools.partial(bwd_kernel, slots),
        grid=(slots // BQ,),
        in_specs=[
            pl.BlockSpec(seg2.shape, lambda i: (0, 0)),
            pl.BlockSpec(memory_space=pltpu.SMEM),
            pl.BlockSpec((H, HA, BQ), lambda i: (0, 0, i)),
            full, full, mfull, mfull, cols, stat, stat,
        ],
        out_specs=[cols, whole, whole, mwhole, mwhole],
        out_shape=[jax.ShapeDtypeStruct((512, slots), BF16)] * 3 + [jax.ShapeDtypeStruct((512, 128), BF16)] * 2,
        scratch_shapes=[
            pltpu.VMEM((H, HA, BQ), BF16),
            pltpu.VMEM((H, HA, BQ), BF16),
            pltpu.VMEM((H, HD, BQ), F32),
            pltpu.VMEM((H, HD, slots), F32),
            pltpu.VMEM((H, HD, slots), F32),
            pltpu.VMEM((H, HD, 128), F32),
            pltpu.VMEM((H, HD, 128), F32),
        ],
        compiler_params=params(),
        name="attend_backward",
    )(seg2, counts, qa, ka, va, km, vm, mgrad, lse, delta)


def tail_kernel(
    g_ref, tok_ref, dq_ref, dk_ref, dv_ref, dkm_ref, dvm_ref, gfirst_ref, vec_ref, bup_ref,
    gtok_ref, gw_ref, wt_ref, acc_ref, sum_ref,
):
    step = pl.program_id(0)

    @pl.when(step == 0)
    def _():
        for j in range(3):
            wt_ref[512 * j : 512 * j + 512, :] = g_ref[:, 16 * j : 16 * j + 16, :].reshape(512, 512).T
        memt = g_ref[:, 48:64, 0:128].reshape(512, 128)
        acc_ref[0:512, :] = jnp.zeros((512, 512), F32)
        acc_ref[512:1024, :] = dot(dkm_ref[...], memt, 1, 1)
        acc_ref[1024:1536, :] = dot(dvm_ref[...], memt, 1, 1)
        sum_ref[...] = jnp.zeros_like(sum_ref)
        sum_ref[:, 1:2] = jnp.sum(dvm_ref[...].astype(F32), axis=1, keepdims=True)

    tok = tok_ref[...]
    dq, dk, dv = dq_ref[...], dk_ref[...], dv_ref[...]
    acc_ref[0:512, :] += dot(dq, tok, 1, 0)
    acc_ref[512:1024, :] += dot(dk, tok, 1, 0)
    acc_ref[1024:1536, :] += dot(dv, tok, 1, 0)
    sum_ref[:, 0:1] += jnp.sum(dq.astype(F32), axis=1, keepdims=True)
    sum_ref[:, 1:2] += jnp.sum(dv.astype(F32), axis=1, keepdims=True)
    gtok_ref[...] = (
        gfirst_ref[...]
        + dot(dq, wt_ref[0:512, :], 0, 0)
        + dot(dk, wt_ref[512:1024, :], 0, 0)
        + dot(dv, wt_ref[1024:1536, :], 0, 0)
    )

    @pl.when(step == pl.num_programs(0) - 1)
    def _():
        for j in range(3):
            gw_ref[:, 16 * j : 16 * j + 16, :] = (
                acc_ref[512 * j : 512 * j + 512, :].T.astype(gw_ref.dtype).reshape(PARTS, 16, 512)
            )
        gmem = dot(wt_ref[512:1024, :], dkm_ref[...], 0, 0) + dot(wt_ref[1024:1536, :], dvm_ref[...], 0, 0)
        gw_ref[:, 48:64, 0:128] = gmem.astype(gw_ref.dtype).reshape(PARTS, 16, 128)
        lane = lax.broadcasted_iota(jnp.int32, (512, 128), 1)
        vecs = jnp.concatenate([vec_ref[...], jnp.zeros((120, 512), F32)], axis=0).T
        vecs = jnp.where(lane < 2, sum_ref[...], vecs)
        gw_ref[:, 48:64, 128:256] = vecs.astype(gw_ref.dtype).reshape(PARTS, 16, 128)
        rows = jnp.concatenate([bup_ref[0:1, 256 * v : 256 * v + 256] for v in range(8)] + [jnp.zeros((8, 256), F32)], axis=0)
        gw_ref[:, 48:64, 256:512] = jnp.broadcast_to(rows[None].astype(gw_ref.dtype), (PARTS, 16, 256))


def tail(g, tokens, dq, dk, dv, dkm, dvm, gfirst, vec, bup, rb=512):
    slots = tokens.shape[0]
    rows = pl.BlockSpec((rb, 512), lambda i: (i, 0))
    cols = pl.BlockSpec((512, rb), lambda i: (0, i))
    mwhole = pl.BlockSpec((512, 128), lambda i: (0, 0))
    once = pl.Buffered(1)
    return pl.pallas_call(
        tail_kernel,
        grid=(slots // rb,),
        in_specs=[
            pl.BlockSpec((PARTS, 64, 512), lambda i: (0, 0, 0), pipeline_mode=once),
            rows, cols, cols, cols, mwhole, mwhole, rows,
            pl.BlockSpec((8, 512), lambda i: (0, 0)),
            pl.BlockSpec((1, 2048), lambda i: (0, 0)),
        ],
        out_specs=[rows, pl.BlockSpec((PARTS, 64, 512), lambda i: (0, 0, 0), pipeline_mode=once)],
        out_shape=[jax.ShapeDtypeStruct((slots, 512), F32), jax.ShapeDtypeStruct((PARTS, 64, 512), BF16)],
        scratch_shapes=[
            pltpu.VMEM((1536, 512), BF16),
            pltpu.VMEM((1536, 512), F32),
            pltpu.VMEM((512, 128), F32),
        ],
        compiler_params=params(),
        name="tail",
    )(g, tokens, dq, dk, dv, dkm, dvm, gfirst, vec, bup)


MESH = pl.DeviceIdType.MESH
AXES = {"z": (8, 4), "y": (4, 2), "x": (2, 2)}
LAYOUT = ("z", "y", "x")


class Place:
    def __init__(self):
        me = lax.axis_index("dp")
        self.me = me
        self.core = me % 2
        self.partner = me + 1 - 2 * self.core
        self.at = {a: (me // stride) % length for a, (stride, length) in AXES.items()}
        self.mine = tuple(self.at[a] for a in LAYOUT)

    def other(self, axis, distance):
        stride, length = AXES[axis]
        j = (self.at[axis] + distance) % length
        return j, self.me + (j - self.at[axis]) * stride

    def greet(self):
        barrier = pltpu.get_barrier_semaphore()
        peers = [self.partner]
        for axis in LAYOUT:
            peers += [self.other(axis, d)[1] for d in range(1, AXES[axis][1])]
        for peer in peers:
            pl.semaphore_signal(barrier, inc=1, device_id=(peer,), device_id_type=MESH)
        pl.semaphore_wait(barrier, len(peers))


class Copies:
    def __init__(self, send, recv):
        self.send, self.recv, self.count, self.open = send, recv, 0, []

    def number(self):
        self.count += 1
        return self.count - 1

    def make(self, src, dst, number, device):
        return pltpu.make_async_remote_copy(
            src_ref=src, dst_ref=dst, send_sem=self.send.at[number], recv_sem=self.recv.at[number],
            device_id=(device,), device_id_type=MESH,
        )

    def start(self, src, dst, number, device):
        copy = self.make(src, dst, number, device)
        copy.start()
        self.open.append(copy)

    def landed(self, block, number, device):
        self.make(block, block, number, device).wait_recv()

    def finish(self):
        for copy in self.open:
            copy.wait_send()
        self.open = []


def run_events(parts):
    live = []
    for index, part in enumerate(parts):
        live.append([next(part), index, part])
    while live:
        live.sort(key=lambda item: item[:2])
        item = live[0]
        try:
            item[0] = next(item[2])
        except StopIteration:
            live.pop(0)


LOAD = {2: 1.0, 4: 4.0}
HOP = 120.0


def gather_part(place, copies, own, whole, rows, order, arrivals):
    size, known, clock, done = rows.stop - rows.start, 1, 0.0, ()

    def block(axis, j, core):
        index = tuple(j if a == axis else (slice(None) if a in done else place.at[a]) for a in LAYOUT)
        return whole.at[index + (core, rows)]

    for axis in order:
        length = AXES[axis][1]
        numbers = [copies.number() for _ in range(2 * length - 2)]
        here = block(axis, place.at[axis], place.core)
        for d in range(1, length):
            copies.start(here if done else own.at[rows], here, numbers[d - 1], place.other(axis, d)[1])
        clock += LOAD[length] * known * size + HOP
        yield clock
        for d in range(1, length):
            j, device = place.other(axis, length - d)
            there = block(axis, j, place.core)
            copies.landed(there, numbers[d - 1], device)
            copies.start(there, there, numbers[length - 2 + d], place.partner)
            arrivals.append((block(axis, j, 1 - place.core), numbers[length - 2 + d]))
        done += (axis,)
        known *= length


def gather_all(place, copies, own, whole, parts):
    arrivals = []
    for rows, _ in parts:
        number = copies.number()
        copies.start(own.at[rows], whole.at[place.mine + (place.core, rows)], number, place.partner)
        arrivals.append((whole.at[place.mine + (1 - place.core, rows)], number))
    run_events([gather_part(place, copies, own, whole, rows, order, arrivals) for rows, order in parts])
    return arrivals


GATHER_PARTS = (
    (slice(0, 32), "zxy"),
    (slice(32, 64), "zyx"),
    (slice(64, 96), "yzx"),
    (slice(96, 128), "xzy"),
    (slice(128, 160), "zxy"),
    (slice(160, 208), "zyx"),
)
GATHER_COPIES = 11 * len(GATHER_PARTS)


def gather_kernel(parts, own_ref, whole_ref, send, recv, local):
    place = Place()
    place.greet()
    copies = Copies(send, recv)
    keep = pltpu.make_async_copy(own_ref, whole_ref.at[place.mine + (place.core,)], local)
    keep.start()
    keep.wait()
    arrivals = gather_all(place, copies, own_ref, whole_ref, parts)
    for block, number in arrivals:
        copies.landed(block, number, place.partner)
    copies.finish()


def gather(packed):
    whole = pl.pallas_call(
        functools.partial(gather_kernel, GATHER_PARTS),
        in_specs=[pl.BlockSpec(memory_space=pltpu.VMEM)],
        out_specs=pl.BlockSpec(memory_space=pl.ANY),
        out_shape=jax.ShapeDtypeStruct((4, 2, 2, 2, ROWS, 512), BF16),
        scratch_shapes=[
            pltpu.SemaphoreType.DMA((GATHER_COPIES,)),
            pltpu.SemaphoreType.DMA((GATHER_COPIES,)),
            pltpu.SemaphoreType.DMA,
        ],
        compiler_params=params(collective_id=0, has_side_effects=True),
        name="gather",
    )(packed)
    return whole.reshape(PARTS, ROWS, 512)


def scatter_part(place, copies, acc, slots, out, rows, order):
    size, clock, done = rows.stop - rows.start, 0.0, ()
    left = 16

    def block(axis, j):
        index = tuple(j if a == axis else (place.at[a] if a in done else slice(None)) for a in LAYOUT)
        return index + (rows,)

    for axis in order:
        length = AXES[axis][1]
        left //= length
        numbers = [copies.number() for _ in range(length - 1)]
        for d in range(1, length):
            j, device = place.other(axis, d)
            copies.start(acc.at[block(axis, j)], slots[axis, d], numbers[d - 1], device)
        clock += LOAD[length] * left * size + HOP
        yield clock
        for d in range(1, length):
            copies.landed(slots[axis, d], numbers[d - 1], place.partner)
        mine = block(axis, place.at[axis])
        total = acc[mine].astype(F32)
        for d in range(1, length):
            total = total + slots[axis, d][...].astype(F32)
        if axis == order[-1]:
            out[rows, :] = total
        else:
            acc[mine] = total.astype(BF16)
        done += (axis,)


SCATTER_PARTS = (
    (slice(64, 96), "yxz"),
    (slice(96, 128), "xyz"),
    (slice(128, 144), "xzy"),
    (slice(144, 160), "yzx"),
    (slice(160, 176), "xzy"),
    (slice(176, 208), "yxz"),
    (slice(0, 32), "xyz"),
    (slice(32, 64), "yxz"),
)
SCATTER_COPIES = 6 * len(SCATTER_PARTS)


def slot_shapes(parts):
    shapes = {}
    for number, (rows, order) in enumerate(parts):
        left = ["z", "y", "x"]
        for axis in order:
            left.remove(axis)
            shape = tuple(AXES[a][1] for a in LAYOUT if a in left) + (rows.stop - rows.start, 512)
            for d in range(1, AXES[axis][1]):
                shapes[number, axis, d] = shape
    return shapes


def scatter_kernel(all_parts, late_ref, early_ref, out_ref, acc, other, send, recv, local, *landing):
    place = Place()
    slots = dict(zip(slot_shapes(all_parts), landing))

    def source(rows, core):
        if rows.start < 64:
            return late_ref.at[:, :, :, core, rows]
        return early_ref.at[:, :, :, core, slice(rows.start - 64, rows.stop - 64)]

    loads = [
        pltpu.make_async_copy(source(rows, place.core), acc.at[:, :, :, rows], local.at[index])
        for index, (rows, _) in enumerate(all_parts)
    ]
    place.greet()
    copies = Copies(send, recv)
    numbers = [copies.number() for _ in all_parts]
    for load, number, (rows, _) in zip(loads, numbers, all_parts):
        copies.start(source(rows, 1 - place.core), other.at[:, :, :, rows], number, place.partner)
        load.start()
    parts = []
    for index, (rows, order) in enumerate(all_parts):
        loads[index].wait()
        copies.landed(other.at[:, :, :, rows], numbers[index], place.partner)

        @pl.loop(0, 4)
        def _(z):
            acc[z, :, :, rows] = (acc[z, :, :, rows].astype(F32) + other[z, :, :, rows].astype(F32)).astype(BF16)

        mine = {key[1:]: slot for key, slot in slots.items() if key[0] == index}
        parts.append(scatter_part(place, copies, acc, mine, out_ref, rows, order))
        next(parts[-1])
    run_events(parts)
    copies.finish()


def scatter(late, early):
    shapes = slot_shapes(SCATTER_PARTS)
    return pl.pallas_call(
        functools.partial(scatter_kernel, SCATTER_PARTS),
        in_specs=[pl.BlockSpec(memory_space=pl.ANY)] * 2,
        out_specs=pl.BlockSpec(memory_space=pltpu.VMEM),
        out_shape=jax.ShapeDtypeStruct((ROWS, 512), F32),
        scratch_shapes=[
            pltpu.VMEM((4, 2, 2, ROWS, 512), BF16),
            pltpu.VMEM((4, 2, 2, ROWS, 512), BF16),
            pltpu.SemaphoreType.DMA((SCATTER_COPIES,)),
            pltpu.SemaphoreType.DMA((SCATTER_COPIES,)),
            pltpu.SemaphoreType.DMA((len(SCATTER_PARTS),)),
        ]
        + [pltpu.VMEM(shape, BF16) for shape in shapes.values()],
        compiler_params=params(collective_id=1, has_side_effects=True),
        name="scatter",
    )(late.reshape(4, 2, 2, 2, 64, 512), early.reshape(4, 2, 2, 2, 144, 512))


NAMES = (
    "memory", "w_query", "b_query", "w_key", "w_value", "b_value", "w_out", "b_out", "gain_attn",
    "shift_attn", "w_up", "b_up", "w_down", "b_down", "gain_ffn", "shift_ffn",
)
VECTORS = ("b_query", "b_value", "b_out", "gain_attn", "shift_attn", "b_down", "gain_ffn", "shift_ffn")


def pad_lanes(value, lanes):
    return jnp.pad(value, ((0, 0), (0, lanes - value.shape[1])))


def pack_part(p, me):
    up = p["w_up"].reshape(16, 4, 512).transpose(1, 0, 2).reshape(64, 512)
    memory = pad_lanes(p["memory"].T, 128)
    vectors = pad_lanes(jnp.stack([p[name] for name in VECTORS], axis=1), 128)
    own = jnp.arange(2048) // 64 == me
    b_up = jnp.where(own, jnp.tile(p["b_up"], PARTS), 0).astype(BF16).reshape(8, 256)
    b_up = jnp.pad(b_up, ((0, 8), (0, 0)))
    small = jnp.concatenate([memory, vectors, b_up], axis=1)
    return jnp.concatenate([p["w_query"], p["w_key"], p["w_value"], small, up, p["w_down"], p["w_out"]], axis=0)


def pack_whole(p):
    parts = []
    for d in range(PARTS):
        mine = {}
        for name in NAMES:
            axis = 1 if name == "memory" else 0
            size = p[name].shape[axis] // PARTS
            mine[name] = lax.slice_in_dim(p[name], d * size, d * size + size, axis=axis)
        parts.append(pack_part(mine, d))
    return jnp.stack(parts)


def unpack_part(early, late, mem_rows, me):
    small = late[48:64]
    vectors = small[:, 128:256]
    b_up = small[0:8, 256:512].reshape(2048)
    out = {
        "memory": small[:, 0:mem_rows].T,
        "w_query": late[0:16],
        "w_key": late[16:32],
        "w_value": late[32:48],
        "w_out": early[0:16],
        "w_up": early[16:80].reshape(4, 16, 512).transpose(1, 0, 2).reshape(16, 2048),
        "w_down": early[80:144],
        "b_up": lax.dynamic_slice_in_dim(b_up, me * 64, 64),
    }
    for index, name in enumerate(VECTORS):
        out[name] = vectors[:, index]
    return out


def shards(n, tokens, segment, counts, *rest):
    p = dict(zip(NAMES, rest[:-1]))
    cotangent = rest[-1]
    slots = tokens.shape[0]
    mem_rows = p["memory"].shape[0]
    me = lax.axis_index("dp")
    if n == PARTS:
        g = gather(pack_part(p, me))
    else:
        g = pack_whole(
            {k: lax.all_gather(v, "dp", axis=1 if k == "memory" else 0, tiled=True) for k, v in p.items()}
        )
    seg2 = segment.reshape(slots // 128, 128)
    qa, ka, va, km, vm = qkv(g, tokens, segment, counts, mem_rows)
    mixt, lse = attend_forward(seg2, counts, qa, ka, va, km, vm)
    output, gfirst, mgrad, delta, early, vec, bup = middle(g, counts, mixt, tokens, cotangent)
    dq, dk, dv, dkm, dvm = attend_backward(seg2, counts, qa, ka, va, km, vm, mgrad, lse, delta)
    gtok, late = tail(g, tokens, dq, dk, dv, dkm, dvm, gfirst, vec, bup)
    if n == PARTS:
        owned = scatter(late, early)
        grads = unpack_part(owned[64:ROWS], owned[0:64], mem_rows, me)
    else:
        parts = [unpack_part(early[d].astype(F32), late[d].astype(F32), mem_rows, d) for d in range(PARTS)]
        grads = {}
        for name in NAMES:
            axis = 1 if name == "memory" else 0
            whole = jnp.concatenate([part[name] for part in parts], axis=axis)
            grads[name] = lax.psum_scatter(whole, "dp", scatter_dimension=axis, tiled=True)
    return (output, gtok) + tuple(grads[name] for name in NAMES)


def solution(mesh):
    n = mesh.shape["dp"]
    row, mat, mem = P("dp"), P("dp", None), P(None, "dp")
    spec = {name: mat if name.startswith("w_") else row for name in NAMES}
    spec["memory"] = mem
    weights = tuple(spec[name] for name in NAMES)
    return jax.shard_map(
        functools.partial(shards, n),
        mesh=mesh,
        in_specs=(mat, row, row) + weights + (mat,),
        out_specs=(mat, mat) + weights,
        check_vma=False,
    )
```

```python
import functools
import jax
import jax.numpy as jnp
from jax import lax
from jax.experimental import pallas as pl
from jax.experimental.pallas import tpu as pltpu
from jax.sharding import PartitionSpec as P

H = 8
HD = 64
HA = 80
EPS = 1e-05
BIG = 1e30
PARTS = 32
ROWS = 208
BQ = 256
BK = 256
MP = 32
F32 = jnp.float32
BF16 = jnp.bfloat16
VMEM_LIMIT = 60 << 20

V_BQ, V_BV, V_BO, V_GA, V_SA, V_BD, V_GF, V_SF = range(8)


def dot(left, right, lc, rc):
    return lax.dot_general(left, right, (((lc,), (rc,)), ((), ())), preferred_element_type=F32)


def params(**kw):
    return pltpu.CompilerParams(vmem_limit_bytes=VMEM_LIMIT, **kw)


def head_block(rows, features):
    block = jnp.concatenate([rows, features], axis=0)
    return block, jnp.concatenate([block, jnp.zeros((128 - HA, rows.shape[1]), BF16)], axis=0).T


def qkv_kernel(
    mem_rows, g_ref, tok_ref, seg_ref, cnt_ref,
    qa_ref, ka_ref, va_ref, kn_ref, vn_ref, km_ref, vm_ref, kmn_ref, vmn_ref, wt_ref,
):
    step = pl.program_id(0)
    rows = tok_ref.shape[0]
    small = g_ref[:, 48:64, :].reshape(512, 512)
    bq = small[:, 128 + V_BQ : 129 + V_BQ].astype(F32)
    bv = small[:, 128 + V_BV : 129 + V_BV].astype(F32)

    @pl.when(step == 0)
    def _():
        for j in range(3):
            wt_ref[512 * j : 512 * j + 512, :] = g_ref[:, 16 * j : 16 * j + 16, :].reshape(512, 512).T
        memt = small[:, 0:128]
        km = dot(wt_ref[512:1024, :], memt, 1, 0).astype(BF16)
        vm = (dot(wt_ref[1024:1536, :], memt, 1, 0) + bv).astype(BF16)
        frow = lax.broadcasted_iota(jnp.int32, (16, 128), 0)
        lane = lax.broadcasted_iota(jnp.int32, (16, 128), 1)
        kf = jnp.where(frow < 3, jnp.where(lane < mem_rows, 0.0, 1.0), jnp.where(frow < 6, 1.0, 0.0)).astype(BF16)
        vf = jnp.where(frow < 3, 1.0, 0.0).astype(BF16)
        for h in range(H):
            km_ref[h], turned = head_block(km[64 * h : 64 * h + 64, :], kf)
            kmn_ref[h] = turned[0:MP]
            vm_ref[h], turned = head_block(vm[64 * h : 64 * h + 64, :], vf)
            vmn_ref[h] = turned[0:MP]

    tok = tok_ref[...]
    q = ((dot(wt_ref[0:512, :], tok, 1, 1) + bq).astype(BF16) * jnp.asarray(HD ** -0.5, BF16))
    k = dot(wt_ref[512:1024, :], tok, 1, 1).astype(BF16)
    v = (dot(wt_ref[1024:1536, :], tok, 1, 1) + bv).astype(BF16)
    frow = lax.broadcasted_iota(jnp.int32, (16, rows), 0)
    seg = jnp.broadcast_to(seg_ref[...], (16, rows))
    pos = lax.broadcasted_iota(jnp.int32, (16, rows), 1) + step * rows
    valid = pos < cnt_ref[0]
    qf = jnp.where((frow < 3) & (frow != seg), -BIG, 0.0).astype(BF16)
    kf = jnp.where(frow < 3, jnp.where(valid & (frow != seg), 0.0, 1.0), jnp.where(frow < 6, 1.0, 0.0)).astype(BF16)
    vf = jnp.where(frow < 3, 1.0, 0.0).astype(BF16)
    for h in range(H):
        s = slice(64 * h, 64 * h + 64)
        qa_ref[h, 0:64, :] = q[s]
        qa_ref[h, 64:80, :] = qf
        ka_ref[h], kn_ref[h] = head_block(k[s], kf)
        va_ref[h], vn_ref[h] = head_block(v[s], vf)


def qkv(g, tokens, segment, counts, mem_rows):
    slots = tokens.shape[0]
    rb = 512
    wide = jax.ShapeDtypeStruct((H, HA, slots), BF16)
    tall = jax.ShapeDtypeStruct((H, slots, 128), BF16)
    mwide = jax.ShapeDtypeStruct((H, HA, 128), BF16)
    mtall = jax.ShapeDtypeStruct((H, MP, 128), BF16)
    blk = pl.BlockSpec((H, HA, rb), lambda i: (0, 0, i))
    tblk = pl.BlockSpec((H, rb, 128), lambda i: (0, i, 0))
    mblk = pl.BlockSpec((H, HA, 128), lambda i: (0, 0, 0))
    mtblk = pl.BlockSpec((H, MP, 128), lambda i: (0, 0, 0))
    return pl.pallas_call(
        functools.partial(qkv_kernel, mem_rows),
        grid=(slots // rb,),
        in_specs=[
            pl.BlockSpec((PARTS, 64, 512), lambda i: (0, 0, 0)),
            pl.BlockSpec((rb, 512), lambda i: (i, 0)),
            pl.BlockSpec((1, rb), lambda i: (0, i)),
            pl.BlockSpec(memory_space=pltpu.SMEM),
        ],
        out_specs=[blk, blk, blk, tblk, tblk, mblk, mblk, mtblk, mtblk],
        out_shape=[wide, wide, wide, tall, tall, mwide, mwide, mtall, mtall],
        scratch_shapes=[pltpu.VMEM((1536, 512), BF16)],
        compiler_params=params(),
        name="qkv",
    )(g, tokens, segment.reshape(1, slots), counts)


def key_ranges(seg, count, slots, out):
    r, c = seg.shape
    pos = lax.broadcasted_iota(jnp.int32, (r, c), 0) * c + lax.broadcasted_iota(jnp.int32, (r, c), 1)
    valid = pos < count
    ends = [jnp.sum(jnp.where(valid & (seg <= s), 1.0, 0.0)).astype(jnp.int32) for s in range(3)]
    for block in range(slots // BQ):
        first = block * BQ
        last = jnp.minimum(first + BQ, count)
        low, high, start = jnp.int32(slots), jnp.int32(0), jnp.int32(0)
        for end in ends:
            hit = (end > first) & (start < last) & (end > start)
            low = jnp.where(hit, jnp.minimum(low, start), low)
            high = jnp.where(hit, jnp.maximum(high, end), high)
            start = end
        begin = low // 128
        blocks = jnp.where(high > low, (high - begin * 128 + BK - 1) // BK, 0)
        out[0, block] = jnp.minimum(begin, slots // 128 - blocks * (BK // 128))
        out[1, block] = blocks


def key_slots(begin, block):
    return pl.ds(pl.multiple_of((begin + block * (BK // 128)) * 128, 128), BK)


def pipelined(blocks, work, first, second):
    @pl.when(blocks > 0)
    def _():
        work((0, first), None)

    pairs = jnp.maximum(blocks - 1, 0) // 2

    @pl.loop(0, pairs)
    def _(i):
        work((2 * i + 1, second), (2 * i, first))
        work((2 * i + 2, first), (2 * i + 1, second))

    j = 2 * pairs

    @pl.when(blocks - j == 2)
    def _():
        work((j + 1, second), (j, first))
        work(None, (j + 1, second))

    @pl.when(blocks - j == 1)
    def _():
        work(None, (j, first))


def fwd_kernel(
    slots, seg_ref, cnt_ref, qa_ref, kn_ref, va_ref, kmn_ref, vm_ref,
    mix_ref, lse_ref, acc_ref, m_ref, sa_ref, sb_ref, range_ref,
):
    step = pl.program_id(0)

    @pl.when(step == 0)
    def _():
        key_ranges(seg_ref[...], cnt_ref[0], slots, range_ref)

    begin, blocks = range_ref[0, step], range_ref[1, step]

    def weights(h, s):
        old = m_ref[h : h + 1, :]
        top = jnp.maximum(old, jnp.max(s, axis=0, keepdims=True))
        return jnp.exp(s - top).astype(BF16), jnp.exp(old - top), top

    def work(new, old):
        kept = {}
        for h in range(H + 1):
            if h < H and new:
                new[1][h] = dot(kn_ref[h, key_slots(begin, new[0]), 0:HA], qa_ref[h], 1, 0)
            if h < H and old:
                kept[h] = weights(h, old[1][h])
            if h > 0 and old:
                p, fade, top = kept.pop(h - 1)
                acc_ref[h - 1] = acc_ref[h - 1] * fade + dot(va_ref[h - 1, :, key_slots(begin, old[0])], p, 1, 0)
                m_ref[h - 1 : h, :] = top

    scores = [dot(kmn_ref[h, :, 0:HA], qa_ref[h], 1, 0) for h in range(H)]
    for h in range(H):
        top = jnp.max(scores[h], axis=0, keepdims=True)
        p = jnp.exp(scores[h] - top).astype(BF16)
        acc_ref[h] = dot(vm_ref[h, :, 0:MP], p, 1, 0)
        m_ref[h : h + 1, :] = top
    pipelined(blocks, work, sa_ref, sb_ref)
    for h in range(H):
        total = acc_ref[h, 64:65, :]
        mix_ref[64 * h : 64 * h + 64, :] = (acc_ref[h, 0:64, :] * (1.0 / total)).astype(BF16)
        lse_ref[h : h + 1, :] = m_ref[h : h + 1, :] + jnp.log(total)


def attend_forward(seg2, counts, qa, kn, va, kmn, vm):
    slots = qa.shape[2]
    once = pl.Buffered(1)

    def whole(a):
        return pl.BlockSpec(a.shape, lambda i: (0, 0, 0), pipeline_mode=once)

    return pl.pallas_call(
        functools.partial(fwd_kernel, slots),
        grid=(slots // BQ,),
        in_specs=[
            pl.BlockSpec(seg2.shape, lambda i: (0, 0)),
            pl.BlockSpec(memory_space=pltpu.SMEM),
            pl.BlockSpec((H, HA, BQ), lambda i: (0, 0, i)),
            whole(kn), whole(va), whole(kmn), whole(vm),
        ],
        out_specs=[pl.BlockSpec((512, BQ), lambda i: (0, i)), pl.BlockSpec((H, BQ), lambda i: (0, i))],
        out_shape=[jax.ShapeDtypeStruct((512, slots), BF16), jax.ShapeDtypeStruct((H, slots), F32)],
        scratch_shapes=[
            pltpu.VMEM((H, HA, BQ), F32),
            pltpu.VMEM((H, BQ), F32),
            pltpu.VMEM((H, BK, BQ), F32),
            pltpu.VMEM((H, BK, BQ), F32),
            pltpu.SMEM((2, slots // BQ), jnp.int32),
        ],
        compiler_params=params(),
        name="attend_forward",
    )(seg2, counts, qa, kn, va, kmn, vm)


def norm_parts(value):
    mean = jnp.mean(value, axis=-1, keepdims=True)
    centred = value - mean
    rstd = lax.rsqrt(jnp.mean(centred * centred, axis=-1, keepdims=True) + EPS)
    return centred * rstd, rstd


def norm_grad(grad_hat, hat, rstd):
    return rstd * (
        grad_hat
        - jnp.mean(grad_hat, axis=-1, keepdims=True)
        - hat * jnp.mean(grad_hat * hat, axis=-1, keepdims=True)
    )


def colsum(value):
    return jnp.sum(value, axis=0, keepdims=True)


def mid_kernel(
    rb, cnt_ref, gs_ref, up_ref, dn_ref, wo_ref, mix_ref, tok_ref, cot_ref,
    out_ref, gfirst_ref, mgrad_ref, delta_ref, gw_ref, vec_ref, bup_ref,
    row_ref, rbup_ref, wup_ref, wdn_ref, aup_ref, adn_ref, ao_ref,
):
    step = pl.program_id(0)

    @pl.when(step == 0)
    def _():
        small = gs_ref[...].reshape(512, 512)
        row_ref[...] = small[:, 128:256].astype(F32).T
        bup = jnp.sum(gs_ref[:, 0:8, 256:512].astype(F32), axis=0)
        for v in range(8):
            rbup_ref[0:1, 256 * v : 256 * v + 256] = bup[v : v + 1, :]
        for c in range(4):
            wup_ref[:, 512 * c : 512 * c + 512] = up_ref[:, 16 * c : 16 * c + 16, :].reshape(512, 512)
        wdn_ref[...] = dn_ref[...].reshape(2048, 512)
        aup_ref[...] = jnp.zeros_like(aup_ref)
        adn_ref[...] = jnp.zeros_like(adn_ref)
        ao_ref[...] = jnp.zeros_like(ao_ref)
        vec_ref[...] = jnp.zeros_like(vec_ref)
        bup_ref[...] = jnp.zeros_like(bup_ref)

    wo = wo_ref[...].reshape(512, 512)

    def row(v):
        return row_ref[v : v + 1, :]

    mixt = mix_ref[...]
    attention = dot(mixt, wo, 0, 0) + row(V_BO)
    hat1, rstd1 = norm_parts(tok_ref[...].astype(F32) + attention)
    first = hat1 * row(V_GA) + row(V_SA)
    first_low = first.astype(BF16)
    hidden = dot(first_low, wup_ref[...], 1, 0) + rbup_ref[...]
    cdf = 0.5 + 0.5 * lax.erf(hidden * (2.0 ** -0.5))
    active = (hidden * cdf).astype(BF16)
    slope = cdf + hidden * jnp.exp(hidden * hidden * -0.5) * 0.3989422804014327
    branch = dot(active, wdn_ref[...], 1, 0) + row(V_BD)
    hat2, rstd2 = norm_parts(first + branch)
    valid = lax.broadcasted_iota(jnp.int32, (rb, 1), 0) + step * rb < cnt_ref[0]
    out_ref[...] = jnp.where(valid, hat2 * row(V_GF) + row(V_SF), 0.0).astype(BF16)

    seed = jnp.where(valid, cot_ref[...].astype(F32), 0.0)
    vec_ref[V_GF : V_GF + 1, :] += colsum(seed * hat2)
    vec_ref[V_SF : V_SF + 1, :] += colsum(seed)
    grad_second = norm_grad(seed * row(V_GF), hat2, rstd2)
    branch_grad = grad_second.astype(BF16)
    adn_ref[...] += dot(active, branch_grad, 0, 0)
    vec_ref[V_BD : V_BD + 1, :] += colsum(branch_grad.astype(F32))
    hidden_grad = (dot(branch_grad, wdn_ref[...], 1, 1) * slope).astype(BF16)
    aup_ref[...] += dot(first_low, hidden_grad, 0, 0)
    bup_ref[...] += colsum(hidden_grad.astype(F32))
    first_grad = grad_second + dot(hidden_grad, wup_ref[...], 1, 1)
    vec_ref[V_GA : V_GA + 1, :] += colsum(first_grad * hat1)
    vec_ref[V_SA : V_SA + 1, :] += colsum(first_grad)
    grad_first = norm_grad(first_grad * row(V_GA), hat1, rstd1)
    gfirst_ref[...] = grad_first
    attention_grad = grad_first.astype(BF16)
    vec_ref[V_BO : V_BO + 1, :] += colsum(attention_grad.astype(F32))
    ao_ref[...] += dot(mixt, attention_grad, 1, 0)
    mgrad = dot(wo, attention_grad, 1, 1).astype(BF16)
    mgrad_ref[...] = mgrad
    prod = mgrad.astype(F32) * mixt.astype(F32)
    for h in range(H):
        delta_ref[h : h + 1, :] = jnp.sum(prod[64 * h : 64 * h + 64, :], axis=0, keepdims=True)

    @pl.when(step == pl.num_programs(0) - 1)
    def _():
        gw_ref[:, 0:16, :] = ao_ref[...].astype(gw_ref.dtype).reshape(PARTS, 16, 512)
        for c in range(4):
            gw_ref[:, 16 + 16 * c : 32 + 16 * c, :] = (
                aup_ref[:, 512 * c : 512 * c + 512].astype(gw_ref.dtype).reshape(PARTS, 16, 512)
            )
        gw_ref[:, 80:144, :] = adn_ref[...].astype(gw_ref.dtype).reshape(PARTS, 64, 512)


def middle(g, counts, mixt, tokens, cotangent, rb=256):
    slots = tokens.shape[0]
    rows = pl.BlockSpec((rb, 512), lambda i: (i, 0))
    cols = pl.BlockSpec((512, rb), lambda i: (0, i))
    once = pl.Buffered(1)
    return pl.pallas_call(
        functools.partial(mid_kernel, rb),
        grid=(slots // rb,),
        in_specs=[
            pl.BlockSpec(memory_space=pltpu.SMEM),
            pl.BlockSpec((PARTS, 16, 512), lambda i: (0, 3, 0), pipeline_mode=once),
            pl.BlockSpec((PARTS, 64, 512), lambda i: (0, 1, 0), pipeline_mode=once),
            pl.BlockSpec((PARTS, 64, 512), lambda i: (0, 2, 0), pipeline_mode=once),
            pl.BlockSpec((PARTS, 16, 512), lambda i: (0, 12, 0), pipeline_mode=once),
            cols, rows, rows,
        ],
        out_specs=[
            rows, rows, cols,
            pl.BlockSpec((H, rb), lambda i: (0, i)),
            pl.BlockSpec((PARTS, 144, 512), lambda i: (0, 0, 0), pipeline_mode=once),
            pl.BlockSpec((8, 512), lambda i: (0, 0)),
            pl.BlockSpec((1, 2048), lambda i: (0, 0)),
        ],
        out_shape=[
            jax.ShapeDtypeStruct((slots, 512), BF16),
            jax.ShapeDtypeStruct((slots, 512), F32),
            jax.ShapeDtypeStruct((512, slots), BF16),
            jax.ShapeDtypeStruct((H, slots), F32),
            jax.ShapeDtypeStruct((PARTS, 144, 512), BF16),
            jax.ShapeDtypeStruct((8, 512), F32),
            jax.ShapeDtypeStruct((1, 2048), F32),
        ],
        scratch_shapes=[
            pltpu.VMEM((128, 512), F32),
            pltpu.VMEM((1, 2048), F32),
            pltpu.VMEM((512, 2048), BF16),
            pltpu.VMEM((2048, 512), BF16),
            pltpu.VMEM((512, 2048), F32),
            pltpu.VMEM((2048, 512), F32),
            pltpu.VMEM((512, 512), F32),
        ],
        compiler_params=params(),
        name="middle",
    )(counts, g, g, g, g, mixt, tokens, cotangent)


def split3(value):
    high = value.astype(BF16)
    rest = value - high.astype(F32)
    mid = rest.astype(BF16)
    return high, mid, (rest - mid.astype(F32)).astype(BF16)


def bwd_kernel(
    slots, seg_ref, cnt_ref, qa_ref, kn_ref, ka_ref, vn_ref, kmn_ref, km_ref, vmn_ref, do_ref, lse_ref, delta_ref,
    dq_ref, dk_ref, dv_ref, dkm_ref, dvm_ref,
    q2_ref, do2_ref, dqa_ref, dka_ref, dva_ref, dkma_ref, dvma_ref, sa_ref, ga_ref, sb_ref, gb_ref, range_ref,
):
    step = pl.program_id(0)

    @pl.when(step == 0)
    def _():
        key_ranges(seg_ref[...], cnt_ref[0], slots, range_ref)
        dka_ref[...] = jnp.zeros_like(dka_ref)
        dva_ref[...] = jnp.zeros_like(dva_ref)
        dkma_ref[...] = jnp.zeros_like(dkma_ref)
        dvma_ref[...] = jnp.zeros_like(dvma_ref)

    begin, blocks = range_ref[0, step], range_ref[1, step]
    frow = lax.broadcasted_iota(jnp.int32, (16, BQ), 0)

    def feature(value, at):
        high, mid, low = (jnp.broadcast_to(v.astype(F32), (16, BQ)) for v in split3(value))
        return jnp.where(frow == at, high, jnp.where(frow == at + 1, mid, jnp.where(frow == at + 2, low, 0.0)))

    for h in range(H):
        q2_ref[h, 0:64, :] = qa_ref[h, 0:64, :]
        q2_ref[h, 64:80, :] = (qa_ref[h, 64:80, :].astype(F32) + feature(-lse_ref[h : h + 1, :], 3)).astype(BF16)
        do2_ref[h, 0:64, :] = do_ref[64 * h : 64 * h + 64, :]
        do2_ref[h, 64:80, :] = feature(-delta_ref[h : h + 1, :], 0).astype(BF16)

    def work(new, old):
        kept = {}
        for h in range(H + 1):
            if h < H and new:
                ks = key_slots(begin, new[0])
                new[1][0][h] = dot(kn_ref[h, ks, 0:HA], q2_ref[h], 1, 0)
                new[1][1][h] = dot(vn_ref[h, ks, 0:HA], do2_ref[h], 1, 0)
            if h < H and old:
                p = jnp.exp(old[1][0][h])
                kept[h] = p.astype(BF16), (p * old[1][1][h]).astype(BF16)
            if h > 0 and old:
                ks = key_slots(begin, old[0])
                p, ds = kept.pop(h - 1)
                dva_ref[h - 1, :, ks] += dot(do2_ref[h - 1, 0:64, :], p, 1, 1)
                dka_ref[h - 1, :, ks] += dot(q2_ref[h - 1, 0:64, :], ds, 1, 1)
                dqa_ref[h - 1] += dot(ka_ref[h - 1, 0:64, ks], ds, 1, 0)

    ps = [jnp.exp(dot(kmn_ref[h, :, 0:HA], q2_ref[h], 1, 0)) for h in range(H)]
    dss = [(ps[h] * dot(vmn_ref[h, :, 0:HA], do2_ref[h], 1, 0)).astype(BF16) for h in range(H)]
    for h in range(H):
        dvma_ref[h, :, 0:MP] += dot(do2_ref[h, 0:64, :], ps[h].astype(BF16), 1, 1)
        dkma_ref[h, :, 0:MP] += dot(q2_ref[h, 0:64, :], dss[h], 1, 1)
        dqa_ref[h] = dot(km_ref[h, 0:64, 0:MP], dss[h], 1, 0)
    pipelined(blocks, work, (sa_ref, ga_ref), (sb_ref, gb_ref))
    for h in range(H):
        dq_ref[64 * h : 64 * h + 64, :] = (dqa_ref[h] * HD ** -0.5).astype(BF16)

    @pl.when(step == pl.num_programs(0) - 1)
    def _():
        for h in range(H):
            s = slice(64 * h, 64 * h + 64)
            dk_ref[s, :] = dka_ref[h].astype(BF16)
            dv_ref[s, :] = dva_ref[h].astype(BF16)
            dkm_ref[s, :] = dkma_ref[h].astype(BF16)
            dvm_ref[s, :] = dvma_ref[h].astype(BF16)


def attend_backward(seg2, counts, qa, kn, ka, vn, kmn, km, vmn, mgrad, lse, delta):
    slots = qa.shape[2]
    once = pl.Buffered(1)

    def full(a):
        return pl.BlockSpec(a.shape, lambda i: (0, 0, 0), pipeline_mode=once)

    cols = pl.BlockSpec((512, BQ), lambda i: (0, i))
    stat = pl.BlockSpec((H, BQ), lambda i: (0, i))
    whole = pl.BlockSpec((512, slots), lambda i: (0, 0), pipeline_mode=once)
    mwhole = pl.BlockSpec((512, 128), lambda i: (0, 0))
    block = pltpu.VMEM((H, BK, BQ), F32)
    return pl.pallas_call(
        functools.partial(bwd_kernel, slots),
        grid=(slots // BQ,),
        in_specs=[
            pl.BlockSpec(seg2.shape, lambda i: (0, 0)),
            pl.BlockSpec(memory_space=pltpu.SMEM),
            pl.BlockSpec((H, HA, BQ), lambda i: (0, 0, i)),
            full(kn), full(ka), full(vn), full(kmn), full(km), full(vmn), cols, stat, stat,
        ],
        out_specs=[cols, whole, whole, mwhole, mwhole],
        out_shape=[jax.ShapeDtypeStruct((512, slots), BF16)] * 3 + [jax.ShapeDtypeStruct((512, 128), BF16)] * 2,
        scratch_shapes=[
            pltpu.VMEM((H, HA, BQ), BF16),
            pltpu.VMEM((H, HA, BQ), BF16),
            pltpu.VMEM((H, HD, BQ), F32),
            pltpu.VMEM((H, HD, slots), F32),
            pltpu.VMEM((H, HD, slots), F32),
            pltpu.VMEM((H, HD, 128), F32),
            pltpu.VMEM((H, HD, 128), F32),
            block, block, block, block,
            pltpu.SMEM((2, slots // BQ), jnp.int32),
        ],
        compiler_params=params(),
        name="attend_backward",
    )(seg2, counts, qa, kn, ka, vn, kmn, km, vmn, mgrad, lse, delta)


def tail_kernel(
    g_ref, tok_ref, dq_ref, dk_ref, dv_ref, dkm_ref, dvm_ref, gfirst_ref, vec_ref, bup_ref,
    gtok_ref, gw_ref, wt_ref, acc_ref, sum_ref,
):
    step = pl.program_id(0)

    @pl.when(step == 0)
    def _():
        for j in range(3):
            wt_ref[512 * j : 512 * j + 512, :] = g_ref[:, 16 * j : 16 * j + 16, :].reshape(512, 512).T
        memt = g_ref[:, 48:64, 0:128].reshape(512, 128)
        acc_ref[0:512, :] = jnp.zeros((512, 512), F32)
        acc_ref[512:1024, :] = dot(dkm_ref[...], memt, 1, 1)
        acc_ref[1024:1536, :] = dot(dvm_ref[...], memt, 1, 1)
        sum_ref[...] = jnp.zeros_like(sum_ref)
        sum_ref[:, 1:2] = jnp.sum(dvm_ref[...].astype(F32), axis=1, keepdims=True)

    tok = tok_ref[...]
    dq, dk, dv = dq_ref[...], dk_ref[...], dv_ref[...]
    acc_ref[0:512, :] += dot(dq, tok, 1, 0)
    acc_ref[512:1024, :] += dot(dk, tok, 1, 0)
    acc_ref[1024:1536, :] += dot(dv, tok, 1, 0)
    sum_ref[:, 0:1] += jnp.sum(dq.astype(F32), axis=1, keepdims=True)
    sum_ref[:, 1:2] += jnp.sum(dv.astype(F32), axis=1, keepdims=True)
    gtok_ref[...] = (
        gfirst_ref[...]
        + dot(dq, wt_ref[0:512, :], 0, 0)
        + dot(dk, wt_ref[512:1024, :], 0, 0)
        + dot(dv, wt_ref[1024:1536, :], 0, 0)
    )

    @pl.when(step == pl.num_programs(0) - 1)
    def _():
        for j in range(3):
            gw_ref[:, 16 * j : 16 * j + 16, :] = (
                acc_ref[512 * j : 512 * j + 512, :].T.astype(gw_ref.dtype).reshape(PARTS, 16, 512)
            )
        gmem = dot(wt_ref[512:1024, :], dkm_ref[...], 0, 0) + dot(wt_ref[1024:1536, :], dvm_ref[...], 0, 0)
        gw_ref[:, 48:64, 0:128] = gmem.astype(gw_ref.dtype).reshape(PARTS, 16, 128)
        lane = lax.broadcasted_iota(jnp.int32, (512, 128), 1)
        vecs = jnp.concatenate([vec_ref[...], jnp.zeros((120, 512), F32)], axis=0).T
        vecs = jnp.where(lane < 2, sum_ref[...], vecs)
        gw_ref[:, 48:64, 128:256] = vecs.astype(gw_ref.dtype).reshape(PARTS, 16, 128)
        rows = jnp.concatenate([bup_ref[0:1, 256 * v : 256 * v + 256] for v in range(8)] + [jnp.zeros((8, 256), F32)], axis=0)
        gw_ref[:, 48:64, 256:512] = jnp.broadcast_to(rows[None].astype(gw_ref.dtype), (PARTS, 16, 256))


def tail(g, tokens, dq, dk, dv, dkm, dvm, gfirst, vec, bup, rb=512):
    slots = tokens.shape[0]
    rows = pl.BlockSpec((rb, 512), lambda i: (i, 0))
    cols = pl.BlockSpec((512, rb), lambda i: (0, i))
    mwhole = pl.BlockSpec((512, 128), lambda i: (0, 0))
    once = pl.Buffered(1)
    return pl.pallas_call(
        tail_kernel,
        grid=(slots // rb,),
        in_specs=[
            pl.BlockSpec((PARTS, 64, 512), lambda i: (0, 0, 0), pipeline_mode=once),
            rows, cols, cols, cols, mwhole, mwhole, rows,
            pl.BlockSpec((8, 512), lambda i: (0, 0)),
            pl.BlockSpec((1, 2048), lambda i: (0, 0)),
        ],
        out_specs=[rows, pl.BlockSpec((PARTS, 64, 512), lambda i: (0, 0, 0), pipeline_mode=once)],
        out_shape=[jax.ShapeDtypeStruct((slots, 512), F32), jax.ShapeDtypeStruct((PARTS, 64, 512), BF16)],
        scratch_shapes=[
            pltpu.VMEM((1536, 512), BF16),
            pltpu.VMEM((1536, 512), F32),
            pltpu.VMEM((512, 128), F32),
        ],
        compiler_params=params(),
        name="tail",
    )(g, tokens, dq, dk, dv, dkm, dvm, gfirst, vec, bup)


MESH = pl.DeviceIdType.MESH
AXES = {"z": (8, 4), "y": (4, 2), "x": (2, 2)}
LAYOUT = ("z", "y", "x")


class Place:
    def __init__(self):
        me = lax.axis_index("dp")
        self.me = me
        self.core = me % 2
        self.partner = me + 1 - 2 * self.core
        self.at = {a: (me // stride) % length for a, (stride, length) in AXES.items()}
        self.mine = tuple(self.at[a] for a in LAYOUT)

    def other(self, axis, distance):
        stride, length = AXES[axis]
        j = (self.at[axis] + distance) % length
        return j, self.me + (j - self.at[axis]) * stride

    def greet(self):
        barrier = pltpu.get_barrier_semaphore()
        peers = [self.partner]
        for axis in LAYOUT:
            peers += [self.other(axis, d)[1] for d in range(1, AXES[axis][1])]
        for peer in peers:
            pl.semaphore_signal(barrier, inc=1, device_id=(peer,), device_id_type=MESH)
        pl.semaphore_wait(barrier, len(peers))


class Copies:
    def __init__(self, send, recv):
        self.send, self.recv, self.count, self.open = send, recv, 0, []

    def number(self):
        self.count += 1
        return self.count - 1

    def make(self, src, dst, number, device):
        return pltpu.make_async_remote_copy(
            src_ref=src, dst_ref=dst, send_sem=self.send.at[number], recv_sem=self.recv.at[number],
            device_id=(device,), device_id_type=MESH,
        )

    def start(self, src, dst, number, device):
        copy = self.make(src, dst, number, device)
        copy.start()
        self.open.append(copy)

    def landed(self, block, number, device):
        self.make(block, block, number, device).wait_recv()

    def finish(self):
        for copy in self.open:
            copy.wait_send()
        self.open = []


def run_events(parts):
    live = []
    for index, part in enumerate(parts):
        live.append([next(part), index, part])
    while live:
        live.sort(key=lambda item: item[:2])
        item = live[0]
        try:
            item[0] = next(item[2])
        except StopIteration:
            live.pop(0)


LOAD = {2: 1.0, 4: 4.0}
HOP = 120.0


def gather_part(place, copies, own, whole, rows, order, arrivals):
    size, known, clock, done = rows.stop - rows.start, 1, 0.0, ()

    def block(axis, j, core):
        index = tuple(j if a == axis else (slice(None) if a in done else place.at[a]) for a in LAYOUT)
        return whole.at[index + (core, rows)]

    for axis in order:
        length = AXES[axis][1]
        numbers = [copies.number() for _ in range(2 * length - 2)]
        here = block(axis, place.at[axis], place.core)
        for d in range(1, length):
            copies.start(here if done else own.at[rows], here, numbers[d - 1], place.other(axis, d)[1])
        clock += LOAD[length] * known * size + HOP
        yield clock
        for d in range(1, length):
            j, device = place.other(axis, length - d)
            there = block(axis, j, place.core)
            copies.landed(there, numbers[d - 1], device)
            copies.start(there, there, numbers[length - 2 + d], place.partner)
            arrivals.append((block(axis, j, 1 - place.core), numbers[length - 2 + d]))
        done += (axis,)
        known *= length


def gather_all(place, copies, own, whole, parts):
    arrivals = []
    for rows, _ in parts:
        number = copies.number()
        copies.start(own.at[rows], whole.at[place.mine + (place.core, rows)], number, place.partner)
        arrivals.append((whole.at[place.mine + (1 - place.core, rows)], number))
    run_events([gather_part(place, copies, own, whole, rows, order, arrivals) for rows, order in parts])
    return arrivals


GATHER_PARTS = (
    (slice(0, 32), "zxy"),
    (slice(32, 64), "zyx"),
    (slice(64, 96), "yzx"),
    (slice(96, 128), "xzy"),
    (slice(128, 160), "zxy"),
    (slice(160, 208), "zyx"),
)
GATHER_COPIES = 11 * len(GATHER_PARTS)


def gather_kernel(parts, own_ref, whole_ref, send, recv, local):
    place = Place()
    place.greet()
    copies = Copies(send, recv)
    keep = pltpu.make_async_copy(own_ref, whole_ref.at[place.mine + (place.core,)], local)
    keep.start()
    keep.wait()
    arrivals = gather_all(place, copies, own_ref, whole_ref, parts)
    for block, number in arrivals:
        copies.landed(block, number, place.partner)
    copies.finish()


def gather(packed):
    whole = pl.pallas_call(
        functools.partial(gather_kernel, GATHER_PARTS),
        in_specs=[pl.BlockSpec(memory_space=pltpu.VMEM)],
        out_specs=pl.BlockSpec(memory_space=pl.ANY),
        out_shape=jax.ShapeDtypeStruct((4, 2, 2, 2, ROWS, 512), BF16),
        scratch_shapes=[
            pltpu.SemaphoreType.DMA((GATHER_COPIES,)),
            pltpu.SemaphoreType.DMA((GATHER_COPIES,)),
            pltpu.SemaphoreType.DMA,
        ],
        compiler_params=params(collective_id=0, has_side_effects=True),
        name="gather",
    )(packed)
    return whole.reshape(PARTS, ROWS, 512)


def scatter_part(place, copies, acc, slots, out, rows, order):
    size, clock, done = rows.stop - rows.start, 0.0, ()
    left = 16

    def block(axis, j):
        index = tuple(j if a == axis else (place.at[a] if a in done else slice(None)) for a in LAYOUT)
        return index + (rows,)

    for axis in order:
        length = AXES[axis][1]
        left //= length
        numbers = [copies.number() for _ in range(length - 1)]
        for d in range(1, length):
            j, device = place.other(axis, d)
            copies.start(acc.at[block(axis, j)], slots[axis, d], numbers[d - 1], device)
        clock += LOAD[length] * left * size + HOP
        yield clock
        for d in range(1, length):
            copies.landed(slots[axis, d], numbers[d - 1], place.partner)
        mine = block(axis, place.at[axis])
        total = acc[mine].astype(F32)
        for d in range(1, length):
            total = total + slots[axis, d][...].astype(F32)
        if axis == order[-1]:
            out[rows, :] = total
        else:
            acc[mine] = total.astype(BF16)
        done += (axis,)


SCATTER_PARTS = (
    (slice(64, 96), "yxz"),
    (slice(96, 128), "xyz"),
    (slice(128, 144), "xzy"),
    (slice(144, 160), "yzx"),
    (slice(160, 176), "xzy"),
    (slice(176, 208), "yxz"),
    (slice(0, 32), "xyz"),
    (slice(32, 64), "yxz"),
)
SCATTER_COPIES = 6 * len(SCATTER_PARTS)


def slot_shapes(parts):
    shapes = {}
    for number, (rows, order) in enumerate(parts):
        left = ["z", "y", "x"]
        for axis in order:
            left.remove(axis)
            shape = tuple(AXES[a][1] for a in LAYOUT if a in left) + (rows.stop - rows.start, 512)
            for d in range(1, AXES[axis][1]):
                shapes[number, axis, d] = shape
    return shapes


def scatter_kernel(all_parts, late_ref, early_ref, out_ref, acc, other, send, recv, local, *landing):
    place = Place()
    slots = dict(zip(slot_shapes(all_parts), landing))

    def source(rows, core):
        if rows.start < 64:
            return late_ref.at[:, :, :, core, rows]
        return early_ref.at[:, :, :, core, slice(rows.start - 64, rows.stop - 64)]

    loads = [
        pltpu.make_async_copy(source(rows, place.core), acc.at[:, :, :, rows], local.at[index])
        for index, (rows, _) in enumerate(all_parts)
    ]
    place.greet()
    copies = Copies(send, recv)
    numbers = [copies.number() for _ in all_parts]
    for load, number, (rows, _) in zip(loads, numbers, all_parts):
        copies.start(source(rows, 1 - place.core), other.at[:, :, :, rows], number, place.partner)
        load.start()
    parts = []
    for index, (rows, order) in enumerate(all_parts):
        loads[index].wait()
        copies.landed(other.at[:, :, :, rows], numbers[index], place.partner)

        @pl.loop(0, 4)
        def _(z):
            acc[z, :, :, rows] = (acc[z, :, :, rows].astype(F32) + other[z, :, :, rows].astype(F32)).astype(BF16)

        mine = {key[1:]: slot for key, slot in slots.items() if key[0] == index}
        parts.append(scatter_part(place, copies, acc, mine, out_ref, rows, order))
        next(parts[-1])
    run_events(parts)
    copies.finish()


def scatter(late, early):
    shapes = slot_shapes(SCATTER_PARTS)
    return pl.pallas_call(
        functools.partial(scatter_kernel, SCATTER_PARTS),
        in_specs=[pl.BlockSpec(memory_space=pl.ANY)] * 2,
        out_specs=pl.BlockSpec(memory_space=pltpu.VMEM),
        out_shape=jax.ShapeDtypeStruct((ROWS, 512), F32),
        scratch_shapes=[
            pltpu.VMEM((4, 2, 2, ROWS, 512), BF16),
            pltpu.VMEM((4, 2, 2, ROWS, 512), BF16),
            pltpu.SemaphoreType.DMA((SCATTER_COPIES,)),
            pltpu.SemaphoreType.DMA((SCATTER_COPIES,)),
            pltpu.SemaphoreType.DMA((len(SCATTER_PARTS),)),
        ]
        + [pltpu.VMEM(shape, BF16) for shape in shapes.values()],
        compiler_params=params(collective_id=1, has_side_effects=True),
        name="scatter",
    )(late.reshape(4, 2, 2, 2, 64, 512), early.reshape(4, 2, 2, 2, 144, 512))


NAMES = (
    "memory", "w_query", "b_query", "w_key", "w_value", "b_value", "w_out", "b_out", "gain_attn",
    "shift_attn", "w_up", "b_up", "w_down", "b_down", "gain_ffn", "shift_ffn",
)
VECTORS = ("b_query", "b_value", "b_out", "gain_attn", "shift_attn", "b_down", "gain_ffn", "shift_ffn")


def pad_lanes(value, lanes):
    return jnp.pad(value, ((0, 0), (0, lanes - value.shape[1])))


def pack_part(p, me):
    up = p["w_up"].reshape(16, 4, 512).transpose(1, 0, 2).reshape(64, 512)
    memory = pad_lanes(p["memory"].T, 128)
    vectors = pad_lanes(jnp.stack([p[name] for name in VECTORS], axis=1), 128)
    own = jnp.arange(2048) // 64 == me
    b_up = jnp.where(own, jnp.tile(p["b_up"], PARTS), 0).astype(BF16).reshape(8, 256)
    b_up = jnp.pad(b_up, ((0, 8), (0, 0)))
    small = jnp.concatenate([memory, vectors, b_up], axis=1)
    return jnp.concatenate([p["w_query"], p["w_key"], p["w_value"], small, up, p["w_down"], p["w_out"]], axis=0)


def pack_whole(p):
    parts = []
    for d in range(PARTS):
        mine = {}
        for name in NAMES:
            axis = 1 if name == "memory" else 0
            size = p[name].shape[axis] // PARTS
            mine[name] = lax.slice_in_dim(p[name], d * size, d * size + size, axis=axis)
        parts.append(pack_part(mine, d))
    return jnp.stack(parts)


def unpack_part(early, late, mem_rows, me):
    small = late[48:64]
    vectors = small[:, 128:256]
    b_up = small[0:8, 256:512].reshape(2048)
    out = {
        "memory": small[:, 0:mem_rows].T,
        "w_query": late[0:16],
        "w_key": late[16:32],
        "w_value": late[32:48],
        "w_out": early[0:16],
        "w_up": early[16:80].reshape(4, 16, 512).transpose(1, 0, 2).reshape(16, 2048),
        "w_down": early[80:144],
        "b_up": lax.dynamic_slice_in_dim(b_up, me * 64, 64),
    }
    for index, name in enumerate(VECTORS):
        out[name] = vectors[:, index]
    return out


def shards(n, tokens, segment, counts, *rest):
    p = dict(zip(NAMES, rest[:-1]))
    cotangent = rest[-1]
    slots = tokens.shape[0]
    mem_rows = p["memory"].shape[0]
    me = lax.axis_index("dp")
    if n == PARTS:
        g = gather(pack_part(p, me))
    else:
        g = pack_whole(
            {k: lax.all_gather(v, "dp", axis=1 if k == "memory" else 0, tiled=True) for k, v in p.items()}
        )
    seg2 = segment.reshape(slots // 128, 128)
    qa, ka, va, kn, vn, km, vm, kmn, vmn = qkv(g, tokens, segment, counts, mem_rows)
    mixt, lse = attend_forward(seg2, counts, qa, kn, va, kmn, vm)
    output, gfirst, mgrad, delta, early, vec, bup = middle(g, counts, mixt, tokens, cotangent)
    dq, dk, dv, dkm, dvm = attend_backward(seg2, counts, qa, kn, ka, vn, kmn, km, vmn, mgrad, lse, delta)
    gtok, late = tail(g, tokens, dq, dk, dv, dkm, dvm, gfirst, vec, bup)
    if n == PARTS:
        owned = scatter(late, early)
        grads = unpack_part(owned[64:ROWS], owned[0:64], mem_rows, me)
    else:
        parts = [unpack_part(early[d].astype(F32), late[d].astype(F32), mem_rows, d) for d in range(PARTS)]
        grads = {}
        for name in NAMES:
            axis = 1 if name == "memory" else 0
            whole = jnp.concatenate([part[name] for part in parts], axis=axis)
            grads[name] = lax.psum_scatter(whole, "dp", scatter_dimension=axis, tiled=True)
    return (output, gtok) + tuple(grads[name] for name in NAMES)


def solution(mesh):
    n = mesh.shape["dp"]
    row, mat, mem = P("dp"), P("dp", None), P(None, "dp")
    spec = {name: mat if name.startswith("w_") else row for name in NAMES}
    spec["memory"] = mem
    weights = tuple(spec[name] for name in NAMES)
    return jax.shard_map(
        functools.partial(shards, n),
        mesh=mesh,
        in_specs=(mat, row, row) + weights + (mat,),
        out_specs=(mat, mat) + weights,
        check_vma=False,
    )
```

```python
import functools
import jax
import jax.numpy as jnp
from jax import lax
from jax.experimental import pallas as pl
from jax.experimental.pallas import tpu as pltpu
from jax.sharding import PartitionSpec as P

H = 8
HD = 64
HA = 80
EPS = 1e-05
BIG = 1e30
PARTS = 32
ROWS = 208
BQ = 256
BK = 256
MP = 32
F32 = jnp.float32
BF16 = jnp.bfloat16
VMEM_LIMIT = 60 << 20

V_BQ, V_BV, V_BO, V_GA, V_SA, V_BD, V_GF, V_SF = range(8)


def dot(left, right, lc, rc):
    return lax.dot_general(left, right, (((lc,), (rc,)), ((), ())), preferred_element_type=F32)


def params(**kw):
    return pltpu.CompilerParams(vmem_limit_bytes=VMEM_LIMIT, **kw)


MESH = pl.DeviceIdType.MESH
AXES = {"z": (8, 4), "y": (4, 2), "x": (2, 2)}
LAYOUT = ("z", "y", "x")


class Place:
    def __init__(self):
        me = lax.axis_index("dp")
        self.me = me
        self.core = me % 2
        self.far = 1 - self.core
        self.partner = me + 1 - 2 * self.core
        self.at = {a: (me // stride) % length for a, (stride, length) in AXES.items()}
        self.mine = tuple(self.at[a] for a in LAYOUT)
        self.others = {}
        for axis, (stride, length) in AXES.items():
            for distance in range(1, length):
                j = (self.at[axis] + distance) % length
                self.others[axis, distance] = j, me + (j - self.at[axis]) * stride

    def other(self, axis, distance):
        return self.others[axis, distance]

    def greet(self):
        barrier = pltpu.get_barrier_semaphore()
        peers = [self.partner]
        for axis in LAYOUT:
            peers += [self.other(axis, d)[1] for d in range(1, AXES[axis][1])]
        for peer in peers:
            pl.semaphore_signal(barrier, inc=1, device_id=(peer,), device_id_type=MESH)
        return lambda: pl.semaphore_wait(barrier, len(peers))


class Copies:
    def __init__(self, send, recv):
        self.send, self.recv, self.count, self.open = send, recv, 0, []

    def number(self):
        self.count += 1
        return self.count - 1

    def make(self, src, dst, number, device):
        return pltpu.make_async_remote_copy(
            src_ref=src, dst_ref=dst, send_sem=self.send.at[number], recv_sem=self.recv.at[number],
            device_id=(device,), device_id_type=MESH,
        )

    def start(self, src, dst, number, device):
        self.make(src(), dst(), number, device).start()
        self.open.append((src, dst, number, device))

    def landed(self, block, number, device):
        self.make(block, block, number, device).wait_recv()

    def finish(self):
        for src, dst, number, device in self.open:
            self.make(src(), dst(), number, device).wait_send()
        self.open = []


def gather_part(place, copies, own, base, whole, rows, order, arrivals):
    done = ()

    def mine():
        return own.at[slice(base + rows.start, base + rows.stop)]

    def block(axis, j, core):
        index = tuple(j if a == axis else (slice(None) if a in done else place.at[a]) for a in LAYOUT)
        return lambda: whole.at[index + (core, rows)]

    for axis in order:
        length = AXES[axis][1]
        numbers = [copies.number() for _ in range(2 * length - 2)]
        here = block(axis, place.at[axis], place.core)
        for d in range(1, length):
            copies.start(here if done else mine, here, numbers[d - 1], place.other(axis, d)[1])
        if not done:
            number = copies.number()
            copies.start(mine, here, number, place.partner)
            arrivals.append((block(axis, place.at[axis], place.far), number))
        yield
        for d in range(1, length):
            j, device = place.other(axis, length - d)
            there = block(axis, j, place.core)
            copies.landed(there(), numbers[d - 1], device)
            number = numbers[length - 2 + d]
            copies.start(there, there, number, place.partner)
            arrivals.append((block(axis, j, place.far), number))
        done += (axis,)
    yield


def advance(parts):
    for part in parts:
        next(part)


def scatter_part(place, copies, acc, slots, out, rows, order):
    done = ()

    def block(axis, j):
        index = tuple(j if a == axis else (place.at[a] if a in done else slice(None)) for a in LAYOUT)
        return index + (rows,)

    def taken(index):
        return lambda: acc.at[index]

    def landing(axis, d):
        return lambda: slots[axis, d]

    for axis in order:
        length = AXES[axis][1]
        numbers = [copies.number() for _ in range(length - 1)]
        for d in range(1, length):
            j, device = place.other(axis, d)
            copies.start(taken(block(axis, j)), landing(axis, d), numbers[d - 1], device)
        yield
        for d in range(1, length):
            copies.landed(slots[axis, d], numbers[d - 1], place.partner)
        mine = block(axis, place.at[axis])
        total = acc[mine].astype(F32)
        for d in range(1, length):
            total = total + slots[axis, d][...].astype(F32)
        if axis == order[-1]:
            out[rows, :] = total
        else:
            acc[mine] = total.astype(BF16)
        done += (axis,)
    yield


def slot_shapes(parts):
    shapes = {}
    for number, (rows, order) in enumerate(parts):
        left = ["z", "y", "x"]
        for axis in order:
            left.remove(axis)
            shape = tuple(AXES[a][1] for a in LAYOUT if a in left) + (rows.stop - rows.start, 512)
            for d in range(1, AXES[axis][1]):
                shapes[number, axis, d] = shape
    return shapes


def join(place, copies, acc, source, other, rows, number):
    copies.landed(other.at[:, :, :, rows], number, place.partner)

    @pl.loop(0, 4)
    def _(z):
        mine = source(z) if source else acc[z, :, :, rows]
        acc[z, :, :, rows] = (mine.astype(F32) + other[z, :, :, rows].astype(F32)).astype(BF16)


VECTORS = ("b_query", "b_value", "b_out", "gain_attn", "shift_attn", "b_down", "gain_ffn", "shift_ffn")
EARLY = 64
LATE = 144
EARLY_PARTS = ((slice(0, 32), "zxy"), (slice(32, 64), "zyx"))
LATE_PARTS = (
    (slice(0, 48), "zxy"),
    (slice(48, 96), "zyx"),
    (slice(96, 128), "yzx"),
    (slice(128, 144), "xzy"),
)
GATHER_COPIES = 11 * (len(EARLY_PARTS) + len(LATE_PARTS))


def head_block(rows, features):
    block = jnp.concatenate([rows, features], axis=0)
    return block, jnp.concatenate([block, jnp.zeros((128 - HA, rows.shape[1]), BF16)], axis=0).T


def pack(own, place, wq, wk, wv, wo, up, dn, memory, vectors, b_up):
    own[0:16] = wq[...]
    own[16:32] = wk[...]
    own[32:48] = wv[...]
    mem_rows = memory.shape[0]
    own[48:64] = jnp.zeros((16, 512), BF16)
    own[48:64, 0:mem_rows] = memory[...].astype(F32).T.astype(BF16)
    own[48:64, 128:136] = vectors[...].astype(F32).T.astype(BF16)
    value = jnp.concatenate([b_up[...].astype(F32)] * 4, axis=1)
    row = lax.broadcasted_iota(jnp.int32, (16, 256), 0)
    lane = lax.broadcasted_iota(jnp.int32, (16, 256), 1)
    own[48:64, 256:512] = jnp.where(row * 4 + lane // 64 == place.me, value, 0.0).astype(BF16)
    for c in range(4):
        own[64 + 16 * c : 80 + 16 * c] = up[:, 512 * c : 512 * c + 512]
    own[128:192] = dn[...]
    own[192:208] = wo[...]


def prepare(mem_rows, early, wt_ref, memt_ref, rows_ref, rbup_ref, bias_ref, km_ref, vm_ref, kmn_ref, vmn_ref):
    for j in range(3):
        wt_ref[512 * j : 512 * j + 512, :] = early[..., 16 * j : 16 * j + 16, :].reshape(512, 512).T
    small = early[..., 48:64, 0:256].reshape(512, 256)
    memt = small[:, 0:128]
    memt_ref[...] = memt
    vectors = small[:, 128:256].astype(F32)
    bias_ref[...] = vectors
    rows_ref[...] = vectors.T[0:8, :]
    bup = jnp.sum(early[..., 48:64, 256:512].reshape(PARTS, 16, 256).astype(F32), axis=0)
    for v in range(8):
        rbup_ref[0:1, 256 * v : 256 * v + 256] = bup[v : v + 1, :]
    bv = vectors[:, V_BV : V_BV + 1]
    km = dot(wt_ref[512:1024, :], memt, 1, 0).astype(BF16)
    vm = (dot(wt_ref[1024:1536, :], memt, 1, 0) + bv).astype(BF16)
    frow = lax.broadcasted_iota(jnp.int32, (16, 128), 0)
    lane = lax.broadcasted_iota(jnp.int32, (16, 128), 1)
    kf = jnp.where(frow < 3, jnp.where(lane < mem_rows, 0.0, 1.0), jnp.where(frow < 6, 1.0, 0.0)).astype(BF16)
    vf = jnp.where(frow < 3, 1.0, 0.0).astype(BF16)
    for h in range(H):
        km_ref[h], turned = head_block(km[64 * h : 64 * h + 64, :], kf)
        kmn_ref[h] = turned[0:MP]
        vm_ref[h], turned = head_block(vm[64 * h : 64 * h + 64, :], vf)
        vmn_ref[h] = turned[0:MP]


def project(step, tok_ref, seg_ref, cnt_ref, wt_ref, bias_ref, qa_ref, ka_ref, va_ref, kn_ref, vn_ref):
    rows = tok_ref.shape[0]
    tok = tok_ref[...]
    bq = bias_ref[:, V_BQ : V_BQ + 1]
    bv = bias_ref[:, V_BV : V_BV + 1]
    q = (dot(wt_ref[0:512, :], tok, 1, 1) + bq).astype(BF16) * jnp.asarray(HD ** -0.5, BF16)
    k = dot(wt_ref[512:1024, :], tok, 1, 1).astype(BF16)
    v = (dot(wt_ref[1024:1536, :], tok, 1, 1) + bv).astype(BF16)
    frow = lax.broadcasted_iota(jnp.int32, (16, rows), 0)
    seg = jnp.broadcast_to(seg_ref[...], (16, rows))
    pos = lax.broadcasted_iota(jnp.int32, (16, rows), 1) + step * rows
    valid = pos < cnt_ref[0]
    qf = jnp.where((frow < 3) & (frow != seg), -BIG, 0.0).astype(BF16)
    kf = jnp.where(frow < 3, jnp.where(valid & (frow != seg), 0.0, 1.0), jnp.where(frow < 6, 1.0, 0.0)).astype(BF16)
    vf = jnp.where(frow < 3, 1.0, 0.0).astype(BF16)
    for h in range(H):
        s = slice(64 * h, 64 * h + 64)
        qa_ref[h, 0:64, :] = q[s]
        qa_ref[h, 64:80, :] = qf
        ka_ref[h], kn_ref[h] = head_block(k[s], kf)
        va_ref[h], vn_ref[h] = head_block(v[s], vf)


def gather_kernel(
    mem_rows, wq, wk, wv, wo, up, dn, memory, vectors, b_up, tok_ref, seg_ref, cnt_ref,
    late_ref, qa_ref, ka_ref, va_ref, kn_ref, vn_ref, km_ref, vm_ref, kmn_ref, vmn_ref,
    wt_ref, memt_ref, rows_ref, rbup_ref, own, early, bias_ref, send, recv, local,
):
    step = pl.program_id(0)
    place = Place()
    copies = Copies(send, recv)
    arrivals, late_arrivals = [], []
    firsts = [gather_part(place, copies, own, 0, early, *part, arrivals) for part in EARLY_PARTS]
    lasts = [gather_part(place, copies, own, EARLY, late_ref, *part, late_arrivals) for part in LATE_PARTS]

    @pl.when(step == 0)
    def _():
        everyone = place.greet()
        pack(own, place, wq, wk, wv, wo, up, dn, memory, vectors, b_up)
        early[place.mine + (place.core,)] = own[0:EARLY]
        everyone()
        advance(firsts)
        keep = pltpu.make_async_copy(own.at[EARLY:ROWS], late_ref.at[place.mine + (place.core,)], local)
        keep.start()
        advance(lasts)
        advance(firsts)
        advance(firsts)
        advance(firsts)
        for block, number in arrivals:
            copies.landed(block(), number, place.partner)
        keep.wait()
        advance(lasts)
        prepare(
            mem_rows, early, wt_ref, memt_ref, rows_ref, rbup_ref, bias_ref,
            km_ref, vm_ref, kmn_ref, vmn_ref,
        )

    project(step, tok_ref, seg_ref, cnt_ref, wt_ref, bias_ref, qa_ref, ka_ref, va_ref, kn_ref, vn_ref)

    @pl.when(step == 1)
    def _():
        advance(lasts)

    @pl.when(step == pl.num_programs(0) - 1)
    def _():
        advance(lasts)
        for block, number in late_arrivals:
            copies.landed(block(), number, place.partner)
        copies.finish()


def project_kernel(
    mem_rows, g_ref, tok_ref, seg_ref, cnt_ref, qa_ref, ka_ref, va_ref, kn_ref, vn_ref, km_ref, vm_ref, kmn_ref, vmn_ref,
    wt_ref, memt_ref, rows_ref, rbup_ref, bias_ref,
):
    step = pl.program_id(0)

    @pl.when(step == 0)
    def _():
        prepare(
            mem_rows, g_ref, wt_ref, memt_ref, rows_ref, rbup_ref, bias_ref, km_ref, vm_ref, kmn_ref, vmn_ref
        )

    project(step, tok_ref, seg_ref, cnt_ref, wt_ref, bias_ref, qa_ref, ka_ref, va_ref, kn_ref, vn_ref)


def projections(p, whole, tokens, segment, counts, mem_rows):
    slots = tokens.shape[0]
    rb = 512

    def fixed(*shape):
        return pl.BlockSpec(shape, lambda i: (0,) * len(shape))

    wide, tall = (H, HA, slots), (H, slots, 128)
    shapes = [wide, wide, wide, tall, tall] + [(H, HA, 128)] * 2 + [(H, MP, 128)] * 2 + [(1536, 512), (512, 128)]
    outs = [jax.ShapeDtypeStruct(s, BF16) for s in shapes]
    outs += [jax.ShapeDtypeStruct((8, 512), F32), jax.ShapeDtypeStruct((1, 2048), F32)]
    blk = pl.BlockSpec((H, HA, rb), lambda i: (0, 0, i))
    tblk = pl.BlockSpec((H, rb, 128), lambda i: (0, i, 0))
    specs = [blk, blk, blk, tblk, tblk] + [fixed(*o.shape) for o in outs[5:]]
    common = [
        pl.BlockSpec((rb, 512), lambda i: (i, 0)),
        pl.BlockSpec((1, rb), lambda i: (0, i)),
        pl.BlockSpec(memory_space=pltpu.SMEM),
    ]
    args = (tokens, segment.reshape(1, slots), counts)
    if whole is not None:
        found = pl.pallas_call(
            functools.partial(project_kernel, mem_rows),
            grid=(slots // rb,),
            in_specs=[fixed(PARTS, EARLY, 512)] + common,
            out_specs=specs,
            out_shape=outs,
            scratch_shapes=[pltpu.VMEM((512, 128), F32)],
            compiler_params=params(),
            name="projections",
        )(whole[:, 0:EARLY], *args)
        return (whole[:, EARLY:],) + tuple(found)
    weights = [p[name] for name in ("w_query", "w_key", "w_value", "w_out", "w_up", "w_down", "memory")]
    weights += [jnp.stack([p[name] for name in VECTORS]), p["b_up"].reshape(1, 64)]
    found = pl.pallas_call(
        functools.partial(gather_kernel, mem_rows),
        grid=(slots // rb,),
        in_specs=[fixed(*w.shape) for w in weights] + common,
        out_specs=[pl.BlockSpec(memory_space=pl.ANY)] + specs,
        out_shape=[jax.ShapeDtypeStruct((4, 2, 2, 2, LATE, 512), BF16)] + outs,
        scratch_shapes=[
            pltpu.VMEM((ROWS, 512), BF16),
            pltpu.VMEM((4, 2, 2, 2, EARLY, 512), BF16),
            pltpu.VMEM((512, 128), F32),
            pltpu.SemaphoreType.DMA((GATHER_COPIES,)),
            pltpu.SemaphoreType.DMA((GATHER_COPIES,)),
            pltpu.SemaphoreType.DMA,
        ],
        compiler_params=params(collective_id=0, has_side_effects=True),
        name="gather_projections",
    )(*weights, *args)
    return (found[0].reshape(PARTS, LATE, 512),) + tuple(found[1:])


def key_ranges(seg, count, slots, out):
    r, c = seg.shape
    pos = lax.broadcasted_iota(jnp.int32, (r, c), 0) * c + lax.broadcasted_iota(jnp.int32, (r, c), 1)
    valid = pos < count
    ends = [jnp.sum(jnp.where(valid & (seg <= s), 1.0, 0.0)).astype(jnp.int32) for s in range(3)]
    for block in range(slots // BQ):
        first = block * BQ
        last = jnp.minimum(first + BQ, count)
        low, high, start = jnp.int32(slots), jnp.int32(0), jnp.int32(0)
        for end in ends:
            hit = (end > first) & (start < last) & (end > start)
            low = jnp.where(hit, jnp.minimum(low, start), low)
            high = jnp.where(hit, jnp.maximum(high, end), high)
            start = end
        begin = low // 128
        blocks = jnp.where(high > low, (high - begin * 128 + BK - 1) // BK, 0)
        out[0, block] = jnp.minimum(begin, slots // 128 - blocks * (BK // 128))
        out[1, block] = blocks


def key_slots(begin, block):
    return pl.ds(pl.multiple_of((begin + block * (BK // 128)) * 128, 128), BK)


def pipelined(blocks, work, first, second):
    @pl.when(blocks > 0)
    def _():
        work((0, first), None)

    pairs = jnp.maximum(blocks - 1, 0) // 2

    @pl.loop(0, pairs)
    def _(i):
        work((2 * i + 1, second), (2 * i, first))
        work((2 * i + 2, first), (2 * i + 1, second))

    j = 2 * pairs

    @pl.when(blocks - j == 2)
    def _():
        work((j + 1, second), (j, first))
        work(None, (j + 1, second))

    @pl.when(blocks - j == 1)
    def _():
        work(None, (j, first))


def fwd_kernel(
    slots, seg_ref, cnt_ref, qa_ref, kn_ref, va_ref, kmn_ref, vm_ref,
    mix_ref, lse_ref, acc_ref, m_ref, sa_ref, sb_ref, range_ref,
):
    step = pl.program_id(0)

    @pl.when(step == 0)
    def _():
        key_ranges(seg_ref[...], cnt_ref[0], slots, range_ref)

    begin, blocks = range_ref[0, step], range_ref[1, step]

    def weights(h, s):
        old = m_ref[h : h + 1, :]
        top = jnp.maximum(old, jnp.max(s, axis=0, keepdims=True))
        return jnp.exp(s - top).astype(BF16), jnp.exp(old - top), top

    def work(new, old):
        kept = {}
        for h in range(H + 1):
            if h < H and new:
                new[1][h] = dot(kn_ref[h, key_slots(begin, new[0]), 0:HA], qa_ref[h], 1, 0)
            if h < H and old:
                kept[h] = weights(h, old[1][h])
            if h > 0 and old:
                p, fade, top = kept.pop(h - 1)
                acc_ref[h - 1] = acc_ref[h - 1] * fade + dot(va_ref[h - 1, :, key_slots(begin, old[0])], p, 1, 0)
                m_ref[h - 1 : h, :] = top

    scores = [dot(kmn_ref[h, :, 0:HA], qa_ref[h], 1, 0) for h in range(H)]
    for h in range(H):
        top = jnp.max(scores[h], axis=0, keepdims=True)
        p = jnp.exp(scores[h] - top).astype(BF16)
        acc_ref[h] = dot(vm_ref[h, :, 0:MP], p, 1, 0)
        m_ref[h : h + 1, :] = top
    pipelined(blocks, work, sa_ref, sb_ref)
    for h in range(H):
        total = acc_ref[h, 64:65, :]
        mix_ref[64 * h : 64 * h + 64, :] = (acc_ref[h, 0:64, :] * (1.0 / total)).astype(BF16)
        lse_ref[h : h + 1, :] = m_ref[h : h + 1, :] + jnp.log(total)


def attend_forward(seg2, counts, qa, kn, va, kmn, vm):
    slots = qa.shape[2]
    once = pl.Buffered(1)

    def whole(a):
        return pl.BlockSpec(a.shape, lambda i: (0, 0, 0), pipeline_mode=once)

    return pl.pallas_call(
        functools.partial(fwd_kernel, slots),
        grid=(slots // BQ,),
        in_specs=[
            pl.BlockSpec(seg2.shape, lambda i: (0, 0)),
            pl.BlockSpec(memory_space=pltpu.SMEM),
            pl.BlockSpec((H, HA, BQ), lambda i: (0, 0, i)),
            whole(kn), whole(va), whole(kmn), whole(vm),
        ],
        out_specs=[pl.BlockSpec((512, BQ), lambda i: (0, i)), pl.BlockSpec((H, BQ), lambda i: (0, i))],
        out_shape=[jax.ShapeDtypeStruct((512, slots), BF16), jax.ShapeDtypeStruct((H, slots), F32)],
        scratch_shapes=[
            pltpu.VMEM((H, HA, BQ), F32),
            pltpu.VMEM((H, BQ), F32),
            pltpu.VMEM((H, BK, BQ), F32),
            pltpu.VMEM((H, BK, BQ), F32),
            pltpu.SMEM((2, slots // BQ), jnp.int32),
        ],
        compiler_params=params(),
        name="attend_forward",
    )(seg2, counts, qa, kn, va, kmn, vm)


def norm_parts(value):
    mean = jnp.mean(value, axis=-1, keepdims=True)
    centred = value - mean
    rstd = lax.rsqrt(jnp.mean(centred * centred, axis=-1, keepdims=True) + EPS)
    return centred * rstd, rstd


def norm_grad(grad_hat, hat, rstd):
    return rstd * (
        grad_hat
        - jnp.mean(grad_hat, axis=-1, keepdims=True)
        - hat * jnp.mean(grad_hat * hat, axis=-1, keepdims=True)
    )


def colsum(value):
    return jnp.sum(value, axis=0, keepdims=True)


def mid_kernel(
    rb, cnt_ref, row_ref, rbup_ref, late_ref, mix_ref, tok_ref, cot_ref,
    out_ref, gfirst_ref, mgrad_ref, delta_ref, gw_ref, vec_ref, bup_ref,
    wup_ref, wdn_ref, aup_ref, adn_ref, ao_ref,
):
    step = pl.program_id(0)

    @pl.when(step == 0)
    def _():
        for c in range(4):
            wup_ref[:, 512 * c : 512 * c + 512] = late_ref[:, 16 * c : 16 * c + 16, :].reshape(512, 512)
        wdn_ref[...] = late_ref[:, 64:128, :].reshape(2048, 512)
        aup_ref[...] = jnp.zeros_like(aup_ref)
        adn_ref[...] = jnp.zeros_like(adn_ref)
        ao_ref[...] = jnp.zeros_like(ao_ref)
        vec_ref[...] = jnp.zeros_like(vec_ref)
        bup_ref[...] = jnp.zeros_like(bup_ref)

    wo = late_ref[:, 128:144, :].reshape(512, 512)

    def row(v):
        return row_ref[v : v + 1, :]

    mixt = mix_ref[...]
    attention = dot(mixt, wo, 0, 0) + row(V_BO)
    hat1, rstd1 = norm_parts(tok_ref[...].astype(F32) + attention)
    first = hat1 * row(V_GA) + row(V_SA)
    first_low = first.astype(BF16)
    hidden = dot(first_low, wup_ref[...], 1, 0) + rbup_ref[...]
    cdf = 0.5 + 0.5 * lax.erf(hidden * (2.0 ** -0.5))
    active = (hidden * cdf).astype(BF16)
    slope = cdf + hidden * jnp.exp(hidden * hidden * -0.5) * 0.3989422804014327
    branch = dot(active, wdn_ref[...], 1, 0) + row(V_BD)
    hat2, rstd2 = norm_parts(first + branch)
    valid = lax.broadcasted_iota(jnp.int32, (rb, 1), 0) + step * rb < cnt_ref[0]
    out_ref[...] = jnp.where(valid, hat2 * row(V_GF) + row(V_SF), 0.0).astype(BF16)

    seed = jnp.where(valid, cot_ref[...].astype(F32), 0.0)
    vec_ref[V_GF : V_GF + 1, :] += colsum(seed * hat2)
    vec_ref[V_SF : V_SF + 1, :] += colsum(seed)
    grad_second = norm_grad(seed * row(V_GF), hat2, rstd2)
    branch_grad = grad_second.astype(BF16)
    adn_ref[...] += dot(active, branch_grad, 0, 0)
    vec_ref[V_BD : V_BD + 1, :] += colsum(branch_grad.astype(F32))
    hidden_grad = (dot(branch_grad, wdn_ref[...], 1, 1) * slope).astype(BF16)
    aup_ref[...] += dot(first_low, hidden_grad, 0, 0)
    bup_ref[...] += colsum(hidden_grad.astype(F32))
    first_grad = grad_second + dot(hidden_grad, wup_ref[...], 1, 1)
    vec_ref[V_GA : V_GA + 1, :] += colsum(first_grad * hat1)
    vec_ref[V_SA : V_SA + 1, :] += colsum(first_grad)
    grad_first = norm_grad(first_grad * row(V_GA), hat1, rstd1)
    gfirst_ref[...] = grad_first
    attention_grad = grad_first.astype(BF16)
    vec_ref[V_BO : V_BO + 1, :] += colsum(attention_grad.astype(F32))
    ao_ref[...] += dot(mixt, attention_grad, 1, 0)
    mgrad = dot(wo, attention_grad, 1, 1).astype(BF16)
    mgrad_ref[...] = mgrad
    prod = mgrad.astype(F32) * mixt.astype(F32)
    for h in range(H):
        delta_ref[h : h + 1, :] = jnp.sum(prod[64 * h : 64 * h + 64, :], axis=0, keepdims=True)

    @pl.when(step == pl.num_programs(0) - 1)
    def _():
        gw_ref[:, 0:16, :] = ao_ref[...].astype(gw_ref.dtype).reshape(PARTS, 16, 512)
        for c in range(4):
            gw_ref[:, 16 + 16 * c : 32 + 16 * c, :] = (
                aup_ref[:, 512 * c : 512 * c + 512].astype(gw_ref.dtype).reshape(PARTS, 16, 512)
            )
        gw_ref[:, 80:144, :] = adn_ref[...].astype(gw_ref.dtype).reshape(PARTS, 64, 512)


def middle(late, rows8, rbup, counts, mixt, tokens, cotangent, rb=256):
    slots = tokens.shape[0]
    rows = pl.BlockSpec((rb, 512), lambda i: (i, 0))
    cols = pl.BlockSpec((512, rb), lambda i: (0, i))
    once = pl.Buffered(1)
    return pl.pallas_call(
        functools.partial(mid_kernel, rb),
        grid=(slots // rb,),
        in_specs=[
            pl.BlockSpec(memory_space=pltpu.SMEM),
            pl.BlockSpec((8, 512), lambda i: (0, 0)),
            pl.BlockSpec((1, 2048), lambda i: (0, 0)),
            pl.BlockSpec((PARTS, LATE, 512), lambda i: (0, 0, 0), pipeline_mode=once),
            cols, rows, rows,
        ],
        out_specs=[
            rows, rows, cols,
            pl.BlockSpec((H, rb), lambda i: (0, i)),
            pl.BlockSpec((PARTS, 144, 512), lambda i: (0, 0, 0), pipeline_mode=once),
            pl.BlockSpec((8, 512), lambda i: (0, 0)),
            pl.BlockSpec((1, 2048), lambda i: (0, 0)),
        ],
        out_shape=[
            jax.ShapeDtypeStruct((slots, 512), BF16),
            jax.ShapeDtypeStruct((slots, 512), F32),
            jax.ShapeDtypeStruct((512, slots), BF16),
            jax.ShapeDtypeStruct((H, slots), F32),
            jax.ShapeDtypeStruct((PARTS, 144, 512), BF16),
            jax.ShapeDtypeStruct((8, 512), F32),
            jax.ShapeDtypeStruct((1, 2048), F32),
        ],
        scratch_shapes=[
            pltpu.VMEM((512, 2048), BF16),
            pltpu.VMEM((2048, 512), BF16),
            pltpu.VMEM((512, 2048), F32),
            pltpu.VMEM((2048, 512), F32),
            pltpu.VMEM((512, 512), F32),
        ],
        compiler_params=params(),
        name="middle",
    )(counts, rows8, rbup, late, mixt, tokens, cotangent)


def split3(value):
    high = value.astype(BF16)
    rest = value - high.astype(F32)
    mid = rest.astype(BF16)
    return high, mid, (rest - mid.astype(F32)).astype(BF16)


def bwd_kernel(
    slots, seg_ref, cnt_ref, qa_ref, kn_ref, ka_ref, vn_ref, kmn_ref, km_ref, vmn_ref, do_ref, lse_ref, delta_ref,
    dq_ref, dk_ref, dv_ref, dkm_ref, dvm_ref,
    q2_ref, do2_ref, dqa_ref, dka_ref, dva_ref, dkma_ref, dvma_ref, sa_ref, ga_ref, sb_ref, gb_ref, range_ref,
):
    step = pl.program_id(0)

    @pl.when(step == 0)
    def _():
        key_ranges(seg_ref[...], cnt_ref[0], slots, range_ref)
        dka_ref[...] = jnp.zeros_like(dka_ref)
        dva_ref[...] = jnp.zeros_like(dva_ref)
        dkma_ref[...] = jnp.zeros_like(dkma_ref)
        dvma_ref[...] = jnp.zeros_like(dvma_ref)

    begin, blocks = range_ref[0, step], range_ref[1, step]
    frow = lax.broadcasted_iota(jnp.int32, (16, BQ), 0)

    def feature(value, at):
        high, mid, low = (jnp.broadcast_to(v.astype(F32), (16, BQ)) for v in split3(value))
        return jnp.where(frow == at, high, jnp.where(frow == at + 1, mid, jnp.where(frow == at + 2, low, 0.0)))

    for h in range(H):
        q2_ref[h, 0:64, :] = qa_ref[h, 0:64, :]
        q2_ref[h, 64:80, :] = (qa_ref[h, 64:80, :].astype(F32) + feature(-lse_ref[h : h + 1, :], 3)).astype(BF16)
        do2_ref[h, 0:64, :] = do_ref[64 * h : 64 * h + 64, :]
        do2_ref[h, 64:80, :] = feature(-delta_ref[h : h + 1, :], 0).astype(BF16)

    def work(new, old):
        kept = {}
        for h in range(H + 1):
            if h < H and new:
                ks = key_slots(begin, new[0])
                new[1][0][h] = dot(kn_ref[h, ks, 0:HA], q2_ref[h], 1, 0)
                new[1][1][h] = dot(vn_ref[h, ks, 0:HA], do2_ref[h], 1, 0)
            if h < H and old:
                p = jnp.exp(old[1][0][h])
                kept[h] = p.astype(BF16), (p * old[1][1][h]).astype(BF16)
            if h > 0 and old:
                ks = key_slots(begin, old[0])
                p, ds = kept.pop(h - 1)
                dva_ref[h - 1, :, ks] += dot(do2_ref[h - 1, 0:64, :], p, 1, 1)
                dka_ref[h - 1, :, ks] += dot(q2_ref[h - 1, 0:64, :], ds, 1, 1)
                dqa_ref[h - 1] += dot(ka_ref[h - 1, 0:64, ks], ds, 1, 0)

    ps = [jnp.exp(dot(kmn_ref[h, :, 0:HA], q2_ref[h], 1, 0)) for h in range(H)]
    dss = [(ps[h] * dot(vmn_ref[h, :, 0:HA], do2_ref[h], 1, 0)).astype(BF16) for h in range(H)]
    for h in range(H):
        dvma_ref[h, :, 0:MP] += dot(do2_ref[h, 0:64, :], ps[h].astype(BF16), 1, 1)
        dkma_ref[h, :, 0:MP] += dot(q2_ref[h, 0:64, :], dss[h], 1, 1)
        dqa_ref[h] = dot(km_ref[h, 0:64, 0:MP], dss[h], 1, 0)
    pipelined(blocks, work, (sa_ref, ga_ref), (sb_ref, gb_ref))
    for h in range(H):
        dq_ref[64 * h : 64 * h + 64, :] = (dqa_ref[h] * HD ** -0.5).astype(BF16)

    @pl.when(step == pl.num_programs(0) - 1)
    def _():
        for h in range(H):
            s = slice(64 * h, 64 * h + 64)
            dk_ref[s, :] = dka_ref[h].astype(BF16)
            dv_ref[s, :] = dva_ref[h].astype(BF16)
            dkm_ref[s, :] = dkma_ref[h].astype(BF16)
            dvm_ref[s, :] = dvma_ref[h].astype(BF16)


def attend_backward(seg2, counts, qa, kn, ka, vn, kmn, km, vmn, mgrad, lse, delta):
    slots = qa.shape[2]
    once = pl.Buffered(1)

    def full(a):
        return pl.BlockSpec(a.shape, lambda i: (0, 0, 0), pipeline_mode=once)

    cols = pl.BlockSpec((512, BQ), lambda i: (0, i))
    stat = pl.BlockSpec((H, BQ), lambda i: (0, i))
    whole = pl.BlockSpec((512, slots), lambda i: (0, 0), pipeline_mode=once)
    mwhole = pl.BlockSpec((512, 128), lambda i: (0, 0))
    block = pltpu.VMEM((H, BK, BQ), F32)
    return pl.pallas_call(
        functools.partial(bwd_kernel, slots),
        grid=(slots // BQ,),
        in_specs=[
            pl.BlockSpec(seg2.shape, lambda i: (0, 0)),
            pl.BlockSpec(memory_space=pltpu.SMEM),
            pl.BlockSpec((H, HA, BQ), lambda i: (0, 0, i)),
            full(kn), full(ka), full(vn), full(kmn), full(km), full(vmn), cols, stat, stat,
        ],
        out_specs=[cols, whole, whole, mwhole, mwhole],
        out_shape=[jax.ShapeDtypeStruct((512, slots), BF16)] * 3 + [jax.ShapeDtypeStruct((512, 128), BF16)] * 2,
        scratch_shapes=[
            pltpu.VMEM((H, HA, BQ), BF16),
            pltpu.VMEM((H, HA, BQ), BF16),
            pltpu.VMEM((H, HD, BQ), F32),
            pltpu.VMEM((H, HD, slots), F32),
            pltpu.VMEM((H, HD, slots), F32),
            pltpu.VMEM((H, HD, 128), F32),
            pltpu.VMEM((H, HD, 128), F32),
            block, block, block, block,
            pltpu.SMEM((2, slots // BQ), jnp.int32),
        ],
        compiler_params=params(),
        name="attend_backward",
    )(seg2, counts, qa, kn, ka, vn, kmn, km, vmn, mgrad, lse, delta)


SUM_EARLY = (
    (slice(0, 48), "yxz"),
    (slice(48, 96), "xyz"),
    (slice(96, 112), "xzy"),
    (slice(112, 144), "yzx"),
)
SUM_LATE = ((slice(144, 176), "xyz"), (slice(176, 208), "yxz"))
SUM_PARTS = SUM_EARLY + SUM_LATE
SUM_COPIES = 6 * len(SUM_PARTS)


def weight_grads(step, tok_ref, dq_ref, dk_ref, dv_ref, dkm_ref, dvm_ref, memt_ref, acc_ref, sum_ref):
    @pl.when(step == 0)
    def _():
        acc_ref[0:512, :] = jnp.zeros((512, 512), F32)
        acc_ref[512:1024, :] = dot(dkm_ref[...], memt_ref[...], 1, 1)
        acc_ref[1024:1536, :] = dot(dvm_ref[...], memt_ref[...], 1, 1)
        sum_ref[...] = jnp.zeros_like(sum_ref)
        sum_ref[:, 1:2] = jnp.sum(dvm_ref[...].astype(F32), axis=1, keepdims=True)

    tok = tok_ref[...]
    dq, dk, dv = dq_ref[...], dk_ref[...], dv_ref[...]
    acc_ref[0:512, :] += dot(dq, tok, 1, 0)
    acc_ref[512:1024, :] += dot(dk, tok, 1, 0)
    acc_ref[1024:1536, :] += dot(dv, tok, 1, 0)
    sum_ref[:, 0:1] += jnp.sum(dq.astype(F32), axis=1, keepdims=True)
    sum_ref[:, 1:2] += jnp.sum(dv.astype(F32), axis=1, keepdims=True)


def late_grads(dkm_ref, dvm_ref, vec_ref, bup_ref, wt_ref, acc_ref, sum_ref, late):
    for j in range(3):
        late(slice(16 * j, 16 * j + 16), slice(0, 512), acc_ref[512 * j : 512 * j + 512, :].T.astype(BF16))
    gmem = dot(wt_ref[512:1024, :], dkm_ref[...], 0, 0) + dot(wt_ref[1024:1536, :], dvm_ref[...], 0, 0)
    late(slice(48, 64), slice(0, 128), gmem.astype(BF16))
    lane = lax.broadcasted_iota(jnp.int32, (512, 128), 1)
    vecs = jnp.concatenate([vec_ref[...], jnp.zeros((120, 512), F32)], axis=0).T
    late(slice(48, 64), slice(128, 256), jnp.where(lane < 2, sum_ref[...], vecs).astype(BF16))
    rows = [bup_ref[0:1, 256 * v : 256 * v + 256] for v in range(8)] + [jnp.zeros((8, 256), F32)]
    rows = jnp.concatenate(rows, axis=0).astype(BF16)
    late(slice(48, 64), slice(256, 512), jnp.broadcast_to(rows[None], (PARTS, 16, 256)).reshape(512, 256))


def token_grads(gtok_ref, gfirst_ref, dq_ref, dk_ref, dv_ref, wt_ref):
    gtok_ref[...] = (
        gfirst_ref[...]
        + dot(dq_ref[...], wt_ref[0:512, :], 0, 0)
        + dot(dk_ref[...], wt_ref[512:1024, :], 0, 0)
        + dot(dv_ref[...], wt_ref[1024:1536, :], 0, 0)
    )


def scatter_kernel(
    half, tok_ref, dq_ref, dk_ref, dv_ref, dkm_ref, dvm_ref, gfirst_ref, vec_ref, bup_ref, wt_ref, memt_ref, early_ref,
    gtok_ref, out_ref, acc_ref, sum_ref, late, parts_sum, other, send, recv, local, *landing,
):
    step = pl.program_id(0)
    place = Place()
    copies = Copies(send, recv)
    slots = dict(zip(slot_shapes(SUM_PARTS), landing))
    crossing = [copies.number() for _ in SUM_PARTS]
    parts = []
    for index, (rows, order) in enumerate(SUM_PARTS):
        mine = {key[1:]: slot for key, slot in slots.items() if key[0] == index}
        parts.append(scatter_part(place, copies, parts_sum, mine, out_ref, rows, order))
    firsts, lasts = parts[: len(SUM_EARLY)], parts[len(SUM_EARLY) :]

    def load(index):
        rows = SUM_EARLY[index][0]
        return pltpu.make_async_copy(
            early_ref.at[:, :, :, place.core, rows], parts_sum.at[:, :, :, rows], local.at[index]
        )

    def cross(source, base, rows, number):
        old = slice(rows.start - base, rows.stop - base)
        copies.start(
            lambda: source.at[:, :, :, place.far, old], lambda: other.at[:, :, :, rows], number, place.partner
        )

    @pl.when(step == 0)
    def _():
        everyone = place.greet()
        for index in range(len(SUM_EARLY)):
            load(index).start()
        everyone()
        for number, (rows, _) in zip(crossing, SUM_EARLY):
            cross(early_ref, 0, rows, number)

    @pl.when(step == 2)
    def _():
        for index, (rows, _) in enumerate(SUM_EARLY):
            load(index).wait()
            join(place, copies, parts_sum, None, other, rows, crossing[index])
            next(firsts[index])

    @pl.when(step < half)
    def _():
        weight_grads(step, tok_ref, dq_ref, dk_ref, dv_ref, dkm_ref, dvm_ref, memt_ref, acc_ref, sum_ref)

    @pl.when(step == half - 1)
    def _():
        def put(rows, lanes, value):
            late[:, :, :, :, rows, lanes] = value.reshape(4, 2, 2, 2, 16, value.shape[1])

        late_grads(dkm_ref, dvm_ref, vec_ref, bup_ref, wt_ref, acc_ref, sum_ref, put)
        for number, (rows, _) in zip(crossing[len(SUM_EARLY) :], SUM_LATE):
            cross(late, LATE, rows, number)
        advance(firsts)

    @pl.when(step >= half)
    def _():
        token_grads(gtok_ref, gfirst_ref, dq_ref, dk_ref, dv_ref, wt_ref)

    @pl.when(step == half)
    def _():
        for index, (rows, _) in enumerate(SUM_LATE):
            join(
                place, copies, parts_sum,
                lambda z, old=slice(rows.start - LATE, rows.stop - LATE): late[z, :, :, place.core, old],
                other, rows, crossing[len(SUM_EARLY) + index],
            )
            next(lasts[index])

    @pl.when(step == half + 1)
    def _():
        advance(firsts)

    @pl.when(step == half + 2)
    def _():
        advance(lasts)

    @pl.when(step == 2 * half - 1)
    def _():
        advance(firsts)
        advance(lasts)
        advance(lasts)
        copies.finish()


def plain_kernel(
    half, tok_ref, dq_ref, dk_ref, dv_ref, dkm_ref, dvm_ref, gfirst_ref, vec_ref, bup_ref, wt_ref, memt_ref,
    gtok_ref, late_ref, acc_ref, sum_ref,
):
    step = pl.program_id(0)

    @pl.when(step < half)
    def _():
        weight_grads(step, tok_ref, dq_ref, dk_ref, dv_ref, dkm_ref, dvm_ref, memt_ref, acc_ref, sum_ref)

    @pl.when(step == half - 1)
    def _():
        def put(rows, lanes, value):
            late_ref[:, rows, lanes] = value.reshape(PARTS, 16, value.shape[1])

        late_grads(dkm_ref, dvm_ref, vec_ref, bup_ref, wt_ref, acc_ref, sum_ref, put)

    @pl.when(step >= half)
    def _():
        token_grads(gtok_ref, gfirst_ref, dq_ref, dk_ref, dv_ref, wt_ref)


def tail(early, tokens, dq, dk, dv, dkm, dvm, gfirst, vec, bup, wt, memt, remote):
    slots = tokens.shape[0]
    rb = 512
    half = slots // rb

    def fixed(*shape):
        return pl.BlockSpec(shape, lambda i: (0,) * len(shape))

    cols = pl.BlockSpec((512, rb), lambda i: (0, i % half))
    later = pl.BlockSpec((rb, 512), lambda i: (jnp.maximum(i - half, 0), 0))
    in_specs = [
        pl.BlockSpec((rb, 512), lambda i: (jnp.minimum(i, half - 1), 0)),
        cols, cols, cols, fixed(512, 128), fixed(512, 128), later,
        fixed(8, 512), fixed(1, 2048), fixed(1536, 512), fixed(512, 128),
    ]
    args = (tokens, dq, dk, dv, dkm, dvm, gfirst, vec, bup, wt, memt)
    gtok = jax.ShapeDtypeStruct((slots, 512), F32)
    scratch = [pltpu.VMEM((1536, 512), F32), pltpu.VMEM((512, 128), F32)]
    if not remote:
        return pl.pallas_call(
            functools.partial(plain_kernel, half),
            grid=(2 * half,),
            in_specs=in_specs,
            out_specs=[later, fixed(PARTS, EARLY, 512)],
            out_shape=[gtok, jax.ShapeDtypeStruct((PARTS, EARLY, 512), BF16)],
            scratch_shapes=scratch,
            compiler_params=params(),
            name="tail",
        )(*args)
    return pl.pallas_call(
        functools.partial(scatter_kernel, half),
        grid=(2 * half,),
        in_specs=in_specs + [pl.BlockSpec(memory_space=pl.ANY)],
        out_specs=[later, fixed(ROWS, 512)],
        out_shape=[gtok, jax.ShapeDtypeStruct((ROWS, 512), F32)],
        scratch_shapes=scratch
        + [
            pltpu.VMEM((4, 2, 2, 2, EARLY, 512), BF16),
            pltpu.VMEM((4, 2, 2, ROWS, 512), BF16),
            pltpu.VMEM((4, 2, 2, ROWS, 512), BF16),
            pltpu.SemaphoreType.DMA((SUM_COPIES,)),
            pltpu.SemaphoreType.DMA((SUM_COPIES,)),
            pltpu.SemaphoreType.DMA((len(SUM_EARLY),)),
        ]
        + [pltpu.VMEM(shape, BF16) for shape in slot_shapes(SUM_PARTS).values()],
        compiler_params=params(collective_id=1, has_side_effects=True),
        name="tail_scatter",
    )(*args, early.reshape(4, 2, 2, 2, LATE, 512))


def unpack_kernel(sum_ref, wo, up, dn, wq, wk, wv, memory, vectors, b_up):
    me = lax.axis_index("dp")
    wo[...] = sum_ref[0:16]
    for c in range(4):
        up[:, 512 * c : 512 * c + 512] = sum_ref[16 + 16 * c : 32 + 16 * c]
    dn[...] = sum_ref[80:144]
    wq[...] = sum_ref[144:160]
    wk[...] = sum_ref[160:176]
    wv[...] = sum_ref[176:192]
    memory[...] = sum_ref[192:208, 0:128].T[0 : memory.shape[0], :]
    vectors[...] = sum_ref[192:208, 128:256].T[0:8, :]
    row = lax.broadcasted_iota(jnp.int32, (16, 256), 0)
    lane = lax.broadcasted_iota(jnp.int32, (16, 256), 1)
    own = jnp.sum(jnp.where(row * 4 + lane // 64 == me, sum_ref[192:208, 256:512], 0.0), axis=0, keepdims=True)
    b_up[...] = own[:, 0:64] + own[:, 64:128] + own[:, 128:192] + own[:, 192:256]


def unpack(sums, mem_rows):
    shapes = [(16, 512), (16, 2048), (64, 512), (16, 512), (16, 512), (16, 512), (mem_rows, 16), (8, 16), (1, 64)]
    found = pl.pallas_call(
        unpack_kernel,
        out_shape=[jax.ShapeDtypeStruct(s, F32) for s in shapes],
        compiler_params=params(),
        name="unpack",
    )(sums)
    out = dict(zip(("w_out", "w_up", "w_down", "w_query", "w_key", "w_value", "memory"), found[:7]))
    for index, name in enumerate(VECTORS):
        out[name] = found[7][index]
    out["b_up"] = found[8].reshape(64)
    return out


NAMES = (
    "memory", "w_query", "b_query", "w_key", "w_value", "b_value", "w_out", "b_out", "gain_attn",
    "shift_attn", "w_up", "b_up", "w_down", "b_down", "gain_ffn", "shift_ffn",
)


def pack_whole(p):
    mem_rows = p["memory"].shape[0]
    mats = [p[name].reshape(PARTS, 16, 512) for name in ("w_query", "w_key", "w_value", "w_out")]
    up = p["w_up"].reshape(PARTS, 16, 4, 512).transpose(0, 2, 1, 3).reshape(PARTS, 64, 512)
    memory = jnp.pad(p["memory"].T, ((0, 0), (0, 128 - mem_rows))).reshape(PARTS, 16, 128)
    vectors = jnp.stack([p[name] for name in VECTORS], axis=1)
    vectors = jnp.pad(vectors, ((0, 0), (0, 120))).reshape(PARTS, 16, 128)
    own = jnp.arange(2048)[None] // 64 == jnp.arange(PARTS)[:, None]
    b_up = jnp.where(own, p["b_up"][None], 0).astype(BF16).reshape(PARTS, 8, 256)
    b_up = jnp.pad(b_up, ((0, 0), (0, 8), (0, 0)))
    small = jnp.concatenate([memory, vectors, b_up], axis=2)
    return jnp.concatenate(mats[:3] + [small, up, p["w_down"].reshape(PARTS, 64, 512), mats[3]], axis=1)


def unpack_whole(early, late, mem_rows):
    small = late[:, 48:64]
    vectors = small[:, :, 128:136].reshape(512, 8)
    out = {
        "memory": small[:, :, 0:mem_rows].reshape(512, mem_rows).T,
        "w_query": late[:, 0:16].reshape(512, 512),
        "w_key": late[:, 16:32].reshape(512, 512),
        "w_value": late[:, 32:48].reshape(512, 512),
        "w_out": early[:, 0:16].reshape(512, 512),
        "w_up": early[:, 16:80].reshape(PARTS, 4, 16, 512).transpose(0, 2, 1, 3).reshape(512, 2048),
        "w_down": early[:, 80:144].reshape(2048, 512),
        "b_up": small[0, 0:8, 256:512].reshape(2048),
    }
    for index, name in enumerate(VECTORS):
        out[name] = vectors[:, index]
    return out


def axis_of(name):
    return 1 if name == "memory" else 0


def shards(n, tokens, segment, counts, *rest):
    p = dict(zip(NAMES, rest[:-1]))
    cotangent = rest[-1]
    slots = tokens.shape[0]
    mem_rows = p["memory"].shape[0]
    whole = None
    if n != PARTS:
        whole = pack_whole({k: lax.all_gather(v, "dp", axis=axis_of(k), tiled=True) for k, v in p.items()})
    found = projections(p, whole, tokens, segment, counts, mem_rows)
    late, qa, ka, va, kn, vn, km, vm, kmn, vmn, wt, memt, rows8, rbup = found
    seg2 = segment.reshape(slots // 128, 128)
    mixt, lse = attend_forward(seg2, counts, qa, kn, va, kmn, vm)
    output, gfirst, mgrad, delta, early, vec, bup = middle(late, rows8, rbup, counts, mixt, tokens, cotangent)
    dq, dk, dv, dkm, dvm = attend_backward(seg2, counts, qa, kn, ka, vn, kmn, km, vmn, mgrad, lse, delta)
    gtok, sums = tail(early, tokens, dq, dk, dv, dkm, dvm, gfirst, vec, bup, wt, memt, n == PARTS)
    if n == PARTS:
        grads = unpack(sums, mem_rows)
    else:
        full = unpack_whole(early.astype(F32), sums.astype(F32), mem_rows)
        grads = {
            k: lax.psum_scatter(v, "dp", scatter_dimension=axis_of(k), tiled=True) for k, v in full.items()
        }
    return (output, gtok) + tuple(grads[name] for name in NAMES)


def solution(mesh):
    n = mesh.shape["dp"]
    row, mat, mem = P("dp"), P("dp", None), P(None, "dp")
    spec = {name: mat if name.startswith("w_") else row for name in NAMES}
    spec["memory"] = mem
    weights = tuple(spec[name] for name in NAMES)
    return jax.shard_map(
        functools.partial(shards, n),
        mesh=mesh,
        in_specs=(mat, row, row) + weights + (mat,),
        out_specs=(mat, mat) + weights,
        check_vma=False,
    )
```

```python
import functools
import jax
import jax.numpy as jnp
from jax import lax
from jax.experimental import pallas as pl
from jax.experimental.pallas import tpu as pltpu
from jax.sharding import PartitionSpec as P

H = 8
HD = 64
HA = 80
EPS = 1e-05
BIG = 1e30
PARTS = 32
ROWS = 208
BQ = 256
BK = 256
MP = 32
LONGEST = 1024
F32 = jnp.float32
BF16 = jnp.bfloat16
VMEM_LIMIT = 60 << 20

V_BQ, V_BV, V_BO, V_GA, V_SA, V_BD, V_GF, V_SF = range(8)


def dot(left, right, lc, rc):
    return lax.dot_general(left, right, (((lc,), (rc,)), ((), ())), preferred_element_type=F32)


def params(**kw):
    return pltpu.CompilerParams(vmem_limit_bytes=VMEM_LIMIT, **kw)


MESH = pl.DeviceIdType.MESH
AXES = {"z": (8, 4), "y": (4, 2), "x": (2, 2)}
LAYOUT = ("z", "y", "x")


class Place:
    def __init__(self):
        me = lax.axis_index("dp")
        self.me = me
        self.core = me % 2
        self.far = 1 - self.core
        self.partner = me + 1 - 2 * self.core
        self.at = {a: (me // stride) % length for a, (stride, length) in AXES.items()}
        self.mine = tuple(self.at[a] for a in LAYOUT)
        self.others = {}
        for axis, (stride, length) in AXES.items():
            for distance in range(1, length):
                j = (self.at[axis] + distance) % length
                self.others[axis, distance] = j, me + (j - self.at[axis]) * stride

    def other(self, axis, distance):
        return self.others[axis, distance]

    def greet(self):
        barrier = pltpu.get_barrier_semaphore()
        peers = [self.partner]
        for axis in LAYOUT:
            peers += [self.other(axis, d)[1] for d in range(1, AXES[axis][1])]
        for peer in peers:
            pl.semaphore_signal(barrier, inc=1, device_id=(peer,), device_id_type=MESH)
        return lambda: pl.semaphore_wait(barrier, len(peers))


class Copies:
    def __init__(self, send, recv):
        self.send, self.recv, self.count, self.open = send, recv, 0, []

    def number(self):
        self.count += 1
        return self.count - 1

    def make(self, src, dst, number, device):
        return pltpu.make_async_remote_copy(
            src_ref=src, dst_ref=dst, send_sem=self.send.at[number], recv_sem=self.recv.at[number],
            device_id=(device,), device_id_type=MESH,
        )

    def start(self, src, dst, number, device):
        self.make(src(), dst(), number, device).start()
        self.open.append((src, dst, number, device))

    def landed(self, block, number, device):
        self.make(block, block, number, device).wait_recv()

    def finish(self):
        for src, dst, number, device in self.open:
            self.make(src(), dst(), number, device).wait_send()
        self.open = []


def gather_part(place, copies, own, base, whole, rows, order, arrivals):
    done = ()

    def mine():
        return own.at[slice(base + rows.start, base + rows.stop)]

    def block(axis, j, core):
        index = tuple(j if a == axis else (slice(None) if a in done else place.at[a]) for a in LAYOUT)
        return lambda: whole.at[index + (core, rows)]

    for axis in order:
        length = AXES[axis][1]
        numbers = [copies.number() for _ in range(2 * length - 2)]
        here = block(axis, place.at[axis], place.core)
        for d in range(1, length):
            copies.start(here if done else mine, here, numbers[d - 1], place.other(axis, d)[1])
        if not done:
            number = copies.number()
            copies.start(mine, here, number, place.partner)
            arrivals.append((block(axis, place.at[axis], place.far), number))
        yield
        for d in range(1, length):
            j, device = place.other(axis, length - d)
            there = block(axis, j, place.core)
            copies.landed(there(), numbers[d - 1], device)
            number = numbers[length - 2 + d]
            copies.start(there, there, number, place.partner)
            arrivals.append((block(axis, j, place.far), number))
        done += (axis,)
    yield


def advance(parts):
    for part in parts:
        next(part)


def scatter_part(place, copies, acc, slots, out, rows, order):
    done = ()

    def block(axis, j):
        index = tuple(j if a == axis else (place.at[a] if a in done else slice(None)) for a in LAYOUT)
        return index + (rows,)

    def taken(index):
        return lambda: acc.at[index]

    def landing(axis, d):
        return lambda: slots[axis, d]

    for axis in order:
        length = AXES[axis][1]
        numbers = [copies.number() for _ in range(length - 1)]
        for d in range(1, length):
            j, device = place.other(axis, d)
            copies.start(taken(block(axis, j)), landing(axis, d), numbers[d - 1], device)
        yield
        for d in range(1, length):
            copies.landed(slots[axis, d], numbers[d - 1], place.partner)
        mine = block(axis, place.at[axis])
        total = acc[mine].astype(F32)
        for d in range(1, length):
            total = total + slots[axis, d][...].astype(F32)
        if axis == order[-1]:
            out[rows, :] = total
        else:
            acc[mine] = total.astype(BF16)
        done += (axis,)
    yield


def slot_shapes(parts):
    shapes = {}
    for number, (rows, order) in enumerate(parts):
        left = ["z", "y", "x"]
        for axis in order:
            left.remove(axis)
            shape = tuple(AXES[a][1] for a in LAYOUT if a in left) + (rows.stop - rows.start, 512)
            for d in range(1, AXES[axis][1]):
                shapes[number, axis, d] = shape
    return shapes


def join(place, copies, acc, source, other, rows, number):
    copies.landed(other.at[:, :, :, rows], number, place.partner)

    @pl.loop(0, 4)
    def _(z):
        mine = source(z) if source else acc[z, :, :, rows]
        acc[z, :, :, rows] = (mine.astype(F32) + other[z, :, :, rows].astype(F32)).astype(BF16)


VECTORS = ("b_query", "b_value", "b_out", "gain_attn", "shift_attn", "b_down", "gain_ffn", "shift_ffn")
EARLY = 64
LATE = 144
EARLY_PARTS = ((slice(0, 32), "zxy"), (slice(32, 64), "zyx"))
LATE_PARTS = (
    (slice(0, 48), "zxy"),
    (slice(48, 96), "zyx"),
    (slice(96, 128), "yzx"),
    (slice(128, 144), "xzy"),
)
GATHER_COPIES = 11 * (len(EARLY_PARTS) + len(LATE_PARTS))


def head_block(rows, features):
    block = jnp.concatenate([rows, features], axis=0)
    return block, jnp.concatenate([block, jnp.zeros((128 - HA, rows.shape[1]), BF16)], axis=0).T


def pack(own, place, wq, wk, wv, wo, up, dn, memory, b_up, vectors):
    own[0:16] = wq[...]
    own[16:32] = wk[...]
    own[32:48] = wv[...]
    own[48:64] = jnp.zeros((16, 512), BF16)
    own[48:64, 0 : memory.shape[1]] = memory[...]
    values = jnp.concatenate([vector[...].astype(F32) for vector in vectors], axis=0)
    own[48:64, 128:136] = values.T.astype(BF16)
    value = jnp.concatenate([b_up[...].astype(F32)] * 4, axis=1)
    row = lax.broadcasted_iota(jnp.int32, (16, 256), 0)
    lane = lax.broadcasted_iota(jnp.int32, (16, 256), 1)
    own[48:64, 256:512] = jnp.where(row * 4 + lane // 64 == place.me, value, 0.0).astype(BF16)
    for c in range(4):
        own[64 + 16 * c : 80 + 16 * c] = up[:, 512 * c : 512 * c + 512]
    own[128:192] = dn[...]
    own[192:208] = wo[...]


def prepare(mem_rows, early, wt_ref, memt_ref, rows_ref, rbup_ref, bias_ref, km_ref, vm_ref, kmn_ref, vmn_ref):
    for j in range(3):
        wt_ref[512 * j : 512 * j + 512, :] = early[..., 16 * j : 16 * j + 16, :].reshape(512, 512).T
    small = early[..., 48:64, 0:256].reshape(512, 256)
    memt = small[:, 0:128]
    memt_ref[...] = memt
    vectors = small[:, 128:256].astype(F32)
    bias_ref[...] = vectors
    rows_ref[...] = vectors.T[0:8, :]
    bup = jnp.sum(early[..., 48:64, 256:512].reshape(PARTS, 16, 256).astype(F32), axis=0)
    for v in range(8):
        rbup_ref[0:1, 256 * v : 256 * v + 256] = bup[v : v + 1, :]
    bv = vectors[:, V_BV : V_BV + 1]
    km = dot(wt_ref[512:1024, :], memt, 1, 0).astype(BF16)
    vm = (dot(wt_ref[1024:1536, :], memt, 1, 0) + bv).astype(BF16)
    frow = lax.broadcasted_iota(jnp.int32, (16, 128), 0)
    lane = lax.broadcasted_iota(jnp.int32, (16, 128), 1)
    kf = jnp.where(frow < 3, jnp.where(lane < mem_rows, 0.0, 1.0), jnp.where(frow < 6, 1.0, 0.0)).astype(BF16)
    vf = jnp.where(frow < 3, 1.0, 0.0).astype(BF16)
    for h in range(H):
        km_ref[h], turned = head_block(km[64 * h : 64 * h + 64, :], kf)
        kmn_ref[h] = turned[0:MP]
        vm_ref[h], turned = head_block(vm[64 * h : 64 * h + 64, :], vf)
        vmn_ref[h] = turned[0:MP]


def project(step, tok_ref, seg_ref, cnt_ref, wt_ref, bias_ref, qa_ref, ka_ref, va_ref, kn_ref, vn_ref):
    rows = tok_ref.shape[0]
    tok = tok_ref[...]
    bq = bias_ref[:, V_BQ : V_BQ + 1]
    bv = bias_ref[:, V_BV : V_BV + 1]
    q = (dot(wt_ref[0:512, :], tok, 1, 1) + bq).astype(BF16) * jnp.asarray(HD ** -0.5, BF16)
    k = dot(wt_ref[512:1024, :], tok, 1, 1).astype(BF16)
    v = (dot(wt_ref[1024:1536, :], tok, 1, 1) + bv).astype(BF16)
    frow = lax.broadcasted_iota(jnp.int32, (16, rows), 0)
    seg = jnp.broadcast_to(seg_ref[...], (16, rows))
    pos = lax.broadcasted_iota(jnp.int32, (16, rows), 1) + step * rows
    valid = pos < cnt_ref[0]
    qf = jnp.where((frow < 3) & (frow != seg), -BIG, 0.0).astype(BF16)
    kf = jnp.where(frow < 3, jnp.where(valid & (frow != seg), 0.0, 1.0), jnp.where(frow < 6, 1.0, 0.0)).astype(BF16)
    vf = jnp.where(frow < 3, 1.0, 0.0).astype(BF16)
    for h in range(H):
        s = slice(64 * h, 64 * h + 64)
        qa_ref[h, 0:64, :] = q[s]
        qa_ref[h, 64:80, :] = qf
        ka_ref[h], kn_ref[h] = head_block(k[s], kf)
        va_ref[h], vn_ref[h] = head_block(v[s], vf)


def gather_kernel(
    mem_rows, half, wq, wk, wv, wo, up, dn, memory, b_up, v0, v1, v2, v3, v4, v5, v6, v7, tok_ref, seg_ref, cnt_ref,
    late_ref, qa_ref, ka_ref, kn_ref, vn_ref, km_ref, kmn_ref, vmn_ref,
    wt_ref, memt_ref, rows_ref, rbup_ref, mix_ref, lse_ref,
    own, early, bias_ref, vm_ref, va_block, qa_all, kn_all, va_all, acc_ref, m_ref, sa_ref, sb_ref, send, recv, local,
):
    step = pl.program_id(0)
    slots = kn_all.shape[1]
    place = Place()
    copies = Copies(send, recv)
    arrivals, late_arrivals = [], []
    firsts = [gather_part(place, copies, own, 0, early, *part, arrivals) for part in EARLY_PARTS]
    lasts = [gather_part(place, copies, own, EARLY, late_ref, *part, late_arrivals) for part in LATE_PARTS]

    @pl.when(step == 0)
    def _():
        everyone = place.greet()
        pack(own, place, wq, wk, wv, wo, up, dn, memory, b_up, (v0, v1, v2, v3, v4, v5, v6, v7))
        early[place.mine + (place.core,)] = own[0:EARLY]
        everyone()
        advance(firsts)
        keep = pltpu.make_async_copy(own.at[EARLY:ROWS], late_ref.at[place.mine + (place.core,)], local)
        keep.start()
        advance(firsts)
        advance(firsts)
        keep.wait()
        advance(lasts)
        advance(firsts)
        for block, number in arrivals:
            copies.landed(block(), number, place.partner)
        prepare(
            mem_rows, early, wt_ref, memt_ref, rows_ref, rbup_ref, bias_ref, km_ref, vm_ref, kmn_ref, vmn_ref,
        )

    @pl.when(step < half)
    def _():
        project(step, tok_ref, seg_ref, cnt_ref, wt_ref, bias_ref, qa_ref, ka_ref, va_block, kn_ref, vn_ref)
        here = pl.ds(pl.multiple_of(step * tok_ref.shape[0], 128), tok_ref.shape[0])
        qa_all[:, :, here] = qa_ref[...]
        va_all[:, :, here] = va_block[...]
        kn_all[:, here, :] = kn_ref[...]

    @pl.when(step == half - 1)
    def _():
        advance(lasts)

    @pl.when(step >= half)
    def _():
        block = step - half
        reach = LONGEST // BQ
        begin = jnp.maximum(block - reach, 0)
        end = jnp.minimum(block + reach + 1, slots // BQ)
        queries = qa_all.at[:, :, pl.ds(pl.multiple_of(block * BQ, BQ), BQ)]
        attend(
            begin * (BQ // 128), (end - begin) * (BQ // BK), queries, kn_all, va_all, kmn_ref, vm_ref, mix_ref, lse_ref,
            acc_ref, m_ref, sa_ref, sb_ref,
        )

    @pl.when(step == half + 2)
    def _():
        advance(lasts)

    @pl.when(step == pl.num_programs(0) - 1)
    def _():
        advance(lasts)
        for block, number in late_arrivals:
            copies.landed(block(), number, place.partner)
        copies.finish()


def project_kernel(
    mem_rows, g_ref, tok_ref, seg_ref, cnt_ref, qa_ref, ka_ref, va_ref, kn_ref, vn_ref, km_ref, vm_ref, kmn_ref, vmn_ref,
    wt_ref, memt_ref, rows_ref, rbup_ref, bias_ref,
):
    step = pl.program_id(0)

    @pl.when(step == 0)
    def _():
        prepare(
            mem_rows, g_ref, wt_ref, memt_ref, rows_ref, rbup_ref, bias_ref, km_ref, vm_ref, kmn_ref, vmn_ref
        )

    project(step, tok_ref, seg_ref, cnt_ref, wt_ref, bias_ref, qa_ref, ka_ref, va_ref, kn_ref, vn_ref)


def fixed(*shape):
    return pl.BlockSpec(shape, lambda i: (0,) * len(shape))


def projections(p, whole, tokens, segment, counts, mem_rows):
    slots = tokens.shape[0]
    rb = 512
    half = slots // rb
    wide, tall = (H, HA, slots), (H, slots, 128)
    mwide, mtall = (H, HA, 128), (H, MP, 128)

    def at(i):
        return jnp.minimum(i, half - 1)

    blk = pl.BlockSpec((H, HA, rb), lambda i: (0, 0, at(i)))
    tblk = pl.BlockSpec((H, rb, 128), lambda i: (0, at(i), 0))
    common = [
        pl.BlockSpec((rb, 512), lambda i: (at(i), 0)),
        pl.BlockSpec((1, rb), lambda i: (0, at(i))),
        pl.BlockSpec(memory_space=pltpu.SMEM),
    ]
    args = (tokens, segment.reshape(1, slots), counts)

    def outs(shapes):
        found = [jax.ShapeDtypeStruct(s, BF16) for s in shapes]
        return found + [jax.ShapeDtypeStruct((8, 512), F32), jax.ShapeDtypeStruct((1, 2048), F32)]

    if whole is not None:
        shapes = outs([wide, wide, wide, tall, tall, mwide, mwide, mtall, mtall, (1536, 512), (512, 128)])
        found = pl.pallas_call(
            functools.partial(project_kernel, mem_rows),
            grid=(half,),
            in_specs=[fixed(PARTS, EARLY, 512)] + common,
            out_specs=[blk, blk, blk, tblk, tblk] + [fixed(*o.shape) for o in shapes[5:]],
            out_shape=shapes,
            scratch_shapes=[pltpu.VMEM((512, 128), F32)],
            compiler_params=params(),
            name="projections",
        )(whole[:, 0:EARLY], *args)
        qa, ka, va, kn, vn, km, vm, kmn, vmn, wt, memt, rows8, rbup = found
        mixt, lse = attend_forward(segment.reshape(slots // 128, 128), counts, qa, kn, va, kmn, vm)
        return whole[:, EARLY:], qa, ka, kn, vn, km, kmn, vmn, wt, memt, rows8, rbup, mixt, lse
    weights = [p[name] for name in ("w_query", "w_key", "w_value", "w_out", "w_up", "w_down")]
    weights += [p["memory"].T, p["b_up"].reshape(1, 64)] + [p[name].reshape(1, 16) for name in VECTORS]
    shapes = outs([wide, wide, tall, tall, mwide, mtall, mtall, (1536, 512), (512, 128)])
    found = pl.pallas_call(
        functools.partial(gather_kernel, mem_rows, half),
        grid=(half + slots // BQ,),
        in_specs=[fixed(*w.shape) for w in weights] + common,
        out_specs=[pl.BlockSpec(memory_space=pl.ANY), blk, blk, tblk, tblk]
        + [fixed(*o.shape) for o in shapes[4:]]
        + [
            pl.BlockSpec((512, BQ), lambda i: (0, jnp.maximum(i - half, 0))),
            pl.BlockSpec((H, BQ), lambda i: (0, jnp.maximum(i - half, 0))),
        ],
        out_shape=[jax.ShapeDtypeStruct((4, 2, 2, 2, LATE, 512), BF16)]
        + shapes
        + [jax.ShapeDtypeStruct((512, slots), BF16), jax.ShapeDtypeStruct((H, slots), F32)],
        scratch_shapes=[
            pltpu.VMEM((ROWS, 512), BF16),
            pltpu.VMEM((4, 2, 2, 2, EARLY, 512), BF16),
            pltpu.VMEM((512, 128), F32),
            pltpu.VMEM(mwide, BF16),
            pltpu.VMEM((H, HA, rb), BF16),
            pltpu.VMEM(wide, BF16),
            pltpu.VMEM(tall, BF16),
            pltpu.VMEM(wide, BF16),
            pltpu.VMEM((H, HA, BQ), F32),
            pltpu.VMEM((H, BQ), F32),
            pltpu.VMEM((H, BK, BQ), F32),
            pltpu.VMEM((H, BK, BQ), F32),
            pltpu.SemaphoreType.DMA((GATHER_COPIES,)),
            pltpu.SemaphoreType.DMA((GATHER_COPIES,)),
            pltpu.SemaphoreType.DMA,
        ],
        compiler_params=params(collective_id=0, has_side_effects=True),
        name="gather_attend",
    )(*weights, *args)
    return (found[0].reshape(PARTS, LATE, 512),) + tuple(found[1:])


def key_ranges(seg, count, slots, out):
    r, c = seg.shape
    pos = lax.broadcasted_iota(jnp.int32, (r, c), 0) * c + lax.broadcasted_iota(jnp.int32, (r, c), 1)
    valid = pos < count
    ends = [jnp.sum(jnp.where(valid & (seg <= s), 1.0, 0.0)).astype(jnp.int32) for s in range(3)]
    for block in range(slots // BQ):
        first = block * BQ
        last = jnp.minimum(first + BQ, count)
        low, high, start = jnp.int32(slots), jnp.int32(0), jnp.int32(0)
        for end in ends:
            hit = (end > first) & (start < last) & (end > start)
            low = jnp.where(hit, jnp.minimum(low, start), low)
            high = jnp.where(hit, jnp.maximum(high, end), high)
            start = end
        begin = low // 128
        blocks = jnp.where(high > low, (high - begin * 128 + BK - 1) // BK, 0)
        out[0, block] = jnp.minimum(begin, slots // 128 - blocks * (BK // 128))
        out[1, block] = blocks


def key_slots(begin, block):
    return pl.ds(pl.multiple_of((begin + block * (BK // 128)) * 128, 128), BK)


def pipelined(blocks, work, first, second):
    @pl.when(blocks > 0)
    def _():
        work((0, first), None)

    pairs = jnp.maximum(blocks - 1, 0) // 2

    @pl.loop(0, pairs)
    def _(i):
        work((2 * i + 1, second), (2 * i, first))
        work((2 * i + 2, first), (2 * i + 1, second))

    j = 2 * pairs

    @pl.when(blocks - j == 2)
    def _():
        work((j + 1, second), (j, first))
        work(None, (j + 1, second))

    @pl.when(blocks - j == 1)
    def _():
        work(None, (j, first))


def attend(begin, blocks, qa_ref, kn_ref, va_ref, kmn_ref, vm_ref, mix_ref, lse_ref, acc_ref, m_ref, sa_ref, sb_ref):
    def weights(h, s):
        old = m_ref[h : h + 1, :]
        top = jnp.maximum(old, jnp.max(s, axis=0, keepdims=True))
        return jnp.exp(s - top).astype(BF16), jnp.exp(old - top), top

    def work(new, old):
        kept = {}
        for h in range(H + 1):
            if h < H and new:
                new[1][h] = dot(kn_ref[h, key_slots(begin, new[0]), 0:HA], qa_ref[h], 1, 0)
            if h < H and old:
                kept[h] = weights(h, old[1][h])
            if h > 0 and old:
                p, fade, top = kept.pop(h - 1)
                acc_ref[h - 1] = acc_ref[h - 1] * fade + dot(va_ref[h - 1, :, key_slots(begin, old[0])], p, 1, 0)
                m_ref[h - 1 : h, :] = top

    scores = [dot(kmn_ref[h, :, 0:HA], qa_ref[h], 1, 0) for h in range(H)]
    for h in range(H):
        top = jnp.max(scores[h], axis=0, keepdims=True)
        p = jnp.exp(scores[h] - top).astype(BF16)
        acc_ref[h] = dot(vm_ref[h, :, 0:MP], p, 1, 0)
        m_ref[h : h + 1, :] = top
    pipelined(blocks, work, sa_ref, sb_ref)
    for h in range(H):
        total = acc_ref[h, 64:65, :]
        mix_ref[64 * h : 64 * h + 64, :] = (acc_ref[h, 0:64, :] * (1.0 / total)).astype(BF16)
        lse_ref[h : h + 1, :] = m_ref[h : h + 1, :] + jnp.log(total)


def fwd_kernel(
    slots, seg_ref, cnt_ref, qa_ref, kn_ref, va_ref, kmn_ref, vm_ref,
    mix_ref, lse_ref, acc_ref, m_ref, sa_ref, sb_ref, range_ref,
):
    step = pl.program_id(0)

    @pl.when(step == 0)
    def _():
        key_ranges(seg_ref[...], cnt_ref[0], slots, range_ref)

    attend(
        range_ref[0, step], range_ref[1, step], qa_ref, kn_ref, va_ref, kmn_ref, vm_ref, mix_ref, lse_ref,
        acc_ref, m_ref, sa_ref, sb_ref,
    )


def attend_forward(seg2, counts, qa, kn, va, kmn, vm):
    slots = qa.shape[2]
    once = pl.Buffered(1)

    def whole(a):
        return pl.BlockSpec(a.shape, lambda i: (0, 0, 0), pipeline_mode=once)

    return pl.pallas_call(
        functools.partial(fwd_kernel, slots),
        grid=(slots // BQ,),
        in_specs=[
            pl.BlockSpec(seg2.shape, lambda i: (0, 0)),
            pl.BlockSpec(memory_space=pltpu.SMEM),
            pl.BlockSpec((H, HA, BQ), lambda i: (0, 0, i)),
            whole(kn), whole(va), whole(kmn), whole(vm),
        ],
        out_specs=[pl.BlockSpec((512, BQ), lambda i: (0, i)), pl.BlockSpec((H, BQ), lambda i: (0, i))],
        out_shape=[jax.ShapeDtypeStruct((512, slots), BF16), jax.ShapeDtypeStruct((H, slots), F32)],
        scratch_shapes=[
            pltpu.VMEM((H, HA, BQ), F32),
            pltpu.VMEM((H, BQ), F32),
            pltpu.VMEM((H, BK, BQ), F32),
            pltpu.VMEM((H, BK, BQ), F32),
            pltpu.SMEM((2, slots // BQ), jnp.int32),
        ],
        compiler_params=params(),
        name="attend_forward",
    )(seg2, counts, qa, kn, va, kmn, vm)


def norm_parts(value):
    mean = jnp.mean(value, axis=-1, keepdims=True)
    centred = value - mean
    rstd = lax.rsqrt(jnp.mean(centred * centred, axis=-1, keepdims=True) + EPS)
    return centred * rstd, rstd


def norm_grad(grad_hat, hat, rstd):
    return rstd * (
        grad_hat
        - jnp.mean(grad_hat, axis=-1, keepdims=True)
        - hat * jnp.mean(grad_hat * hat, axis=-1, keepdims=True)
    )


def colsum(value):
    return jnp.sum(value, axis=0, keepdims=True)


SUB = 256
FC = 512


def mid_kernel(
    rb, cnt_ref, row_ref, rbup_ref, late_ref, mix_ref, tok_ref, cot_ref,
    out_ref, gfirst_ref, mgrad_ref, delta_ref, gw_ref, vec_ref, bup_ref,
    wup_ref, wdn_ref, aup_ref, adn_ref, ao_ref, *scratch,
):
    step = pl.program_id(0)
    subs = rb // SUB

    @pl.when(step == 0)
    def _():
        for c in range(4):
            wup_ref[:, 512 * c : 512 * c + 512] = late_ref[:, 16 * c : 16 * c + 16, :].reshape(512, 512)
        wdn_ref[...] = late_ref[:, 64:128, :].reshape(2048, 512)
        aup_ref[...] = jnp.zeros_like(aup_ref)
        adn_ref[...] = jnp.zeros_like(adn_ref)
        ao_ref[...] = jnp.zeros_like(ao_ref)
        vec_ref[...] = jnp.zeros_like(vec_ref)
        bup_ref[...] = jnp.zeros_like(bup_ref)

    wo = late_ref[:, 128:144, :].reshape(512, 512)

    def row(v):
        return row_ref[v : v + 1, :]

    class Block:
        def __init__(self, index):
            self.s = slice(SUB * index, SUB * index + SUB)
            self.first_row = step * rb + SUB * index
            self.active, self.slope, self.hgrad = scratch[3 * (index % 2) : 3 * (index % 2) + 3]
            self.up_part, self.dact_part = {}, {}

        def head(self):
            self.mixt = mix_ref[:, self.s]
            attention = dot(self.mixt, wo, 0, 0) + row(V_BO)
            self.hat1, self.rstd1 = norm_parts(tok_ref[self.s, :].astype(F32) + attention)
            self.first = self.hat1 * row(V_GA) + row(V_SA)
            self.low = self.first.astype(BF16)
            self.branch = self.first + row(V_BD)

        def up(self, c):
            f = slice(FC * c, FC * c + FC)
            self.up_part[c] = dot(self.low, wup_ref[:, f], 1, 0) + rbup_ref[:, f]

        def gelu(self, c):
            f = slice(FC * c, FC * c + FC)
            hidden = self.up_part.pop(c)
            cdf = 0.5 + 0.5 * lax.erf(hidden * (2.0 ** -0.5))
            self.active[:, f] = (hidden * cdf).astype(BF16)
            self.slope[:, f] = cdf + hidden * jnp.exp(hidden * hidden * -0.5) * 0.3989422804014327

        def down(self, c):
            f = slice(FC * c, FC * c + FC)
            self.branch = self.branch + dot(self.active[:, f], wdn_ref[f, :], 1, 0)

        def turn(self):
            hat2, rstd2 = norm_parts(self.branch)
            valid = lax.broadcasted_iota(jnp.int32, (SUB, 1), 0) + self.first_row < cnt_ref[0]
            out_ref[self.s, :] = jnp.where(valid, hat2 * row(V_GF) + row(V_SF), 0.0).astype(BF16)
            seed = jnp.where(valid, cot_ref[self.s, :].astype(F32), 0.0)
            vec_ref[V_GF : V_GF + 1, :] += colsum(seed * hat2)
            vec_ref[V_SF : V_SF + 1, :] += colsum(seed)
            self.total = norm_grad(seed * row(V_GF), hat2, rstd2)
            self.bgrad = self.total.astype(BF16)
            vec_ref[V_BD : V_BD + 1, :] += colsum(self.bgrad.astype(F32))

        def dact(self, c):
            f = slice(FC * c, FC * c + FC)
            self.dact_part[c] = dot(self.bgrad, wdn_ref[f, :], 1, 1)

        def grad_down(self, c):
            f = slice(FC * c, FC * c + FC)
            adn_ref[f, :] += dot(self.active[:, f], self.bgrad, 0, 0)

        def hidden_grad(self, c):
            f = slice(FC * c, FC * c + FC)
            grad = (self.dact_part.pop(c) * self.slope[:, f]).astype(BF16)
            self.hgrad[:, f] = grad
            bup_ref[:, f] += colsum(grad.astype(F32))

        def grad_up(self, c):
            f = slice(FC * c, FC * c + FC)
            aup_ref[:, f] += dot(self.low, self.hgrad[:, f], 0, 0)

        def first_grad(self, c):
            f = slice(FC * c, FC * c + FC)
            self.total = self.total + dot(self.hgrad[:, f], wup_ref[:, f], 1, 1)

        def finish(self):
            vec_ref[V_GA : V_GA + 1, :] += colsum(self.total * self.hat1)
            vec_ref[V_SA : V_SA + 1, :] += colsum(self.total)
            grad_first = norm_grad(self.total * row(V_GA), self.hat1, self.rstd1)
            gfirst_ref[self.s, :] = grad_first
            agrad = grad_first.astype(BF16)
            vec_ref[V_BO : V_BO + 1, :] += colsum(agrad.astype(F32))
            mgrad = dot(wo, agrad, 1, 1).astype(BF16)
            ao_ref[...] += dot(self.mixt, agrad, 1, 0)
            mgrad_ref[:, self.s] = mgrad
            prod = mgrad.astype(F32) * self.mixt.astype(F32)
            for h in range(H):
                delta_ref[h : h + 1, self.s] = jnp.sum(prod[64 * h : 64 * h + 64, :], axis=0, keepdims=True)

    chunks = 2048 // FC

    def both(ahead, behind):
        if ahead:
            ahead.head()
            ahead.up(0)
        for c in range(chunks):
            if behind:
                behind.dact(c)
            if ahead and c + 1 < chunks:
                ahead.up(c + 1)
            if behind:
                behind.grad_down(c)
            if ahead:
                ahead.gelu(c)
            if behind:
                behind.hidden_grad(c)
                behind.grad_up(c)
                behind.first_grad(c)
            if ahead:
                ahead.down(c)
        if behind:
            behind.finish()
        if ahead:
            ahead.turn()

    blocks = [Block(index) for index in range(subs)]
    for ahead, behind in zip(blocks + [None], [None] + blocks):
        both(ahead, behind)

    @pl.when(step == pl.num_programs(0) - 1)
    def _():
        gw_ref[:, 0:16, :] = ao_ref[...].astype(gw_ref.dtype).reshape(PARTS, 16, 512)
        for c in range(4):
            gw_ref[:, 16 + 16 * c : 32 + 16 * c, :] = (
                aup_ref[:, 512 * c : 512 * c + 512].astype(gw_ref.dtype).reshape(PARTS, 16, 512)
            )
        gw_ref[:, 80:144, :] = adn_ref[...].astype(gw_ref.dtype).reshape(PARTS, 64, 512)


def middle(late, rows8, rbup, counts, mixt, tokens, cotangent, rb=512):
    slots = tokens.shape[0]
    rows = pl.BlockSpec((rb, 512), lambda i: (i, 0))
    cols = pl.BlockSpec((512, rb), lambda i: (0, i))
    once = pl.Buffered(1)
    return pl.pallas_call(
        functools.partial(mid_kernel, rb),
        grid=(slots // rb,),
        in_specs=[
            pl.BlockSpec(memory_space=pltpu.SMEM),
            pl.BlockSpec((8, 512), lambda i: (0, 0)),
            pl.BlockSpec((1, 2048), lambda i: (0, 0)),
            pl.BlockSpec((PARTS, LATE, 512), lambda i: (0, 0, 0), pipeline_mode=once),
            cols, rows, rows,
        ],
        out_specs=[
            rows, rows, cols,
            pl.BlockSpec((H, rb), lambda i: (0, i)),
            pl.BlockSpec((PARTS, 144, 512), lambda i: (0, 0, 0), pipeline_mode=once),
            pl.BlockSpec((8, 512), lambda i: (0, 0)),
            pl.BlockSpec((1, 2048), lambda i: (0, 0)),
        ],
        out_shape=[
            jax.ShapeDtypeStruct((slots, 512), BF16),
            jax.ShapeDtypeStruct((slots, 512), F32),
            jax.ShapeDtypeStruct((512, slots), BF16),
            jax.ShapeDtypeStruct((H, slots), F32),
            jax.ShapeDtypeStruct((PARTS, 144, 512), BF16),
            jax.ShapeDtypeStruct((8, 512), F32),
            jax.ShapeDtypeStruct((1, 2048), F32),
        ],
        scratch_shapes=[
            pltpu.VMEM((512, 2048), BF16),
            pltpu.VMEM((2048, 512), BF16),
            pltpu.VMEM((512, 2048), F32),
            pltpu.VMEM((2048, 512), F32),
            pltpu.VMEM((512, 512), F32),
        ]
        + [pltpu.VMEM((SUB, 2048), BF16), pltpu.VMEM((SUB, 2048), F32), pltpu.VMEM((SUB, 2048), BF16)] * 2,
        compiler_params=params(),
        name="middle",
    )(counts, rows8, rbup, late, mixt, tokens, cotangent)


def split3(value):
    high = value.astype(BF16)
    rest = value - high.astype(F32)
    mid = rest.astype(BF16)
    return high, mid, (rest - mid.astype(F32)).astype(BF16)


def bwd_kernel(
    slots, seg_ref, cnt_ref, qa_ref, kn_ref, ka_ref, vn_ref, kmn_ref, km_ref, vmn_ref, do_ref, lse_ref, delta_ref,
    dq_ref, dk_ref, dv_ref, dkm_ref, dvm_ref,
    q2_ref, do2_ref, dqa_ref, dka_ref, dva_ref, dkma_ref, dvma_ref, sa_ref, ga_ref, sb_ref, gb_ref, range_ref,
):
    step = pl.program_id(0)

    @pl.when(step == 0)
    def _():
        key_ranges(seg_ref[...], cnt_ref[0], slots, range_ref)
        dka_ref[...] = jnp.zeros_like(dka_ref)
        dva_ref[...] = jnp.zeros_like(dva_ref)
        dkma_ref[...] = jnp.zeros_like(dkma_ref)
        dvma_ref[...] = jnp.zeros_like(dvma_ref)

    begin, blocks = range_ref[0, step], range_ref[1, step]
    frow = lax.broadcasted_iota(jnp.int32, (16, BQ), 0)

    def feature(value, at):
        high, mid, low = (jnp.broadcast_to(v.astype(F32), (16, BQ)) for v in split3(value))
        return jnp.where(frow == at, high, jnp.where(frow == at + 1, mid, jnp.where(frow == at + 2, low, 0.0)))

    for h in range(H):
        q2_ref[h, 0:64, :] = qa_ref[h, 0:64, :]
        q2_ref[h, 64:80, :] = (qa_ref[h, 64:80, :].astype(F32) + feature(-lse_ref[h : h + 1, :], 3)).astype(BF16)
        do2_ref[h, 0:64, :] = do_ref[64 * h : 64 * h + 64, :]
        do2_ref[h, 64:80, :] = feature(-delta_ref[h : h + 1, :], 0).astype(BF16)

    def work(new, old):
        kept = {}
        for h in range(H + 1):
            if h < H and new:
                ks = key_slots(begin, new[0])
                new[1][0][h] = dot(kn_ref[h, ks, 0:HA], q2_ref[h], 1, 0)
                new[1][1][h] = dot(vn_ref[h, ks, 0:HA], do2_ref[h], 1, 0)
            if h < H and old:
                p = jnp.exp(old[1][0][h])
                kept[h] = p.astype(BF16), (p * old[1][1][h]).astype(BF16)
            if h > 0 and old:
                ks = key_slots(begin, old[0])
                p, ds = kept.pop(h - 1)
                dva_ref[h - 1, :, ks] += dot(do2_ref[h - 1, 0:64, :], p, 1, 1)
                dka_ref[h - 1, :, ks] += dot(q2_ref[h - 1, 0:64, :], ds, 1, 1)
                dqa_ref[h - 1] += dot(ka_ref[h - 1, 0:64, ks], ds, 1, 0)

    ps = [jnp.exp(dot(kmn_ref[h, :, 0:HA], q2_ref[h], 1, 0)) for h in range(H)]
    dss = [(ps[h] * dot(vmn_ref[h, :, 0:HA], do2_ref[h], 1, 0)).astype(BF16) for h in range(H)]
    for h in range(H):
        dvma_ref[h, :, 0:MP] += dot(do2_ref[h, 0:64, :], ps[h].astype(BF16), 1, 1)
        dkma_ref[h, :, 0:MP] += dot(q2_ref[h, 0:64, :], dss[h], 1, 1)
        dqa_ref[h] = dot(km_ref[h, 0:64, 0:MP], dss[h], 1, 0)
    pipelined(blocks, work, (sa_ref, ga_ref), (sb_ref, gb_ref))
    for h in range(H):
        dq_ref[64 * h : 64 * h + 64, :] = (dqa_ref[h] * HD ** -0.5).astype(BF16)

    @pl.when(step == pl.num_programs(0) - 1)
    def _():
        for h in range(H):
            s = slice(64 * h, 64 * h + 64)
            dk_ref[s, :] = dka_ref[h].astype(BF16)
            dv_ref[s, :] = dva_ref[h].astype(BF16)
            dkm_ref[s, :] = dkma_ref[h].astype(BF16)
            dvm_ref[s, :] = dvma_ref[h].astype(BF16)


def attend_backward(seg2, counts, qa, kn, ka, vn, kmn, km, vmn, mgrad, lse, delta):
    slots = qa.shape[2]
    once = pl.Buffered(1)

    def full(a):
        return pl.BlockSpec(a.shape, lambda i: (0, 0, 0), pipeline_mode=once)

    cols = pl.BlockSpec((512, BQ), lambda i: (0, i))
    stat = pl.BlockSpec((H, BQ), lambda i: (0, i))
    whole = pl.BlockSpec((512, slots), lambda i: (0, 0), pipeline_mode=once)
    mwhole = pl.BlockSpec((512, 128), lambda i: (0, 0))
    block = pltpu.VMEM((H, BK, BQ), F32)
    return pl.pallas_call(
        functools.partial(bwd_kernel, slots),
        grid=(slots // BQ,),
        in_specs=[
            pl.BlockSpec(seg2.shape, lambda i: (0, 0)),
            pl.BlockSpec(memory_space=pltpu.SMEM),
            pl.BlockSpec((H, HA, BQ), lambda i: (0, 0, i)),
            full(kn), full(ka), full(vn), full(kmn), full(km), full(vmn), cols, stat, stat,
        ],
        out_specs=[cols, whole, whole, mwhole, mwhole],
        out_shape=[jax.ShapeDtypeStruct((512, slots), BF16)] * 3 + [jax.ShapeDtypeStruct((512, 128), BF16)] * 2,
        scratch_shapes=[
            pltpu.VMEM((H, HA, BQ), BF16),
            pltpu.VMEM((H, HA, BQ), BF16),
            pltpu.VMEM((H, HD, BQ), F32),
            pltpu.VMEM((H, HD, slots), F32),
            pltpu.VMEM((H, HD, slots), F32),
            pltpu.VMEM((H, HD, 128), F32),
            pltpu.VMEM((H, HD, 128), F32),
            block, block, block, block,
            pltpu.SMEM((2, slots // BQ), jnp.int32),
        ],
        compiler_params=params(),
        name="attend_backward",
    )(seg2, counts, qa, kn, ka, vn, kmn, km, vmn, mgrad, lse, delta)


SUM_EARLY = (
    (slice(0, 48), "yxz"),
    (slice(48, 96), "xyz"),
    (slice(96, 112), "xzy"),
    (slice(112, 144), "yzx"),
)
SUM_LATE = ((slice(144, 176), "xyz"), (slice(176, 208), "yxz"))
SUM_PARTS = SUM_EARLY + SUM_LATE
SUM_COPIES = 6 * len(SUM_PARTS)


def weight_grads(step, tok_ref, dq_ref, dk_ref, dv_ref, dkm_ref, dvm_ref, memt_ref, acc_ref, sum_ref):
    @pl.when(step == 0)
    def _():
        acc_ref[0:512, :] = jnp.zeros((512, 512), F32)
        acc_ref[512:1024, :] = dot(dkm_ref[...], memt_ref[...], 1, 1)
        acc_ref[1024:1536, :] = dot(dvm_ref[...], memt_ref[...], 1, 1)
        sum_ref[...] = jnp.zeros_like(sum_ref)
        sum_ref[:, 1:2] = jnp.sum(dvm_ref[...].astype(F32), axis=1, keepdims=True)

    tok = tok_ref[...]
    dq, dk, dv = dq_ref[...], dk_ref[...], dv_ref[...]
    acc_ref[0:512, :] += dot(dq, tok, 1, 0)
    acc_ref[512:1024, :] += dot(dk, tok, 1, 0)
    acc_ref[1024:1536, :] += dot(dv, tok, 1, 0)
    sum_ref[:, 0:1] += jnp.sum(dq.astype(F32), axis=1, keepdims=True)
    sum_ref[:, 1:2] += jnp.sum(dv.astype(F32), axis=1, keepdims=True)


def late_grads(dkm_ref, dvm_ref, vec_ref, bup_ref, wt_ref, acc_ref, sum_ref, late):
    for j in range(3):
        late(slice(16 * j, 16 * j + 16), slice(0, 512), acc_ref[512 * j : 512 * j + 512, :].T.astype(BF16))
    gmem = dot(wt_ref[512:1024, :], dkm_ref[...], 0, 0) + dot(wt_ref[1024:1536, :], dvm_ref[...], 0, 0)
    late(slice(48, 64), slice(0, 128), gmem.astype(BF16))
    lane = lax.broadcasted_iota(jnp.int32, (512, 128), 1)
    vecs = jnp.concatenate([vec_ref[...], jnp.zeros((120, 512), F32)], axis=0).T
    late(slice(48, 64), slice(128, 256), jnp.where(lane < 2, sum_ref[...], vecs).astype(BF16))
    rows = [bup_ref[0:1, 256 * v : 256 * v + 256] for v in range(8)] + [jnp.zeros((8, 256), F32)]
    rows = jnp.concatenate(rows, axis=0).astype(BF16)
    late(slice(48, 64), slice(256, 512), jnp.broadcast_to(rows[None], (PARTS, 16, 256)).reshape(512, 256))


def token_grads(gtok_ref, gfirst_ref, dq_ref, dk_ref, dv_ref, wt_ref):
    gtok_ref[...] = (
        gfirst_ref[...]
        + dot(dq_ref[...], wt_ref[0:512, :], 0, 0)
        + dot(dk_ref[...], wt_ref[512:1024, :], 0, 0)
        + dot(dv_ref[...], wt_ref[1024:1536, :], 0, 0)
    )


def scatter_kernel(
    half, tok_ref, dq_ref, dk_ref, dv_ref, dkm_ref, dvm_ref, gfirst_ref, vec_ref, bup_ref, wt_ref, memt_ref, early_ref,
    gtok_ref, out_ref, acc_ref, sum_ref, late, parts_sum, other, send, recv, local, *landing,
):
    step = pl.program_id(0)
    place = Place()
    copies = Copies(send, recv)
    slots = dict(zip(slot_shapes(SUM_PARTS), landing))
    crossing = [copies.number() for _ in SUM_PARTS]
    parts = []
    for index, (rows, order) in enumerate(SUM_PARTS):
        mine = {key[1:]: slot for key, slot in slots.items() if key[0] == index}
        parts.append(scatter_part(place, copies, parts_sum, mine, out_ref, rows, order))
    firsts, lasts = parts[: len(SUM_EARLY)], parts[len(SUM_EARLY) :]

    def load(index):
        rows = SUM_EARLY[index][0]
        return pltpu.make_async_copy(
            early_ref.at[:, :, :, place.core, rows], parts_sum.at[:, :, :, rows], local.at[index]
        )

    def cross(source, base, rows, number):
        old = slice(rows.start - base, rows.stop - base)
        copies.start(
            lambda: source.at[:, :, :, place.far, old], lambda: other.at[:, :, :, rows], number, place.partner
        )

    @pl.when(step == 0)
    def _():
        everyone = place.greet()
        for index in range(len(SUM_EARLY)):
            load(index).start()
        everyone()
        for number, (rows, _) in zip(crossing, SUM_EARLY):
            cross(early_ref, 0, rows, number)

    @pl.when(step == 2)
    def _():
        for index, (rows, _) in enumerate(SUM_EARLY):
            load(index).wait()
            join(place, copies, parts_sum, None, other, rows, crossing[index])
            next(firsts[index])

    @pl.when(step < half)
    def _():
        weight_grads(step, tok_ref, dq_ref, dk_ref, dv_ref, dkm_ref, dvm_ref, memt_ref, acc_ref, sum_ref)

    @pl.when(step == half - 1)
    def _():
        def put(rows, lanes, value):
            late[:, :, :, :, rows, lanes] = value.reshape(4, 2, 2, 2, 16, value.shape[1])

        late_grads(dkm_ref, dvm_ref, vec_ref, bup_ref, wt_ref, acc_ref, sum_ref, put)
        for number, (rows, _) in zip(crossing[len(SUM_EARLY) :], SUM_LATE):
            cross(late, LATE, rows, number)
        advance(firsts)

    @pl.when(step >= half)
    def _():
        token_grads(gtok_ref, gfirst_ref, dq_ref, dk_ref, dv_ref, wt_ref)

    @pl.when(step == half)
    def _():
        for index, (rows, _) in enumerate(SUM_LATE):
            join(
                place, copies, parts_sum,
                lambda z, old=slice(rows.start - LATE, rows.stop - LATE): late[z, :, :, place.core, old],
                other, rows, crossing[len(SUM_EARLY) + index],
            )
            next(lasts[index])

    @pl.when(step == half + 1)
    def _():
        advance(firsts)

    @pl.when(step == half + 2)
    def _():
        advance(lasts)

    @pl.when(step == 2 * half - 1)
    def _():
        advance(firsts)
        advance(lasts)
        advance(lasts)
        copies.finish()


def plain_kernel(
    half, tok_ref, dq_ref, dk_ref, dv_ref, dkm_ref, dvm_ref, gfirst_ref, vec_ref, bup_ref, wt_ref, memt_ref,
    gtok_ref, late_ref, acc_ref, sum_ref,
):
    step = pl.program_id(0)

    @pl.when(step < half)
    def _():
        weight_grads(step, tok_ref, dq_ref, dk_ref, dv_ref, dkm_ref, dvm_ref, memt_ref, acc_ref, sum_ref)

    @pl.when(step == half - 1)
    def _():
        def put(rows, lanes, value):
            late_ref[:, rows, lanes] = value.reshape(PARTS, 16, value.shape[1])

        late_grads(dkm_ref, dvm_ref, vec_ref, bup_ref, wt_ref, acc_ref, sum_ref, put)

    @pl.when(step >= half)
    def _():
        token_grads(gtok_ref, gfirst_ref, dq_ref, dk_ref, dv_ref, wt_ref)


def tail(early, tokens, dq, dk, dv, dkm, dvm, gfirst, vec, bup, wt, memt, remote):
    slots = tokens.shape[0]
    rb = 512
    half = slots // rb

    cols = pl.BlockSpec((512, rb), lambda i: (0, i % half))
    later = pl.BlockSpec((rb, 512), lambda i: (jnp.maximum(i - half, 0), 0))
    in_specs = [
        pl.BlockSpec((rb, 512), lambda i: (jnp.minimum(i, half - 1), 0)),
        cols, cols, cols, fixed(512, 128), fixed(512, 128), later,
        fixed(8, 512), fixed(1, 2048), fixed(1536, 512), fixed(512, 128),
    ]
    args = (tokens, dq, dk, dv, dkm, dvm, gfirst, vec, bup, wt, memt)
    gtok = jax.ShapeDtypeStruct((slots, 512), F32)
    scratch = [pltpu.VMEM((1536, 512), F32), pltpu.VMEM((512, 128), F32)]
    if not remote:
        return pl.pallas_call(
            functools.partial(plain_kernel, half),
            grid=(2 * half,),
            in_specs=in_specs,
            out_specs=[later, fixed(PARTS, EARLY, 512)],
            out_shape=[gtok, jax.ShapeDtypeStruct((PARTS, EARLY, 512), BF16)],
            scratch_shapes=scratch,
            compiler_params=params(),
            name="tail",
        )(*args)
    return pl.pallas_call(
        functools.partial(scatter_kernel, half),
        grid=(2 * half,),
        in_specs=in_specs + [pl.BlockSpec(memory_space=pl.ANY)],
        out_specs=[later, fixed(ROWS, 512)],
        out_shape=[gtok, jax.ShapeDtypeStruct((ROWS, 512), F32)],
        scratch_shapes=scratch
        + [
            pltpu.VMEM((4, 2, 2, 2, EARLY, 512), BF16),
            pltpu.VMEM((4, 2, 2, ROWS, 512), BF16),
            pltpu.VMEM((4, 2, 2, ROWS, 512), BF16),
            pltpu.SemaphoreType.DMA((SUM_COPIES,)),
            pltpu.SemaphoreType.DMA((SUM_COPIES,)),
            pltpu.SemaphoreType.DMA((len(SUM_EARLY),)),
        ]
        + [pltpu.VMEM(shape, BF16) for shape in slot_shapes(SUM_PARTS).values()],
        compiler_params=params(collective_id=1, has_side_effects=True),
        name="tail_scatter",
    )(*args, early.reshape(4, 2, 2, 2, LATE, 512))


def unpack_kernel(sum_ref, wo, up, dn, wq, wk, wv, memory, b_up, *vectors):
    me = lax.axis_index("dp")
    wo[...] = sum_ref[0:16]
    for c in range(4):
        up[:, 512 * c : 512 * c + 512] = sum_ref[16 + 16 * c : 32 + 16 * c]
    dn[...] = sum_ref[80:144]
    wq[...] = sum_ref[144:160]
    wk[...] = sum_ref[160:176]
    wv[...] = sum_ref[176:192]
    memory[...] = sum_ref[192:208, 0 : memory.shape[1]]
    turned = sum_ref[192:208, 128:256].T
    for index, vector in enumerate(vectors):
        vector[...] = turned[index : index + 1, :]
    row = lax.broadcasted_iota(jnp.int32, (16, 256), 0)
    lane = lax.broadcasted_iota(jnp.int32, (16, 256), 1)
    own = jnp.sum(jnp.where(row * 4 + lane // 64 == me, sum_ref[192:208, 256:512], 0.0), axis=0, keepdims=True)
    b_up[...] = own[:, 0:64] + own[:, 64:128] + own[:, 128:192] + own[:, 192:256]


def unpack(sums, mem_rows):
    shapes = [(16, 512), (16, 2048), (64, 512), (16, 512), (16, 512), (16, 512), (16, mem_rows), (1, 64)] + [(1, 16)] * 8
    found = pl.pallas_call(
        unpack_kernel,
        out_shape=[jax.ShapeDtypeStruct(s, F32) for s in shapes],
        compiler_params=params(),
        name="unpack",
    )(sums)
    out = dict(zip(("w_out", "w_up", "w_down", "w_query", "w_key", "w_value", "memory"), found[:7]))
    out["memory"] = out["memory"].T
    out["b_up"] = found[7].reshape(64)
    for name, value in zip(VECTORS, found[8:]):
        out[name] = value.reshape(16)
    return out


NAMES = (
    "memory", "w_query", "b_query", "w_key", "w_value", "b_value", "w_out", "b_out", "gain_attn",
    "shift_attn", "w_up", "b_up", "w_down", "b_down", "gain_ffn", "shift_ffn",
)


def pack_whole(p):
    mem_rows = p["memory"].shape[0]
    mats = [p[name].reshape(PARTS, 16, 512) for name in ("w_query", "w_key", "w_value", "w_out")]
    up = p["w_up"].reshape(PARTS, 16, 4, 512).transpose(0, 2, 1, 3).reshape(PARTS, 64, 512)
    memory = jnp.pad(p["memory"].T, ((0, 0), (0, 128 - mem_rows))).reshape(PARTS, 16, 128)
    vectors = jnp.stack([p[name] for name in VECTORS], axis=1)
    vectors = jnp.pad(vectors, ((0, 0), (0, 120))).reshape(PARTS, 16, 128)
    own = jnp.arange(2048)[None] // 64 == jnp.arange(PARTS)[:, None]
    b_up = jnp.where(own, p["b_up"][None], 0).astype(BF16).reshape(PARTS, 8, 256)
    b_up = jnp.pad(b_up, ((0, 0), (0, 8), (0, 0)))
    small = jnp.concatenate([memory, vectors, b_up], axis=2)
    return jnp.concatenate(mats[:3] + [small, up, p["w_down"].reshape(PARTS, 64, 512), mats[3]], axis=1)


def unpack_whole(early, late, mem_rows):
    small = late[:, 48:64]
    vectors = small[:, :, 128:136].reshape(512, 8)
    out = {
        "memory": small[:, :, 0:mem_rows].reshape(512, mem_rows).T,
        "w_query": late[:, 0:16].reshape(512, 512),
        "w_key": late[:, 16:32].reshape(512, 512),
        "w_value": late[:, 32:48].reshape(512, 512),
        "w_out": early[:, 0:16].reshape(512, 512),
        "w_up": early[:, 16:80].reshape(PARTS, 4, 16, 512).transpose(0, 2, 1, 3).reshape(512, 2048),
        "w_down": early[:, 80:144].reshape(2048, 512),
        "b_up": small[0, 0:8, 256:512].reshape(2048),
    }
    for index, name in enumerate(VECTORS):
        out[name] = vectors[:, index]
    return out


def axis_of(name):
    return 1 if name == "memory" else 0


def shards(n, tokens, segment, counts, *rest):
    p = dict(zip(NAMES, rest[:-1]))
    cotangent = rest[-1]
    slots = tokens.shape[0]
    mem_rows = p["memory"].shape[0]
    whole = None
    if n != PARTS:
        whole = pack_whole({k: lax.all_gather(v, "dp", axis=axis_of(k), tiled=True) for k, v in p.items()})
    found = projections(p, whole, tokens, segment, counts, mem_rows)
    late, qa, ka, kn, vn, km, kmn, vmn, wt, memt, rows8, rbup, mixt, lse = found
    seg2 = segment.reshape(slots // 128, 128)
    output, gfirst, mgrad, delta, early, vec, bup = middle(late, rows8, rbup, counts, mixt, tokens, cotangent)
    dq, dk, dv, dkm, dvm = attend_backward(seg2, counts, qa, kn, ka, vn, kmn, km, vmn, mgrad, lse, delta)
    gtok, sums = tail(early, tokens, dq, dk, dv, dkm, dvm, gfirst, vec, bup, wt, memt, n == PARTS)
    if n == PARTS:
        grads = unpack(sums, mem_rows)
    else:
        full = unpack_whole(early.astype(F32), sums.astype(F32), mem_rows)
        grads = {
            k: lax.psum_scatter(v, "dp", scatter_dimension=axis_of(k), tiled=True) for k, v in full.items()
        }
    return (output, gtok) + tuple(grads[name] for name in NAMES)


def solution(mesh):
    n = mesh.shape["dp"]
    row, mat, mem = P("dp"), P("dp", None), P(None, "dp")
    spec = {name: mat if name.startswith("w_") else row for name in NAMES}
    spec["memory"] = mem
    weights = tuple(spec[name] for name in NAMES)
    return jax.shard_map(
        functools.partial(shards, n),
        mesh=mesh,
        in_specs=(mat, row, row) + weights + (mat,),
        out_specs=(mat, mat) + weights,
        check_vma=False,
    )
```

```python
import functools
import jax
import jax.numpy as jnp
from jax import lax
from jax.experimental import pallas as pl
from jax.experimental.pallas import tpu as pltpu
from jax.sharding import PartitionSpec as P

H = 8
HD = 64
HA = 80
EPS = 1e-05
BIG = 1e30
PARTS = 32
ROWS = 208
BQ = 256
BK = 256
MP = 32
LONGEST = 1024
F32 = jnp.float32
BF16 = jnp.bfloat16
VMEM_LIMIT = 60 << 20

V_BQ, V_BV, V_BO, V_GA, V_SA, V_BD, V_GF, V_SF = range(8)


def dot(left, right, lc, rc):
    return lax.dot_general(left, right, (((lc,), (rc,)), ((), ())), preferred_element_type=F32)


def params(**kw):
    return pltpu.CompilerParams(vmem_limit_bytes=VMEM_LIMIT, **kw)


MESH = pl.DeviceIdType.MESH
AXES = {"z": (8, 4), "y": (4, 2), "x": (2, 2)}
LAYOUT = ("z", "y", "x")


class Place:
    def __init__(self):
        me = lax.axis_index("dp")
        self.me = me
        self.core = me % 2
        self.far = 1 - self.core
        self.partner = me + 1 - 2 * self.core
        self.at = {a: (me // stride) % length for a, (stride, length) in AXES.items()}
        self.mine = tuple(self.at[a] for a in LAYOUT)
        self.others = {}
        for axis, (stride, length) in AXES.items():
            for distance in range(1, length):
                j = (self.at[axis] + distance) % length
                self.others[axis, distance] = j, me + (j - self.at[axis]) * stride
        self.peers = [self.partner] + [device for _, device in self.others.values()]

    def other(self, axis, distance):
        return self.others[axis, distance]

    def greet(self):
        for peer in self.peers:
            pl.semaphore_signal(
                pltpu.get_barrier_semaphore(), inc=1, device_id=(peer,), device_id_type=MESH
            )

    def met(self):
        pl.semaphore_wait(pltpu.get_barrier_semaphore(), len(self.peers))


class Copies:
    def __init__(self, send, recv):
        self.send, self.recv, self.count, self.open = send, recv, 0, []

    def number(self):
        self.count += 1
        return self.count - 1

    def make(self, src, dst, number, device):
        return pltpu.make_async_remote_copy(
            src_ref=src, dst_ref=dst, send_sem=self.send.at[number], recv_sem=self.recv.at[number],
            device_id=(device,), device_id_type=MESH,
        )

    def start(self, src, dst, number, device):
        self.make(src(), dst(), number, device).start()
        self.open.append((src, dst, number, device))

    def landed(self, block, number, device):
        self.make(block, block, number, device).wait_recv()

    def finish(self):
        for src, dst, number, device in self.open:
            self.make(src(), dst(), number, device).wait_send()
        self.open = []


def gather_part(place, copies, own, base, whole, rows, order, arrivals):
    done = ()

    def mine():
        return own.at[slice(base + rows.start, base + rows.stop)]

    def block(axis, j, core):
        index = tuple(j if a == axis else (slice(None) if a in done else place.at[a]) for a in LAYOUT)
        return lambda: whole.at[index + (core, rows)]

    for axis in order:
        length = AXES[axis][1]
        numbers = [copies.number() for _ in range(2 * length - 2)]
        here = block(axis, place.at[axis], place.core)
        for d in range(1, length):
            copies.start(here if done else mine, here, numbers[d - 1], place.other(axis, d)[1])
        if not done:
            number = copies.number()
            copies.start(mine, here, number, place.partner)
            arrivals.append((block(axis, place.at[axis], place.far), number))
        yield
        for d in range(1, length):
            j, device = place.other(axis, length - d)
            there = block(axis, j, place.core)
            copies.landed(there(), numbers[d - 1], device)
            number = numbers[length - 2 + d]
            copies.start(there, there, number, place.partner)
            arrivals.append((block(axis, j, place.far), number))
        done += (axis,)
    yield


def advance(parts):
    for part in parts:
        next(part)


def scatter_part(place, copies, acc, slots, out, rows, order):
    done = ()

    def block(axis, j):
        index = tuple(j if a == axis else (place.at[a] if a in done else slice(None)) for a in LAYOUT)
        return index + (rows,)

    def taken(index):
        return lambda: acc.at[index]

    def landing(axis, d):
        return lambda: slots[axis, d]

    for axis in order:
        length = AXES[axis][1]
        numbers = [copies.number() for _ in range(length - 1)]
        for d in range(1, length):
            j, device = place.other(axis, d)
            copies.start(taken(block(axis, j)), landing(axis, d), numbers[d - 1], device)
        yield
        for d in range(1, length):
            copies.landed(slots[axis, d], numbers[d - 1], place.partner)
        mine = block(axis, place.at[axis])
        total = acc[mine].astype(F32)
        for d in range(1, length):
            total = total + slots[axis, d][...].astype(F32)
        if axis == order[-1]:
            out[rows, :] = total
        else:
            acc[mine] = total.astype(BF16)
        done += (axis,)
    yield


def slot_shapes(parts):
    shapes = {}
    for number, (rows, order) in enumerate(parts):
        left = ["z", "y", "x"]
        for axis in order:
            left.remove(axis)
            shape = tuple(AXES[a][1] for a in LAYOUT if a in left) + (rows.stop - rows.start, 512)
            for d in range(1, AXES[axis][1]):
                shapes[number, axis, d] = shape
    return shapes


def join(place, copies, acc, source, other, rows, number):
    copies.landed(other.at[:, :, :, rows], number, place.partner)

    @pl.loop(0, 4)
    def _(z):
        mine = source(z) if source else acc[z, :, :, rows]
        acc[z, :, :, rows] = (mine.astype(F32) + other[z, :, :, rows].astype(F32)).astype(BF16)


VECTORS = ("b_query", "b_value", "b_out", "gain_attn", "shift_attn", "b_down", "gain_ffn", "shift_ffn")
EARLY = 64
LATE = 144
EARLY_PARTS = ((slice(0, 32), "zxy"), (slice(32, 64), "zyx"))
LATE_PARTS = (
    (slice(0, 48), "zxy"),
    (slice(48, 96), "zyx"),
    (slice(96, 128), "yzx"),
    (slice(128, 144), "xzy"),
)
GATHER_COPIES = 11 * (len(EARLY_PARTS) + len(LATE_PARTS))


def head_block(rows, features):
    block = jnp.concatenate([rows, features], axis=0)
    return block, jnp.concatenate([block, jnp.zeros((128 - HA, rows.shape[1]), BF16)], axis=0).T


def pack(own, place, wq, wk, wv, wo, up, dn, memory, b_up, vectors):
    own[0:16] = wq[...]
    own[16:32] = wk[...]
    own[32:48] = wv[...]
    own[48:64] = jnp.zeros((16, 512), BF16)
    own[48:64, 0 : memory.shape[1]] = memory[...]
    values = jnp.concatenate([vector[...].astype(F32) for vector in vectors], axis=0)
    own[48:64, 128:136] = values.T.astype(BF16)
    value = jnp.concatenate([b_up[...].astype(F32)] * 4, axis=1)
    row = lax.broadcasted_iota(jnp.int32, (16, 256), 0)
    lane = lax.broadcasted_iota(jnp.int32, (16, 256), 1)
    own[48:64, 256:512] = jnp.where(row * 4 + lane // 64 == place.me, value, 0.0).astype(BF16)
    for c in range(4):
        own[64 + 16 * c : 80 + 16 * c] = up[:, 512 * c : 512 * c + 512]
    own[128:192] = dn[...]
    own[192:208] = wo[...]


def prepare(mem_rows, early, wt_ref, memt_ref, rows_ref, rbup_ref, bias_ref, km_ref, vm_ref, kmn_ref, vmn_ref):
    for j in range(3):
        wt_ref[512 * j : 512 * j + 512, :] = early[..., 16 * j : 16 * j + 16, :].reshape(512, 512).T
    small = early[..., 48:64, 0:256].reshape(512, 256)
    memt = small[:, 0:128]
    memt_ref[...] = memt
    vectors = small[:, 128:256].astype(F32)
    bias_ref[...] = vectors
    rows_ref[...] = vectors.T[0:8, :]
    bup = jnp.sum(early[..., 48:64, 256:512].reshape(PARTS, 16, 256).astype(F32), axis=0)
    for v in range(8):
        rbup_ref[0:1, 256 * v : 256 * v + 256] = bup[v : v + 1, :]
    bv = vectors[:, V_BV : V_BV + 1]
    km = dot(wt_ref[512:1024, :], memt, 1, 0).astype(BF16)
    vm = (dot(wt_ref[1024:1536, :], memt, 1, 0) + bv).astype(BF16)
    frow = lax.broadcasted_iota(jnp.int32, (16, 128), 0)
    lane = lax.broadcasted_iota(jnp.int32, (16, 128), 1)
    kf = jnp.where(frow < 3, jnp.where(lane < mem_rows, 0.0, 1.0), jnp.where(frow < 6, 1.0, 0.0)).astype(BF16)
    vf = jnp.where(frow < 3, 1.0, 0.0).astype(BF16)
    for h in range(H):
        km_ref[h], turned = head_block(km[64 * h : 64 * h + 64, :], kf)
        kmn_ref[h] = turned[0:MP]
        vm_ref[h], turned = head_block(vm[64 * h : 64 * h + 64, :], vf)
        vmn_ref[h] = turned[0:MP]


def project(step, tok_ref, seg_ref, cnt_ref, wt_ref, bias_ref, qa_ref, ka_ref, va_ref):
    rows = tok_ref.shape[0]
    tok = tok_ref[...]
    bq = bias_ref[:, V_BQ : V_BQ + 1]
    bv = bias_ref[:, V_BV : V_BV + 1]
    q = (dot(wt_ref[0:512, :], tok, 1, 1) + bq).astype(BF16) * jnp.asarray(HD ** -0.5, BF16)
    k = dot(wt_ref[512:1024, :], tok, 1, 1).astype(BF16)
    v = (dot(wt_ref[1024:1536, :], tok, 1, 1) + bv).astype(BF16)
    frow = lax.broadcasted_iota(jnp.int32, (16, rows), 0)
    seg = jnp.broadcast_to(seg_ref[...], (16, rows))
    pos = lax.broadcasted_iota(jnp.int32, (16, rows), 1) + step * rows
    valid = pos < cnt_ref[0]
    qf = jnp.where((frow < 3) & (frow != seg), -BIG, 0.0).astype(BF16)
    kf = jnp.where(frow < 3, jnp.where(valid & (frow != seg), 0.0, 1.0), jnp.where(frow < 6, 1.0, 0.0)).astype(BF16)
    vf = jnp.where(frow < 3, 1.0, 0.0).astype(BF16)
    for h in range(H):
        s = slice(64 * h, 64 * h + 64)
        qa_ref[h, 0:64, :] = q[s]
        qa_ref[h, 64:80, :] = qf
        ka_ref[h, 0:64, :] = k[s]
        ka_ref[h, 64:80, :] = kf
        va_ref[h, 0:64, :] = v[s]
        va_ref[h, 64:80, :] = vf


def gather_kernel(
    mem_rows, half, wq, wk, wv, wo, up, dn, memory, b_up, v0, v1, v2, v3, v4, v5, v6, v7, tok_ref, seg_ref, cnt_ref,
    late_ref, qa_ref, ka_ref, va_ref, km_ref, kmn_ref, vmn_ref,
    wt_ref, memt_ref, rows_ref, rbup_ref, mix_ref, lse_ref,
    own, early, bias_ref, vm_ref, qa_all, ka_all, va_all, acc_ref, m_ref, sa_ref, sb_ref, send, recv, local,
):
    step = pl.program_id(0)
    slots = ka_all.shape[2]
    place = Place()
    copies = Copies(send, recv)
    arrivals, late_arrivals = [], []
    firsts = [gather_part(place, copies, own, 0, early, *part, arrivals) for part in EARLY_PARTS]
    lasts = [gather_part(place, copies, own, EARLY, late_ref, *part, late_arrivals) for part in LATE_PARTS]

    @pl.when(step == 0)
    def _():
        place.greet()
        pack(own, place, wq, wk, wv, wo, up, dn, memory, b_up, (v0, v1, v2, v3, v4, v5, v6, v7))
        early[place.mine + (place.core,)] = own[0:EARLY]
        place.met()
        advance(firsts)
        keep = pltpu.make_async_copy(own.at[EARLY:ROWS], late_ref.at[place.mine + (place.core,)], local)
        keep.start()
        advance(firsts)
        advance(firsts)
        keep.wait()
        advance(lasts)
        advance(firsts)
        for block, number in arrivals:
            copies.landed(block(), number, place.partner)
        prepare(
            mem_rows, early, wt_ref, memt_ref, rows_ref, rbup_ref, bias_ref, km_ref, vm_ref, kmn_ref, vmn_ref,
        )

    @pl.when(step < half)
    def _():
        project(step, tok_ref, seg_ref, cnt_ref, wt_ref, bias_ref, qa_ref, ka_ref, va_ref)
        here = pl.ds(pl.multiple_of(step * tok_ref.shape[0], 128), tok_ref.shape[0])
        qa_all[:, :, here] = qa_ref[...]
        ka_all[:, :, here] = ka_ref[...]
        va_all[:, :, here] = va_ref[...]

    @pl.when(step == half - 1)
    def _():
        advance(lasts)

    @pl.when(step >= half)
    def _():
        block = step - half
        reach = LONGEST // BQ
        begin = jnp.maximum(block - reach, 0)
        end = jnp.minimum(block + reach + 1, slots // BQ)
        queries = qa_all.at[:, :, pl.ds(pl.multiple_of(block * BQ, BQ), BQ)]
        attend(
            begin * (BQ // 128), (end - begin) * (BQ // BK), queries, ka_all, va_all, kmn_ref, vm_ref, mix_ref, lse_ref,
            acc_ref, m_ref, sa_ref, sb_ref,
        )

    @pl.when(step == half + 2)
    def _():
        advance(lasts)

    @pl.when(step == pl.num_programs(0) - 1)
    def _():
        advance(lasts)
        for block, number in late_arrivals:
            copies.landed(block(), number, place.partner)
        copies.finish()


def project_kernel(
    mem_rows, g_ref, tok_ref, seg_ref, cnt_ref, qa_ref, ka_ref, va_ref, km_ref, vm_ref, kmn_ref, vmn_ref,
    wt_ref, memt_ref, rows_ref, rbup_ref, bias_ref,
):
    step = pl.program_id(0)

    @pl.when(step == 0)
    def _():
        prepare(
            mem_rows, g_ref, wt_ref, memt_ref, rows_ref, rbup_ref, bias_ref, km_ref, vm_ref, kmn_ref, vmn_ref
        )

    project(step, tok_ref, seg_ref, cnt_ref, wt_ref, bias_ref, qa_ref, ka_ref, va_ref)


def fixed(*shape):
    return pl.BlockSpec(shape, lambda i: (0,) * len(shape))


def projections(p, whole, tokens, segment, counts, mem_rows):
    slots = tokens.shape[0]
    rb = 512
    half = slots // rb
    wide = (H, HA, slots)
    mwide, mtall = (H, HA, 128), (H, MP, 128)

    def at(i):
        return jnp.minimum(i, half - 1)

    blk = pl.BlockSpec((H, HA, rb), lambda i: (0, 0, at(i)))
    common = [
        pl.BlockSpec((rb, 512), lambda i: (at(i), 0)),
        pl.BlockSpec((1, rb), lambda i: (0, at(i))),
        pl.BlockSpec(memory_space=pltpu.SMEM),
    ]
    args = (tokens, segment.reshape(1, slots), counts)

    def outs(shapes):
        found = [jax.ShapeDtypeStruct(s, BF16) for s in shapes]
        return found + [jax.ShapeDtypeStruct((8, 512), F32), jax.ShapeDtypeStruct((1, 2048), F32)]

    if whole is not None:
        shapes = outs([wide, wide, wide, mwide, mwide, mtall, mtall, (1536, 512), (512, 128)])
        found = pl.pallas_call(
            functools.partial(project_kernel, mem_rows),
            grid=(half,),
            in_specs=[fixed(PARTS, EARLY, 512)] + common,
            out_specs=[blk, blk, blk] + [fixed(*o.shape) for o in shapes[3:]],
            out_shape=shapes,
            scratch_shapes=[pltpu.VMEM((512, 128), F32)],
            compiler_params=params(),
            name="projections",
        )(whole[:, 0:EARLY], *args)
        qa, ka, va, km, vm, kmn, vmn, wt, memt, rows8, rbup = found
        mixt, lse = attend_forward(segment.reshape(slots // 128, 128), counts, qa, ka, va, kmn, vm)
        return whole[:, EARLY:], qa, ka, va, km, kmn, vmn, wt, memt, rows8, rbup, mixt, lse
    weights = [p[name] for name in ("w_query", "w_key", "w_value", "w_out", "w_up", "w_down")]
    weights += [p["memory"].T, p["b_up"].reshape(1, 64)] + [p[name].reshape(1, 16) for name in VECTORS]
    shapes = outs([wide, wide, wide, mwide, mtall, mtall, (1536, 512), (512, 128)])
    found = pl.pallas_call(
        functools.partial(gather_kernel, mem_rows, half),
        grid=(half + slots // BQ,),
        in_specs=[fixed(*w.shape) for w in weights] + common,
        out_specs=[pl.BlockSpec(memory_space=pl.ANY), blk, blk, blk]
        + [fixed(*o.shape) for o in shapes[3:]]
        + [
            pl.BlockSpec((512, BQ), lambda i: (0, jnp.maximum(i - half, 0))),
            pl.BlockSpec((H, BQ), lambda i: (0, jnp.maximum(i - half, 0))),
        ],
        out_shape=[jax.ShapeDtypeStruct((4, 2, 2, 2, LATE, 512), BF16)]
        + shapes
        + [jax.ShapeDtypeStruct((512, slots), BF16), jax.ShapeDtypeStruct((H, slots), F32)],
        scratch_shapes=[
            pltpu.VMEM((ROWS, 512), BF16),
            pltpu.VMEM((4, 2, 2, 2, EARLY, 512), BF16),
            pltpu.VMEM((512, 128), F32),
            pltpu.VMEM(mwide, BF16),
            pltpu.VMEM(wide, BF16),
            pltpu.VMEM(wide, BF16),
            pltpu.VMEM(wide, BF16),
            pltpu.VMEM((H, HA, BQ), F32),
            pltpu.VMEM((H, BQ), F32),
            pltpu.VMEM((H, BK, BQ), F32),
            pltpu.VMEM((H, BK, BQ), F32),
            pltpu.SemaphoreType.DMA((GATHER_COPIES,)),
            pltpu.SemaphoreType.DMA((GATHER_COPIES,)),
            pltpu.SemaphoreType.DMA,
        ],
        compiler_params=params(collective_id=0, has_side_effects=True),
        name="gather_attend",
    )(*weights, *args)
    return (found[0].reshape(PARTS, LATE, 512),) + tuple(found[1:])


def key_ranges(seg, count, slots, out):
    r, c = seg.shape
    pos = lax.broadcasted_iota(jnp.int32, (r, c), 0) * c + lax.broadcasted_iota(jnp.int32, (r, c), 1)
    valid = pos < count
    ends = [jnp.sum(jnp.where(valid & (seg <= s), 1.0, 0.0)).astype(jnp.int32) for s in range(3)]
    for block in range(slots // BQ):
        first = block * BQ
        last = jnp.minimum(first + BQ, count)
        low, high, start = jnp.int32(slots), jnp.int32(0), jnp.int32(0)
        for end in ends:
            hit = (end > first) & (start < last) & (end > start)
            low = jnp.where(hit, jnp.minimum(low, start), low)
            high = jnp.where(hit, jnp.maximum(high, end), high)
            start = end
        begin = low // 128
        blocks = jnp.where(high > low, (high - begin * 128 + BK - 1) // BK, 0)
        out[0, block] = jnp.minimum(begin, slots // 128 - blocks * (BK // 128))
        out[1, block] = blocks


def key_slots(begin, block):
    return pl.ds(pl.multiple_of((begin + block * (BK // 128)) * 128, 128), BK)


def pipelined(blocks, work, first, second):
    @pl.when(blocks > 0)
    def _():
        work((0, first), None)

    pairs = jnp.maximum(blocks - 1, 0) // 2

    @pl.loop(0, pairs)
    def _(i):
        work((2 * i + 1, second), (2 * i, first))
        work((2 * i + 2, first), (2 * i + 1, second))

    j = 2 * pairs

    @pl.when(blocks - j == 2)
    def _():
        work((j + 1, second), (j, first))
        work(None, (j + 1, second))

    @pl.when(blocks - j == 1)
    def _():
        work(None, (j, first))


def attend(begin, blocks, qa_ref, ka_ref, va_ref, kmn_ref, vm_ref, mix_ref, lse_ref, acc_ref, m_ref, sa_ref, sb_ref):
    def weights(h, s):
        old = m_ref[h : h + 1, :]
        top = jnp.maximum(old, jnp.max(s, axis=0, keepdims=True))
        return jnp.exp(s - top).astype(BF16), jnp.exp(old - top), top

    def work(new, old):
        kept = {}
        for h in range(H + 1):
            if h < H and new:
                new[1][h] = dot(ka_ref[h, :, key_slots(begin, new[0])], qa_ref[h], 0, 0)
            if h < H and old:
                kept[h] = weights(h, old[1][h])
            if h > 0 and old:
                p, fade, top = kept.pop(h - 1)
                acc_ref[h - 1] = acc_ref[h - 1] * fade + dot(va_ref[h - 1, :, key_slots(begin, old[0])], p, 1, 0)
                m_ref[h - 1 : h, :] = top

    scores = [dot(kmn_ref[h, :, 0:HA], qa_ref[h], 1, 0) for h in range(H)]
    for h in range(H):
        top = jnp.max(scores[h], axis=0, keepdims=True)
        p = jnp.exp(scores[h] - top).astype(BF16)
        acc_ref[h] = dot(vm_ref[h, :, 0:MP], p, 1, 0)
        m_ref[h : h + 1, :] = top
    pipelined(blocks, work, sa_ref, sb_ref)
    for h in range(H):
        total = acc_ref[h, 64:65, :]
        mix_ref[64 * h : 64 * h + 64, :] = (acc_ref[h, 0:64, :] * (1.0 / total)).astype(BF16)
        lse_ref[h : h + 1, :] = m_ref[h : h + 1, :] + jnp.log(total)


def fwd_kernel(
    slots, seg_ref, cnt_ref, qa_ref, ka_ref, va_ref, kmn_ref, vm_ref,
    mix_ref, lse_ref, acc_ref, m_ref, sa_ref, sb_ref, range_ref,
):
    step = pl.program_id(0)

    @pl.when(step == 0)
    def _():
        key_ranges(seg_ref[...], cnt_ref[0], slots, range_ref)

    attend(
        range_ref[0, step], range_ref[1, step], qa_ref, ka_ref, va_ref, kmn_ref, vm_ref, mix_ref, lse_ref,
        acc_ref, m_ref, sa_ref, sb_ref,
    )


def attend_forward(seg2, counts, qa, ka, va, kmn, vm):
    slots = qa.shape[2]
    once = pl.Buffered(1)

    def whole(a):
        return pl.BlockSpec(a.shape, lambda i: (0, 0, 0), pipeline_mode=once)

    return pl.pallas_call(
        functools.partial(fwd_kernel, slots),
        grid=(slots // BQ,),
        in_specs=[
            pl.BlockSpec(seg2.shape, lambda i: (0, 0)),
            pl.BlockSpec(memory_space=pltpu.SMEM),
            pl.BlockSpec((H, HA, BQ), lambda i: (0, 0, i)),
            whole(ka), whole(va), whole(kmn), whole(vm),
        ],
        out_specs=[pl.BlockSpec((512, BQ), lambda i: (0, i)), pl.BlockSpec((H, BQ), lambda i: (0, i))],
        out_shape=[jax.ShapeDtypeStruct((512, slots), BF16), jax.ShapeDtypeStruct((H, slots), F32)],
        scratch_shapes=[
            pltpu.VMEM((H, HA, BQ), F32),
            pltpu.VMEM((H, BQ), F32),
            pltpu.VMEM((H, BK, BQ), F32),
            pltpu.VMEM((H, BK, BQ), F32),
            pltpu.SMEM((2, slots // BQ), jnp.int32),
        ],
        compiler_params=params(),
        name="attend_forward",
    )(seg2, counts, qa, ka, va, kmn, vm)


def norm_parts(value):
    mean = jnp.mean(value, axis=-1, keepdims=True)
    centred = value - mean
    rstd = lax.rsqrt(jnp.mean(centred * centred, axis=-1, keepdims=True) + EPS)
    return centred * rstd, rstd


def norm_grad(grad_hat, hat, rstd):
    return rstd * (
        grad_hat
        - jnp.mean(grad_hat, axis=-1, keepdims=True)
        - hat * jnp.mean(grad_hat * hat, axis=-1, keepdims=True)
    )


def colsum(value):
    return jnp.sum(value, axis=0, keepdims=True)


SUB = 512
FC = 512


def mid_kernel(
    rb, cnt_ref, row_ref, rbup_ref, late_ref, mix_ref, tok_ref, cot_ref,
    out_ref, gfirst_ref, mgrad_ref, delta_ref, gw_ref, vec_ref, bup_ref,
    aup_ref, adn_ref, ao_ref, *scratch,
):
    step = pl.program_id(0)
    subs = rb // SUB

    @pl.when(step == 0)
    def _():
        aup_ref[...] = jnp.zeros_like(aup_ref)
        adn_ref[...] = jnp.zeros_like(adn_ref)
        ao_ref[...] = jnp.zeros_like(ao_ref)
        vec_ref[...] = jnp.zeros_like(vec_ref)
        bup_ref[...] = jnp.zeros_like(bup_ref)

    wo = late_ref[:, 128:144, :].reshape(512, 512)

    def w_up(c):
        return late_ref[:, 16 * c : 16 * c + 16, :].reshape(512, 512)

    def w_down(c):
        return late_ref[8 * c : 8 * c + 8, 64:128, :].reshape(512, 512)

    def row(v):
        return row_ref[v : v + 1, :]

    class Block:
        def __init__(self, index):
            self.s = slice(SUB * index, SUB * index + SUB)
            self.first_row = step * rb + SUB * index
            self.active, self.slope, self.hgrad = scratch[3 * (index % 2) : 3 * (index % 2) + 3]
            self.up_part, self.dact_part = {}, {}

        def head(self):
            self.mixt = mix_ref[:, self.s]
            attention = dot(self.mixt, wo, 0, 0) + row(V_BO)
            self.hat1, self.rstd1 = norm_parts(tok_ref[self.s, :].astype(F32) + attention)
            self.first = self.hat1 * row(V_GA) + row(V_SA)
            self.low = self.first.astype(BF16)
            self.branch = self.first + row(V_BD)

        def up(self, c):
            f = slice(FC * c, FC * c + FC)
            self.up_part[c] = dot(self.low, w_up(c), 1, 0) + rbup_ref[:, f]

        def gelu(self, c):
            f = slice(FC * c, FC * c + FC)
            hidden = self.up_part.pop(c)
            cdf = 0.5 + 0.5 * lax.erf(hidden * (2.0 ** -0.5))
            self.active[:, f] = (hidden * cdf).astype(BF16)
            self.slope[:, f] = cdf + hidden * jnp.exp(hidden * hidden * -0.5) * 0.3989422804014327

        def down(self, c):
            f = slice(FC * c, FC * c + FC)
            self.branch = self.branch + dot(self.active[:, f], w_down(c), 1, 0)

        def turn(self):
            hat2, rstd2 = norm_parts(self.branch)
            valid = lax.broadcasted_iota(jnp.int32, (SUB, 1), 0) + self.first_row < cnt_ref[0]
            out_ref[self.s, :] = jnp.where(valid, hat2 * row(V_GF) + row(V_SF), 0.0).astype(BF16)
            seed = jnp.where(valid, cot_ref[self.s, :].astype(F32), 0.0)
            vec_ref[V_GF : V_GF + 1, :] += colsum(seed * hat2)
            vec_ref[V_SF : V_SF + 1, :] += colsum(seed)
            self.total = norm_grad(seed * row(V_GF), hat2, rstd2)
            self.bgrad = self.total.astype(BF16)
            vec_ref[V_BD : V_BD + 1, :] += colsum(self.bgrad.astype(F32))

        def dact(self, c):
            f = slice(FC * c, FC * c + FC)
            self.dact_part[c] = dot(self.bgrad, w_down(c), 1, 1)

        def grad_down(self, c):
            f = slice(FC * c, FC * c + FC)
            adn_ref[f, :] += dot(self.active[:, f], self.bgrad, 0, 0)

        def hidden_grad(self, c):
            f = slice(FC * c, FC * c + FC)
            grad = (self.dact_part.pop(c) * self.slope[:, f]).astype(BF16)
            self.hgrad[:, f] = grad
            bup_ref[:, f] += colsum(grad.astype(F32))

        def grad_up(self, c):
            f = slice(FC * c, FC * c + FC)
            aup_ref[:, f] += dot(self.low, self.hgrad[:, f], 0, 0)

        def first_grad(self, c):
            f = slice(FC * c, FC * c + FC)
            self.total = self.total + dot(self.hgrad[:, f], w_up(c), 1, 1)

        def finish(self):
            vec_ref[V_GA : V_GA + 1, :] += colsum(self.total * self.hat1)
            vec_ref[V_SA : V_SA + 1, :] += colsum(self.total)
            grad_first = norm_grad(self.total * row(V_GA), self.hat1, self.rstd1)
            gfirst_ref[self.s, :] = grad_first
            agrad = grad_first.astype(BF16)
            vec_ref[V_BO : V_BO + 1, :] += colsum(agrad.astype(F32))
            mgrad = dot(wo, agrad, 1, 1).astype(BF16)
            ao_ref[...] += dot(self.mixt, agrad, 1, 0)
            mgrad_ref[:, self.s] = mgrad
            prod = mgrad.astype(F32) * self.mixt.astype(F32)
            for h in range(H):
                delta_ref[h : h + 1, self.s] = jnp.sum(prod[64 * h : 64 * h + 64, :], axis=0, keepdims=True)

    chunks = 2048 // FC

    def both(ahead, behind):
        if ahead:
            ahead.head()
            ahead.up(0)
        for c in range(chunks):
            if behind:
                behind.dact(c)
            if ahead and c + 1 < chunks:
                ahead.up(c + 1)
            if behind:
                behind.grad_down(c)
            if ahead:
                ahead.gelu(c)
            if behind:
                behind.hidden_grad(c)
                behind.grad_up(c)
                behind.first_grad(c)
            if ahead:
                ahead.down(c)
        if behind:
            behind.finish()
        if ahead:
            ahead.turn()

    blocks = [Block(index) for index in range(subs)]
    for ahead, behind in zip(blocks + [None], [None] + blocks):
        both(ahead, behind)

    @pl.when(step == pl.num_programs(0) - 1)
    def _():
        gw_ref[:, 0:16, :] = ao_ref[...].astype(gw_ref.dtype).reshape(PARTS, 16, 512)
        for c in range(4):
            gw_ref[:, 16 + 16 * c : 32 + 16 * c, :] = (
                aup_ref[:, 512 * c : 512 * c + 512].astype(gw_ref.dtype).reshape(PARTS, 16, 512)
            )
        gw_ref[:, 80:144, :] = adn_ref[...].astype(gw_ref.dtype).reshape(PARTS, 64, 512)


def middle(late, rows8, rbup, counts, mixt, tokens, cotangent, rb=512):
    slots = tokens.shape[0]
    rows = pl.BlockSpec((rb, 512), lambda i: (i, 0))
    cols = pl.BlockSpec((512, rb), lambda i: (0, i))
    once = pl.Buffered(1)
    return pl.pallas_call(
        functools.partial(mid_kernel, rb),
        grid=(slots // rb,),
        in_specs=[
            pl.BlockSpec(memory_space=pltpu.SMEM),
            pl.BlockSpec((8, 512), lambda i: (0, 0)),
            pl.BlockSpec((1, 2048), lambda i: (0, 0)),
            pl.BlockSpec((PARTS, LATE, 512), lambda i: (0, 0, 0), pipeline_mode=once),
            cols, rows, rows,
        ],
        out_specs=[
            rows, rows, cols,
            pl.BlockSpec((H, rb), lambda i: (0, i)),
            pl.BlockSpec((PARTS, 144, 512), lambda i: (0, 0, 0), pipeline_mode=once),
            pl.BlockSpec((8, 512), lambda i: (0, 0)),
            pl.BlockSpec((1, 2048), lambda i: (0, 0)),
        ],
        out_shape=[
            jax.ShapeDtypeStruct((slots, 512), BF16),
            jax.ShapeDtypeStruct((slots, 512), F32),
            jax.ShapeDtypeStruct((512, slots), BF16),
            jax.ShapeDtypeStruct((H, slots), F32),
            jax.ShapeDtypeStruct((PARTS, 144, 512), BF16),
            jax.ShapeDtypeStruct((8, 512), F32),
            jax.ShapeDtypeStruct((1, 2048), F32),
        ],
        scratch_shapes=[
            pltpu.VMEM((512, 2048), F32),
            pltpu.VMEM((2048, 512), F32),
            pltpu.VMEM((512, 512), F32),
        ]
        + [pltpu.VMEM((SUB, 2048), BF16), pltpu.VMEM((SUB, 2048), F32), pltpu.VMEM((SUB, 2048), BF16)] * 2,
        compiler_params=params(),
        name="middle",
    )(counts, rows8, rbup, late, mixt, tokens, cotangent)


def split3(value):
    high = value.astype(BF16)
    rest = value - high.astype(F32)
    mid = rest.astype(BF16)
    return high, mid, (rest - mid.astype(F32)).astype(BF16)


def attend_back(
    begin, blocks, qa_ref, ka_ref, va_ref, kmn_ref, km_ref, vmn_ref, do_ref, lse_ref, delta_ref,
    q2_ref, do2_ref, dqa_ref, dka_ref, dva_ref, dkma_ref, dvma_ref, sa_ref, ga_ref, sb_ref, gb_ref,
):
    frow = lax.broadcasted_iota(jnp.int32, (16, BQ), 0)

    def feature(value, at):
        high, mid, low = (jnp.broadcast_to(v.astype(F32), (16, BQ)) for v in split3(value))
        return jnp.where(frow == at, high, jnp.where(frow == at + 1, mid, jnp.where(frow == at + 2, low, 0.0)))

    for h in range(H):
        q2_ref[h, 0:64, :] = qa_ref[h, 0:64, :]
        q2_ref[h, 64:80, :] = (qa_ref[h, 64:80, :].astype(F32) + feature(-lse_ref[h : h + 1, :], 3)).astype(BF16)
        do2_ref[h, 0:64, :] = do_ref[64 * h : 64 * h + 64, :]
        do2_ref[h, 64:80, :] = feature(-delta_ref[h : h + 1, :], 0).astype(BF16)

    def work(new, old):
        kept = {}
        for h in range(H + 1):
            if h < H and new:
                ks = key_slots(begin, new[0])
                new[1][0][h] = dot(ka_ref[h, :, ks], q2_ref[h], 0, 0)
                new[1][1][h] = dot(va_ref[h, :, ks], do2_ref[h], 0, 0)
            if h < H and old:
                p = jnp.exp(old[1][0][h])
                kept[h] = p.astype(BF16), (p * old[1][1][h]).astype(BF16)
            if h > 0 and old:
                ks = key_slots(begin, old[0])
                p, ds = kept.pop(h - 1)
                dva_ref[h - 1, :, ks] += dot(do2_ref[h - 1, 0:64, :], p, 1, 1)
                dka_ref[h - 1, :, ks] += dot(q2_ref[h - 1, 0:64, :], ds, 1, 1)
                dqa_ref[h - 1] += dot(ka_ref[h - 1, 0:64, ks], ds, 1, 0)

    ps = [jnp.exp(dot(kmn_ref[h, :, 0:HA], q2_ref[h], 1, 0)) for h in range(H)]
    dss = [(ps[h] * dot(vmn_ref[h, :, 0:HA], do2_ref[h], 1, 0)).astype(BF16) for h in range(H)]
    for h in range(H):
        dvma_ref[h, :, 0:MP] += dot(do2_ref[h, 0:64, :], ps[h].astype(BF16), 1, 1)
        dkma_ref[h, :, 0:MP] += dot(q2_ref[h, 0:64, :], dss[h], 1, 1)
        dqa_ref[h] = dot(km_ref[h, 0:64, 0:MP], dss[h], 1, 0)
    pipelined(blocks, work, (sa_ref, ga_ref), (sb_ref, gb_ref))


def bwd_kernel(
    slots, seg_ref, cnt_ref, qa_ref, ka_ref, va_ref, kmn_ref, km_ref, vmn_ref, do_ref, lse_ref, delta_ref,
    dq_ref, dk_ref, dv_ref, dkm_ref, dvm_ref,
    q2_ref, do2_ref, dqa_ref, dka_ref, dva_ref, dkma_ref, dvma_ref, sa_ref, ga_ref, sb_ref, gb_ref, range_ref,
):
    step = pl.program_id(0)

    @pl.when(step == 0)
    def _():
        key_ranges(seg_ref[...], cnt_ref[0], slots, range_ref)
        for ref in (dka_ref, dva_ref, dkma_ref, dvma_ref):
            ref[...] = jnp.zeros_like(ref)

    attend_back(
        range_ref[0, step], range_ref[1, step], qa_ref, ka_ref, va_ref, kmn_ref, km_ref, vmn_ref, do_ref, lse_ref,
        delta_ref, q2_ref, do2_ref, dqa_ref, dka_ref, dva_ref, dkma_ref, dvma_ref, sa_ref, ga_ref, sb_ref, gb_ref,
    )
    for h in range(H):
        dq_ref[64 * h : 64 * h + 64, :] = (dqa_ref[h] * HD ** -0.5).astype(BF16)

    @pl.when(step == pl.num_programs(0) - 1)
    def _():
        for h in range(H):
            s = slice(64 * h, 64 * h + 64)
            dk_ref[s, :] = dka_ref[h].astype(BF16)
            dv_ref[s, :] = dva_ref[h].astype(BF16)
            dkm_ref[s, :] = dkma_ref[h].astype(BF16)
            dvm_ref[s, :] = dvma_ref[h].astype(BF16)


def attend_backward(seg2, counts, qa, ka, va, kmn, km, vmn, mgrad, lse, delta):
    slots = qa.shape[2]
    once = pl.Buffered(1)

    def full(a):
        return pl.BlockSpec(a.shape, lambda i: (0, 0, 0), pipeline_mode=once)

    cols = pl.BlockSpec((512, BQ), lambda i: (0, i))
    stat = pl.BlockSpec((H, BQ), lambda i: (0, i))
    whole = pl.BlockSpec((512, slots), lambda i: (0, 0), pipeline_mode=once)
    mwhole = pl.BlockSpec((512, 128), lambda i: (0, 0))
    block = pltpu.VMEM((H, BK, BQ), F32)
    return pl.pallas_call(
        functools.partial(bwd_kernel, slots),
        grid=(slots // BQ,),
        in_specs=[
            pl.BlockSpec(seg2.shape, lambda i: (0, 0)),
            pl.BlockSpec(memory_space=pltpu.SMEM),
            pl.BlockSpec((H, HA, BQ), lambda i: (0, 0, i)),
            full(ka), full(va), full(kmn), full(km), full(vmn), cols, stat, stat,
        ],
        out_specs=[cols, whole, whole, mwhole, mwhole],
        out_shape=[jax.ShapeDtypeStruct((512, slots), BF16)] * 3 + [jax.ShapeDtypeStruct((512, 128), BF16)] * 2,
        scratch_shapes=[
            pltpu.VMEM((H, HA, BQ), BF16),
            pltpu.VMEM((H, HA, BQ), BF16),
            pltpu.VMEM((H, HD, BQ), F32),
            pltpu.VMEM((H, HD, slots), F32),
            pltpu.VMEM((H, HD, slots), F32),
            pltpu.VMEM((H, HD, 128), F32),
            pltpu.VMEM((H, HD, 128), F32),
            block, block, block, block,
            pltpu.SMEM((2, slots // BQ), jnp.int32),
        ],
        compiler_params=params(),
        name="attend_backward",
    )(seg2, counts, qa, ka, va, kmn, km, vmn, mgrad, lse, delta)


SUM_EARLY = (
    (slice(0, 48), "yxz"),
    (slice(48, 96), "xyz"),
    (slice(96, 112), "xzy"),
    (slice(112, 144), "yzx"),
)
SUM_LATE = ((slice(144, 160), "xyz"), (slice(160, 176), "yxz"), (slice(176, 192), "xyz"), (slice(192, 208), "yxz"))
SUM_PARTS = SUM_EARLY + SUM_LATE
SUM_COPIES = 6 * len(SUM_PARTS)


def weight_grads(step, tok_ref, dq_ref, dk_ref, dv_ref, dkm_ref, dvm_ref, memt_ref, acc_ref, sum_ref):
    @pl.when(step == 0)
    def _():
        acc_ref[0:512, :] = jnp.zeros((512, 512), F32)
        acc_ref[512:1024, :] = dot(dkm_ref[...], memt_ref[...], 1, 1)
        acc_ref[1024:1536, :] = dot(dvm_ref[...], memt_ref[...], 1, 1)
        sum_ref[...] = jnp.zeros_like(sum_ref)
        sum_ref[:, 1:2] = jnp.sum(dvm_ref[...].astype(F32), axis=1, keepdims=True)

    tok = tok_ref[...]
    dq, dk, dv = dq_ref[...], dk_ref[...], dv_ref[...]
    acc_ref[0:512, :] += dot(dq, tok, 1, 0)
    acc_ref[512:1024, :] += dot(dk, tok, 1, 0)
    acc_ref[1024:1536, :] += dot(dv, tok, 1, 0)
    sum_ref[:, 0:1] += jnp.sum(dq.astype(F32), axis=1, keepdims=True)
    sum_ref[:, 1:2] += jnp.sum(dv.astype(F32), axis=1, keepdims=True)


def late_grads(dkm_ref, dvm_ref, vec_ref, bup_ref, wt_ref, acc_ref, sum_ref, late):
    for j in range(3):
        late(slice(16 * j, 16 * j + 16), slice(0, 512), acc_ref[512 * j : 512 * j + 512, :].T.astype(BF16))
    gmem = dot(wt_ref[512:1024, :], dkm_ref[...], 0, 0) + dot(wt_ref[1024:1536, :], dvm_ref[...], 0, 0)
    late(slice(48, 64), slice(0, 128), gmem.astype(BF16))
    lane = lax.broadcasted_iota(jnp.int32, (512, 128), 1)
    vecs = jnp.concatenate([vec_ref[...], jnp.zeros((120, 512), F32)], axis=0).T
    late(slice(48, 64), slice(128, 256), jnp.where(lane < 2, sum_ref[...], vecs).astype(BF16))
    rows = [bup_ref[0:1, 256 * v : 256 * v + 256] for v in range(8)] + [jnp.zeros((8, 256), F32)]
    rows = jnp.concatenate(rows, axis=0).astype(BF16)
    late(slice(48, 64), slice(256, 512), jnp.broadcast_to(rows[None], (PARTS, 16, 256)).reshape(512, 256))


def token_grads(gtok_ref, gfirst_ref, dq_ref, dk_ref, dv_ref, wt_ref):
    gtok_ref[...] = (
        gfirst_ref[...]
        + dot(dq_ref[...], wt_ref[0:512, :], 0, 0)
        + dot(dk_ref[...], wt_ref[512:1024, :], 0, 0)
        + dot(dv_ref[...], wt_ref[1024:1536, :], 0, 0)
    )


def scatter_kernel(
    blocks, qa_ref, ka_ref, va_ref, kmn_ref, km_ref, vmn_ref, do_ref, lse_ref, delta_ref,
    tok_ref, gfirst_ref, vec_ref, bup_ref, wt_ref, memt_ref, early_ref, gtok_ref, out_ref,
    q2_ref, do2_ref, dqa_ref, dka_ref, dva_ref, dkma_ref, dvma_ref, sa_ref, ga_ref, sb_ref, gb_ref,
    dq_ref, dk_ref, dv_ref, dkm_ref, dvm_ref,
    acc_ref, sum_ref, late, parts_sum, other, send, recv, local, *landing,
):
    step = pl.program_id(0)
    place = Place()
    copies = Copies(send, recv)
    slots = dict(zip(slot_shapes(SUM_PARTS), landing))
    crossing = [copies.number() for _ in SUM_PARTS]
    parts = []
    for index, (rows, order) in enumerate(SUM_PARTS):
        mine = {key[1:]: slot for key, slot in slots.items() if key[0] == index}
        parts.append(scatter_part(place, copies, parts_sum, mine, out_ref, rows, order))
    firsts, lasts = parts[: len(SUM_EARLY)], parts[len(SUM_EARLY) :]

    def load(index):
        rows = SUM_EARLY[index][0]
        return pltpu.make_async_copy(
            early_ref.at[:, :, :, place.core, rows], parts_sum.at[:, :, :, rows], local.at[index]
        )

    def cross(source, base, rows, number):
        old = slice(rows.start - base, rows.stop - base)
        copies.start(
            lambda: source.at[:, :, :, place.far, old], lambda: other.at[:, :, :, rows], number, place.partner
        )

    @pl.when(step == 0)
    def _():
        place.greet()
        for index in range(len(SUM_EARLY)):
            load(index).start()
        for ref in (dka_ref, dva_ref, dkma_ref, dvma_ref, sum_ref):
            ref[...] = jnp.zeros_like(ref)
        acc_ref[0:512, :] = jnp.zeros((512, 512), F32)

    @pl.when(step < blocks)
    def _():
        reach = LONGEST // BQ
        begin = jnp.maximum(step - reach, 0)
        end = jnp.minimum(step + reach + 1, blocks)
        attend_back(
            begin * (BQ // 128), (end - begin) * (BQ // BK), qa_ref, ka_ref, va_ref, kmn_ref, km_ref, vmn_ref,
            do_ref, lse_ref, delta_ref, q2_ref, do2_ref, dqa_ref, dka_ref, dva_ref, dkma_ref, dvma_ref,
            sa_ref, ga_ref, sb_ref, gb_ref,
        )
        here = pl.ds(pl.multiple_of(step * BQ, BQ), BQ)
        for h in range(H):
            dq_ref[64 * h : 64 * h + 64, here] = (dqa_ref[h] * HD ** -0.5).astype(BF16)
        dq = dq_ref[:, here]
        acc_ref[0:512, :] += dot(dq, tok_ref[here, :], 1, 0)
        sum_ref[:, 0:1] += jnp.sum(dq.astype(F32), axis=1, keepdims=True)

    @pl.when(step == 0)
    def _():
        place.met()
        for number, (rows, _) in zip(crossing, SUM_EARLY):
            cross(early_ref, 0, rows, number)

    @pl.when(step == 1)
    def _():
        for index, (rows, _) in enumerate(SUM_EARLY):
            load(index).wait()
            join(place, copies, parts_sum, None, other, rows, crossing[index])
            next(firsts[index])

    @pl.when(step == 3)
    def _():
        advance(firsts)

    @pl.when(step == 5)
    def _():
        advance(firsts)

    @pl.when(step == blocks - 1)
    def _():
        advance(firsts)

    @pl.when(step == blocks)
    def _():
        for h in range(H):
            s = slice(64 * h, 64 * h + 64)
            dk_ref[s, :] = dka_ref[h].astype(BF16)
            dv_ref[s, :] = dva_ref[h].astype(BF16)
            dkm_ref[s, :] = dkma_ref[h].astype(BF16)
            dvm_ref[s, :] = dvma_ref[h].astype(BF16)
        tok, dv, dvm = tok_ref[...], dv_ref[...], dvm_ref[...]
        acc_ref[512:1024, :] = dot(dk_ref[...], tok, 1, 0) + dot(dkm_ref[...], memt_ref[...], 1, 1)
        acc_ref[1024:1536, :] = dot(dv, tok, 1, 0) + dot(dvm, memt_ref[...], 1, 1)
        sum_ref[:, 1:2] = jnp.sum(dv.astype(F32), axis=1, keepdims=True) + jnp.sum(
            dvm.astype(F32), axis=1, keepdims=True
        )

        def put(rows, lanes, value):
            late[:, :, :, :, rows, lanes] = value.reshape(4, 2, 2, 2, 16, value.shape[1])

        late_grads(dkm_ref, dvm_ref, vec_ref, bup_ref, wt_ref, acc_ref, sum_ref, put)
        for number, (rows, _) in zip(crossing[len(SUM_EARLY) :], SUM_LATE):
            cross(late, LATE, rows, number)

    @pl.when(step > blocks)
    def _():
        rows = gtok_ref.shape[0]
        here = pl.ds(pl.multiple_of((step - blocks - 1) * rows, 128), rows)
        token_grads(gtok_ref, gfirst_ref, dq_ref.at[:, here], dk_ref.at[:, here], dv_ref.at[:, here], wt_ref)

    @pl.when(step == blocks + 1)
    def _():
        for index, (rows, _) in enumerate(SUM_LATE):
            join(
                place, copies, parts_sum,
                lambda z, old=slice(rows.start - LATE, rows.stop - LATE): late[z, :, :, place.core, old],
                other, rows, crossing[len(SUM_EARLY) + index],
            )
            next(lasts[index])

    @pl.when(step == blocks + 3)
    def _():
        advance(lasts)

    @pl.when(step == pl.num_programs(0) - 1)
    def _():
        advance(lasts)
        advance(lasts)
        copies.finish()


def backward(seg2, counts, early, tokens, qa, ka, va, kmn, km, vmn, mgrad, lse, delta, gfirst, vec, bup, wt, memt, remote):
    if not remote:
        dq, dk, dv, dkm, dvm = attend_backward(seg2, counts, qa, ka, va, kmn, km, vmn, mgrad, lse, delta)
        return tail(tokens, dq, dk, dv, dkm, dvm, gfirst, vec, bup, wt, memt)
    slots = tokens.shape[0]
    rb = 512
    blocks = slots // BQ
    once = pl.Buffered(1)

    def full(a):
        return pl.BlockSpec(a.shape, lambda i: (0,) * len(a.shape), pipeline_mode=once)

    def at(i):
        return jnp.minimum(i, blocks - 1)

    later = pl.BlockSpec((rb, 512), lambda i: (jnp.maximum(i - blocks - 1, 0), 0))
    stat = pl.BlockSpec((H, BQ), lambda i: (0, at(i)))
    score = pltpu.VMEM((H, BK, BQ), F32)
    return pl.pallas_call(
        functools.partial(scatter_kernel, blocks),
        grid=(blocks + 1 + slots // rb,),
        in_specs=[
            pl.BlockSpec((H, HA, BQ), lambda i: (0, 0, at(i))),
            full(ka), full(va), full(kmn), full(km), full(vmn),
            pl.BlockSpec((512, BQ), lambda i: (0, at(i))), stat, stat,
            full(tokens), later, full(vec), full(bup), full(wt), full(memt),
            pl.BlockSpec(memory_space=pl.ANY),
        ],
        out_specs=[later, fixed(ROWS, 512)],
        out_shape=[jax.ShapeDtypeStruct((slots, 512), F32), jax.ShapeDtypeStruct((ROWS, 512), F32)],
        scratch_shapes=[
            pltpu.VMEM((H, HA, BQ), BF16),
            pltpu.VMEM((H, HA, BQ), BF16),
            pltpu.VMEM((H, HD, BQ), F32),
            pltpu.VMEM((H, HD, slots), F32),
            pltpu.VMEM((H, HD, slots), F32),
            pltpu.VMEM((H, HD, 128), F32),
            pltpu.VMEM((H, HD, 128), F32),
            score, score, score, score,
            pltpu.VMEM((512, slots), BF16),
            pltpu.VMEM((512, slots), BF16),
            pltpu.VMEM((512, slots), BF16),
            pltpu.VMEM((512, 128), BF16),
            pltpu.VMEM((512, 128), BF16),
            pltpu.VMEM((1536, 512), F32),
            pltpu.VMEM((512, 128), F32),
            pltpu.VMEM((4, 2, 2, 2, EARLY, 512), BF16),
            pltpu.VMEM((4, 2, 2, ROWS, 512), BF16),
            pltpu.VMEM((4, 2, 2, ROWS, 512), BF16),
            pltpu.SemaphoreType.DMA((SUM_COPIES,)),
            pltpu.SemaphoreType.DMA((SUM_COPIES,)),
            pltpu.SemaphoreType.DMA((len(SUM_EARLY),)),
        ]
        + [pltpu.VMEM(shape, BF16) for shape in slot_shapes(SUM_PARTS).values()],
        compiler_params=params(collective_id=1, has_side_effects=True),
        name="backward_scatter",
    )(
        qa, ka, va, kmn, km, vmn, mgrad, lse, delta, tokens, gfirst, vec, bup, wt, memt,
        early.reshape(4, 2, 2, 2, LATE, 512),
    )


def plain_kernel(
    half, tok_ref, dq_ref, dk_ref, dv_ref, dkm_ref, dvm_ref, gfirst_ref, vec_ref, bup_ref, wt_ref, memt_ref,
    gtok_ref, late_ref, acc_ref, sum_ref,
):
    step = pl.program_id(0)

    @pl.when(step < half)
    def _():
        weight_grads(step, tok_ref, dq_ref, dk_ref, dv_ref, dkm_ref, dvm_ref, memt_ref, acc_ref, sum_ref)

    @pl.when(step == half - 1)
    def _():
        def put(rows, lanes, value):
            late_ref[:, rows, lanes] = value.reshape(PARTS, 16, value.shape[1])

        late_grads(dkm_ref, dvm_ref, vec_ref, bup_ref, wt_ref, acc_ref, sum_ref, put)

    @pl.when(step >= half)
    def _():
        token_grads(gtok_ref, gfirst_ref, dq_ref, dk_ref, dv_ref, wt_ref)


def tail(tokens, dq, dk, dv, dkm, dvm, gfirst, vec, bup, wt, memt):
    slots = tokens.shape[0]
    rb = 512
    half = slots // rb
    cols = pl.BlockSpec((512, rb), lambda i: (0, i % half))
    later = pl.BlockSpec((rb, 512), lambda i: (jnp.maximum(i - half, 0), 0))
    return pl.pallas_call(
        functools.partial(plain_kernel, half),
        grid=(2 * half,),
        in_specs=[
            pl.BlockSpec((rb, 512), lambda i: (jnp.minimum(i, half - 1), 0)),
            cols, cols, cols, fixed(512, 128), fixed(512, 128), later,
            fixed(8, 512), fixed(1, 2048), fixed(1536, 512), fixed(512, 128),
        ],
        out_specs=[later, fixed(PARTS, EARLY, 512)],
        out_shape=[jax.ShapeDtypeStruct((slots, 512), F32), jax.ShapeDtypeStruct((PARTS, EARLY, 512), BF16)],
        scratch_shapes=[pltpu.VMEM((1536, 512), F32), pltpu.VMEM((512, 128), F32)],
        compiler_params=params(),
        name="tail",
    )(tokens, dq, dk, dv, dkm, dvm, gfirst, vec, bup, wt, memt)


def unpack_kernel(sum_ref, wo, up, dn, wq, wk, wv, memory, b_up, *vectors):
    me = lax.axis_index("dp")
    wo[...] = sum_ref[0:16]
    for c in range(4):
        up[:, 512 * c : 512 * c + 512] = sum_ref[16 + 16 * c : 32 + 16 * c]
    dn[...] = sum_ref[80:144]
    wq[...] = sum_ref[144:160]
    wk[...] = sum_ref[160:176]
    wv[...] = sum_ref[176:192]
    memory[...] = sum_ref[192:208, 0 : memory.shape[1]]
    turned = sum_ref[192:208, 128:256].T
    for index, vector in enumerate(vectors):
        vector[...] = turned[index : index + 1, :]
    row = lax.broadcasted_iota(jnp.int32, (16, 256), 0)
    lane = lax.broadcasted_iota(jnp.int32, (16, 256), 1)
    own = jnp.sum(jnp.where(row * 4 + lane // 64 == me, sum_ref[192:208, 256:512], 0.0), axis=0, keepdims=True)
    b_up[...] = own[:, 0:64] + own[:, 64:128] + own[:, 128:192] + own[:, 192:256]


def unpack(sums, mem_rows):
    shapes = [(16, 512), (16, 2048), (64, 512), (16, 512), (16, 512), (16, 512), (16, mem_rows), (1, 64)] + [(1, 16)] * 8
    found = pl.pallas_call(
        unpack_kernel,
        out_shape=[jax.ShapeDtypeStruct(s, F32) for s in shapes],
        compiler_params=params(),
        name="unpack",
    )(sums)
    out = dict(zip(("w_out", "w_up", "w_down", "w_query", "w_key", "w_value", "memory"), found[:7]))
    out["memory"] = out["memory"].T
    out["b_up"] = found[7].reshape(64)
    for name, value in zip(VECTORS, found[8:]):
        out[name] = value.reshape(16)
    return out


NAMES = (
    "memory", "w_query", "b_query", "w_key", "w_value", "b_value", "w_out", "b_out", "gain_attn",
    "shift_attn", "w_up", "b_up", "w_down", "b_down", "gain_ffn", "shift_ffn",
)


def pack_whole(p):
    mem_rows = p["memory"].shape[0]
    mats = [p[name].reshape(PARTS, 16, 512) for name in ("w_query", "w_key", "w_value", "w_out")]
    up = p["w_up"].reshape(PARTS, 16, 4, 512).transpose(0, 2, 1, 3).reshape(PARTS, 64, 512)
    memory = jnp.pad(p["memory"].T, ((0, 0), (0, 128 - mem_rows))).reshape(PARTS, 16, 128)
    vectors = jnp.stack([p[name] for name in VECTORS], axis=1)
    vectors = jnp.pad(vectors, ((0, 0), (0, 120))).reshape(PARTS, 16, 128)
    own = jnp.arange(2048)[None] // 64 == jnp.arange(PARTS)[:, None]
    b_up = jnp.where(own, p["b_up"][None], 0).astype(BF16).reshape(PARTS, 8, 256)
    b_up = jnp.pad(b_up, ((0, 0), (0, 8), (0, 0)))
    small = jnp.concatenate([memory, vectors, b_up], axis=2)
    return jnp.concatenate(mats[:3] + [small, up, p["w_down"].reshape(PARTS, 64, 512), mats[3]], axis=1)


def unpack_whole(early, late, mem_rows):
    small = late[:, 48:64]
    vectors = small[:, :, 128:136].reshape(512, 8)
    out = {
        "memory": small[:, :, 0:mem_rows].reshape(512, mem_rows).T,
        "w_query": late[:, 0:16].reshape(512, 512),
        "w_key": late[:, 16:32].reshape(512, 512),
        "w_value": late[:, 32:48].reshape(512, 512),
        "w_out": early[:, 0:16].reshape(512, 512),
        "w_up": early[:, 16:80].reshape(PARTS, 4, 16, 512).transpose(0, 2, 1, 3).reshape(512, 2048),
        "w_down": early[:, 80:144].reshape(2048, 512),
        "b_up": small[0, 0:8, 256:512].reshape(2048),
    }
    for index, name in enumerate(VECTORS):
        out[name] = vectors[:, index]
    return out


def axis_of(name):
    return 1 if name == "memory" else 0


def shards(n, tokens, segment, counts, *rest):
    p = dict(zip(NAMES, rest[:-1]))
    cotangent = rest[-1]
    slots = tokens.shape[0]
    mem_rows = p["memory"].shape[0]
    whole = None
    if n != PARTS:
        whole = pack_whole({k: lax.all_gather(v, "dp", axis=axis_of(k), tiled=True) for k, v in p.items()})
    found = projections(p, whole, tokens, segment, counts, mem_rows)
    late, qa, ka, va, km, kmn, vmn, wt, memt, rows8, rbup, mixt, lse = found
    seg2 = segment.reshape(slots // 128, 128)
    output, gfirst, mgrad, delta, early, vec, bup = middle(late, rows8, rbup, counts, mixt, tokens, cotangent)
    gtok, sums = backward(
        seg2, counts, early, tokens, qa, ka, va, kmn, km, vmn, mgrad, lse, delta, gfirst, vec, bup, wt, memt, n == PARTS
    )
    if n == PARTS:
        grads = unpack(sums, mem_rows)
    else:
        full = unpack_whole(early.astype(F32), sums.astype(F32), mem_rows)
        grads = {
            k: lax.psum_scatter(v, "dp", scatter_dimension=axis_of(k), tiled=True) for k, v in full.items()
        }
    return (output, gtok) + tuple(grads[name] for name in NAMES)


def solution(mesh):
    n = mesh.shape["dp"]
    row, mat, mem = P("dp"), P("dp", None), P(None, "dp")
    spec = {name: mat if name.startswith("w_") else row for name in NAMES}
    spec["memory"] = mem
    weights = tuple(spec[name] for name in NAMES)
    return jax.shard_map(
        functools.partial(shards, n),
        mesh=mesh,
        in_specs=(mat, row, row) + weights + (mat,),
        out_specs=(mat, mat) + weights,
        check_vma=False,
    )
```

```python
import functools
import jax
import jax.numpy as jnp
from jax import lax
from jax.experimental import pallas as pl
from jax.experimental.pallas import tpu as pltpu
from jax.sharding import PartitionSpec as P

H = 8
HD = 64
HA = 80
EPS = 1e-05
BIG = 1e30
PARTS = 32
ROWS = 208
BQ = 256
BK = 256
MP = 32
LONGEST = 1024
F32 = jnp.float32
BF16 = jnp.bfloat16
VMEM_LIMIT = 60 << 20

V_BQ, V_BV, V_BO, V_GA, V_SA, V_BD, V_GF, V_SF = range(8)


def dot(left, right, lc, rc):
    return lax.dot_general(left, right, (((lc,), (rc,)), ((), ())), preferred_element_type=F32)


def params(**kw):
    return pltpu.CompilerParams(vmem_limit_bytes=VMEM_LIMIT, **kw)


MESH = pl.DeviceIdType.MESH
AXES = {"z": (8, 4), "y": (4, 2), "x": (2, 2)}
LAYOUT = ("z", "y", "x")


class Place:
    def __init__(self):
        me = lax.axis_index("dp")
        self.me = me
        self.core = me % 2
        self.far = 1 - self.core
        self.partner = me + 1 - 2 * self.core
        self.at = {a: (me // stride) % length for a, (stride, length) in AXES.items()}
        self.mine = tuple(self.at[a] for a in LAYOUT)
        self.others = {}
        for axis, (stride, length) in AXES.items():
            for distance in range(1, length):
                j = (self.at[axis] + distance) % length
                self.others[axis, distance] = j, me + (j - self.at[axis]) * stride
        self.peers = [self.partner] + [device for _, device in self.others.values()]

    def other(self, axis, distance):
        return self.others[axis, distance]

    def greet(self):
        for peer in self.peers:
            pl.semaphore_signal(
                pltpu.get_barrier_semaphore(), inc=1, device_id=(peer,), device_id_type=MESH
            )

    def met(self):
        pl.semaphore_wait(pltpu.get_barrier_semaphore(), len(self.peers))


class Copies:
    def __init__(self, send, recv):
        self.send, self.recv, self.count, self.open = send, recv, 0, []

    def number(self):
        self.count += 1
        return self.count - 1

    def make(self, src, dst, number, device):
        return pltpu.make_async_remote_copy(
            src_ref=src, dst_ref=dst, send_sem=self.send.at[number], recv_sem=self.recv.at[number],
            device_id=(device,), device_id_type=MESH,
        )

    def start(self, src, dst, number, device):
        self.make(src(), dst(), number, device).start()
        self.open.append((src, dst, number, device))

    def landed(self, block, number, device):
        self.make(block, block, number, device).wait_recv()

    def finish(self):
        for src, dst, number, device in self.open:
            self.make(src(), dst(), number, device).wait_send()
        self.open = []


def gather_part(place, copies, own, base, whole, rows, order, arrivals):
    done = ()

    def mine():
        return own.at[slice(base + rows.start, base + rows.stop)]

    def block(axis, j, core):
        index = tuple(j if a == axis else (slice(None) if a in done else place.at[a]) for a in LAYOUT)
        return lambda: whole.at[index + (core, rows)]

    for axis in order:
        length = AXES[axis][1]
        numbers = [copies.number() for _ in range(2 * length - 2)]
        here = block(axis, place.at[axis], place.core)
        for d in range(1, length):
            copies.start(here if done else mine, here, numbers[d - 1], place.other(axis, d)[1])
        if not done:
            number = copies.number()
            copies.start(mine, here, number, place.partner)
            arrivals.append((block(axis, place.at[axis], place.far), number))
        yield
        for d in range(1, length):
            j, device = place.other(axis, length - d)
            there = block(axis, j, place.core)
            copies.landed(there(), numbers[d - 1], device)
            number = numbers[length - 2 + d]
            copies.start(there, there, number, place.partner)
            arrivals.append((block(axis, j, place.far), number))
        done += (axis,)
    yield


def advance(parts):
    for part in parts:
        next(part)


def scatter_part(place, copies, acc, slots, out, rows, order):
    done = ()

    def block(axis, j):
        index = tuple(j if a == axis else (place.at[a] if a in done else slice(None)) for a in LAYOUT)
        return index + (rows,)

    def taken(index):
        return lambda: acc.at[index]

    def landing(axis, d):
        return lambda: slots[axis, d]

    for axis in order:
        length = AXES[axis][1]
        numbers = [copies.number() for _ in range(length - 1)]
        for d in range(1, length):
            j, device = place.other(axis, d)
            copies.start(taken(block(axis, j)), landing(axis, d), numbers[d - 1], device)
        yield
        for d in range(1, length):
            copies.landed(slots[axis, d], numbers[d - 1], place.partner)
        mine = block(axis, place.at[axis])
        total = acc[mine].astype(F32)
        for d in range(1, length):
            total = total + slots[axis, d][...].astype(F32)
        if axis == order[-1]:
            out[rows, :] = total
        else:
            acc[mine] = total.astype(BF16)
        done += (axis,)
    yield


def slot_shapes(parts):
    shapes = {}
    for number, (rows, order) in enumerate(parts):
        left = ["z", "y", "x"]
        for axis in order:
            left.remove(axis)
            shape = tuple(AXES[a][1] for a in LAYOUT if a in left) + (rows.stop - rows.start, 512)
            for d in range(1, AXES[axis][1]):
                shapes[number, axis, d] = shape
    return shapes


def join(place, copies, acc, source, other, rows, number):
    copies.landed(other.at[:, :, :, rows], number, place.partner)

    @pl.loop(0, 4)
    def _(z):
        mine = source(z) if source else acc[z, :, :, rows]
        acc[z, :, :, rows] = (mine.astype(F32) + other[z, :, :, rows].astype(F32)).astype(BF16)


VECTORS = ("b_query", "b_value", "b_out", "gain_attn", "shift_attn", "b_down", "gain_ffn", "shift_ffn")
EARLY = 64
LATE = 144
EARLY_PARTS = ((slice(0, 16), "zxy"), (slice(16, 32), "zyx"), (slice(32, 48), "zxy"), (slice(48, 64), "zyx"))
LATE_PARTS = (
    (slice(0, 48), "zxy"),
    (slice(48, 96), "zyx"),
    (slice(96, 128), "yzx"),
    (slice(128, 144), "xzy"),
)
GATHER_COPIES = 11 * (len(EARLY_PARTS) + len(LATE_PARTS))


def head_block(rows, features):
    block = jnp.concatenate([rows, features], axis=0)
    return block, jnp.concatenate([block, jnp.zeros((128 - HA, rows.shape[1]), BF16)], axis=0).T


def pack(own, place, wq, wk, wv, wo, up, dn, memory, b_up, vectors):
    own[0:16] = wq[...]
    own[16:32] = wk[...]
    own[32:48] = wv[...]
    own[48:64] = jnp.zeros((16, 512), BF16)
    own[48:64, 0 : memory.shape[1]] = memory[...]
    values = jnp.concatenate([vector[...].astype(F32) for vector in vectors], axis=0)
    own[48:64, 128:136] = values.T.astype(BF16)
    value = jnp.concatenate([b_up[...].astype(F32)] * 4, axis=1)
    row = lax.broadcasted_iota(jnp.int32, (16, 256), 0)
    lane = lax.broadcasted_iota(jnp.int32, (16, 256), 1)
    own[48:64, 256:512] = jnp.where(row * 4 + lane // 64 == place.me, value, 0.0).astype(BF16)
    for c in range(4):
        own[64 + 16 * c : 80 + 16 * c] = up[:, 512 * c : 512 * c + 512]
    own[128:192] = dn[...]
    own[192:208] = wo[...]


def prepare(mem_rows, early, wt_ref, memt_ref, rows_ref, rbup_ref, bias_ref, km_ref, vm_ref, kmn_ref, vmn_ref):
    for j in range(3):
        wt_ref[512 * j : 512 * j + 512, :] = early[..., 16 * j : 16 * j + 16, :].reshape(512, 512).T
    small = early[..., 48:64, 0:256].reshape(512, 256)
    memt = small[:, 0:128]
    memt_ref[...] = memt
    vectors = small[:, 128:256].astype(F32)
    bias_ref[...] = vectors
    rows_ref[...] = vectors.T[0:8, :]
    bup = jnp.sum(early[..., 48:64, 256:512].reshape(PARTS, 16, 256).astype(F32), axis=0)
    for v in range(8):
        rbup_ref[0:1, 256 * v : 256 * v + 256] = bup[v : v + 1, :]
    bv = vectors[:, V_BV : V_BV + 1]
    km = dot(wt_ref[512:1024, :], memt, 1, 0).astype(BF16)
    vm = (dot(wt_ref[1024:1536, :], memt, 1, 0) + bv).astype(BF16)
    frow = lax.broadcasted_iota(jnp.int32, (16, 128), 0)
    lane = lax.broadcasted_iota(jnp.int32, (16, 128), 1)
    kf = jnp.where(frow < 3, jnp.where(lane < mem_rows, 0.0, 1.0), jnp.where(frow < 6, 1.0, 0.0)).astype(BF16)
    vf = jnp.where(frow < 3, 1.0, 0.0).astype(BF16)
    for h in range(H):
        km_ref[h], turned = head_block(km[64 * h : 64 * h + 64, :], kf)
        kmn_ref[h] = turned[0:MP]
        vm_ref[h], turned = head_block(vm[64 * h : 64 * h + 64, :], vf)
        vmn_ref[h] = turned[0:MP]


def project(step, tok_ref, seg_ref, cnt_ref, wt_ref, bias_ref, qa_ref, ka_ref, va_ref):
    rows = tok_ref.shape[0]
    tok = tok_ref[...]
    bq = bias_ref[:, V_BQ : V_BQ + 1]
    bv = bias_ref[:, V_BV : V_BV + 1]
    q = (dot(wt_ref[0:512, :], tok, 1, 1) + bq).astype(BF16) * jnp.asarray(HD ** -0.5, BF16)
    k = dot(wt_ref[512:1024, :], tok, 1, 1).astype(BF16)
    v = (dot(wt_ref[1024:1536, :], tok, 1, 1) + bv).astype(BF16)
    frow = lax.broadcasted_iota(jnp.int32, (16, rows), 0)
    seg = jnp.broadcast_to(seg_ref[...], (16, rows))
    pos = lax.broadcasted_iota(jnp.int32, (16, rows), 1) + step * rows
    valid = pos < cnt_ref[0]
    qf = jnp.where((frow < 3) & (frow != seg), -BIG, 0.0).astype(BF16)
    kf = jnp.where(frow < 3, jnp.where(valid & (frow != seg), 0.0, 1.0), jnp.where(frow < 6, 1.0, 0.0)).astype(BF16)
    vf = jnp.where(frow < 3, 1.0, 0.0).astype(BF16)
    for h in range(H):
        s = slice(64 * h, 64 * h + 64)
        qa_ref[h, 0:64, :] = q[s]
        qa_ref[h, 64:80, :] = qf
        ka_ref[h, 0:64, :] = k[s]
        ka_ref[h, 64:80, :] = kf
        va_ref[h, 0:64, :] = v[s]
        va_ref[h, 64:80, :] = vf


def gather_kernel(
    mem_rows, half, wq, wk, wv, wo, up, dn, memory, b_up, v0, v1, v2, v3, v4, v5, v6, v7, tok_ref, seg_ref, cnt_ref,
    late_ref, qa_ref, ka_ref, va_ref, km_ref, kmn_ref, vmn_ref,
    wt_ref, memt_ref, rows_ref, rbup_ref, mix_ref, lse_ref,
    own, early, bias_ref, vm_ref, qa_all, ka_all, va_all, acc_ref, m_ref, sa_ref, sb_ref, send, recv, local,
):
    step = pl.program_id(0)
    slots = ka_all.shape[2]
    place = Place()
    copies = Copies(send, recv)
    arrivals, late_arrivals = [], []
    firsts = [gather_part(place, copies, own, 0, early, *part, arrivals) for part in EARLY_PARTS]
    lasts = [gather_part(place, copies, own, EARLY, late_ref, *part, late_arrivals) for part in LATE_PARTS]

    @pl.when(step == 0)
    def _():
        place.greet()
        pack(own, place, wq, wk, wv, wo, up, dn, memory, b_up, (v0, v1, v2, v3, v4, v5, v6, v7))
        early[place.mine + (place.core,)] = own[0:EARLY]
        place.met()
        advance(firsts)
        keep = pltpu.make_async_copy(own.at[EARLY:ROWS], late_ref.at[place.mine + (place.core,)], local)
        keep.start()
        advance(firsts)
        advance(firsts)
        keep.wait()
        advance(lasts)
        advance(firsts)
        for block, number in arrivals:
            copies.landed(block(), number, place.partner)
        prepare(
            mem_rows, early, wt_ref, memt_ref, rows_ref, rbup_ref, bias_ref, km_ref, vm_ref, kmn_ref, vmn_ref,
        )

    @pl.when(step < half)
    def _():
        project(step, tok_ref, seg_ref, cnt_ref, wt_ref, bias_ref, qa_ref, ka_ref, va_ref)
        here = pl.ds(pl.multiple_of(step * tok_ref.shape[0], 128), tok_ref.shape[0])
        qa_all[:, :, here] = qa_ref[...]
        ka_all[:, :, here] = ka_ref[...]
        va_all[:, :, here] = va_ref[...]

    @pl.when(step == half - 1)
    def _():
        advance(lasts)

    @pl.when(step >= half)
    def _():
        block = step - half
        reach = LONGEST // BQ
        begin = jnp.maximum(block - reach, 0)
        end = jnp.minimum(block + reach + 1, slots // BQ)
        queries = qa_all.at[:, :, pl.ds(pl.multiple_of(block * BQ, BQ), BQ)]
        attend(
            begin * (BQ // 128), (end - begin) * (BQ // BK), queries, ka_all, va_all, kmn_ref, vm_ref, mix_ref, lse_ref,
            acc_ref, m_ref, sa_ref, sb_ref,
        )

    @pl.when(step == half + 2)
    def _():
        advance(lasts)

    @pl.when(step == pl.num_programs(0) - 1)
    def _():
        advance(lasts)
        for block, number in late_arrivals:
            copies.landed(block(), number, place.partner)
        copies.finish()


def project_kernel(
    mem_rows, g_ref, tok_ref, seg_ref, cnt_ref, qa_ref, ka_ref, va_ref, km_ref, vm_ref, kmn_ref, vmn_ref,
    wt_ref, memt_ref, rows_ref, rbup_ref, bias_ref,
):
    step = pl.program_id(0)

    @pl.when(step == 0)
    def _():
        prepare(
            mem_rows, g_ref, wt_ref, memt_ref, rows_ref, rbup_ref, bias_ref, km_ref, vm_ref, kmn_ref, vmn_ref
        )

    project(step, tok_ref, seg_ref, cnt_ref, wt_ref, bias_ref, qa_ref, ka_ref, va_ref)


def fixed(*shape):
    return pl.BlockSpec(shape, lambda i: (0,) * len(shape))


def projections(p, whole, tokens, segment, counts, mem_rows):
    slots = tokens.shape[0]
    rb = 512
    half = slots // rb
    wide = (H, HA, slots)
    mwide, mtall = (H, HA, 128), (H, MP, 128)

    def at(i):
        return jnp.minimum(i, half - 1)

    blk = pl.BlockSpec((H, HA, rb), lambda i: (0, 0, at(i)))
    common = [
        pl.BlockSpec((rb, 512), lambda i: (at(i), 0)),
        pl.BlockSpec((1, rb), lambda i: (0, at(i))),
        pl.BlockSpec(memory_space=pltpu.SMEM),
    ]
    args = (tokens, segment.reshape(1, slots), counts)

    def outs(shapes):
        found = [jax.ShapeDtypeStruct(s, BF16) for s in shapes]
        return found + [jax.ShapeDtypeStruct((8, 512), F32), jax.ShapeDtypeStruct((1, 2048), F32)]

    if whole is not None:
        shapes = outs([wide, wide, wide, mwide, mwide, mtall, mtall, (1536, 512), (512, 128)])
        found = pl.pallas_call(
            functools.partial(project_kernel, mem_rows),
            grid=(half,),
            in_specs=[fixed(PARTS, EARLY, 512)] + common,
            out_specs=[blk, blk, blk] + [fixed(*o.shape) for o in shapes[3:]],
            out_shape=shapes,
            scratch_shapes=[pltpu.VMEM((512, 128), F32)],
            compiler_params=params(),
            name="projections",
        )(whole[:, 0:EARLY], *args)
        qa, ka, va, km, vm, kmn, vmn, wt, memt, rows8, rbup = found
        mixt, lse = attend_forward(segment.reshape(slots // 128, 128), counts, qa, ka, va, kmn, vm)
        return whole[:, EARLY:], qa, ka, va, km, kmn, vmn, wt, memt, rows8, rbup, mixt, lse
    weights = [p[name] for name in ("w_query", "w_key", "w_value", "w_out", "w_up", "w_down")]
    weights += [p["memory"].T, p["b_up"].reshape(1, 64)] + [p[name].reshape(1, 16) for name in VECTORS]
    shapes = outs([wide, wide, wide, mwide, mtall, mtall, (1536, 512), (512, 128)])
    found = pl.pallas_call(
        functools.partial(gather_kernel, mem_rows, half),
        grid=(half + slots // BQ,),
        in_specs=[fixed(*w.shape) for w in weights] + common,
        out_specs=[pl.BlockSpec(memory_space=pl.ANY), blk, blk, blk]
        + [fixed(*o.shape) for o in shapes[3:]]
        + [
            pl.BlockSpec((512, BQ), lambda i: (0, jnp.maximum(i - half, 0))),
            pl.BlockSpec((H, BQ), lambda i: (0, jnp.maximum(i - half, 0))),
        ],
        out_shape=[jax.ShapeDtypeStruct((4, 2, 2, 2, LATE, 512), BF16)]
        + shapes
        + [jax.ShapeDtypeStruct((512, slots), BF16), jax.ShapeDtypeStruct((H, slots), F32)],
        scratch_shapes=[
            pltpu.VMEM((ROWS, 512), BF16),
            pltpu.VMEM((4, 2, 2, 2, EARLY, 512), BF16),
            pltpu.VMEM((512, 128), F32),
            pltpu.VMEM(mwide, BF16),
            pltpu.VMEM(wide, BF16),
            pltpu.VMEM(wide, BF16),
            pltpu.VMEM(wide, BF16),
            pltpu.VMEM((H, HA, BQ), F32),
            pltpu.VMEM((H, BQ), F32),
            pltpu.VMEM((H, BK, BQ), F32),
            pltpu.VMEM((H, BK, BQ), F32),
            pltpu.SemaphoreType.DMA((GATHER_COPIES,)),
            pltpu.SemaphoreType.DMA((GATHER_COPIES,)),
            pltpu.SemaphoreType.DMA,
        ],
        compiler_params=params(collective_id=0, has_side_effects=True),
        name="gather_attend",
    )(*weights, *args)
    return (found[0].reshape(PARTS, LATE, 512),) + tuple(found[1:])


def key_ranges(seg, count, slots, out):
    r, c = seg.shape
    pos = lax.broadcasted_iota(jnp.int32, (r, c), 0) * c + lax.broadcasted_iota(jnp.int32, (r, c), 1)
    valid = pos < count
    ends = [jnp.sum(jnp.where(valid & (seg <= s), 1.0, 0.0)).astype(jnp.int32) for s in range(3)]
    for block in range(slots // BQ):
        first = block * BQ
        last = jnp.minimum(first + BQ, count)
        low, high, start = jnp.int32(slots), jnp.int32(0), jnp.int32(0)
        for end in ends:
            hit = (end > first) & (start < last) & (end > start)
            low = jnp.where(hit, jnp.minimum(low, start), low)
            high = jnp.where(hit, jnp.maximum(high, end), high)
            start = end
        begin = low // 128
        blocks = jnp.where(high > low, (high - begin * 128 + BK - 1) // BK, 0)
        out[0, block] = jnp.minimum(begin, slots // 128 - blocks * (BK // 128))
        out[1, block] = blocks


def key_slots(begin, block):
    return pl.ds(pl.multiple_of((begin + block * (BK // 128)) * 128, 128), BK)


def pipelined(blocks, work, first, second):
    @pl.when(blocks > 0)
    def _():
        work((0, first), None)

    pairs = jnp.maximum(blocks - 1, 0) // 2

    @pl.loop(0, pairs)
    def _(i):
        work((2 * i + 1, second), (2 * i, first))
        work((2 * i + 2, first), (2 * i + 1, second))

    j = 2 * pairs

    @pl.when(blocks - j == 2)
    def _():
        work((j + 1, second), (j, first))
        work(None, (j + 1, second))

    @pl.when(blocks - j == 1)
    def _():
        work(None, (j, first))


def attend(begin, blocks, qa_ref, ka_ref, va_ref, kmn_ref, vm_ref, mix_ref, lse_ref, acc_ref, m_ref, sa_ref, sb_ref):
    def weights(h, s):
        old = m_ref[h : h + 1, :]
        top = jnp.maximum(old, jnp.max(s, axis=0, keepdims=True))
        return jnp.exp(s - top).astype(BF16), jnp.exp(old - top), top

    def work(new, old):
        kept = {}
        for h in range(H + 1):
            if h < H and new:
                new[1][h] = dot(ka_ref[h, :, key_slots(begin, new[0])], qa_ref[h], 0, 0)
            if h < H and old:
                kept[h] = weights(h, old[1][h])
            if h > 0 and old:
                p, fade, top = kept.pop(h - 1)
                acc_ref[h - 1] = acc_ref[h - 1] * fade + dot(va_ref[h - 1, :, key_slots(begin, old[0])], p, 1, 0)
                m_ref[h - 1 : h, :] = top

    scores = [dot(kmn_ref[h, :, 0:HA], qa_ref[h], 1, 0) for h in range(H)]
    for h in range(H):
        top = jnp.max(scores[h], axis=0, keepdims=True)
        p = jnp.exp(scores[h] - top).astype(BF16)
        acc_ref[h] = dot(vm_ref[h, :, 0:MP], p, 1, 0)
        m_ref[h : h + 1, :] = top
    pipelined(blocks, work, sa_ref, sb_ref)
    for h in range(H):
        total = acc_ref[h, 64:65, :]
        mix_ref[64 * h : 64 * h + 64, :] = (acc_ref[h, 0:64, :] * (1.0 / total)).astype(BF16)
        lse_ref[h : h + 1, :] = m_ref[h : h + 1, :] + jnp.log(total)


def fwd_kernel(
    slots, seg_ref, cnt_ref, qa_ref, ka_ref, va_ref, kmn_ref, vm_ref,
    mix_ref, lse_ref, acc_ref, m_ref, sa_ref, sb_ref, range_ref,
):
    step = pl.program_id(0)

    @pl.when(step == 0)
    def _():
        key_ranges(seg_ref[...], cnt_ref[0], slots, range_ref)

    attend(
        range_ref[0, step], range_ref[1, step], qa_ref, ka_ref, va_ref, kmn_ref, vm_ref, mix_ref, lse_ref,
        acc_ref, m_ref, sa_ref, sb_ref,
    )


def attend_forward(seg2, counts, qa, ka, va, kmn, vm):
    slots = qa.shape[2]
    once = pl.Buffered(1)

    def whole(a):
        return pl.BlockSpec(a.shape, lambda i: (0, 0, 0), pipeline_mode=once)

    return pl.pallas_call(
        functools.partial(fwd_kernel, slots),
        grid=(slots // BQ,),
        in_specs=[
            pl.BlockSpec(seg2.shape, lambda i: (0, 0)),
            pl.BlockSpec(memory_space=pltpu.SMEM),
            pl.BlockSpec((H, HA, BQ), lambda i: (0, 0, i)),
            whole(ka), whole(va), whole(kmn), whole(vm),
        ],
        out_specs=[pl.BlockSpec((512, BQ), lambda i: (0, i)), pl.BlockSpec((H, BQ), lambda i: (0, i))],
        out_shape=[jax.ShapeDtypeStruct((512, slots), BF16), jax.ShapeDtypeStruct((H, slots), F32)],
        scratch_shapes=[
            pltpu.VMEM((H, HA, BQ), F32),
            pltpu.VMEM((H, BQ), F32),
            pltpu.VMEM((H, BK, BQ), F32),
            pltpu.VMEM((H, BK, BQ), F32),
            pltpu.SMEM((2, slots // BQ), jnp.int32),
        ],
        compiler_params=params(),
        name="attend_forward",
    )(seg2, counts, qa, ka, va, kmn, vm)


def norm_parts(value):
    mean = jnp.mean(value, axis=-1, keepdims=True)
    centred = value - mean
    rstd = lax.rsqrt(jnp.mean(centred * centred, axis=-1, keepdims=True) + EPS)
    return centred * rstd, rstd


def norm_grad(grad_hat, hat, rstd):
    return rstd * (
        grad_hat
        - jnp.mean(grad_hat, axis=-1, keepdims=True)
        - hat * jnp.mean(grad_hat * hat, axis=-1, keepdims=True)
    )


def colsum(value):
    return jnp.sum(value, axis=0, keepdims=True)


SUB = 512
FC = 512


def mid_kernel(
    rb, cnt_ref, row_ref, rbup_ref, late_ref, mix_ref, tok_ref, cot_ref,
    out_ref, gfirst_ref, mgrad_ref, delta_ref, gw_ref, vec_ref, bup_ref,
    aup_ref, adn_ref, ao_ref, *scratch,
):
    step = pl.program_id(0)
    subs = rb // SUB

    @pl.when(step == 0)
    def _():
        aup_ref[...] = jnp.zeros_like(aup_ref)
        adn_ref[...] = jnp.zeros_like(adn_ref)
        ao_ref[...] = jnp.zeros_like(ao_ref)
        vec_ref[...] = jnp.zeros_like(vec_ref)
        bup_ref[...] = jnp.zeros_like(bup_ref)

    wo = late_ref[:, 128:144, :].reshape(512, 512)

    def w_up(c):
        return late_ref[:, 16 * c : 16 * c + 16, :].reshape(512, 512)

    def w_down(c):
        return late_ref[8 * c : 8 * c + 8, 64:128, :].reshape(512, 512)

    def row(v):
        return row_ref[v : v + 1, :]

    class Block:
        def __init__(self, index):
            self.s = slice(SUB * index, SUB * index + SUB)
            self.first_row = step * rb + SUB * index
            self.active, self.slope, self.hgrad = scratch[3 * (index % 2) : 3 * (index % 2) + 3]
            self.up_part, self.dact_part = {}, {}

        def head(self):
            self.mixt = mix_ref[:, self.s]
            attention = dot(self.mixt, wo, 0, 0) + row(V_BO)
            self.hat1, self.rstd1 = norm_parts(tok_ref[self.s, :].astype(F32) + attention)
            self.first = self.hat1 * row(V_GA) + row(V_SA)
            self.low = self.first.astype(BF16)
            self.branch = self.first + row(V_BD)

        def up(self, c):
            f = slice(FC * c, FC * c + FC)
            self.up_part[c] = dot(self.low, w_up(c), 1, 0) + rbup_ref[:, f]

        def gelu(self, c):
            f = slice(FC * c, FC * c + FC)
            hidden = self.up_part.pop(c)
            cdf = 0.5 + 0.5 * lax.erf(hidden * (2.0 ** -0.5))
            self.active[:, f] = (hidden * cdf).astype(BF16)
            self.slope[:, f] = cdf + hidden * jnp.exp(hidden * hidden * -0.5) * 0.3989422804014327

        def down(self, c):
            f = slice(FC * c, FC * c + FC)
            self.branch = self.branch + dot(self.active[:, f], w_down(c), 1, 0)

        def turn(self):
            hat2, rstd2 = norm_parts(self.branch)
            valid = lax.broadcasted_iota(jnp.int32, (SUB, 1), 0) + self.first_row < cnt_ref[0]
            out_ref[self.s, :] = jnp.where(valid, hat2 * row(V_GF) + row(V_SF), 0.0).astype(BF16)
            seed = jnp.where(valid, cot_ref[self.s, :].astype(F32), 0.0)
            vec_ref[V_GF : V_GF + 1, :] += colsum(seed * hat2)
            vec_ref[V_SF : V_SF + 1, :] += colsum(seed)
            self.total = norm_grad(seed * row(V_GF), hat2, rstd2)
            self.bgrad = self.total.astype(BF16)
            vec_ref[V_BD : V_BD + 1, :] += colsum(self.bgrad.astype(F32))

        def dact(self, c):
            f = slice(FC * c, FC * c + FC)
            self.dact_part[c] = dot(self.bgrad, w_down(c), 1, 1)

        def grad_down(self, c):
            f = slice(FC * c, FC * c + FC)
            adn_ref[f, :] += dot(self.active[:, f], self.bgrad, 0, 0)

        def hidden_grad(self, c):
            f = slice(FC * c, FC * c + FC)
            grad = (self.dact_part.pop(c) * self.slope[:, f]).astype(BF16)
            self.hgrad[:, f] = grad
            bup_ref[:, f] += colsum(grad.astype(F32))

        def grad_up(self, c):
            f = slice(FC * c, FC * c + FC)
            aup_ref[:, f] += dot(self.low, self.hgrad[:, f], 0, 0)

        def first_grad(self, c):
            f = slice(FC * c, FC * c + FC)
            self.total = self.total + dot(self.hgrad[:, f], w_up(c), 1, 1)

        def finish(self):
            vec_ref[V_GA : V_GA + 1, :] += colsum(self.total * self.hat1)
            vec_ref[V_SA : V_SA + 1, :] += colsum(self.total)
            grad_first = norm_grad(self.total * row(V_GA), self.hat1, self.rstd1)
            gfirst_ref[self.s, :] = grad_first
            agrad = grad_first.astype(BF16)
            vec_ref[V_BO : V_BO + 1, :] += colsum(agrad.astype(F32))
            mgrad = dot(wo, agrad, 1, 1).astype(BF16)
            ao_ref[...] += dot(self.mixt, agrad, 1, 0)
            mgrad_ref[:, self.s] = mgrad
            prod = mgrad.astype(F32) * self.mixt.astype(F32)
            for h in range(H):
                delta_ref[h : h + 1, self.s] = jnp.sum(prod[64 * h : 64 * h + 64, :], axis=0, keepdims=True)

    chunks = 2048 // FC

    def both(ahead, behind):
        if ahead:
            ahead.head()
            ahead.up(0)
        for c in range(chunks):
            if behind:
                behind.dact(c)
            if ahead and c + 1 < chunks:
                ahead.up(c + 1)
            if behind:
                behind.grad_down(c)
            if ahead:
                ahead.gelu(c)
            if behind:
                behind.hidden_grad(c)
                behind.grad_up(c)
                behind.first_grad(c)
            if ahead:
                ahead.down(c)
        if behind:
            behind.finish()
        if ahead:
            ahead.turn()

    blocks = [Block(index) for index in range(subs)]
    for ahead, behind in zip(blocks + [None], [None] + blocks):
        both(ahead, behind)

    @pl.when(step == pl.num_programs(0) - 1)
    def _():
        gw_ref[:, 0:16, :] = ao_ref[...].astype(gw_ref.dtype).reshape(PARTS, 16, 512)
        for c in range(4):
            gw_ref[:, 16 + 16 * c : 32 + 16 * c, :] = (
                aup_ref[:, 512 * c : 512 * c + 512].astype(gw_ref.dtype).reshape(PARTS, 16, 512)
            )
        gw_ref[:, 80:144, :] = adn_ref[...].astype(gw_ref.dtype).reshape(PARTS, 64, 512)


def middle(late, rows8, rbup, counts, mixt, tokens, cotangent, rb=512):
    slots = tokens.shape[0]
    rows = pl.BlockSpec((rb, 512), lambda i: (i, 0))
    cols = pl.BlockSpec((512, rb), lambda i: (0, i))
    once = pl.Buffered(1)
    return pl.pallas_call(
        functools.partial(mid_kernel, rb),
        grid=(slots // rb,),
        in_specs=[
            pl.BlockSpec(memory_space=pltpu.SMEM),
            pl.BlockSpec((8, 512), lambda i: (0, 0)),
            pl.BlockSpec((1, 2048), lambda i: (0, 0)),
            pl.BlockSpec((PARTS, LATE, 512), lambda i: (0, 0, 0), pipeline_mode=once),
            cols, rows, rows,
        ],
        out_specs=[
            rows, rows, cols,
            pl.BlockSpec((H, rb), lambda i: (0, i)),
            pl.BlockSpec((PARTS, 144, 512), lambda i: (0, 0, 0), pipeline_mode=once),
            pl.BlockSpec((8, 512), lambda i: (0, 0)),
            pl.BlockSpec((1, 2048), lambda i: (0, 0)),
        ],
        out_shape=[
            jax.ShapeDtypeStruct((slots, 512), BF16),
            jax.ShapeDtypeStruct((slots, 512), F32),
            jax.ShapeDtypeStruct((512, slots), BF16),
            jax.ShapeDtypeStruct((H, slots), F32),
            jax.ShapeDtypeStruct((PARTS, 144, 512), BF16),
            jax.ShapeDtypeStruct((8, 512), F32),
            jax.ShapeDtypeStruct((1, 2048), F32),
        ],
        scratch_shapes=[
            pltpu.VMEM((512, 2048), F32),
            pltpu.VMEM((2048, 512), F32),
            pltpu.VMEM((512, 512), F32),
        ]
        + [pltpu.VMEM((SUB, 2048), BF16), pltpu.VMEM((SUB, 2048), F32), pltpu.VMEM((SUB, 2048), BF16)] * 2,
        compiler_params=params(),
        name="middle",
    )(counts, rows8, rbup, late, mixt, tokens, cotangent)


def split3(value):
    high = value.astype(BF16)
    rest = value - high.astype(F32)
    mid = rest.astype(BF16)
    return high, mid, (rest - mid.astype(F32)).astype(BF16)


def attend_back(
    begin, blocks, qa_ref, ka_ref, va_ref, kmn_ref, km_ref, vmn_ref, do_ref, lse_ref, delta_ref,
    q2_ref, do2_ref, dqa_ref, dka_ref, dva_ref, dkma_ref, dvma_ref, sa_ref, ga_ref, sb_ref, gb_ref,
):
    frow = lax.broadcasted_iota(jnp.int32, (16, BQ), 0)

    def feature(value, at):
        high, mid, low = (jnp.broadcast_to(v.astype(F32), (16, BQ)) for v in split3(value))
        return jnp.where(frow == at, high, jnp.where(frow == at + 1, mid, jnp.where(frow == at + 2, low, 0.0)))

    for h in range(H):
        q2_ref[h, 0:64, :] = qa_ref[h, 0:64, :]
        q2_ref[h, 64:80, :] = (qa_ref[h, 64:80, :].astype(F32) + feature(-lse_ref[h : h + 1, :], 3)).astype(BF16)
        do2_ref[h, 0:64, :] = do_ref[64 * h : 64 * h + 64, :]
        do2_ref[h, 64:80, :] = feature(-delta_ref[h : h + 1, :], 0).astype(BF16)

    def work(new, old):
        kept = {}
        for h in range(H + 1):
            if h < H and new:
                ks = key_slots(begin, new[0])
                new[1][0][h] = dot(ka_ref[h, :, ks], q2_ref[h], 0, 0)
                new[1][1][h] = dot(va_ref[h, :, ks], do2_ref[h], 0, 0)
            if h < H and old:
                p = jnp.exp(old[1][0][h])
                kept[h] = p.astype(BF16), (p * old[1][1][h]).astype(BF16)
            if h > 0 and old:
                ks = key_slots(begin, old[0])
                p, ds = kept.pop(h - 1)
                dva_ref[h - 1, :, ks] += dot(do2_ref[h - 1, 0:64, :], p, 1, 1)
                dka_ref[h - 1, :, ks] += dot(q2_ref[h - 1, 0:64, :], ds, 1, 1)
                dqa_ref[h - 1] += dot(ka_ref[h - 1, 0:64, ks], ds, 1, 0)

    ps = [jnp.exp(dot(kmn_ref[h, :, 0:HA], q2_ref[h], 1, 0)) for h in range(H)]
    dss = [(ps[h] * dot(vmn_ref[h, :, 0:HA], do2_ref[h], 1, 0)).astype(BF16) for h in range(H)]
    for h in range(H):
        dvma_ref[h, :, 0:MP] += dot(do2_ref[h, 0:64, :], ps[h].astype(BF16), 1, 1)
        dkma_ref[h, :, 0:MP] += dot(q2_ref[h, 0:64, :], dss[h], 1, 1)
        dqa_ref[h] = dot(km_ref[h, 0:64, 0:MP], dss[h], 1, 0)
    pipelined(blocks, work, (sa_ref, ga_ref), (sb_ref, gb_ref))


def bwd_kernel(
    slots, seg_ref, cnt_ref, qa_ref, ka_ref, va_ref, kmn_ref, km_ref, vmn_ref, do_ref, lse_ref, delta_ref,
    dq_ref, dk_ref, dv_ref, dkm_ref, dvm_ref,
    q2_ref, do2_ref, dqa_ref, dka_ref, dva_ref, dkma_ref, dvma_ref, sa_ref, ga_ref, sb_ref, gb_ref, range_ref,
):
    step = pl.program_id(0)

    @pl.when(step == 0)
    def _():
        key_ranges(seg_ref[...], cnt_ref[0], slots, range_ref)
        for ref in (dka_ref, dva_ref, dkma_ref, dvma_ref):
            ref[...] = jnp.zeros_like(ref)

    attend_back(
        range_ref[0, step], range_ref[1, step], qa_ref, ka_ref, va_ref, kmn_ref, km_ref, vmn_ref, do_ref, lse_ref,
        delta_ref, q2_ref, do2_ref, dqa_ref, dka_ref, dva_ref, dkma_ref, dvma_ref, sa_ref, ga_ref, sb_ref, gb_ref,
    )
    for h in range(H):
        dq_ref[64 * h : 64 * h + 64, :] = (dqa_ref[h] * HD ** -0.5).astype(BF16)

    @pl.when(step == pl.num_programs(0) - 1)
    def _():
        for h in range(H):
            s = slice(64 * h, 64 * h + 64)
            dk_ref[s, :] = dka_ref[h].astype(BF16)
            dv_ref[s, :] = dva_ref[h].astype(BF16)
            dkm_ref[s, :] = dkma_ref[h].astype(BF16)
            dvm_ref[s, :] = dvma_ref[h].astype(BF16)


def attend_backward(seg2, counts, qa, ka, va, kmn, km, vmn, mgrad, lse, delta):
    slots = qa.shape[2]
    once = pl.Buffered(1)

    def full(a):
        return pl.BlockSpec(a.shape, lambda i: (0, 0, 0), pipeline_mode=once)

    cols = pl.BlockSpec((512, BQ), lambda i: (0, i))
    stat = pl.BlockSpec((H, BQ), lambda i: (0, i))
    whole = pl.BlockSpec((512, slots), lambda i: (0, 0), pipeline_mode=once)
    mwhole = pl.BlockSpec((512, 128), lambda i: (0, 0))
    block = pltpu.VMEM((H, BK, BQ), F32)
    return pl.pallas_call(
        functools.partial(bwd_kernel, slots),
        grid=(slots // BQ,),
        in_specs=[
            pl.BlockSpec(seg2.shape, lambda i: (0, 0)),
            pl.BlockSpec(memory_space=pltpu.SMEM),
            pl.BlockSpec((H, HA, BQ), lambda i: (0, 0, i)),
            full(ka), full(va), full(kmn), full(km), full(vmn), cols, stat, stat,
        ],
        out_specs=[cols, whole, whole, mwhole, mwhole],
        out_shape=[jax.ShapeDtypeStruct((512, slots), BF16)] * 3 + [jax.ShapeDtypeStruct((512, 128), BF16)] * 2,
        scratch_shapes=[
            pltpu.VMEM((H, HA, BQ), BF16),
            pltpu.VMEM((H, HA, BQ), BF16),
            pltpu.VMEM((H, HD, BQ), F32),
            pltpu.VMEM((H, HD, slots), F32),
            pltpu.VMEM((H, HD, slots), F32),
            pltpu.VMEM((H, HD, 128), F32),
            pltpu.VMEM((H, HD, 128), F32),
            block, block, block, block,
            pltpu.SMEM((2, slots // BQ), jnp.int32),
        ],
        compiler_params=params(),
        name="attend_backward",
    )(seg2, counts, qa, ka, va, kmn, km, vmn, mgrad, lse, delta)


SUM_EARLY = (
    (slice(0, 48), "yxz"),
    (slice(48, 96), "xyz"),
    (slice(96, 112), "xzy"),
    (slice(112, 144), "yzx"),
)
SUM_LATE = ((slice(144, 160), "xyz"), (slice(160, 176), "yxz"), (slice(176, 192), "xyz"), (slice(192, 208), "yxz"))
SUM_PARTS = SUM_EARLY + SUM_LATE
SUM_COPIES = 6 * len(SUM_PARTS)


def weight_grads(step, tok_ref, dq_ref, dk_ref, dv_ref, dkm_ref, dvm_ref, memt_ref, acc_ref, sum_ref):
    @pl.when(step == 0)
    def _():
        acc_ref[0:512, :] = jnp.zeros((512, 512), F32)
        acc_ref[512:1024, :] = dot(dkm_ref[...], memt_ref[...], 1, 1)
        acc_ref[1024:1536, :] = dot(dvm_ref[...], memt_ref[...], 1, 1)
        sum_ref[...] = jnp.zeros_like(sum_ref)
        sum_ref[:, 1:2] = jnp.sum(dvm_ref[...].astype(F32), axis=1, keepdims=True)

    tok = tok_ref[...]
    dq, dk, dv = dq_ref[...], dk_ref[...], dv_ref[...]
    acc_ref[0:512, :] += dot(dq, tok, 1, 0)
    acc_ref[512:1024, :] += dot(dk, tok, 1, 0)
    acc_ref[1024:1536, :] += dot(dv, tok, 1, 0)
    sum_ref[:, 0:1] += jnp.sum(dq.astype(F32), axis=1, keepdims=True)
    sum_ref[:, 1:2] += jnp.sum(dv.astype(F32), axis=1, keepdims=True)


def matrix_grad(j, acc_ref):
    return acc_ref[512 * j : 512 * j + 512, :].T.astype(BF16)


def small_grads(dkm_ref, dvm_ref, vec_ref, bup_ref, wt_ref, sum_ref, late):
    gmem = dot(wt_ref[512:1024, :], dkm_ref[...], 0, 0) + dot(wt_ref[1024:1536, :], dvm_ref[...], 0, 0)
    late(slice(48, 64), slice(0, 128), gmem.astype(BF16))
    lane = lax.broadcasted_iota(jnp.int32, (512, 128), 1)
    vecs = jnp.concatenate([vec_ref[...], jnp.zeros((120, 512), F32)], axis=0).T
    late(slice(48, 64), slice(128, 256), jnp.where(lane < 2, sum_ref[...], vecs).astype(BF16))
    rows = [bup_ref[0:1, 256 * v : 256 * v + 256] for v in range(8)] + [jnp.zeros((8, 256), F32)]
    rows = jnp.concatenate(rows, axis=0).astype(BF16)
    late(slice(48, 64), slice(256, 512), jnp.broadcast_to(rows[None], (PARTS, 16, 256)).reshape(512, 256))


def token_grads(gtok_ref, gfirst_ref, dq_ref, dk_ref, dv_ref, wt_ref):
    gtok_ref[...] = (
        gfirst_ref[...]
        + dot(dq_ref[...], wt_ref[0:512, :], 0, 0)
        + dot(dk_ref[...], wt_ref[512:1024, :], 0, 0)
        + dot(dv_ref[...], wt_ref[1024:1536, :], 0, 0)
    )


def scatter_kernel(
    blocks, qa_ref, ka_ref, va_ref, kmn_ref, km_ref, vmn_ref, do_ref, lse_ref, delta_ref,
    tok_ref, gfirst_ref, vec_ref, bup_ref, wt_ref, memt_ref, early_ref, gtok_ref, out_ref,
    q2_ref, do2_ref, dqa_ref, dka_ref, dva_ref, dkma_ref, dvma_ref, sa_ref, ga_ref, sb_ref, gb_ref,
    dq_ref, dk_ref, dv_ref, dkm_ref, dvm_ref,
    acc_ref, sum_ref, late, parts_sum, other, send, recv, local, *landing,
):
    step = pl.program_id(0)
    place = Place()
    copies = Copies(send, recv)
    slots = dict(zip(slot_shapes(SUM_PARTS), landing))
    crossing = [copies.number() for _ in SUM_PARTS]
    parts = []
    for index, (rows, order) in enumerate(SUM_PARTS):
        mine = {key[1:]: slot for key, slot in slots.items() if key[0] == index}
        parts.append(scatter_part(place, copies, parts_sum, mine, out_ref, rows, order))
    firsts, lasts = parts[: len(SUM_EARLY)], parts[len(SUM_EARLY) :]

    def load(index):
        rows = SUM_EARLY[index][0]
        return pltpu.make_async_copy(
            early_ref.at[:, :, :, place.core, rows], parts_sum.at[:, :, :, rows], local.at[index]
        )

    def cross(source, base, rows, number):
        old = slice(rows.start - base, rows.stop - base)
        copies.start(
            lambda: source.at[:, :, :, place.far, old], lambda: other.at[:, :, :, rows], number, place.partner
        )

    @pl.when(step == 0)
    def _():
        place.greet()
        for index in range(len(SUM_EARLY)):
            load(index).start()
        for ref in (dka_ref, dva_ref, dkma_ref, dvma_ref, sum_ref):
            ref[...] = jnp.zeros_like(ref)
        acc_ref[0:512, :] = jnp.zeros((512, 512), F32)

    @pl.when(step < blocks)
    def _():
        reach = LONGEST // BQ
        begin = jnp.maximum(step - reach, 0)
        end = jnp.minimum(step + reach + 1, blocks)
        attend_back(
            begin * (BQ // 128), (end - begin) * (BQ // BK), qa_ref, ka_ref, va_ref, kmn_ref, km_ref, vmn_ref,
            do_ref, lse_ref, delta_ref, q2_ref, do2_ref, dqa_ref, dka_ref, dva_ref, dkma_ref, dvma_ref,
            sa_ref, ga_ref, sb_ref, gb_ref,
        )
        here = pl.ds(pl.multiple_of(step * BQ, BQ), BQ)
        for h in range(H):
            dq_ref[64 * h : 64 * h + 64, here] = (dqa_ref[h] * HD ** -0.5).astype(BF16)
        dq = dq_ref[:, here]
        acc_ref[0:512, :] += dot(dq, tok_ref[here, :], 1, 0)
        sum_ref[:, 0:1] += jnp.sum(dq.astype(F32), axis=1, keepdims=True)

    @pl.when(step == 0)
    def _():
        place.met()
        for number, (rows, _) in zip(crossing, SUM_EARLY):
            cross(early_ref, 0, rows, number)

    @pl.when(step == 1)
    def _():
        for index, (rows, _) in enumerate(SUM_EARLY):
            load(index).wait()
            join(place, copies, parts_sum, None, other, rows, crossing[index])
            next(firsts[index])

    @pl.when(step == 3)
    def _():
        advance(firsts)

    @pl.when(step == 5)
    def _():
        advance(firsts)

    @pl.when(step == blocks - 1)
    def _():
        advance(firsts)

    def put(rows, lanes, value):
        late[:, :, :, :, rows, lanes] = value.reshape(4, 2, 2, 2, 16, value.shape[1])

    def depart(index):
        cross(late, LATE, SUM_LATE[index][0], crossing[len(SUM_EARLY) + index])

    def onward(index):
        rows = SUM_LATE[index][0]
        old = slice(rows.start - LATE, rows.stop - LATE)
        join(
            place, copies, parts_sum, lambda z: late[z, :, :, place.core, old], other, rows,
            crossing[len(SUM_EARLY) + index],
        )
        next(lasts[index])

    @pl.when(step == blocks)
    def _():
        put(slice(0, 16), slice(0, 512), matrix_grad(0, acc_ref))
        depart(0)
        tok = tok_ref[...]
        for j, whole, part, memory, memory_part in (
            (1, dka_ref, dk_ref, dkma_ref, dkm_ref),
            (2, dva_ref, dv_ref, dvma_ref, dvm_ref),
        ):
            for h in range(H):
                s = slice(64 * h, 64 * h + 64)
                part[s, :] = whole[h].astype(BF16)
                memory_part[s, :] = memory[h].astype(BF16)
            acc_ref[512 * j : 512 * j + 512, :] = dot(part[...], tok, 1, 0) + dot(
                memory_part[...], memt_ref[...], 1, 1
            )
            put(slice(16 * j, 16 * j + 16), slice(0, 512), matrix_grad(j, acc_ref))
            depart(j)
            onward(j - 1)
        sum_ref[:, 1:2] = jnp.sum(dv_ref[...].astype(F32), axis=1, keepdims=True) + jnp.sum(
            dvm_ref[...].astype(F32), axis=1, keepdims=True
        )
        small_grads(dkm_ref, dvm_ref, vec_ref, bup_ref, wt_ref, sum_ref, put)
        depart(3)
        onward(2)

    @pl.when(step > blocks)
    def _():
        rows = gtok_ref.shape[0]
        here = pl.ds(pl.multiple_of((step - blocks - 1) * rows, 128), rows)
        token_grads(gtok_ref, gfirst_ref, dq_ref.at[:, here], dk_ref.at[:, here], dv_ref.at[:, here], wt_ref)

    @pl.when(step == blocks + 1)
    def _():
        onward(3)

    @pl.when(step == blocks + 2)
    def _():
        advance(lasts[0:2])

    @pl.when(step == blocks + 3)
    def _():
        advance(lasts[2:4])

    @pl.when(step == pl.num_programs(0) - 1)
    def _():
        advance(lasts)
        advance(lasts)
        copies.finish()


def backward(seg2, counts, early, tokens, qa, ka, va, kmn, km, vmn, mgrad, lse, delta, gfirst, vec, bup, wt, memt, remote):
    if not remote:
        dq, dk, dv, dkm, dvm = attend_backward(seg2, counts, qa, ka, va, kmn, km, vmn, mgrad, lse, delta)
        return tail(tokens, dq, dk, dv, dkm, dvm, gfirst, vec, bup, wt, memt)
    slots = tokens.shape[0]
    rb = 512
    blocks = slots // BQ
    once = pl.Buffered(1)

    def full(a):
        return pl.BlockSpec(a.shape, lambda i: (0,) * len(a.shape), pipeline_mode=once)

    def at(i):
        return jnp.minimum(i, blocks - 1)

    later = pl.BlockSpec((rb, 512), lambda i: (jnp.maximum(i - blocks - 1, 0), 0))
    stat = pl.BlockSpec((H, BQ), lambda i: (0, at(i)))
    score = pltpu.VMEM((H, BK, BQ), F32)
    return pl.pallas_call(
        functools.partial(scatter_kernel, blocks),
        grid=(blocks + 1 + slots // rb,),
        in_specs=[
            pl.BlockSpec((H, HA, BQ), lambda i: (0, 0, at(i))),
            full(ka), full(va), full(kmn), full(km), full(vmn),
            pl.BlockSpec((512, BQ), lambda i: (0, at(i))), stat, stat,
            full(tokens), later, full(vec), full(bup), full(wt), full(memt),
            pl.BlockSpec(memory_space=pl.ANY),
        ],
        out_specs=[later, fixed(ROWS, 512)],
        out_shape=[jax.ShapeDtypeStruct((slots, 512), F32), jax.ShapeDtypeStruct((ROWS, 512), F32)],
        scratch_shapes=[
            pltpu.VMEM((H, HA, BQ), BF16),
            pltpu.VMEM((H, HA, BQ), BF16),
            pltpu.VMEM((H, HD, BQ), F32),
            pltpu.VMEM((H, HD, slots), F32),
            pltpu.VMEM((H, HD, slots), F32),
            pltpu.VMEM((H, HD, 128), F32),
            pltpu.VMEM((H, HD, 128), F32),
            score, score, score, score,
            pltpu.VMEM((512, slots), BF16),
            pltpu.VMEM((512, slots), BF16),
            pltpu.VMEM((512, slots), BF16),
            pltpu.VMEM((512, 128), BF16),
            pltpu.VMEM((512, 128), BF16),
            pltpu.VMEM((1536, 512), F32),
            pltpu.VMEM((512, 128), F32),
            pltpu.VMEM((4, 2, 2, 2, EARLY, 512), BF16),
            pltpu.VMEM((4, 2, 2, ROWS, 512), BF16),
            pltpu.VMEM((4, 2, 2, ROWS, 512), BF16),
            pltpu.SemaphoreType.DMA((SUM_COPIES,)),
            pltpu.SemaphoreType.DMA((SUM_COPIES,)),
            pltpu.SemaphoreType.DMA((len(SUM_EARLY),)),
        ]
        + [pltpu.VMEM(shape, BF16) for shape in slot_shapes(SUM_PARTS).values()],
        compiler_params=params(collective_id=1, has_side_effects=True),
        name="backward_scatter",
    )(
        qa, ka, va, kmn, km, vmn, mgrad, lse, delta, tokens, gfirst, vec, bup, wt, memt,
        early.reshape(4, 2, 2, 2, LATE, 512),
    )


def plain_kernel(
    half, tok_ref, dq_ref, dk_ref, dv_ref, dkm_ref, dvm_ref, gfirst_ref, vec_ref, bup_ref, wt_ref, memt_ref,
    gtok_ref, late_ref, acc_ref, sum_ref,
):
    step = pl.program_id(0)

    @pl.when(step < half)
    def _():
        weight_grads(step, tok_ref, dq_ref, dk_ref, dv_ref, dkm_ref, dvm_ref, memt_ref, acc_ref, sum_ref)

    @pl.when(step == half - 1)
    def _():
        def put(rows, lanes, value):
            late_ref[:, rows, lanes] = value.reshape(PARTS, 16, value.shape[1])

        for j in range(3):
            put(slice(16 * j, 16 * j + 16), slice(0, 512), matrix_grad(j, acc_ref))
        small_grads(dkm_ref, dvm_ref, vec_ref, bup_ref, wt_ref, sum_ref, put)

    @pl.when(step >= half)
    def _():
        token_grads(gtok_ref, gfirst_ref, dq_ref, dk_ref, dv_ref, wt_ref)


def tail(tokens, dq, dk, dv, dkm, dvm, gfirst, vec, bup, wt, memt):
    slots = tokens.shape[0]
    rb = 512
    half = slots // rb
    cols = pl.BlockSpec((512, rb), lambda i: (0, i % half))
    later = pl.BlockSpec((rb, 512), lambda i: (jnp.maximum(i - half, 0), 0))
    return pl.pallas_call(
        functools.partial(plain_kernel, half),
        grid=(2 * half,),
        in_specs=[
            pl.BlockSpec((rb, 512), lambda i: (jnp.minimum(i, half - 1), 0)),
            cols, cols, cols, fixed(512, 128), fixed(512, 128), later,
            fixed(8, 512), fixed(1, 2048), fixed(1536, 512), fixed(512, 128),
        ],
        out_specs=[later, fixed(PARTS, EARLY, 512)],
        out_shape=[jax.ShapeDtypeStruct((slots, 512), F32), jax.ShapeDtypeStruct((PARTS, EARLY, 512), BF16)],
        scratch_shapes=[pltpu.VMEM((1536, 512), F32), pltpu.VMEM((512, 128), F32)],
        compiler_params=params(),
        name="tail",
    )(tokens, dq, dk, dv, dkm, dvm, gfirst, vec, bup, wt, memt)


def unpack_kernel(sum_ref, part_ref, gtok_ref, wo, up, dn, wq, wk, wv, memory, b_up, *rest):
    vectors, (block, arrive, leave) = rest[:8], rest[8:]
    count = arrive.shape[0]
    rows = block.shape[0] // count
    spans = [slice(rows * k, rows * k + rows) for k in range(count)]
    loads = [pltpu.make_async_copy(part_ref.at[s], block.at[s], arrive.at[k]) for k, s in enumerate(spans)]
    stores = [pltpu.make_async_copy(block.at[s], gtok_ref.at[s], leave.at[k]) for k, s in enumerate(spans)]
    for load in loads:
        load.start()
    me = lax.axis_index("dp")
    wo[...] = sum_ref[0:16]
    for c in range(4):
        up[:, 512 * c : 512 * c + 512] = sum_ref[16 + 16 * c : 32 + 16 * c]
    dn[...] = sum_ref[80:144]
    wq[...] = sum_ref[144:160]
    wk[...] = sum_ref[160:176]
    wv[...] = sum_ref[176:192]
    memory[...] = sum_ref[192:208, 0 : memory.shape[1]]
    turned = sum_ref[192:208, 128:256].T
    for index, vector in enumerate(vectors):
        vector[...] = turned[index : index + 1, :]
    row = lax.broadcasted_iota(jnp.int32, (16, 256), 0)
    lane = lax.broadcasted_iota(jnp.int32, (16, 256), 1)
    own = jnp.sum(jnp.where(row * 4 + lane // 64 == me, sum_ref[192:208, 256:512], 0.0), axis=0, keepdims=True)
    b_up[...] = own[:, 0:64] + own[:, 64:128] + own[:, 128:192] + own[:, 192:256]
    for load, store in zip(loads, stores):
        load.wait()
        store.start()
    for store in stores:
        store.wait()


def unpack(sums, part, mem_rows):
    shapes = [(16, 512), (16, 2048), (64, 512), (16, 512), (16, 512), (16, 512), (16, mem_rows), (1, 64)] + [(1, 16)] * 8
    found = pl.pallas_call(
        unpack_kernel,
        in_specs=[pl.BlockSpec(memory_space=pltpu.VMEM), pl.BlockSpec(memory_space=pl.ANY)],
        out_specs=[pl.BlockSpec(memory_space=pl.ANY)] + [pl.BlockSpec(memory_space=pltpu.VMEM)] * len(shapes),
        out_shape=[jax.ShapeDtypeStruct(s, F32) for s in [part.shape] + shapes],
        scratch_shapes=[
            pltpu.VMEM(part.shape, F32),
            pltpu.SemaphoreType.DMA((4,)),
            pltpu.SemaphoreType.DMA((4,)),
        ],
        compiler_params=params(),
        name="unpack",
    )(sums, part)
    gtok, found = found[0], found[1:]
    out = dict(zip(("w_out", "w_up", "w_down", "w_query", "w_key", "w_value", "memory"), found[:7]))
    out["memory"] = out["memory"].T
    out["b_up"] = found[7].reshape(64)
    for name, value in zip(VECTORS, found[8:]):
        out[name] = value.reshape(16)
    return gtok, out


NAMES = (
    "memory", "w_query", "b_query", "w_key", "w_value", "b_value", "w_out", "b_out", "gain_attn",
    "shift_attn", "w_up", "b_up", "w_down", "b_down", "gain_ffn", "shift_ffn",
)


def pack_whole(p):
    mem_rows = p["memory"].shape[0]
    mats = [p[name].reshape(PARTS, 16, 512) for name in ("w_query", "w_key", "w_value", "w_out")]
    up = p["w_up"].reshape(PARTS, 16, 4, 512).transpose(0, 2, 1, 3).reshape(PARTS, 64, 512)
    memory = jnp.pad(p["memory"].T, ((0, 0), (0, 128 - mem_rows))).reshape(PARTS, 16, 128)
    vectors = jnp.stack([p[name] for name in VECTORS], axis=1)
    vectors = jnp.pad(vectors, ((0, 0), (0, 120))).reshape(PARTS, 16, 128)
    own = jnp.arange(2048)[None] // 64 == jnp.arange(PARTS)[:, None]
    b_up = jnp.where(own, p["b_up"][None], 0).astype(BF16).reshape(PARTS, 8, 256)
    b_up = jnp.pad(b_up, ((0, 0), (0, 8), (0, 0)))
    small = jnp.concatenate([memory, vectors, b_up], axis=2)
    return jnp.concatenate(mats[:3] + [small, up, p["w_down"].reshape(PARTS, 64, 512), mats[3]], axis=1)


def unpack_whole(early, late, mem_rows):
    small = late[:, 48:64]
    vectors = small[:, :, 128:136].reshape(512, 8)
    out = {
        "memory": small[:, :, 0:mem_rows].reshape(512, mem_rows).T,
        "w_query": late[:, 0:16].reshape(512, 512),
        "w_key": late[:, 16:32].reshape(512, 512),
        "w_value": late[:, 32:48].reshape(512, 512),
        "w_out": early[:, 0:16].reshape(512, 512),
        "w_up": early[:, 16:80].reshape(PARTS, 4, 16, 512).transpose(0, 2, 1, 3).reshape(512, 2048),
        "w_down": early[:, 80:144].reshape(2048, 512),
        "b_up": small[0, 0:8, 256:512].reshape(2048),
    }
    for index, name in enumerate(VECTORS):
        out[name] = vectors[:, index]
    return out


def axis_of(name):
    return 1 if name == "memory" else 0


def shards(n, tokens, segment, counts, *rest):
    p = dict(zip(NAMES, rest[:-1]))
    cotangent = rest[-1]
    slots = tokens.shape[0]
    mem_rows = p["memory"].shape[0]
    whole = None
    if n != PARTS:
        whole = pack_whole({k: lax.all_gather(v, "dp", axis=axis_of(k), tiled=True) for k, v in p.items()})
    found = projections(p, whole, tokens, segment, counts, mem_rows)
    late, qa, ka, va, km, kmn, vmn, wt, memt, rows8, rbup, mixt, lse = found
    seg2 = segment.reshape(slots // 128, 128)
    output, gfirst, mgrad, delta, early, vec, bup = middle(late, rows8, rbup, counts, mixt, tokens, cotangent)
    gtok, sums = backward(
        seg2, counts, early, tokens, qa, ka, va, kmn, km, vmn, mgrad, lse, delta, gfirst, vec, bup, wt, memt, n == PARTS
    )
    if n == PARTS:
        gtok, grads = unpack(sums, gtok, mem_rows)
    else:
        full = unpack_whole(early.astype(F32), sums.astype(F32), mem_rows)
        grads = {
            k: lax.psum_scatter(v, "dp", scatter_dimension=axis_of(k), tiled=True) for k, v in full.items()
        }
    return (output, gtok) + tuple(grads[name] for name in NAMES)


def solution(mesh):
    n = mesh.shape["dp"]
    row, mat, mem = P("dp"), P("dp", None), P(None, "dp")
    spec = {name: mat if name.startswith("w_") else row for name in NAMES}
    spec["memory"] = mem
    weights = tuple(spec[name] for name in NAMES)
    return jax.shard_map(
        functools.partial(shards, n),
        mesh=mesh,
        in_specs=(mat, row, row) + weights + (mat,),
        out_specs=(mat, mat) + weights,
        check_vma=False,
    )
```

```python
import functools
import jax
import jax.numpy as jnp
from jax import lax
from jax.experimental import pallas as pl
from jax.experimental.pallas import tpu as pltpu
from jax.sharding import PartitionSpec as P

H = 8
HD = 64
HA = 80
EPS = 1e-05
BIG = 1e30
PARTS = 32
ROWS = 208
BQ = 256
BK = 256
MP = 32
LONGEST = 1024
F32 = jnp.float32
BF16 = jnp.bfloat16
VMEM_LIMIT = 60 << 20

V_BQ, V_BV, V_BO, V_GA, V_SA, V_BD, V_GF, V_SF = range(8)


def dot(left, right, lc, rc):
    return lax.dot_general(left, right, (((lc,), (rc,)), ((), ())), preferred_element_type=F32)


def params(**kw):
    return pltpu.CompilerParams(vmem_limit_bytes=VMEM_LIMIT, **kw)


MESH = pl.DeviceIdType.MESH
AXES = {"z": (8, 4), "y": (4, 2), "x": (2, 2)}
LAYOUT = ("z", "y", "x")


class Place:
    def __init__(self):
        me = lax.axis_index("dp")
        self.me = me
        self.core = me % 2
        self.far = 1 - self.core
        self.partner = me + 1 - 2 * self.core
        self.at = {a: (me // stride) % length for a, (stride, length) in AXES.items()}
        self.mine = tuple(self.at[a] for a in LAYOUT)
        self.others = {}
        for axis, (stride, length) in AXES.items():
            for distance in range(1, length):
                j = (self.at[axis] + distance) % length
                self.others[axis, distance] = j, me + (j - self.at[axis]) * stride
        self.peers = [self.partner] + [device for _, device in self.others.values()]

    def other(self, axis, distance):
        return self.others[axis, distance]

    def greet(self):
        for peer in self.peers:
            pl.semaphore_signal(
                pltpu.get_barrier_semaphore(), inc=1, device_id=(peer,), device_id_type=MESH
            )

    def met(self):
        pl.semaphore_wait(pltpu.get_barrier_semaphore(), len(self.peers))


class Copies:
    def __init__(self, send, recv):
        self.send, self.recv, self.count, self.open = send, recv, 0, []

    def number(self):
        self.count += 1
        return self.count - 1

    def make(self, src, dst, number, device):
        return pltpu.make_async_remote_copy(
            src_ref=src, dst_ref=dst, send_sem=self.send.at[number], recv_sem=self.recv.at[number],
            device_id=(device,), device_id_type=MESH,
        )

    def start(self, src, dst, number, device):
        self.make(src(), dst(), number, device).start()
        self.open.append((src, dst, number, device))

    def landed(self, block, number, device):
        self.make(block, block, number, device).wait_recv()

    def finish(self):
        for src, dst, number, device in self.open:
            self.make(src(), dst(), number, device).wait_send()
        self.open = []


def gather_part(place, copies, own, base, whole, rows, order, arrivals):
    done = ()

    def mine():
        return own.at[slice(base + rows.start, base + rows.stop)]

    def block(axis, j, core):
        index = tuple(j if a == axis else (slice(None) if a in done else place.at[a]) for a in LAYOUT)
        return lambda: whole.at[index + (core, rows)]

    for axis in order:
        length = AXES[axis][1]
        numbers = [copies.number() for _ in range(2 * length - 2)]
        here = block(axis, place.at[axis], place.core)
        for d in range(1, length):
            copies.start(here if done else mine, here, numbers[d - 1], place.other(axis, d)[1])
        if not done:
            number = copies.number()
            copies.start(mine, here, number, place.partner)
            arrivals.append((block(axis, place.at[axis], place.far), number))
        yield
        for d in range(1, length):
            j, device = place.other(axis, length - d)
            there = block(axis, j, place.core)
            copies.landed(there(), numbers[d - 1], device)
            number = numbers[length - 2 + d]
            copies.start(there, there, number, place.partner)
            arrivals.append((block(axis, j, place.far), number))
        done += (axis,)
    yield


def advance(parts):
    for part in parts:
        next(part)


def scatter_part(place, copies, acc, slots, out, rows, order):
    done = ()

    def block(axis, j):
        index = tuple(j if a == axis else (place.at[a] if a in done else slice(None)) for a in LAYOUT)
        return index + (rows,)

    def taken(index):
        return lambda: acc.at[index]

    def landing(axis, d):
        return lambda: slots[axis, d]

    for axis in order:
        length = AXES[axis][1]
        numbers = [copies.number() for _ in range(length - 1)]
        for d in range(1, length):
            j, device = place.other(axis, d)
            copies.start(taken(block(axis, j)), landing(axis, d), numbers[d - 1], device)
        yield
        for d in range(1, length):
            copies.landed(slots[axis, d], numbers[d - 1], place.partner)
        mine = block(axis, place.at[axis])
        total = acc[mine].astype(F32)
        for d in range(1, length):
            total = total + slots[axis, d][...].astype(F32)
        if axis == order[-1]:
            out[rows, :] = total
        else:
            acc[mine] = total.astype(BF16)
        done += (axis,)
    yield


def slot_shapes(parts):
    shapes = {}
    for number, (rows, order) in enumerate(parts):
        left = ["z", "y", "x"]
        for axis in order:
            left.remove(axis)
            shape = tuple(AXES[a][1] for a in LAYOUT if a in left) + (rows.stop - rows.start, 512)
            for d in range(1, AXES[axis][1]):
                shapes[number, axis, d] = shape
    return shapes


def join(place, copies, acc, source, other, rows, number):
    copies.landed(other.at[:, :, :, rows], number, place.partner)

    @pl.loop(0, 4)
    def _(z):
        mine = source(z) if source else acc[z, :, :, rows]
        acc[z, :, :, rows] = (mine.astype(F32) + other[z, :, :, rows].astype(F32)).astype(BF16)


VECTORS = ("b_query", "b_value", "b_out", "gain_attn", "shift_attn", "b_down", "gain_ffn", "shift_ffn")
EARLY = 64
LATE = 144
EARLY_PARTS = ((slice(0, 16), "zxy"), (slice(16, 32), "zyx"), (slice(32, 48), "zxy"), (slice(48, 64), "zyx"))
LATE_PARTS = (
    (slice(0, 48), "zxy"),
    (slice(48, 96), "zyx"),
    (slice(96, 128), "yzx"),
    (slice(128, 144), "xzy"),
)
GATHER_COPIES = 11 * (len(EARLY_PARTS) + len(LATE_PARTS))


def head_block(rows, features):
    block = jnp.concatenate([rows, features], axis=0)
    return block, jnp.concatenate([block, jnp.zeros((128 - HA, rows.shape[1]), BF16)], axis=0).T


def pack(own, place, wq, wk, wv, wo, up, dn, memory, b_up, vectors):
    own[0:16] = wq[...]
    own[16:32] = wk[...]
    own[32:48] = wv[...]
    own[48:64] = jnp.zeros((16, 512), BF16)
    own[48:64, 0 : memory.shape[1]] = memory[...]
    values = jnp.concatenate([vector[...].astype(F32) for vector in vectors], axis=0)
    own[48:64, 128:136] = values.T.astype(BF16)
    value = jnp.concatenate([b_up[...].astype(F32)] * 4, axis=1)
    row = lax.broadcasted_iota(jnp.int32, (16, 256), 0)
    lane = lax.broadcasted_iota(jnp.int32, (16, 256), 1)
    own[48:64, 256:512] = jnp.where(row * 4 + lane // 64 == place.me, value, 0.0).astype(BF16)
    for c in range(4):
        own[64 + 16 * c : 80 + 16 * c] = up[:, 512 * c : 512 * c + 512]
    own[128:192] = dn[...]
    own[192:208] = wo[...]


def prepare(mem_rows, early, wt_ref, memt_ref, rows_ref, rbup_ref, bias_ref, km_ref, vm_ref, kmn_ref, vmn_ref):
    for j in range(3):
        wt_ref[512 * j : 512 * j + 512, :] = early[..., 16 * j : 16 * j + 16, :].reshape(512, 512).T
    small = early[..., 48:64, 0:256].reshape(512, 256)
    memt = small[:, 0:128]
    memt_ref[...] = memt
    vectors = small[:, 128:256].astype(F32)
    bias_ref[...] = vectors
    rows_ref[...] = vectors.T[0:8, :]
    bup = jnp.sum(early[..., 48:64, 256:512].reshape(PARTS, 16, 256).astype(F32), axis=0)
    for v in range(8):
        rbup_ref[0:1, 256 * v : 256 * v + 256] = bup[v : v + 1, :]
    bv = vectors[:, V_BV : V_BV + 1]
    km = dot(wt_ref[512:1024, :], memt, 1, 0).astype(BF16)
    vm = (dot(wt_ref[1024:1536, :], memt, 1, 0) + bv).astype(BF16)
    frow = lax.broadcasted_iota(jnp.int32, (16, 128), 0)
    lane = lax.broadcasted_iota(jnp.int32, (16, 128), 1)
    kf = jnp.where(frow < 3, jnp.where(lane < mem_rows, 0.0, 1.0), jnp.where(frow < 6, 1.0, 0.0)).astype(BF16)
    vf = jnp.where(frow < 3, 1.0, 0.0).astype(BF16)
    for h in range(H):
        km_ref[h], turned = head_block(km[64 * h : 64 * h + 64, :], kf)
        kmn_ref[h] = turned[0:MP]
        vm_ref[h], turned = head_block(vm[64 * h : 64 * h + 64, :], vf)
        vmn_ref[h] = turned[0:MP]


def project(step, tok_ref, seg_ref, cnt_ref, wt_ref, bias_ref, qa_ref, ka_ref, va_ref):
    rows = tok_ref.shape[0]
    tok = tok_ref[...]
    bq = bias_ref[:, V_BQ : V_BQ + 1]
    bv = bias_ref[:, V_BV : V_BV + 1]
    q = (dot(wt_ref[0:512, :], tok, 1, 1) + bq).astype(BF16) * jnp.asarray(HD ** -0.5, BF16)
    k = dot(wt_ref[512:1024, :], tok, 1, 1).astype(BF16)
    v = (dot(wt_ref[1024:1536, :], tok, 1, 1) + bv).astype(BF16)
    frow = lax.broadcasted_iota(jnp.int32, (16, rows), 0)
    seg = jnp.broadcast_to(seg_ref[...], (16, rows))
    pos = lax.broadcasted_iota(jnp.int32, (16, rows), 1) + step * rows
    valid = pos < cnt_ref[0]
    qf = jnp.where((frow < 3) & (frow != seg), -BIG, 0.0).astype(BF16)
    kf = jnp.where(frow < 3, jnp.where(valid & (frow != seg), 0.0, 1.0), jnp.where(frow < 6, 1.0, 0.0)).astype(BF16)
    vf = jnp.where(frow < 3, 1.0, 0.0).astype(BF16)
    for h in range(H):
        s = slice(64 * h, 64 * h + 64)
        qa_ref[h, 0:64, :] = q[s]
        qa_ref[h, 64:80, :] = qf
        ka_ref[h, 0:64, :] = k[s]
        ka_ref[h, 64:80, :] = kf
        va_ref[h, 0:64, :] = v[s]
        va_ref[h, 64:80, :] = vf


def gather_kernel(
    mem_rows, half, wq, wk, wv, wo, up, dn, memory, b_up, v0, v1, v2, v3, v4, v5, v6, v7, tok_ref, seg_ref, cnt_ref,
    late_ref, qa_ref, ka_ref, va_ref, km_ref, kmn_ref, vmn_ref,
    wt_ref, memt_ref, rows_ref, rbup_ref, mix_ref, lse_ref,
    own, early, bias_ref, vm_ref, qa_all, ka_all, va_all, acc_ref, m_ref, sa_ref, sb_ref, send, recv, local,
):
    step = pl.program_id(0)
    slots = ka_all.shape[2]
    place = Place()
    copies = Copies(send, recv)
    arrivals, late_arrivals = [], []
    firsts = [gather_part(place, copies, own, 0, early, *part, arrivals) for part in EARLY_PARTS]
    lasts = [gather_part(place, copies, own, EARLY, late_ref, *part, late_arrivals) for part in LATE_PARTS]

    @pl.when(step == 0)
    def _():
        place.greet()
        pack(own, place, wq, wk, wv, wo, up, dn, memory, b_up, (v0, v1, v2, v3, v4, v5, v6, v7))
        early[place.mine + (place.core,)] = own[0:EARLY]
        place.met()
        advance(firsts)
        keep = pltpu.make_async_copy(own.at[EARLY:ROWS], late_ref.at[place.mine + (place.core,)], local)
        keep.start()
        advance(firsts)
        advance(firsts)
        keep.wait()
        advance(lasts)
        advance(firsts)
        for block, number in arrivals:
            copies.landed(block(), number, place.partner)
        prepare(
            mem_rows, early, wt_ref, memt_ref, rows_ref, rbup_ref, bias_ref, km_ref, vm_ref, kmn_ref, vmn_ref,
        )

    @pl.when(step < half)
    def _():
        project(step, tok_ref, seg_ref, cnt_ref, wt_ref, bias_ref, qa_ref, ka_ref, va_ref)
        here = pl.ds(pl.multiple_of(step * tok_ref.shape[0], 128), tok_ref.shape[0])
        qa_all[:, :, here] = qa_ref[...]
        ka_all[:, :, here] = ka_ref[...]
        va_all[:, :, here] = va_ref[...]

    @pl.when(step == half - 1)
    def _():
        advance(lasts)

    @pl.when(step >= half)
    def _():
        block = step - half
        reach = LONGEST // BQ
        begin = jnp.maximum(block - reach, 0)
        end = jnp.minimum(block + reach + 1, slots // BQ)
        queries = qa_all.at[:, :, pl.ds(pl.multiple_of(block * BQ, BQ), BQ)]
        attend(
            True, begin * (BQ // 128), (end - begin) * (BQ // BK), queries, ka_all, va_all, kmn_ref, vm_ref, mix_ref, lse_ref,
            acc_ref, m_ref, sa_ref, sb_ref,
        )

    @pl.when(step == half + 2)
    def _():
        advance(lasts)

    @pl.when(step == pl.num_programs(0) - 1)
    def _():
        advance(lasts)
        for block, number in late_arrivals:
            copies.landed(block(), number, place.partner)
        copies.finish()


def project_kernel(
    mem_rows, g_ref, tok_ref, seg_ref, cnt_ref, qa_ref, ka_ref, va_ref, km_ref, vm_ref, kmn_ref, vmn_ref,
    wt_ref, memt_ref, rows_ref, rbup_ref, bias_ref,
):
    step = pl.program_id(0)

    @pl.when(step == 0)
    def _():
        prepare(
            mem_rows, g_ref, wt_ref, memt_ref, rows_ref, rbup_ref, bias_ref, km_ref, vm_ref, kmn_ref, vmn_ref
        )

    project(step, tok_ref, seg_ref, cnt_ref, wt_ref, bias_ref, qa_ref, ka_ref, va_ref)


def fixed(*shape):
    return pl.BlockSpec(shape, lambda i: (0,) * len(shape))


def projections(p, whole, tokens, segment, counts, mem_rows):
    slots = tokens.shape[0]
    rb = 512
    half = slots // rb
    wide = (H, HA, slots)
    mwide, mtall = (H, HA, 128), (H, MP, 128)

    def at(i):
        return jnp.minimum(i, half - 1)

    blk = pl.BlockSpec((H, HA, rb), lambda i: (0, 0, at(i)))
    common = [
        pl.BlockSpec((rb, 512), lambda i: (at(i), 0)),
        pl.BlockSpec((1, rb), lambda i: (0, at(i))),
        pl.BlockSpec(memory_space=pltpu.SMEM),
    ]
    args = (tokens, segment.reshape(1, slots), counts)

    def outs(shapes):
        found = [jax.ShapeDtypeStruct(s, BF16) for s in shapes]
        return found + [jax.ShapeDtypeStruct((8, 512), F32), jax.ShapeDtypeStruct((1, 2048), F32)]

    if whole is not None:
        shapes = outs([wide, wide, wide, mwide, mwide, mtall, mtall, (1536, 512), (512, 128)])
        found = pl.pallas_call(
            functools.partial(project_kernel, mem_rows),
            grid=(half,),
            in_specs=[fixed(PARTS, EARLY, 512)] + common,
            out_specs=[blk, blk, blk] + [fixed(*o.shape) for o in shapes[3:]],
            out_shape=shapes,
            scratch_shapes=[pltpu.VMEM((512, 128), F32)],
            compiler_params=params(),
            name="projections",
        )(whole[:, 0:EARLY], *args)
        qa, ka, va, km, vm, kmn, vmn, wt, memt, rows8, rbup = found
        mixt, lse = attend_forward(segment.reshape(slots // 128, 128), counts, qa, ka, va, kmn, vm)
        return whole[:, EARLY:], qa, ka, va, km, kmn, vmn, wt, memt, rows8, rbup, mixt, lse
    weights = [p[name] for name in ("w_query", "w_key", "w_value", "w_out", "w_up", "w_down")]
    weights += [p["memory"].T, p["b_up"].reshape(1, 64)] + [p[name].reshape(1, 16) for name in VECTORS]
    shapes = outs([wide, wide, wide, mwide, mtall, mtall, (1536, 512), (512, 128)])
    found = pl.pallas_call(
        functools.partial(gather_kernel, mem_rows, half),
        grid=(half + slots // BQ,),
        in_specs=[fixed(*w.shape) for w in weights] + common,
        out_specs=[pl.BlockSpec(memory_space=pl.ANY), blk, blk, blk]
        + [fixed(*o.shape) for o in shapes[3:]]
        + [
            pl.BlockSpec((512, BQ), lambda i: (0, jnp.maximum(i - half, 0))),
            pl.BlockSpec((H, BQ), lambda i: (0, jnp.maximum(i - half, 0))),
        ],
        out_shape=[jax.ShapeDtypeStruct((4, 2, 2, 2, LATE, 512), BF16)]
        + shapes
        + [jax.ShapeDtypeStruct((512, slots), BF16), jax.ShapeDtypeStruct((H, slots), F32)],
        scratch_shapes=[
            pltpu.VMEM((ROWS, 512), BF16),
            pltpu.VMEM((4, 2, 2, 2, EARLY, 512), BF16),
            pltpu.VMEM((512, 128), F32),
            pltpu.VMEM(mwide, BF16),
            pltpu.VMEM(wide, BF16),
            pltpu.VMEM(wide, BF16),
            pltpu.VMEM(wide, BF16),
            pltpu.VMEM((H, HA, BQ), F32),
            pltpu.VMEM((H, BQ), F32),
            pltpu.VMEM((H, BK, BQ), F32),
            pltpu.VMEM((H, BK, BQ), F32),
            pltpu.SemaphoreType.DMA((GATHER_COPIES,)),
            pltpu.SemaphoreType.DMA((GATHER_COPIES,)),
            pltpu.SemaphoreType.DMA,
        ],
        compiler_params=params(collective_id=0, has_side_effects=True),
        name="gather_attend",
    )(*weights, *args)
    return (found[0].reshape(PARTS, LATE, 512),) + tuple(found[1:])


def key_ranges(seg, count, slots, out):
    r, c = seg.shape
    pos = lax.broadcasted_iota(jnp.int32, (r, c), 0) * c + lax.broadcasted_iota(jnp.int32, (r, c), 1)
    valid = pos < count
    ends = [jnp.sum(jnp.where(valid & (seg <= s), 1.0, 0.0)).astype(jnp.int32) for s in range(3)]
    for block in range(slots // BQ):
        first = block * BQ
        last = jnp.minimum(first + BQ, count)
        low, high, start = jnp.int32(slots), jnp.int32(0), jnp.int32(0)
        for end in ends:
            hit = (end > first) & (start < last) & (end > start)
            low = jnp.where(hit, jnp.minimum(low, start), low)
            high = jnp.where(hit, jnp.maximum(high, end), high)
            start = end
        begin = low // 128
        blocks = jnp.where(high > low, (high - begin * 128 + BK - 1) // BK, 0)
        out[0, block] = jnp.minimum(begin, slots // 128 - blocks * (BK // 128))
        out[1, block] = blocks


def key_slots(begin, block):
    return pl.ds(pl.multiple_of((begin + block * (BK // 128)) * 128, 128), BK)


def pipelined(blocks, work, first, second, started):
    if not started:

        @pl.when(blocks > 0)
        def _():
            work((0, first), None)

    pairs = jnp.maximum(blocks - 1, 0) // 2

    @pl.loop(0, pairs)
    def _(i):
        work((2 * i + 1, second), (2 * i, first))
        work((2 * i + 2, first), (2 * i + 1, second))

    j = 2 * pairs

    @pl.when(blocks - j == 2)
    def _():
        work((j + 1, second), (j, first))
        work(None, (j + 1, second))

    @pl.when(blocks - j == 1)
    def _():
        work(None, (j, first))


def attend(
    sure, begin, blocks, qa_ref, ka_ref, va_ref, kmn_ref, vm_ref, mix_ref, lse_ref, acc_ref, m_ref, sa_ref, sb_ref
):
    def weights(h, s):
        old = m_ref[h : h + 1, :]
        top = jnp.maximum(old, jnp.max(s, axis=0, keepdims=True))
        return jnp.exp(s - top).astype(BF16), jnp.exp(old - top), top

    def work(new, old):
        kept = {}
        for h in range(H + 1):
            if h < H and new:
                new[1][h] = dot(ka_ref[h, :, key_slots(begin, new[0])], qa_ref[h], 0, 0)
            if h < H and old:
                kept[h] = weights(h, old[1][h])
            if h > 0 and old:
                p, fade, top = kept.pop(h - 1)
                acc_ref[h - 1] = acc_ref[h - 1] * fade + dot(va_ref[h - 1, :, key_slots(begin, old[0])], p, 1, 0)
                m_ref[h - 1 : h, :] = top

    scores = [dot(kmn_ref[h, :, 0:HA], qa_ref[h], 1, 0) for h in range(H)]
    if sure:
        work((0, sa_ref), None)
    for h in range(H):
        top = jnp.max(scores[h], axis=0, keepdims=True)
        p = jnp.exp(scores[h] - top).astype(BF16)
        acc_ref[h] = dot(vm_ref[h, :, 0:MP], p, 1, 0)
        m_ref[h : h + 1, :] = top
    pipelined(blocks, work, sa_ref, sb_ref, sure)
    for h in range(H):
        total = acc_ref[h, 64:65, :]
        mix_ref[64 * h : 64 * h + 64, :] = (acc_ref[h, 0:64, :] * (1.0 / total)).astype(BF16)
        lse_ref[h : h + 1, :] = m_ref[h : h + 1, :] + jnp.log(total)


def fwd_kernel(
    slots, seg_ref, cnt_ref, qa_ref, ka_ref, va_ref, kmn_ref, vm_ref,
    mix_ref, lse_ref, acc_ref, m_ref, sa_ref, sb_ref, range_ref,
):
    step = pl.program_id(0)

    @pl.when(step == 0)
    def _():
        key_ranges(seg_ref[...], cnt_ref[0], slots, range_ref)

    attend(
        False, range_ref[0, step], range_ref[1, step], qa_ref, ka_ref, va_ref, kmn_ref, vm_ref, mix_ref, lse_ref,
        acc_ref, m_ref, sa_ref, sb_ref,
    )


def attend_forward(seg2, counts, qa, ka, va, kmn, vm):
    slots = qa.shape[2]
    once = pl.Buffered(1)

    def whole(a):
        return pl.BlockSpec(a.shape, lambda i: (0, 0, 0), pipeline_mode=once)

    return pl.pallas_call(
        functools.partial(fwd_kernel, slots),
        grid=(slots // BQ,),
        in_specs=[
            pl.BlockSpec(seg2.shape, lambda i: (0, 0)),
            pl.BlockSpec(memory_space=pltpu.SMEM),
            pl.BlockSpec((H, HA, BQ), lambda i: (0, 0, i)),
            whole(ka), whole(va), whole(kmn), whole(vm),
        ],
        out_specs=[pl.BlockSpec((512, BQ), lambda i: (0, i)), pl.BlockSpec((H, BQ), lambda i: (0, i))],
        out_shape=[jax.ShapeDtypeStruct((512, slots), BF16), jax.ShapeDtypeStruct((H, slots), F32)],
        scratch_shapes=[
            pltpu.VMEM((H, HA, BQ), F32),
            pltpu.VMEM((H, BQ), F32),
            pltpu.VMEM((H, BK, BQ), F32),
            pltpu.VMEM((H, BK, BQ), F32),
            pltpu.SMEM((2, slots // BQ), jnp.int32),
        ],
        compiler_params=params(),
        name="attend_forward",
    )(seg2, counts, qa, ka, va, kmn, vm)


def norm_parts(value):
    mean = jnp.mean(value, axis=-1, keepdims=True)
    centred = value - mean
    rstd = lax.rsqrt(jnp.mean(centred * centred, axis=-1, keepdims=True) + EPS)
    return centred * rstd, rstd


def norm_grad(grad_hat, hat, rstd):
    return rstd * (
        grad_hat
        - jnp.mean(grad_hat, axis=-1, keepdims=True)
        - hat * jnp.mean(grad_hat * hat, axis=-1, keepdims=True)
    )


def colsum(value):
    return jnp.sum(value, axis=0, keepdims=True)


SUB = 512
FC = 512


def mid_kernel(
    rb, cnt_ref, row_ref, rbup_ref, late_ref, mix_ref, tok_ref, cot_ref,
    out_ref, gfirst_ref, mgrad_ref, delta_ref, gw_ref, vec_ref, bup_ref,
    aup_ref, adn_ref, ao_ref, *scratch,
):
    step = pl.program_id(0)
    subs = rb // SUB

    @pl.when(step == 0)
    def _():
        aup_ref[...] = jnp.zeros_like(aup_ref)
        adn_ref[...] = jnp.zeros_like(adn_ref)
        ao_ref[...] = jnp.zeros_like(ao_ref)
        vec_ref[...] = jnp.zeros_like(vec_ref)
        bup_ref[...] = jnp.zeros_like(bup_ref)

    wo = late_ref[:, 128:144, :].reshape(512, 512)

    def w_up(c):
        return late_ref[:, 16 * c : 16 * c + 16, :].reshape(512, 512)

    def w_down(c):
        return late_ref[8 * c : 8 * c + 8, 64:128, :].reshape(512, 512)

    def row(v):
        return row_ref[v : v + 1, :]

    class Block:
        def __init__(self, index):
            self.s = slice(SUB * index, SUB * index + SUB)
            self.first_row = step * rb + SUB * index
            self.active, self.slope, self.hgrad = scratch[3 * (index % 2) : 3 * (index % 2) + 3]
            self.up_part, self.dact_part = {}, {}

        def head(self):
            self.mixt = mix_ref[:, self.s]
            attention = dot(self.mixt, wo, 0, 0) + row(V_BO)
            self.hat1, self.rstd1 = norm_parts(tok_ref[self.s, :].astype(F32) + attention)
            self.first = self.hat1 * row(V_GA) + row(V_SA)
            self.low = self.first.astype(BF16)
            self.branch = self.first + row(V_BD)

        def up(self, c):
            f = slice(FC * c, FC * c + FC)
            self.up_part[c] = dot(self.low, w_up(c), 1, 0) + rbup_ref[:, f]

        def gelu(self, c):
            f = slice(FC * c, FC * c + FC)
            hidden = self.up_part.pop(c)
            cdf = 0.5 + 0.5 * lax.erf(hidden * (2.0 ** -0.5))
            self.active[:, f] = (hidden * cdf).astype(BF16)
            self.slope[:, f] = cdf + hidden * jnp.exp(hidden * hidden * -0.5) * 0.3989422804014327

        def down(self, c):
            f = slice(FC * c, FC * c + FC)
            self.branch = self.branch + dot(self.active[:, f], w_down(c), 1, 0)

        def turn(self):
            hat2, rstd2 = norm_parts(self.branch)
            valid = lax.broadcasted_iota(jnp.int32, (SUB, 1), 0) + self.first_row < cnt_ref[0]
            out_ref[self.s, :] = jnp.where(valid, hat2 * row(V_GF) + row(V_SF), 0.0).astype(BF16)
            seed = jnp.where(valid, cot_ref[self.s, :].astype(F32), 0.0)
            vec_ref[V_GF : V_GF + 1, :] += colsum(seed * hat2)
            vec_ref[V_SF : V_SF + 1, :] += colsum(seed)
            self.total = norm_grad(seed * row(V_GF), hat2, rstd2)
            self.bgrad = self.total.astype(BF16)
            vec_ref[V_BD : V_BD + 1, :] += colsum(self.bgrad.astype(F32))

        def dact(self, c):
            f = slice(FC * c, FC * c + FC)
            self.dact_part[c] = dot(self.bgrad, w_down(c), 1, 1)

        def grad_down(self, c):
            f = slice(FC * c, FC * c + FC)
            adn_ref[f, :] += dot(self.active[:, f], self.bgrad, 0, 0)

        def hidden_grad(self, c):
            f = slice(FC * c, FC * c + FC)
            grad = (self.dact_part.pop(c) * self.slope[:, f]).astype(BF16)
            self.hgrad[:, f] = grad
            bup_ref[:, f] += colsum(grad.astype(F32))

        def grad_up(self, c):
            f = slice(FC * c, FC * c + FC)
            aup_ref[:, f] += dot(self.low, self.hgrad[:, f], 0, 0)

        def first_grad(self, c):
            f = slice(FC * c, FC * c + FC)
            self.total = self.total + dot(self.hgrad[:, f], w_up(c), 1, 1)

        def finish(self):
            vec_ref[V_GA : V_GA + 1, :] += colsum(self.total * self.hat1)
            vec_ref[V_SA : V_SA + 1, :] += colsum(self.total)
            grad_first = norm_grad(self.total * row(V_GA), self.hat1, self.rstd1)
            gfirst_ref[self.s, :] = grad_first
            agrad = grad_first.astype(BF16)
            vec_ref[V_BO : V_BO + 1, :] += colsum(agrad.astype(F32))
            mgrad = dot(wo, agrad, 1, 1).astype(BF16)
            ao_ref[...] += dot(self.mixt, agrad, 1, 0)
            mgrad_ref[:, self.s] = mgrad
            prod = mgrad.astype(F32) * self.mixt.astype(F32)
            for h in range(H):
                delta_ref[h : h + 1, self.s] = jnp.sum(prod[64 * h : 64 * h + 64, :], axis=0, keepdims=True)

    chunks = 2048 // FC

    def both(ahead, behind):
        if ahead:
            ahead.head()
            ahead.up(0)
        for c in range(chunks):
            if behind:
                behind.dact(c)
            if ahead and c + 1 < chunks:
                ahead.up(c + 1)
            if behind:
                behind.grad_down(c)
            if ahead:
                ahead.gelu(c)
            if behind:
                behind.hidden_grad(c)
                behind.grad_up(c)
                behind.first_grad(c)
            if ahead:
                ahead.down(c)
        if behind:
            behind.finish()
        if ahead:
            ahead.turn()

    blocks = [Block(index) for index in range(subs)]
    for ahead, behind in zip(blocks + [None], [None] + blocks):
        both(ahead, behind)

    @pl.when(step == pl.num_programs(0) - 1)
    def _():
        gw_ref[:, 0:16, :] = ao_ref[...].astype(gw_ref.dtype).reshape(PARTS, 16, 512)
        for c in range(4):
            gw_ref[:, 16 + 16 * c : 32 + 16 * c, :] = (
                aup_ref[:, 512 * c : 512 * c + 512].astype(gw_ref.dtype).reshape(PARTS, 16, 512)
            )
        gw_ref[:, 80:144, :] = adn_ref[...].astype(gw_ref.dtype).reshape(PARTS, 64, 512)


def middle(late, rows8, rbup, counts, mixt, tokens, cotangent, rb=512):
    slots = tokens.shape[0]
    rows = pl.BlockSpec((rb, 512), lambda i: (i, 0))
    cols = pl.BlockSpec((512, rb), lambda i: (0, i))
    once = pl.Buffered(1)
    return pl.pallas_call(
        functools.partial(mid_kernel, rb),
        grid=(slots // rb,),
        in_specs=[
            pl.BlockSpec(memory_space=pltpu.SMEM),
            pl.BlockSpec((8, 512), lambda i: (0, 0)),
            pl.BlockSpec((1, 2048), lambda i: (0, 0)),
            pl.BlockSpec((PARTS, LATE, 512), lambda i: (0, 0, 0), pipeline_mode=once),
            cols, rows, rows,
        ],
        out_specs=[
            rows, rows, cols,
            pl.BlockSpec((H, rb), lambda i: (0, i)),
            pl.BlockSpec((PARTS, 144, 512), lambda i: (0, 0, 0), pipeline_mode=once),
            pl.BlockSpec((8, 512), lambda i: (0, 0)),
            pl.BlockSpec((1, 2048), lambda i: (0, 0)),
        ],
        out_shape=[
            jax.ShapeDtypeStruct((slots, 512), BF16),
            jax.ShapeDtypeStruct((slots, 512), F32),
            jax.ShapeDtypeStruct((512, slots), BF16),
            jax.ShapeDtypeStruct((H, slots), F32),
            jax.ShapeDtypeStruct((PARTS, 144, 512), BF16),
            jax.ShapeDtypeStruct((8, 512), F32),
            jax.ShapeDtypeStruct((1, 2048), F32),
        ],
        scratch_shapes=[
            pltpu.VMEM((512, 2048), F32),
            pltpu.VMEM((2048, 512), F32),
            pltpu.VMEM((512, 512), F32),
        ]
        + [pltpu.VMEM((SUB, 2048), BF16), pltpu.VMEM((SUB, 2048), F32), pltpu.VMEM((SUB, 2048), BF16)] * 2,
        compiler_params=params(),
        name="middle",
    )(counts, rows8, rbup, late, mixt, tokens, cotangent)


def split3(value):
    high = value.astype(BF16)
    rest = value - high.astype(F32)
    mid = rest.astype(BF16)
    return high, mid, (rest - mid.astype(F32)).astype(BF16)


def attend_back(
    sure, begin, blocks, qa_ref, ka_ref, va_ref, kmn_ref, km_ref, vmn_ref, do_ref, lse_ref, delta_ref,
    q2_ref, do2_ref, dqa_ref, dka_ref, dva_ref, dkma_ref, dvma_ref, sa_ref, ga_ref, sb_ref, gb_ref,
):
    frow = lax.broadcasted_iota(jnp.int32, (16, BQ), 0)

    def feature(value, at):
        high, mid, low = (jnp.broadcast_to(v.astype(F32), (16, BQ)) for v in split3(value))
        return jnp.where(frow == at, high, jnp.where(frow == at + 1, mid, jnp.where(frow == at + 2, low, 0.0)))

    for h in range(H):
        q2_ref[h, 0:64, :] = qa_ref[h, 0:64, :]
        q2_ref[h, 64:80, :] = (qa_ref[h, 64:80, :].astype(F32) + feature(-lse_ref[h : h + 1, :], 3)).astype(BF16)
        do2_ref[h, 0:64, :] = do_ref[64 * h : 64 * h + 64, :]
        do2_ref[h, 64:80, :] = feature(-delta_ref[h : h + 1, :], 0).astype(BF16)

    def work(new, old):
        kept = {}
        for h in range(H + 1):
            if h < H and new:
                ks = key_slots(begin, new[0])
                new[1][0][h] = dot(ka_ref[h, :, ks], q2_ref[h], 0, 0)
                new[1][1][h] = dot(va_ref[h, :, ks], do2_ref[h], 0, 0)
            if h < H and old:
                p = jnp.exp(old[1][0][h])
                kept[h] = p.astype(BF16), (p * old[1][1][h]).astype(BF16)
            if h > 0 and old:
                ks = key_slots(begin, old[0])
                p, ds = kept.pop(h - 1)
                dva_ref[h - 1, :, ks] += dot(do2_ref[h - 1, 0:64, :], p, 1, 1)
                dka_ref[h - 1, :, ks] += dot(q2_ref[h - 1, 0:64, :], ds, 1, 1)
                dqa_ref[h - 1] += dot(ka_ref[h - 1, 0:64, ks], ds, 1, 0)

    ps = [dot(kmn_ref[h, :, 0:HA], q2_ref[h], 1, 0) for h in range(H)]
    dps = [dot(vmn_ref[h, :, 0:HA], do2_ref[h], 1, 0) for h in range(H)]
    if sure:
        work((0, (sa_ref, ga_ref)), None)
    ps = [jnp.exp(p) for p in ps]
    dss = [(p * dp).astype(BF16) for p, dp in zip(ps, dps)]
    for h in range(H):
        dvma_ref[h, :, 0:MP] += dot(do2_ref[h, 0:64, :], ps[h].astype(BF16), 1, 1)
        dkma_ref[h, :, 0:MP] += dot(q2_ref[h, 0:64, :], dss[h], 1, 1)
        dqa_ref[h] = dot(km_ref[h, 0:64, 0:MP], dss[h], 1, 0)
    pipelined(blocks, work, (sa_ref, ga_ref), (sb_ref, gb_ref), sure)


def bwd_kernel(
    slots, seg_ref, cnt_ref, qa_ref, ka_ref, va_ref, kmn_ref, km_ref, vmn_ref, do_ref, lse_ref, delta_ref,
    dq_ref, dk_ref, dv_ref, dkm_ref, dvm_ref,
    q2_ref, do2_ref, dqa_ref, dka_ref, dva_ref, dkma_ref, dvma_ref, sa_ref, ga_ref, sb_ref, gb_ref, range_ref,
):
    step = pl.program_id(0)

    @pl.when(step == 0)
    def _():
        key_ranges(seg_ref[...], cnt_ref[0], slots, range_ref)
        for ref in (dka_ref, dva_ref, dkma_ref, dvma_ref):
            ref[...] = jnp.zeros_like(ref)

    attend_back(
        False, range_ref[0, step], range_ref[1, step], qa_ref, ka_ref, va_ref, kmn_ref, km_ref, vmn_ref, do_ref, lse_ref,
        delta_ref, q2_ref, do2_ref, dqa_ref, dka_ref, dva_ref, dkma_ref, dvma_ref, sa_ref, ga_ref, sb_ref, gb_ref,
    )
    for h in range(H):
        dq_ref[64 * h : 64 * h + 64, :] = (dqa_ref[h] * HD ** -0.5).astype(BF16)

    @pl.when(step == pl.num_programs(0) - 1)
    def _():
        for h in range(H):
            s = slice(64 * h, 64 * h + 64)
            dk_ref[s, :] = dka_ref[h].astype(BF16)
            dv_ref[s, :] = dva_ref[h].astype(BF16)
            dkm_ref[s, :] = dkma_ref[h].astype(BF16)
            dvm_ref[s, :] = dvma_ref[h].astype(BF16)


def attend_backward(seg2, counts, qa, ka, va, kmn, km, vmn, mgrad, lse, delta):
    slots = qa.shape[2]
    once = pl.Buffered(1)

    def full(a):
        return pl.BlockSpec(a.shape, lambda i: (0, 0, 0), pipeline_mode=once)

    cols = pl.BlockSpec((512, BQ), lambda i: (0, i))
    stat = pl.BlockSpec((H, BQ), lambda i: (0, i))
    whole = pl.BlockSpec((512, slots), lambda i: (0, 0), pipeline_mode=once)
    mwhole = pl.BlockSpec((512, 128), lambda i: (0, 0))
    block = pltpu.VMEM((H, BK, BQ), F32)
    return pl.pallas_call(
        functools.partial(bwd_kernel, slots),
        grid=(slots // BQ,),
        in_specs=[
            pl.BlockSpec(seg2.shape, lambda i: (0, 0)),
            pl.BlockSpec(memory_space=pltpu.SMEM),
            pl.BlockSpec((H, HA, BQ), lambda i: (0, 0, i)),
            full(ka), full(va), full(kmn), full(km), full(vmn), cols, stat, stat,
        ],
        out_specs=[cols, whole, whole, mwhole, mwhole],
        out_shape=[jax.ShapeDtypeStruct((512, slots), BF16)] * 3 + [jax.ShapeDtypeStruct((512, 128), BF16)] * 2,
        scratch_shapes=[
            pltpu.VMEM((H, HA, BQ), BF16),
            pltpu.VMEM((H, HA, BQ), BF16),
            pltpu.VMEM((H, HD, BQ), F32),
            pltpu.VMEM((H, HD, slots), F32),
            pltpu.VMEM((H, HD, slots), F32),
            pltpu.VMEM((H, HD, 128), F32),
            pltpu.VMEM((H, HD, 128), F32),
            block, block, block, block,
            pltpu.SMEM((2, slots // BQ), jnp.int32),
        ],
        compiler_params=params(),
        name="attend_backward",
    )(seg2, counts, qa, ka, va, kmn, km, vmn, mgrad, lse, delta)


SUM_EARLY = (
    (slice(0, 48), "yxz"),
    (slice(48, 96), "xyz"),
    (slice(96, 112), "xzy"),
    (slice(112, 144), "yzx"),
)
SUM_LATE = ((slice(144, 160), "xyz"), (slice(160, 176), "yxz"), (slice(176, 192), "xyz"), (slice(192, 208), "yxz"))
SUM_PARTS = SUM_EARLY + SUM_LATE
SUM_COPIES = 6 * len(SUM_PARTS)


def weight_grads(step, tok_ref, dq_ref, dk_ref, dv_ref, dkm_ref, dvm_ref, memt_ref, acc_ref, sum_ref):
    @pl.when(step == 0)
    def _():
        acc_ref[0:512, :] = jnp.zeros((512, 512), F32)
        acc_ref[512:1024, :] = dot(dkm_ref[...], memt_ref[...], 1, 1)
        acc_ref[1024:1536, :] = dot(dvm_ref[...], memt_ref[...], 1, 1)
        sum_ref[...] = jnp.zeros_like(sum_ref)
        sum_ref[:, 1:2] = jnp.sum(dvm_ref[...].astype(F32), axis=1, keepdims=True)

    tok = tok_ref[...]
    dq, dk, dv = dq_ref[...], dk_ref[...], dv_ref[...]
    acc_ref[0:512, :] += dot(dq, tok, 1, 0)
    acc_ref[512:1024, :] += dot(dk, tok, 1, 0)
    acc_ref[1024:1536, :] += dot(dv, tok, 1, 0)
    sum_ref[:, 0:1] += jnp.sum(dq.astype(F32), axis=1, keepdims=True)
    sum_ref[:, 1:2] += jnp.sum(dv.astype(F32), axis=1, keepdims=True)


def matrix_grad(j, acc_ref):
    return acc_ref[512 * j : 512 * j + 512, :].T.astype(BF16)


def small_grads(dkm_ref, dvm_ref, vec_ref, bup_ref, wt_ref, sum_ref, late):
    gmem = dot(wt_ref[512:1024, :], dkm_ref[...], 0, 0) + dot(wt_ref[1024:1536, :], dvm_ref[...], 0, 0)
    late(slice(48, 64), slice(0, 128), gmem.astype(BF16))
    lane = lax.broadcasted_iota(jnp.int32, (512, 128), 1)
    vecs = jnp.concatenate([vec_ref[...], jnp.zeros((120, 512), F32)], axis=0).T
    late(slice(48, 64), slice(128, 256), jnp.where(lane < 2, sum_ref[...], vecs).astype(BF16))
    rows = [bup_ref[0:1, 256 * v : 256 * v + 256] for v in range(8)] + [jnp.zeros((8, 256), F32)]
    rows = jnp.concatenate(rows, axis=0).astype(BF16)
    late(slice(48, 64), slice(256, 512), jnp.broadcast_to(rows[None], (PARTS, 16, 256)).reshape(512, 256))


def token_grads(gtok_ref, gfirst_ref, dq_ref, dk_ref, dv_ref, wt_ref):
    gtok_ref[...] = (
        gfirst_ref[...]
        + dot(dq_ref[...], wt_ref[0:512, :], 0, 0)
        + dot(dk_ref[...], wt_ref[512:1024, :], 0, 0)
        + dot(dv_ref[...], wt_ref[1024:1536, :], 0, 0)
    )


def scatter_kernel(
    blocks, qa_ref, ka_ref, va_ref, kmn_ref, km_ref, vmn_ref, do_ref, lse_ref, delta_ref,
    tok_hbm, gfirst_ref, vec_ref, bup_ref, wt_hbm, memt_ref, early_ref, gtok_ref, out_ref,
    q2_ref, do2_ref, dqa_ref, dka_ref, dva_ref, dkma_ref, dvma_ref, sa_ref, ga_ref, sb_ref, gb_ref,
    dq_ref, dk_ref, dv_ref, dkm_ref, dvm_ref,
    tok_ref, wt_ref, acc_ref, sum_ref, late, parts_sum, other, send, recv, local, fetch, *landing,
):
    step = pl.program_id(0)
    place = Place()
    copies = Copies(send, recv)
    slots = dict(zip(slot_shapes(SUM_PARTS), landing))
    crossing = [copies.number() for _ in SUM_PARTS]
    parts = []
    for index, (rows, order) in enumerate(SUM_PARTS):
        mine = {key[1:]: slot for key, slot in slots.items() if key[0] == index}
        parts.append(scatter_part(place, copies, parts_sum, mine, out_ref, rows, order))
    firsts, lasts = parts[: len(SUM_EARLY)], parts[len(SUM_EARLY) :]

    def load(index):
        rows = SUM_EARLY[index][0]
        return pltpu.make_async_copy(
            early_ref.at[:, :, :, place.core, rows], parts_sum.at[:, :, :, rows], local.at[index]
        )

    def fetches():
        return (
            pltpu.make_async_copy(tok_hbm, tok_ref, fetch.at[0]),
            pltpu.make_async_copy(wt_hbm, wt_ref, fetch.at[1]),
        )

    def cross(source, base, rows, number):
        old = slice(rows.start - base, rows.stop - base)
        copies.start(
            lambda: source.at[:, :, :, place.far, old], lambda: other.at[:, :, :, rows], number, place.partner
        )

    @pl.when(step == 0)
    def _():
        place.greet()
        for copy in fetches():
            copy.start()
        for index in range(len(SUM_EARLY)):
            load(index).start()
        for ref in (dka_ref, dva_ref, dkma_ref, dvma_ref, sum_ref):
            ref[...] = jnp.zeros_like(ref)

    @pl.when(step < blocks)
    def _():
        reach = LONGEST // BQ
        begin = jnp.maximum(step - reach, 0)
        end = jnp.minimum(step + reach + 1, blocks)
        attend_back(
            True, begin * (BQ // 128), (end - begin) * (BQ // BK), qa_ref, ka_ref, va_ref, kmn_ref, km_ref, vmn_ref,
            do_ref, lse_ref, delta_ref, q2_ref, do2_ref, dqa_ref, dka_ref, dva_ref, dkma_ref, dvma_ref,
            sa_ref, ga_ref, sb_ref, gb_ref,
        )
        here = pl.ds(pl.multiple_of(step * BQ, BQ), BQ)
        for h in range(H):
            dq_ref[64 * h : 64 * h + 64, here] = (dqa_ref[h] * HD ** -0.5).astype(BF16)

    @pl.when(step == 0)
    def _():
        for copy in fetches():
            copy.wait()
        place.met()
        for number, (rows, _) in zip(crossing, SUM_EARLY):
            cross(early_ref, 0, rows, number)

    @pl.when(step == 1)
    def _():
        for index, (rows, _) in enumerate(SUM_EARLY):
            load(index).wait()
            join(place, copies, parts_sum, None, other, rows, crossing[index])
            next(firsts[index])

    @pl.when(step == 3)
    def _():
        advance(firsts)

    @pl.when(step == 5)
    def _():
        advance(firsts)

    @pl.when(step == blocks - 1)
    def _():
        advance(firsts)

    def put(rows, lanes, value):
        late[:, :, :, :, rows, lanes] = value.reshape(4, 2, 2, 2, 16, value.shape[1])

    def depart(index):
        cross(late, LATE, SUM_LATE[index][0], crossing[len(SUM_EARLY) + index])

    def onward(index):
        rows = SUM_LATE[index][0]
        old = slice(rows.start - LATE, rows.stop - LATE)
        join(
            place, copies, parts_sum, lambda z: late[z, :, :, place.core, old], other, rows,
            crossing[len(SUM_EARLY) + index],
        )
        next(lasts[index])

    @pl.when(step == blocks)
    def _():
        tok = tok_ref[...]
        acc_ref[0:512, :] = dot(dq_ref[...], tok, 1, 0)
        put(slice(0, 16), slice(0, 512), matrix_grad(0, acc_ref))
        depart(0)
        for j, whole, part, memory, memory_part in (
            (1, dka_ref, dk_ref, dkma_ref, dkm_ref),
            (2, dva_ref, dv_ref, dvma_ref, dvm_ref),
        ):
            for h in range(H):
                s = slice(64 * h, 64 * h + 64)
                part[s, :] = whole[h].astype(BF16)
                memory_part[s, :] = memory[h].astype(BF16)
            acc_ref[512 * j : 512 * j + 512, :] = dot(part[...], tok, 1, 0) + dot(
                memory_part[...], memt_ref[...], 1, 1
            )
            put(slice(16 * j, 16 * j + 16), slice(0, 512), matrix_grad(j, acc_ref))
            depart(j)
            onward(j - 1)
        sum_ref[:, 0:1] = jnp.sum(dq_ref[...].astype(F32), axis=1, keepdims=True)
        sum_ref[:, 1:2] = jnp.sum(dv_ref[...].astype(F32), axis=1, keepdims=True) + jnp.sum(
            dvm_ref[...].astype(F32), axis=1, keepdims=True
        )
        small_grads(dkm_ref, dvm_ref, vec_ref, bup_ref, wt_ref, sum_ref, put)
        depart(3)
        onward(2)

    @pl.when(step > blocks)
    def _():
        rows = gtok_ref.shape[0]
        here = pl.ds(pl.multiple_of((step - blocks - 1) * rows, 128), rows)
        token_grads(gtok_ref, gfirst_ref, dq_ref.at[:, here], dk_ref.at[:, here], dv_ref.at[:, here], wt_ref)

    @pl.when(step == blocks + 1)
    def _():
        onward(3)

    @pl.when(step == blocks + 2)
    def _():
        advance(lasts[0:2])

    @pl.when(step == blocks + 3)
    def _():
        advance(lasts[2:4])

    @pl.when(step == pl.num_programs(0) - 1)
    def _():
        advance(lasts)
        advance(lasts)
        copies.finish()


def backward(seg2, counts, early, tokens, qa, ka, va, kmn, km, vmn, mgrad, lse, delta, gfirst, vec, bup, wt, memt, remote):
    if not remote:
        dq, dk, dv, dkm, dvm = attend_backward(seg2, counts, qa, ka, va, kmn, km, vmn, mgrad, lse, delta)
        return tail(tokens, dq, dk, dv, dkm, dvm, gfirst, vec, bup, wt, memt)
    slots = tokens.shape[0]
    rb = 512
    blocks = slots // BQ
    once = pl.Buffered(1)

    def full(a):
        return pl.BlockSpec(a.shape, lambda i: (0,) * len(a.shape), pipeline_mode=once)

    def at(i):
        return jnp.minimum(i, blocks - 1)

    later = pl.BlockSpec((rb, 512), lambda i: (jnp.maximum(i - blocks - 1, 0), 0))
    stat = pl.BlockSpec((H, BQ), lambda i: (0, at(i)))
    score = pltpu.VMEM((H, BK, BQ), F32)
    hbm = pl.BlockSpec(memory_space=pl.ANY)
    return pl.pallas_call(
        functools.partial(scatter_kernel, blocks),
        grid=(blocks + 1 + slots // rb,),
        in_specs=[
            pl.BlockSpec((H, HA, BQ), lambda i: (0, 0, at(i))),
            full(ka), full(va), full(kmn), full(km), full(vmn),
            pl.BlockSpec((512, BQ), lambda i: (0, at(i))), stat, stat,
            hbm, later, full(vec), full(bup), hbm, full(memt),
            hbm,
        ],
        out_specs=[later, fixed(ROWS, 512)],
        out_shape=[jax.ShapeDtypeStruct((slots, 512), F32), jax.ShapeDtypeStruct((ROWS, 512), F32)],
        scratch_shapes=[
            pltpu.VMEM((H, HA, BQ), BF16),
            pltpu.VMEM((H, HA, BQ), BF16),
            pltpu.VMEM((H, HD, BQ), F32),
            pltpu.VMEM((H, HD, slots), F32),
            pltpu.VMEM((H, HD, slots), F32),
            pltpu.VMEM((H, HD, 128), F32),
            pltpu.VMEM((H, HD, 128), F32),
            score, score, score, score,
            pltpu.VMEM((512, slots), BF16),
            pltpu.VMEM((512, slots), BF16),
            pltpu.VMEM((512, slots), BF16),
            pltpu.VMEM((512, 128), BF16),
            pltpu.VMEM((512, 128), BF16),
            pltpu.VMEM(tokens.shape, BF16),
            pltpu.VMEM(wt.shape, BF16),
            pltpu.VMEM((1536, 512), F32),
            pltpu.VMEM((512, 128), F32),
            pltpu.VMEM((4, 2, 2, 2, EARLY, 512), BF16),
            pltpu.VMEM((4, 2, 2, ROWS, 512), BF16),
            pltpu.VMEM((4, 2, 2, ROWS, 512), BF16),
            pltpu.SemaphoreType.DMA((SUM_COPIES,)),
            pltpu.SemaphoreType.DMA((SUM_COPIES,)),
            pltpu.SemaphoreType.DMA((len(SUM_EARLY),)),
            pltpu.SemaphoreType.DMA((2,)),
        ]
        + [pltpu.VMEM(shape, BF16) for shape in slot_shapes(SUM_PARTS).values()],
        compiler_params=params(collective_id=1, has_side_effects=True),
        name="backward_scatter",
    )(
        qa, ka, va, kmn, km, vmn, mgrad, lse, delta, tokens, gfirst, vec, bup, wt, memt,
        early.reshape(4, 2, 2, 2, LATE, 512),
    )


def plain_kernel(
    half, tok_ref, dq_ref, dk_ref, dv_ref, dkm_ref, dvm_ref, gfirst_ref, vec_ref, bup_ref, wt_ref, memt_ref,
    gtok_ref, late_ref, acc_ref, sum_ref,
):
    step = pl.program_id(0)

    @pl.when(step < half)
    def _():
        weight_grads(step, tok_ref, dq_ref, dk_ref, dv_ref, dkm_ref, dvm_ref, memt_ref, acc_ref, sum_ref)

    @pl.when(step == half - 1)
    def _():
        def put(rows, lanes, value):
            late_ref[:, rows, lanes] = value.reshape(PARTS, 16, value.shape[1])

        for j in range(3):
            put(slice(16 * j, 16 * j + 16), slice(0, 512), matrix_grad(j, acc_ref))
        small_grads(dkm_ref, dvm_ref, vec_ref, bup_ref, wt_ref, sum_ref, put)

    @pl.when(step >= half)
    def _():
        token_grads(gtok_ref, gfirst_ref, dq_ref, dk_ref, dv_ref, wt_ref)


def tail(tokens, dq, dk, dv, dkm, dvm, gfirst, vec, bup, wt, memt):
    slots = tokens.shape[0]
    rb = 512
    half = slots // rb
    cols = pl.BlockSpec((512, rb), lambda i: (0, i % half))
    later = pl.BlockSpec((rb, 512), lambda i: (jnp.maximum(i - half, 0), 0))
    return pl.pallas_call(
        functools.partial(plain_kernel, half),
        grid=(2 * half,),
        in_specs=[
            pl.BlockSpec((rb, 512), lambda i: (jnp.minimum(i, half - 1), 0)),
            cols, cols, cols, fixed(512, 128), fixed(512, 128), later,
            fixed(8, 512), fixed(1, 2048), fixed(1536, 512), fixed(512, 128),
        ],
        out_specs=[later, fixed(PARTS, EARLY, 512)],
        out_shape=[jax.ShapeDtypeStruct((slots, 512), F32), jax.ShapeDtypeStruct((PARTS, EARLY, 512), BF16)],
        scratch_shapes=[pltpu.VMEM((1536, 512), F32), pltpu.VMEM((512, 128), F32)],
        compiler_params=params(),
        name="tail",
    )(tokens, dq, dk, dv, dkm, dvm, gfirst, vec, bup, wt, memt)


def unpack_kernel(sum_hbm, part_ref, gtok_ref, wo, up, dn, wq, wk, wv, memory, b_up, *rest):
    vectors, (sum_ref, block, ready, arrive, leave) = rest[:8], rest[8:]
    count = arrive.shape[0]
    rows = block.shape[0] // count
    spans = [slice(rows * k, rows * k + rows) for k in range(count)]
    loads = [pltpu.make_async_copy(part_ref.at[s], block.at[s], arrive.at[k]) for k, s in enumerate(spans)]
    stores = [pltpu.make_async_copy(block.at[s], gtok_ref.at[s], leave.at[k]) for k, s in enumerate(spans)]
    sums = pltpu.make_async_copy(sum_hbm, sum_ref, ready)
    sums.start()
    for load in loads:
        load.start()
    me = lax.axis_index("dp")
    sums.wait()
    wo[...] = sum_ref[0:16]
    for c in range(4):
        up[:, 512 * c : 512 * c + 512] = sum_ref[16 + 16 * c : 32 + 16 * c]
    dn[...] = sum_ref[80:144]
    wq[...] = sum_ref[144:160]
    wk[...] = sum_ref[160:176]
    wv[...] = sum_ref[176:192]
    memory[...] = sum_ref[192:208, 0 : memory.shape[1]]
    turned = sum_ref[192:208, 128:256].T
    for index, vector in enumerate(vectors):
        vector[...] = turned[index : index + 1, :]
    row = lax.broadcasted_iota(jnp.int32, (16, 256), 0)
    lane = lax.broadcasted_iota(jnp.int32, (16, 256), 1)
    own = jnp.sum(jnp.where(row * 4 + lane // 64 == me, sum_ref[192:208, 256:512], 0.0), axis=0, keepdims=True)
    b_up[...] = own[:, 0:64] + own[:, 64:128] + own[:, 128:192] + own[:, 192:256]
    for load, store in zip(loads, stores):
        load.wait()
        store.start()
    for store in stores:
        store.wait()


def unpack(sums, part, mem_rows):
    shapes = [(16, 512), (16, 2048), (64, 512), (16, 512), (16, 512), (16, 512), (16, mem_rows), (1, 64)] + [(1, 16)] * 8
    found = pl.pallas_call(
        unpack_kernel,
        in_specs=[pl.BlockSpec(memory_space=pl.ANY)] * 2,
        out_specs=[pl.BlockSpec(memory_space=pl.ANY)] + [pl.BlockSpec(memory_space=pltpu.VMEM)] * len(shapes),
        out_shape=[jax.ShapeDtypeStruct(s, F32) for s in [part.shape] + shapes],
        scratch_shapes=[
            pltpu.VMEM(sums.shape, F32),
            pltpu.VMEM(part.shape, F32),
            pltpu.SemaphoreType.DMA,
            pltpu.SemaphoreType.DMA((4,)),
            pltpu.SemaphoreType.DMA((4,)),
        ],
        compiler_params=params(),
        name="unpack",
    )(sums, part)
    gtok, found = found[0], found[1:]
    out = dict(zip(("w_out", "w_up", "w_down", "w_query", "w_key", "w_value", "memory"), found[:7]))
    out["memory"] = out["memory"].T
    out["b_up"] = found[7].reshape(64)
    for name, value in zip(VECTORS, found[8:]):
        out[name] = value.reshape(16)
    return gtok, out


NAMES = (
    "memory", "w_query", "b_query", "w_key", "w_value", "b_value", "w_out", "b_out", "gain_attn",
    "shift_attn", "w_up", "b_up", "w_down", "b_down", "gain_ffn", "shift_ffn",
)


def pack_whole(p):
    mem_rows = p["memory"].shape[0]
    mats = [p[name].reshape(PARTS, 16, 512) for name in ("w_query", "w_key", "w_value", "w_out")]
    up = p["w_up"].reshape(PARTS, 16, 4, 512).transpose(0, 2, 1, 3).reshape(PARTS, 64, 512)
    memory = jnp.pad(p["memory"].T, ((0, 0), (0, 128 - mem_rows))).reshape(PARTS, 16, 128)
    vectors = jnp.stack([p[name] for name in VECTORS], axis=1)
    vectors = jnp.pad(vectors, ((0, 0), (0, 120))).reshape(PARTS, 16, 128)
    own = jnp.arange(2048)[None] // 64 == jnp.arange(PARTS)[:, None]
    b_up = jnp.where(own, p["b_up"][None], 0).astype(BF16).reshape(PARTS, 8, 256)
    b_up = jnp.pad(b_up, ((0, 0), (0, 8), (0, 0)))
    small = jnp.concatenate([memory, vectors, b_up], axis=2)
    return jnp.concatenate(mats[:3] + [small, up, p["w_down"].reshape(PARTS, 64, 512), mats[3]], axis=1)


def unpack_whole(early, late, mem_rows):
    small = late[:, 48:64]
    vectors = small[:, :, 128:136].reshape(512, 8)
    out = {
        "memory": small[:, :, 0:mem_rows].reshape(512, mem_rows).T,
        "w_query": late[:, 0:16].reshape(512, 512),
        "w_key": late[:, 16:32].reshape(512, 512),
        "w_value": late[:, 32:48].reshape(512, 512),
        "w_out": early[:, 0:16].reshape(512, 512),
        "w_up": early[:, 16:80].reshape(PARTS, 4, 16, 512).transpose(0, 2, 1, 3).reshape(512, 2048),
        "w_down": early[:, 80:144].reshape(2048, 512),
        "b_up": small[0, 0:8, 256:512].reshape(2048),
    }
    for index, name in enumerate(VECTORS):
        out[name] = vectors[:, index]
    return out


def axis_of(name):
    return 1 if name == "memory" else 0


def shards(n, tokens, segment, counts, *rest):
    p = dict(zip(NAMES, rest[:-1]))
    cotangent = rest[-1]
    slots = tokens.shape[0]
    mem_rows = p["memory"].shape[0]
    whole = None
    if n != PARTS:
        whole = pack_whole({k: lax.all_gather(v, "dp", axis=axis_of(k), tiled=True) for k, v in p.items()})
    found = projections(p, whole, tokens, segment, counts, mem_rows)
    late, qa, ka, va, km, kmn, vmn, wt, memt, rows8, rbup, mixt, lse = found
    seg2 = segment.reshape(slots // 128, 128)
    output, gfirst, mgrad, delta, early, vec, bup = middle(late, rows8, rbup, counts, mixt, tokens, cotangent)
    gtok, sums = backward(
        seg2, counts, early, tokens, qa, ka, va, kmn, km, vmn, mgrad, lse, delta, gfirst, vec, bup, wt, memt, n == PARTS
    )
    if n == PARTS:
        gtok, grads = unpack(sums, gtok, mem_rows)
    else:
        full = unpack_whole(early.astype(F32), sums.astype(F32), mem_rows)
        grads = {
            k: lax.psum_scatter(v, "dp", scatter_dimension=axis_of(k), tiled=True) for k, v in full.items()
        }
    return (output, gtok) + tuple(grads[name] for name in NAMES)


def solution(mesh):
    n = mesh.shape["dp"]
    row, mat, mem = P("dp"), P("dp", None), P(None, "dp")
    spec = {name: mat if name.startswith("w_") else row for name in NAMES}
    spec["memory"] = mem
    weights = tuple(spec[name] for name in NAMES)
    return jax.shard_map(
        functools.partial(shards, n),
        mesh=mesh,
        in_specs=(mat, row, row) + weights + (mat,),
        out_specs=(mat, mat) + weights,
        check_vma=False,
    )
```

```python
import functools
import jax
import jax.numpy as jnp
from jax import lax
from jax.experimental import pallas as pl
from jax.experimental.pallas import tpu as pltpu
from jax.sharding import PartitionSpec as P

H = 8
HD = 64
HA = 80
EPS = 1e-05
BIG = 1e30
PARTS = 32
ROWS = 208
BQ = 256
BK = 256
MP = 32
LONGEST = 1024
F32 = jnp.float32
BF16 = jnp.bfloat16
VMEM_LIMIT = 60 << 20

V_BQ, V_BV, V_BO, V_GA, V_SA, V_BD, V_GF, V_SF = range(8)


def dot(left, right, lc, rc):
    return lax.dot_general(left, right, (((lc,), (rc,)), ((), ())), preferred_element_type=F32)


def params(**kw):
    return pltpu.CompilerParams(vmem_limit_bytes=VMEM_LIMIT, **kw)


MESH = pl.DeviceIdType.MESH
AXES = {"z": (8, 4), "y": (4, 2), "x": (2, 2)}
LAYOUT = ("z", "y", "x")


class Place:
    def __init__(self):
        me = lax.axis_index("dp")
        self.me = me
        self.core = me % 2
        self.far = 1 - self.core
        self.partner = me + 1 - 2 * self.core
        self.at = {a: (me // stride) % length for a, (stride, length) in AXES.items()}
        self.mine = tuple(self.at[a] for a in LAYOUT)
        self.others = {}
        for axis, (stride, length) in AXES.items():
            for distance in range(1, length):
                j = (self.at[axis] + distance) % length
                self.others[axis, distance] = j, me + (j - self.at[axis]) * stride
        self.peers = [self.partner] + [device for _, device in self.others.values()]

    def other(self, axis, distance):
        return self.others[axis, distance]

    def greet(self):
        for peer in self.peers:
            pl.semaphore_signal(
                pltpu.get_barrier_semaphore(), inc=1, device_id=(peer,), device_id_type=MESH
            )

    def met(self):
        pl.semaphore_wait(pltpu.get_barrier_semaphore(), len(self.peers))


class Copies:
    def __init__(self, send, recv):
        self.send, self.recv, self.count, self.open = send, recv, 0, []

    def number(self):
        self.count += 1
        return self.count - 1

    def make(self, src, dst, number, device):
        return pltpu.make_async_remote_copy(
            src_ref=src, dst_ref=dst, send_sem=self.send.at[number], recv_sem=self.recv.at[number],
            device_id=(device,), device_id_type=MESH,
        )

    def start(self, src, dst, number, device):
        self.make(src(), dst(), number, device).start()
        self.open.append((src, dst, number, device))

    def landed(self, block, number, device):
        self.make(block, block, number, device).wait_recv()

    def finish(self):
        for src, dst, number, device in self.open:
            self.make(src(), dst(), number, device).wait_send()
        self.open = []


def gather_part(place, copies, own, base, whole, rows, order, arrivals):
    done = ()

    def mine():
        return own.at[slice(base + rows.start, base + rows.stop)]

    def block(axis, j, core):
        index = tuple(j if a == axis else (slice(None) if a in done else place.at[a]) for a in LAYOUT)
        return lambda: whole.at[index + (core, rows)]

    for axis in order:
        length = AXES[axis][1]
        numbers = [copies.number() for _ in range(2 * length - 2)]
        here = block(axis, place.at[axis], place.core)
        for d in range(1, length):
            copies.start(here if done else mine, here, numbers[d - 1], place.other(axis, d)[1])
        if not done:
            number = copies.number()
            copies.start(mine, here, number, place.partner)
            arrivals.append((block(axis, place.at[axis], place.far), number))
        yield
        for d in range(1, length):
            j, device = place.other(axis, length - d)
            there = block(axis, j, place.core)
            copies.landed(there(), numbers[d - 1], device)
            number = numbers[length - 2 + d]
            copies.start(there, there, number, place.partner)
            arrivals.append((block(axis, j, place.far), number))
        done += (axis,)
    yield


def advance(parts):
    for part in parts:
        next(part)


def scatter_part(place, copies, acc, slots, out, rows, order):
    done = ()

    def block(axis, j):
        index = tuple(j if a == axis else (place.at[a] if a in done else slice(None)) for a in LAYOUT)
        return index + (rows,)

    def taken(index):
        return lambda: acc.at[index]

    def landing(axis, d):
        return lambda: slots[axis, d]

    for axis in order:
        length = AXES[axis][1]
        numbers = [copies.number() for _ in range(length - 1)]
        for d in range(1, length):
            j, device = place.other(axis, d)
            copies.start(taken(block(axis, j)), landing(axis, d), numbers[d - 1], device)
        yield
        for d in range(1, length):
            copies.landed(slots[axis, d], numbers[d - 1], place.partner)
        mine = block(axis, place.at[axis])
        total = acc[mine].astype(F32)
        for d in range(1, length):
            total = total + slots[axis, d][...].astype(F32)
        if axis == order[-1]:
            out[rows, :] = total
        else:
            acc[mine] = total.astype(BF16)
        done += (axis,)
    yield


def slot_shapes(parts):
    shapes = {}
    for number, (rows, order) in enumerate(parts):
        left = ["z", "y", "x"]
        for axis in order:
            left.remove(axis)
            shape = tuple(AXES[a][1] for a in LAYOUT if a in left) + (rows.stop - rows.start, 512)
            for d in range(1, AXES[axis][1]):
                shapes[number, axis, d] = shape
    return shapes


def join(place, copies, acc, source, other, rows, number):
    copies.landed(other.at[:, :, :, rows], number, place.partner)

    @pl.loop(0, 4)
    def _(z):
        mine = source(z) if source else acc[z, :, :, rows]
        acc[z, :, :, rows] = (mine.astype(F32) + other[z, :, :, rows].astype(F32)).astype(BF16)


VECTORS = ("b_query", "b_value", "b_out", "gain_attn", "shift_attn", "b_down", "gain_ffn", "shift_ffn")
EARLY = 64
LATE = 144
EARLY_PARTS = ((slice(0, 16), "zxy"), (slice(16, 32), "zyx"), (slice(32, 48), "zxy"), (slice(48, 64), "zyx"))
LATE_PARTS = (
    (slice(0, 48), "zxy"),
    (slice(48, 96), "zyx"),
    (slice(96, 128), "yzx"),
    (slice(128, 144), "xzy"),
)
GATHER_COPIES = 11 * (len(EARLY_PARTS) + len(LATE_PARTS))


def head_block(rows, features):
    block = jnp.concatenate([rows, features], axis=0)
    return block, jnp.concatenate([block, jnp.zeros((128 - HA, rows.shape[1]), BF16)], axis=0).T


def pack(own, place, wq, wk, wv, wo, up, dn, memory, b_up, vectors):
    own[0:16] = wq[...]
    own[16:32] = wk[...]
    own[32:48] = wv[...]
    own[48:64] = jnp.zeros((16, 512), BF16)
    own[48:64, 0 : memory.shape[1]] = memory[...]
    values = jnp.concatenate([vector[...].astype(F32) for vector in vectors], axis=0)
    own[48:64, 128:136] = values.T.astype(BF16)
    value = jnp.concatenate([b_up[...].astype(F32)] * 4, axis=1)
    row = lax.broadcasted_iota(jnp.int32, (16, 256), 0)
    lane = lax.broadcasted_iota(jnp.int32, (16, 256), 1)
    own[48:64, 256:512] = jnp.where(row * 4 + lane // 64 == place.me, value, 0.0).astype(BF16)
    for c in range(4):
        own[64 + 16 * c : 80 + 16 * c] = up[:, 512 * c : 512 * c + 512]
    own[128:192] = dn[...]
    own[192:208] = wo[...]


def prepare(mem_rows, early, wt_ref, memt_ref, rows_ref, rbup_ref, bias_ref, km_ref, vm_ref, kmn_ref, vmn_ref):
    for j in range(3):
        wt_ref[512 * j : 512 * j + 512, :] = early[..., 16 * j : 16 * j + 16, :].reshape(512, 512).T
    small = early[..., 48:64, 0:256].reshape(512, 256)
    memt = small[:, 0:128]
    memt_ref[...] = memt
    vectors = small[:, 128:256].astype(F32)
    bias_ref[...] = vectors
    rows_ref[...] = vectors.T[0:8, :]
    bup = jnp.sum(early[..., 48:64, 256:512].reshape(PARTS, 16, 256).astype(F32), axis=0)
    for v in range(8):
        rbup_ref[0:1, 256 * v : 256 * v + 256] = bup[v : v + 1, :]
    bv = vectors[:, V_BV : V_BV + 1]
    km = dot(wt_ref[512:1024, :], memt, 1, 0).astype(BF16)
    vm = (dot(wt_ref[1024:1536, :], memt, 1, 0) + bv).astype(BF16)
    frow = lax.broadcasted_iota(jnp.int32, (16, 128), 0)
    lane = lax.broadcasted_iota(jnp.int32, (16, 128), 1)
    kf = jnp.where(frow < 3, jnp.where(lane < mem_rows, 0.0, 1.0), jnp.where(frow < 6, 1.0, 0.0)).astype(BF16)
    vf = jnp.where(frow < 3, 1.0, 0.0).astype(BF16)
    for h in range(H):
        km_ref[h], turned = head_block(km[64 * h : 64 * h + 64, :], kf)
        kmn_ref[h] = turned[0:MP]
        vm_ref[h], turned = head_block(vm[64 * h : 64 * h + 64, :], vf)
        vmn_ref[h] = turned[0:MP]


def project(step, tok_ref, seg_ref, cnt_ref, wt_ref, bias_ref, qa_ref, ka_ref, va_ref):
    rows = tok_ref.shape[0]
    tok = tok_ref[...]
    bq = bias_ref[:, V_BQ : V_BQ + 1]
    bv = bias_ref[:, V_BV : V_BV + 1]
    q = (dot(wt_ref[0:512, :], tok, 1, 1) + bq).astype(BF16) * jnp.asarray(HD ** -0.5, BF16)
    k = dot(wt_ref[512:1024, :], tok, 1, 1).astype(BF16)
    v = (dot(wt_ref[1024:1536, :], tok, 1, 1) + bv).astype(BF16)
    frow = lax.broadcasted_iota(jnp.int32, (16, rows), 0)
    seg = jnp.broadcast_to(seg_ref[...], (16, rows))
    pos = lax.broadcasted_iota(jnp.int32, (16, rows), 1) + step * rows
    valid = pos < cnt_ref[0]
    qf = jnp.where((frow < 3) & (frow != seg), -BIG, 0.0).astype(BF16)
    kf = jnp.where(frow < 3, jnp.where(valid & (frow != seg), 0.0, 1.0), jnp.where(frow < 6, 1.0, 0.0)).astype(BF16)
    vf = jnp.where(frow < 3, 1.0, 0.0).astype(BF16)
    for h in range(H):
        s = slice(64 * h, 64 * h + 64)
        qa_ref[h, 0:64, :] = q[s]
        qa_ref[h, 64:80, :] = qf
        ka_ref[h, 0:64, :] = k[s]
        ka_ref[h, 64:80, :] = kf
        va_ref[h, 0:64, :] = v[s]
        va_ref[h, 64:80, :] = vf


def gather_kernel(
    mem_rows, half, wq, wk, wv, wo, up, dn, memory, b_up, v0, v1, v2, v3, v4, v5, v6, v7, tok_ref, seg_ref, cnt_ref,
    late_ref, qa_ref, ka_ref, va_ref, km_ref, kmn_ref, vmn_ref,
    wt_ref, memt_ref, rows_ref, rbup_ref, mix_ref, lse_ref,
    own, early, bias_ref, vm_ref, qa_all, ka_all, va_all, acc_ref, m_ref, sa_ref, sb_ref, send, recv, local,
):
    step = pl.program_id(0)
    slots = ka_all.shape[2]
    place = Place()
    copies = Copies(send, recv)
    arrivals, late_arrivals = [], []
    firsts = [gather_part(place, copies, own, 0, early, *part, arrivals) for part in EARLY_PARTS]
    lasts = [gather_part(place, copies, own, EARLY, late_ref, *part, late_arrivals) for part in LATE_PARTS]

    @pl.when(step == 0)
    def _():
        place.greet()
        pack(own, place, wq, wk, wv, wo, up, dn, memory, b_up, (v0, v1, v2, v3, v4, v5, v6, v7))
        early[place.mine + (place.core,)] = own[0:EARLY]
        place.met()
        advance(firsts)
        keep = pltpu.make_async_copy(own.at[EARLY:ROWS], late_ref.at[place.mine + (place.core,)], local)
        keep.start()
        advance(firsts)
        advance(firsts)
        keep.wait()
        advance(lasts)
        advance(firsts)
        for block, number in arrivals:
            copies.landed(block(), number, place.partner)
        prepare(
            mem_rows, early, wt_ref, memt_ref, rows_ref, rbup_ref, bias_ref, km_ref, vm_ref, kmn_ref, vmn_ref,
        )

    @pl.when(step < half)
    def _():
        project(step, tok_ref, seg_ref, cnt_ref, wt_ref, bias_ref, qa_ref, ka_ref, va_ref)
        here = pl.ds(pl.multiple_of(step * tok_ref.shape[0], 128), tok_ref.shape[0])
        qa_all[:, :, here] = qa_ref[...]
        ka_all[:, :, here] = ka_ref[...]
        va_all[:, :, here] = va_ref[...]

    @pl.when(step == half - 1)
    def _():
        advance(lasts)

    @pl.when(step >= half)
    def _():
        block = step - half
        reach = LONGEST // BQ
        begin = jnp.maximum(block - reach, 0)
        end = jnp.minimum(block + reach + 1, slots // BQ)
        queries = qa_all.at[:, :, pl.ds(pl.multiple_of(block * BQ, BQ), BQ)]
        attend(
            True, begin * (BQ // 128), (end - begin) * (BQ // BK), queries, ka_all, va_all, kmn_ref, vm_ref, mix_ref, lse_ref,
            acc_ref, m_ref, sa_ref, sb_ref,
        )

    @pl.when(step == half + 2)
    def _():
        advance(lasts)

    @pl.when(step == pl.num_programs(0) - 1)
    def _():
        advance(lasts)
        for block, number in late_arrivals:
            copies.landed(block(), number, place.partner)
        copies.finish()


def project_kernel(
    mem_rows, g_ref, tok_ref, seg_ref, cnt_ref, qa_ref, ka_ref, va_ref, km_ref, vm_ref, kmn_ref, vmn_ref,
    wt_ref, memt_ref, rows_ref, rbup_ref, bias_ref,
):
    step = pl.program_id(0)

    @pl.when(step == 0)
    def _():
        prepare(
            mem_rows, g_ref, wt_ref, memt_ref, rows_ref, rbup_ref, bias_ref, km_ref, vm_ref, kmn_ref, vmn_ref
        )

    project(step, tok_ref, seg_ref, cnt_ref, wt_ref, bias_ref, qa_ref, ka_ref, va_ref)


def fixed(*shape):
    return pl.BlockSpec(shape, lambda i: (0,) * len(shape))


def projections(p, whole, tokens, segment, counts, mem_rows):
    slots = tokens.shape[0]
    rb = 512
    half = slots // rb
    wide = (H, HA, slots)
    mwide, mtall = (H, HA, 128), (H, MP, 128)

    def at(i):
        return jnp.minimum(i, half - 1)

    blk = pl.BlockSpec((H, HA, rb), lambda i: (0, 0, at(i)))
    common = [
        pl.BlockSpec((rb, 512), lambda i: (at(i), 0)),
        pl.BlockSpec((1, rb), lambda i: (0, at(i))),
        pl.BlockSpec(memory_space=pltpu.SMEM),
    ]
    args = (tokens, segment.reshape(1, slots), counts)

    def outs(shapes):
        found = [jax.ShapeDtypeStruct(s, BF16) for s in shapes]
        return found + [jax.ShapeDtypeStruct((8, 512), F32), jax.ShapeDtypeStruct((1, 2048), F32)]

    if whole is not None:
        shapes = outs([wide, wide, wide, mwide, mwide, mtall, mtall, (1536, 512), (512, 128)])
        found = pl.pallas_call(
            functools.partial(project_kernel, mem_rows),
            grid=(half,),
            in_specs=[fixed(PARTS, EARLY, 512)] + common,
            out_specs=[blk, blk, blk] + [fixed(*o.shape) for o in shapes[3:]],
            out_shape=shapes,
            scratch_shapes=[pltpu.VMEM((512, 128), F32)],
            compiler_params=params(),
            name="projections",
        )(whole[:, 0:EARLY], *args)
        qa, ka, va, km, vm, kmn, vmn, wt, memt, rows8, rbup = found
        mixt, lse = attend_forward(segment.reshape(slots // 128, 128), counts, qa, ka, va, kmn, vm)
        return whole[:, EARLY:], qa, ka, va, km, kmn, vmn, wt, memt, rows8, rbup, mixt, lse
    weights = [p[name] for name in ("w_query", "w_key", "w_value", "w_out", "w_up", "w_down")]
    weights += [p["memory"].T, p["b_up"].reshape(1, 64)] + [p[name].reshape(1, 16) for name in VECTORS]
    shapes = outs([wide, wide, wide, mwide, mtall, mtall, (1536, 512), (512, 128)])
    found = pl.pallas_call(
        functools.partial(gather_kernel, mem_rows, half),
        grid=(half + slots // BQ,),
        in_specs=[fixed(*w.shape) for w in weights] + common,
        out_specs=[pl.BlockSpec(memory_space=pl.ANY), blk, blk, blk]
        + [fixed(*o.shape) for o in shapes[3:]]
        + [
            pl.BlockSpec((512, BQ), lambda i: (0, jnp.maximum(i - half, 0))),
            pl.BlockSpec((H, BQ), lambda i: (0, jnp.maximum(i - half, 0))),
        ],
        out_shape=[jax.ShapeDtypeStruct((4, 2, 2, 2, LATE, 512), BF16)]
        + shapes
        + [jax.ShapeDtypeStruct((512, slots), BF16), jax.ShapeDtypeStruct((H, slots), F32)],
        scratch_shapes=[
            pltpu.VMEM((ROWS, 512), BF16),
            pltpu.VMEM((4, 2, 2, 2, EARLY, 512), BF16),
            pltpu.VMEM((512, 128), F32),
            pltpu.VMEM(mwide, BF16),
            pltpu.VMEM(wide, BF16),
            pltpu.VMEM(wide, BF16),
            pltpu.VMEM(wide, BF16),
            pltpu.VMEM((H, HA, BQ), F32),
            pltpu.VMEM((H, BQ), F32),
            pltpu.VMEM((H, BK, BQ), F32),
            pltpu.VMEM((H, BK, BQ), F32),
            pltpu.SemaphoreType.DMA((GATHER_COPIES,)),
            pltpu.SemaphoreType.DMA((GATHER_COPIES,)),
            pltpu.SemaphoreType.DMA,
        ],
        compiler_params=params(collective_id=0, has_side_effects=True),
        name="gather_attend",
    )(*weights, *args)
    return (found[0].reshape(PARTS, LATE, 512),) + tuple(found[1:])


def key_ranges(seg, count, slots, out):
    r, c = seg.shape
    pos = lax.broadcasted_iota(jnp.int32, (r, c), 0) * c + lax.broadcasted_iota(jnp.int32, (r, c), 1)
    valid = pos < count
    ends = [jnp.sum(jnp.where(valid & (seg <= s), 1.0, 0.0)).astype(jnp.int32) for s in range(3)]
    for block in range(slots // BQ):
        first = block * BQ
        last = jnp.minimum(first + BQ, count)
        low, high, start = jnp.int32(slots), jnp.int32(0), jnp.int32(0)
        for end in ends:
            hit = (end > first) & (start < last) & (end > start)
            low = jnp.where(hit, jnp.minimum(low, start), low)
            high = jnp.where(hit, jnp.maximum(high, end), high)
            start = end
        begin = low // 128
        blocks = jnp.where(high > low, (high - begin * 128 + BK - 1) // BK, 0)
        out[0, block] = jnp.minimum(begin, slots // 128 - blocks * (BK // 128))
        out[1, block] = blocks


def key_slots(begin, block):
    return pl.ds(pl.multiple_of((begin + block * (BK // 128)) * 128, 128), BK)


def pipelined(blocks, work, first, second, started, finish):
    if not started:

        @pl.when(blocks > 0)
        def _():
            work((0, first), None)

        pl.when(blocks == 0)(finish)

    pairs = jnp.maximum(blocks - 1, 0) // 2

    def two(j):
        work((j + 1, second), (j, first))
        work((j + 2, first), (j + 1, second))

    @pl.loop(0, pairs // 2)
    def _(i):
        two(4 * i)
        two(4 * i + 2)

    @pl.when(pairs % 2 == 1)
    def _():
        two(2 * pairs - 2)

    j = 2 * pairs

    @pl.when(blocks - j == 2)
    def _():
        work((j + 1, second), (j, first))
        work(None, (j + 1, second))
        finish()

    @pl.when(blocks - j == 1)
    def _():
        work(None, (j, first))
        finish()


def attend(
    sure, begin, blocks, qa_ref, ka_ref, va_ref, kmn_ref, vm_ref, mix_ref, lse_ref, acc_ref, m_ref, sa_ref, sb_ref
):
    def weights(h, s):
        old = m_ref[h : h + 1, :]
        top = jnp.maximum(old, jnp.max(s, axis=0, keepdims=True))
        return jnp.exp(s - top).astype(BF16), jnp.exp(old - top), top

    def work(new, old):
        kept = {}
        for h in range(H + 1):
            if h < H and new:
                new[1][h] = dot(ka_ref[h, :, key_slots(begin, new[0])], qa_ref[h], 0, 0)
            if h < H and old:
                kept[h] = weights(h, old[1][h])
            if h > 0 and old:
                p, fade, top = kept.pop(h - 1)
                acc_ref[h - 1] = acc_ref[h - 1] * fade + dot(va_ref[h - 1, :, key_slots(begin, old[0])], p, 1, 0)
                m_ref[h - 1 : h, :] = top

    scores = [dot(kmn_ref[h, :, 0:HA], qa_ref[h], 1, 0) for h in range(H)]
    if sure:
        work((0, sa_ref), None)
    for h in range(H):
        top = jnp.max(scores[h], axis=0, keepdims=True)
        p = jnp.exp(scores[h] - top).astype(BF16)
        acc_ref[h] = dot(vm_ref[h, :, 0:MP], p, 1, 0)
        m_ref[h : h + 1, :] = top

    def finish():
        for h in range(H):
            total = acc_ref[h, 64:65, :]
            mix_ref[64 * h : 64 * h + 64, :] = (acc_ref[h, 0:64, :] * (1.0 / total)).astype(BF16)
            lse_ref[h : h + 1, :] = m_ref[h : h + 1, :] + jnp.log(total)

    pipelined(blocks, work, sa_ref, sb_ref, sure, finish)


def fwd_kernel(
    slots, seg_ref, cnt_ref, qa_ref, ka_ref, va_ref, kmn_ref, vm_ref,
    mix_ref, lse_ref, acc_ref, m_ref, sa_ref, sb_ref, range_ref,
):
    step = pl.program_id(0)

    @pl.when(step == 0)
    def _():
        key_ranges(seg_ref[...], cnt_ref[0], slots, range_ref)

    attend(
        False, range_ref[0, step], range_ref[1, step], qa_ref, ka_ref, va_ref, kmn_ref, vm_ref, mix_ref, lse_ref,
        acc_ref, m_ref, sa_ref, sb_ref,
    )


def attend_forward(seg2, counts, qa, ka, va, kmn, vm):
    slots = qa.shape[2]
    once = pl.Buffered(1)

    def whole(a):
        return pl.BlockSpec(a.shape, lambda i: (0, 0, 0), pipeline_mode=once)

    return pl.pallas_call(
        functools.partial(fwd_kernel, slots),
        grid=(slots // BQ,),
        in_specs=[
            pl.BlockSpec(seg2.shape, lambda i: (0, 0)),
            pl.BlockSpec(memory_space=pltpu.SMEM),
            pl.BlockSpec((H, HA, BQ), lambda i: (0, 0, i)),
            whole(ka), whole(va), whole(kmn), whole(vm),
        ],
        out_specs=[pl.BlockSpec((512, BQ), lambda i: (0, i)), pl.BlockSpec((H, BQ), lambda i: (0, i))],
        out_shape=[jax.ShapeDtypeStruct((512, slots), BF16), jax.ShapeDtypeStruct((H, slots), F32)],
        scratch_shapes=[
            pltpu.VMEM((H, HA, BQ), F32),
            pltpu.VMEM((H, BQ), F32),
            pltpu.VMEM((H, BK, BQ), F32),
            pltpu.VMEM((H, BK, BQ), F32),
            pltpu.SMEM((2, slots // BQ), jnp.int32),
        ],
        compiler_params=params(),
        name="attend_forward",
    )(seg2, counts, qa, ka, va, kmn, vm)


def norm_parts(value):
    mean = jnp.mean(value, axis=-1, keepdims=True)
    centred = value - mean
    rstd = lax.rsqrt(jnp.mean(centred * centred, axis=-1, keepdims=True) + EPS)
    return centred * rstd, rstd


def norm_grad(grad_hat, hat, rstd):
    return rstd * (
        grad_hat
        - jnp.mean(grad_hat, axis=-1, keepdims=True)
        - hat * jnp.mean(grad_hat * hat, axis=-1, keepdims=True)
    )


def colsum(value):
    return jnp.sum(value, axis=0, keepdims=True)


SUB = 512
FC = 512


def mid_kernel(
    rb, cnt_ref, row_ref, rbup_ref, late_ref, mix_ref, tok_ref, cot_ref,
    out_ref, gfirst_ref, mgrad_ref, delta_ref, gw_ref, vec_ref, bup_ref,
    aup_ref, adn_ref, ao_ref, *scratch,
):
    step = pl.program_id(0)
    subs = rb // SUB

    @pl.when(step == 0)
    def _():
        aup_ref[...] = jnp.zeros_like(aup_ref)
        adn_ref[...] = jnp.zeros_like(adn_ref)
        ao_ref[...] = jnp.zeros_like(ao_ref)
        vec_ref[...] = jnp.zeros_like(vec_ref)
        bup_ref[...] = jnp.zeros_like(bup_ref)

    wo = late_ref[:, 128:144, :].reshape(512, 512)

    def w_up(c):
        return late_ref[:, 16 * c : 16 * c + 16, :].reshape(512, 512)

    def w_down(c):
        return late_ref[8 * c : 8 * c + 8, 64:128, :].reshape(512, 512)

    def row(v):
        return row_ref[v : v + 1, :]

    class Block:
        def __init__(self, index):
            self.s = slice(SUB * index, SUB * index + SUB)
            self.first_row = step * rb + SUB * index
            self.active, self.slope, self.hgrad = scratch[3 * (index % 2) : 3 * (index % 2) + 3]
            self.up_part, self.dact_part = {}, {}

        def head(self):
            self.mixt = mix_ref[:, self.s]
            attention = dot(self.mixt, wo, 0, 0) + row(V_BO)
            self.hat1, self.rstd1 = norm_parts(tok_ref[self.s, :].astype(F32) + attention)
            self.first = self.hat1 * row(V_GA) + row(V_SA)
            self.low = self.first.astype(BF16)
            self.branch = self.first + row(V_BD)

        def up(self, c):
            f = slice(FC * c, FC * c + FC)
            self.up_part[c] = dot(self.low, w_up(c), 1, 0) + rbup_ref[:, f]

        def gelu(self, c):
            f = slice(FC * c, FC * c + FC)
            hidden = self.up_part.pop(c)
            cdf = 0.5 + 0.5 * lax.erf(hidden * (2.0 ** -0.5))
            self.active[:, f] = (hidden * cdf).astype(BF16)
            self.slope[:, f] = cdf + hidden * jnp.exp(hidden * hidden * -0.5) * 0.3989422804014327

        def down(self, c):
            f = slice(FC * c, FC * c + FC)
            self.branch = self.branch + dot(self.active[:, f], w_down(c), 1, 0)

        def turn(self):
            hat2, rstd2 = norm_parts(self.branch)
            valid = lax.broadcasted_iota(jnp.int32, (SUB, 1), 0) + self.first_row < cnt_ref[0]
            out_ref[self.s, :] = jnp.where(valid, hat2 * row(V_GF) + row(V_SF), 0.0).astype(BF16)
            seed = jnp.where(valid, cot_ref[self.s, :].astype(F32), 0.0)
            vec_ref[V_GF : V_GF + 1, :] += colsum(seed * hat2)
            vec_ref[V_SF : V_SF + 1, :] += colsum(seed)
            self.total = norm_grad(seed * row(V_GF), hat2, rstd2)
            self.bgrad = self.total.astype(BF16)
            vec_ref[V_BD : V_BD + 1, :] += colsum(self.bgrad.astype(F32))

        def dact(self, c):
            f = slice(FC * c, FC * c + FC)
            self.dact_part[c] = dot(self.bgrad, w_down(c), 1, 1)

        def grad_down(self, c):
            f = slice(FC * c, FC * c + FC)
            adn_ref[f, :] += dot(self.active[:, f], self.bgrad, 0, 0)

        def hidden_grad(self, c):
            f = slice(FC * c, FC * c + FC)
            grad = (self.dact_part.pop(c) * self.slope[:, f]).astype(BF16)
            self.hgrad[:, f] = grad
            bup_ref[:, f] += colsum(grad.astype(F32))

        def grad_up(self, c):
            f = slice(FC * c, FC * c + FC)
            aup_ref[:, f] += dot(self.low, self.hgrad[:, f], 0, 0)

        def first_grad(self, c):
            f = slice(FC * c, FC * c + FC)
            self.total = self.total + dot(self.hgrad[:, f], w_up(c), 1, 1)

        def finish(self):
            vec_ref[V_GA : V_GA + 1, :] += colsum(self.total * self.hat1)
            vec_ref[V_SA : V_SA + 1, :] += colsum(self.total)
            grad_first = norm_grad(self.total * row(V_GA), self.hat1, self.rstd1)
            gfirst_ref[self.s, :] = grad_first
            agrad = grad_first.astype(BF16)
            vec_ref[V_BO : V_BO + 1, :] += colsum(agrad.astype(F32))
            mgrad = dot(wo, agrad, 1, 1).astype(BF16)
            ao_ref[...] += dot(self.mixt, agrad, 1, 0)
            mgrad_ref[:, self.s] = mgrad
            prod = mgrad.astype(F32) * self.mixt.astype(F32)
            for h in range(H):
                delta_ref[h : h + 1, self.s] = jnp.sum(prod[64 * h : 64 * h + 64, :], axis=0, keepdims=True)

    chunks = 2048 // FC

    def both(ahead, behind):
        if ahead:
            ahead.head()
            ahead.up(0)
        for c in range(chunks):
            if behind:
                behind.dact(c)
            if ahead and c + 1 < chunks:
                ahead.up(c + 1)
            if behind:
                behind.grad_down(c)
            if ahead:
                ahead.gelu(c)
            if behind:
                behind.hidden_grad(c)
                behind.grad_up(c)
                behind.first_grad(c)
            if ahead:
                ahead.down(c)
        if behind:
            behind.finish()
        if ahead:
            ahead.turn()

    blocks = [Block(index) for index in range(subs)]
    for ahead, behind in zip(blocks + [None], [None] + blocks):
        both(ahead, behind)

    @pl.when(step == pl.num_programs(0) - 1)
    def _():
        gw_ref[:, 0:16, :] = ao_ref[...].astype(gw_ref.dtype).reshape(PARTS, 16, 512)
        for c in range(4):
            gw_ref[:, 16 + 16 * c : 32 + 16 * c, :] = (
                aup_ref[:, 512 * c : 512 * c + 512].astype(gw_ref.dtype).reshape(PARTS, 16, 512)
            )
        gw_ref[:, 80:144, :] = adn_ref[...].astype(gw_ref.dtype).reshape(PARTS, 64, 512)


def middle(late, rows8, rbup, counts, mixt, tokens, cotangent, rb=512):
    slots = tokens.shape[0]
    rows = pl.BlockSpec((rb, 512), lambda i: (i, 0))
    cols = pl.BlockSpec((512, rb), lambda i: (0, i))
    once = pl.Buffered(1)
    return pl.pallas_call(
        functools.partial(mid_kernel, rb),
        grid=(slots // rb,),
        in_specs=[
            pl.BlockSpec(memory_space=pltpu.SMEM),
            pl.BlockSpec((8, 512), lambda i: (0, 0)),
            pl.BlockSpec((1, 2048), lambda i: (0, 0)),
            pl.BlockSpec((PARTS, LATE, 512), lambda i: (0, 0, 0), pipeline_mode=once),
            cols, rows, rows,
        ],
        out_specs=[
            rows, rows, cols,
            pl.BlockSpec((H, rb), lambda i: (0, i)),
            pl.BlockSpec((PARTS, 144, 512), lambda i: (0, 0, 0), pipeline_mode=once),
            pl.BlockSpec((8, 512), lambda i: (0, 0)),
            pl.BlockSpec((1, 2048), lambda i: (0, 0)),
        ],
        out_shape=[
            jax.ShapeDtypeStruct((slots, 512), BF16),
            jax.ShapeDtypeStruct((slots, 512), F32),
            jax.ShapeDtypeStruct((512, slots), BF16),
            jax.ShapeDtypeStruct((H, slots), F32),
            jax.ShapeDtypeStruct((PARTS, 144, 512), BF16),
            jax.ShapeDtypeStruct((8, 512), F32),
            jax.ShapeDtypeStruct((1, 2048), F32),
        ],
        scratch_shapes=[
            pltpu.VMEM((512, 2048), F32),
            pltpu.VMEM((2048, 512), F32),
            pltpu.VMEM((512, 512), F32),
        ]
        + [pltpu.VMEM((SUB, 2048), BF16), pltpu.VMEM((SUB, 2048), F32), pltpu.VMEM((SUB, 2048), BF16)] * 2,
        compiler_params=params(),
        name="middle",
    )(counts, rows8, rbup, late, mixt, tokens, cotangent)


def split3(value):
    high = value.astype(BF16)
    rest = value - high.astype(F32)
    mid = rest.astype(BF16)
    return high, mid, (rest - mid.astype(F32)).astype(BF16)


def attend_back(
    sure, finish, begin, blocks, qa_ref, ka_ref, va_ref, kmn_ref, km_ref, vmn_ref, do_ref, lse_ref, delta_ref,
    q2_ref, do2_ref, dqa_ref, dka_ref, dva_ref, dkma_ref, dvma_ref, sa_ref, ga_ref, sb_ref, gb_ref,
):
    frow = lax.broadcasted_iota(jnp.int32, (16, BQ), 0)

    def feature(value, at):
        high, mid, low = (jnp.broadcast_to(v.astype(F32), (16, BQ)) for v in split3(value))
        return jnp.where(frow == at, high, jnp.where(frow == at + 1, mid, jnp.where(frow == at + 2, low, 0.0)))

    for h in range(H):
        q2_ref[h, 0:64, :] = qa_ref[h, 0:64, :]
        q2_ref[h, 64:80, :] = (qa_ref[h, 64:80, :].astype(F32) + feature(-lse_ref[h : h + 1, :], 3)).astype(BF16)
        do2_ref[h, 0:64, :] = do_ref[64 * h : 64 * h + 64, :]
        do2_ref[h, 64:80, :] = feature(-delta_ref[h : h + 1, :], 0).astype(BF16)

    def work(new, old):
        kept = {}
        for h in range(H + 1):
            if h < H and new:
                ks = key_slots(begin, new[0])
                new[1][0][h] = dot(ka_ref[h, :, ks], q2_ref[h], 0, 0)
                new[1][1][h] = dot(va_ref[h, :, ks], do2_ref[h], 0, 0)
            if h < H and old:
                p = jnp.exp(old[1][0][h])
                kept[h] = p.astype(BF16), (p * old[1][1][h]).astype(BF16)
            if h > 0 and old:
                ks = key_slots(begin, old[0])
                p, ds = kept.pop(h - 1)
                dva_ref[h - 1, :, ks] += dot(do2_ref[h - 1, 0:64, :], p, 1, 1)
                dka_ref[h - 1, :, ks] += dot(q2_ref[h - 1, 0:64, :], ds, 1, 1)
                dqa_ref[h - 1] += dot(ka_ref[h - 1, 0:64, ks], ds, 1, 0)

    ps = [dot(kmn_ref[h, :, 0:HA], q2_ref[h], 1, 0) for h in range(H)]
    dps = [dot(vmn_ref[h, :, 0:HA], do2_ref[h], 1, 0) for h in range(H)]
    if sure:
        work((0, (sa_ref, ga_ref)), None)
    ps = [jnp.exp(p) for p in ps]
    dss = [(p * dp).astype(BF16) for p, dp in zip(ps, dps)]
    for h in range(H):
        dvma_ref[h, :, 0:MP] += dot(do2_ref[h, 0:64, :], ps[h].astype(BF16), 1, 1)
        dkma_ref[h, :, 0:MP] += dot(q2_ref[h, 0:64, :], dss[h], 1, 1)
        dqa_ref[h] = dot(km_ref[h, 0:64, 0:MP], dss[h], 1, 0)
    pipelined(blocks, work, (sa_ref, ga_ref), (sb_ref, gb_ref), sure, finish)


def bwd_kernel(
    slots, seg_ref, cnt_ref, qa_ref, ka_ref, va_ref, kmn_ref, km_ref, vmn_ref, do_ref, lse_ref, delta_ref,
    dq_ref, dk_ref, dv_ref, dkm_ref, dvm_ref,
    q2_ref, do2_ref, dqa_ref, dka_ref, dva_ref, dkma_ref, dvma_ref, sa_ref, ga_ref, sb_ref, gb_ref, range_ref,
):
    step = pl.program_id(0)

    @pl.when(step == 0)
    def _():
        key_ranges(seg_ref[...], cnt_ref[0], slots, range_ref)
        for ref in (dka_ref, dva_ref, dkma_ref, dvma_ref):
            ref[...] = jnp.zeros_like(ref)

    def finish():
        for h in range(H):
            dq_ref[64 * h : 64 * h + 64, :] = (dqa_ref[h] * HD ** -0.5).astype(BF16)

    attend_back(
        False, finish, range_ref[0, step], range_ref[1, step], qa_ref, ka_ref, va_ref, kmn_ref, km_ref, vmn_ref, do_ref, lse_ref,
        delta_ref, q2_ref, do2_ref, dqa_ref, dka_ref, dva_ref, dkma_ref, dvma_ref, sa_ref, ga_ref, sb_ref, gb_ref,
    )

    @pl.when(step == pl.num_programs(0) - 1)
    def _():
        for h in range(H):
            s = slice(64 * h, 64 * h + 64)
            dk_ref[s, :] = dka_ref[h].astype(BF16)
            dv_ref[s, :] = dva_ref[h].astype(BF16)
            dkm_ref[s, :] = dkma_ref[h].astype(BF16)
            dvm_ref[s, :] = dvma_ref[h].astype(BF16)


def attend_backward(seg2, counts, qa, ka, va, kmn, km, vmn, mgrad, lse, delta):
    slots = qa.shape[2]
    once = pl.Buffered(1)

    def full(a):
        return pl.BlockSpec(a.shape, lambda i: (0, 0, 0), pipeline_mode=once)

    cols = pl.BlockSpec((512, BQ), lambda i: (0, i))
    stat = pl.BlockSpec((H, BQ), lambda i: (0, i))
    whole = pl.BlockSpec((512, slots), lambda i: (0, 0), pipeline_mode=once)
    mwhole = pl.BlockSpec((512, 128), lambda i: (0, 0))
    block = pltpu.VMEM((H, BK, BQ), F32)
    return pl.pallas_call(
        functools.partial(bwd_kernel, slots),
        grid=(slots // BQ,),
        in_specs=[
            pl.BlockSpec(seg2.shape, lambda i: (0, 0)),
            pl.BlockSpec(memory_space=pltpu.SMEM),
            pl.BlockSpec((H, HA, BQ), lambda i: (0, 0, i)),
            full(ka), full(va), full(kmn), full(km), full(vmn), cols, stat, stat,
        ],
        out_specs=[cols, whole, whole, mwhole, mwhole],
        out_shape=[jax.ShapeDtypeStruct((512, slots), BF16)] * 3 + [jax.ShapeDtypeStruct((512, 128), BF16)] * 2,
        scratch_shapes=[
            pltpu.VMEM((H, HA, BQ), BF16),
            pltpu.VMEM((H, HA, BQ), BF16),
            pltpu.VMEM((H, HD, BQ), F32),
            pltpu.VMEM((H, HD, slots), F32),
            pltpu.VMEM((H, HD, slots), F32),
            pltpu.VMEM((H, HD, 128), F32),
            pltpu.VMEM((H, HD, 128), F32),
            block, block, block, block,
            pltpu.SMEM((2, slots // BQ), jnp.int32),
        ],
        compiler_params=params(),
        name="attend_backward",
    )(seg2, counts, qa, ka, va, kmn, km, vmn, mgrad, lse, delta)


SUM_EARLY = (
    (slice(0, 48), "yxz"),
    (slice(48, 96), "xyz"),
    (slice(96, 112), "xzy"),
    (slice(112, 144), "yzx"),
)
SUM_LATE = ((slice(144, 160), "xyz"), (slice(160, 176), "yxz"), (slice(176, 192), "xyz"), (slice(192, 208), "yxz"))
SUM_PARTS = SUM_EARLY + SUM_LATE
SUM_COPIES = 6 * len(SUM_PARTS)


def weight_grads(step, tok_ref, dq_ref, dk_ref, dv_ref, dkm_ref, dvm_ref, memt_ref, acc_ref, sum_ref):
    @pl.when(step == 0)
    def _():
        acc_ref[0:512, :] = jnp.zeros((512, 512), F32)
        acc_ref[512:1024, :] = dot(dkm_ref[...], memt_ref[...], 1, 1)
        acc_ref[1024:1536, :] = dot(dvm_ref[...], memt_ref[...], 1, 1)
        sum_ref[...] = jnp.zeros_like(sum_ref)
        sum_ref[:, 1:2] = jnp.sum(dvm_ref[...].astype(F32), axis=1, keepdims=True)

    tok = tok_ref[...]
    dq, dk, dv = dq_ref[...], dk_ref[...], dv_ref[...]
    acc_ref[0:512, :] += dot(dq, tok, 1, 0)
    acc_ref[512:1024, :] += dot(dk, tok, 1, 0)
    acc_ref[1024:1536, :] += dot(dv, tok, 1, 0)
    sum_ref[:, 0:1] += jnp.sum(dq.astype(F32), axis=1, keepdims=True)
    sum_ref[:, 1:2] += jnp.sum(dv.astype(F32), axis=1, keepdims=True)


def matrix_grad(j, acc_ref):
    return acc_ref[512 * j : 512 * j + 512, :].T.astype(BF16)


def small_grads(dkm_ref, dvm_ref, vec_ref, bup_ref, wt_ref, sum_ref, late):
    gmem = dot(wt_ref[512:1024, :], dkm_ref[...], 0, 0) + dot(wt_ref[1024:1536, :], dvm_ref[...], 0, 0)
    late(slice(48, 64), slice(0, 128), gmem.astype(BF16))
    lane = lax.broadcasted_iota(jnp.int32, (512, 128), 1)
    vecs = jnp.concatenate([vec_ref[...], jnp.zeros((120, 512), F32)], axis=0).T
    late(slice(48, 64), slice(128, 256), jnp.where(lane < 2, sum_ref[...], vecs).astype(BF16))
    rows = [bup_ref[0:1, 256 * v : 256 * v + 256] for v in range(8)] + [jnp.zeros((8, 256), F32)]
    rows = jnp.concatenate(rows, axis=0).astype(BF16)
    late(slice(48, 64), slice(256, 512), jnp.broadcast_to(rows[None], (PARTS, 16, 256)).reshape(512, 256))


def token_grads(gtok_ref, gfirst_ref, dq_ref, dk_ref, dv_ref, wt_ref):
    gtok_ref[...] = (
        gfirst_ref[...]
        + dot(dq_ref[...], wt_ref[0:512, :], 0, 0)
        + dot(dk_ref[...], wt_ref[512:1024, :], 0, 0)
        + dot(dv_ref[...], wt_ref[1024:1536, :], 0, 0)
    )


def scatter_kernel(
    blocks, qa_ref, ka_ref, va_ref, kmn_ref, km_ref, vmn_ref, do_ref, lse_ref, delta_ref,
    tok_hbm, gfirst_ref, vec_ref, bup_ref, wt_hbm, memt_ref, early_ref, gtok_ref, out_ref,
    q2_ref, do2_ref, dqa_ref, dka_ref, dva_ref, dkma_ref, dvma_ref, sa_ref, ga_ref, sb_ref, gb_ref,
    dq_ref, dk_ref, dv_ref, dkm_ref, dvm_ref,
    tok_ref, wt_ref, acc_ref, sum_ref, late, parts_sum, other, send, recv, local, fetch, *landing,
):
    step = pl.program_id(0)
    place = Place()
    copies = Copies(send, recv)
    slots = dict(zip(slot_shapes(SUM_PARTS), landing))
    crossing = [copies.number() for _ in SUM_PARTS]
    parts = []
    for index, (rows, order) in enumerate(SUM_PARTS):
        mine = {key[1:]: slot for key, slot in slots.items() if key[0] == index}
        parts.append(scatter_part(place, copies, parts_sum, mine, out_ref, rows, order))
    firsts, lasts = parts[: len(SUM_EARLY)], parts[len(SUM_EARLY) :]

    def load(index):
        rows = SUM_EARLY[index][0]
        return pltpu.make_async_copy(
            early_ref.at[:, :, :, place.core, rows], parts_sum.at[:, :, :, rows], local.at[index]
        )

    def fetches():
        return (
            pltpu.make_async_copy(tok_hbm, tok_ref, fetch.at[0]),
            pltpu.make_async_copy(wt_hbm, wt_ref, fetch.at[1]),
        )

    def cross(source, base, rows, number):
        old = slice(rows.start - base, rows.stop - base)
        copies.start(
            lambda: source.at[:, :, :, place.far, old], lambda: other.at[:, :, :, rows], number, place.partner
        )

    @pl.when(step == 0)
    def _():
        place.greet()
        for copy in fetches():
            copy.start()
        for index in range(len(SUM_EARLY)):
            load(index).start()
        for ref in (dka_ref, dva_ref, dkma_ref, dvma_ref, sum_ref):
            ref[...] = jnp.zeros_like(ref)

    @pl.when(step < blocks)
    def _():
        reach = LONGEST // BQ
        begin = jnp.maximum(step - reach, 0)
        end = jnp.minimum(step + reach + 1, blocks)
        here = pl.ds(pl.multiple_of(step * BQ, BQ), BQ)

        def finish():
            for h in range(H):
                dq_ref[64 * h : 64 * h + 64, here] = (dqa_ref[h] * HD ** -0.5).astype(BF16)

        attend_back(
            True, finish, begin * (BQ // 128), (end - begin) * (BQ // BK), qa_ref, ka_ref, va_ref, kmn_ref, km_ref, vmn_ref,
            do_ref, lse_ref, delta_ref, q2_ref, do2_ref, dqa_ref, dka_ref, dva_ref, dkma_ref, dvma_ref,
            sa_ref, ga_ref, sb_ref, gb_ref,
        )

    @pl.when(step == 0)
    def _():
        for copy in fetches():
            copy.wait()
        place.met()
        for number, (rows, _) in zip(crossing, SUM_EARLY):
            cross(early_ref, 0, rows, number)

    @pl.when(step == 1)
    def _():
        for index, (rows, _) in enumerate(SUM_EARLY):
            load(index).wait()
            join(place, copies, parts_sum, None, other, rows, crossing[index])
            next(firsts[index])

    @pl.when(step == 3)
    def _():
        advance(firsts)

    @pl.when(step == 5)
    def _():
        advance(firsts)

    @pl.when(step == blocks - 1)
    def _():
        advance(firsts)

    def put(rows, lanes, value):
        late[:, :, :, :, rows, lanes] = value.reshape(4, 2, 2, 2, 16, value.shape[1])

    def depart(index):
        cross(late, LATE, SUM_LATE[index][0], crossing[len(SUM_EARLY) + index])

    def onward(index):
        rows = SUM_LATE[index][0]
        old = slice(rows.start - LATE, rows.stop - LATE)
        join(
            place, copies, parts_sum, lambda z: late[z, :, :, place.core, old], other, rows,
            crossing[len(SUM_EARLY) + index],
        )
        next(lasts[index])

    @pl.when(step == blocks)
    def _():
        tok = tok_ref[...]
        acc_ref[0:512, :] = dot(dq_ref[...], tok, 1, 0)
        put(slice(0, 16), slice(0, 512), matrix_grad(0, acc_ref))
        depart(0)
        for j, whole, part, memory, memory_part in (
            (1, dka_ref, dk_ref, dkma_ref, dkm_ref),
            (2, dva_ref, dv_ref, dvma_ref, dvm_ref),
        ):
            for h in range(H):
                s = slice(64 * h, 64 * h + 64)
                part[s, :] = whole[h].astype(BF16)
                memory_part[s, :] = memory[h].astype(BF16)
            acc_ref[512 * j : 512 * j + 512, :] = dot(part[...], tok, 1, 0) + dot(
                memory_part[...], memt_ref[...], 1, 1
            )
            put(slice(16 * j, 16 * j + 16), slice(0, 512), matrix_grad(j, acc_ref))
            depart(j)
            onward(j - 1)
        sum_ref[:, 0:1] = jnp.sum(dq_ref[...].astype(F32), axis=1, keepdims=True)
        sum_ref[:, 1:2] = jnp.sum(dv_ref[...].astype(F32), axis=1, keepdims=True) + jnp.sum(
            dvm_ref[...].astype(F32), axis=1, keepdims=True
        )
        small_grads(dkm_ref, dvm_ref, vec_ref, bup_ref, wt_ref, sum_ref, put)
        depart(3)
        onward(2)

    @pl.when(step > blocks)
    def _():
        rows = gtok_ref.shape[0]
        here = pl.ds(pl.multiple_of((step - blocks - 1) * rows, 128), rows)
        token_grads(gtok_ref, gfirst_ref, dq_ref.at[:, here], dk_ref.at[:, here], dv_ref.at[:, here], wt_ref)

    @pl.when(step == blocks + 1)
    def _():
        onward(3)

    @pl.when(step == blocks + 2)
    def _():
        advance(lasts[0:2])

    @pl.when(step == blocks + 3)
    def _():
        advance(lasts[2:4])

    @pl.when(step == pl.num_programs(0) - 1)
    def _():
        advance(lasts)
        advance(lasts)
        copies.finish()


def backward(seg2, counts, early, tokens, qa, ka, va, kmn, km, vmn, mgrad, lse, delta, gfirst, vec, bup, wt, memt, remote):
    if not remote:
        dq, dk, dv, dkm, dvm = attend_backward(seg2, counts, qa, ka, va, kmn, km, vmn, mgrad, lse, delta)
        return tail(tokens, dq, dk, dv, dkm, dvm, gfirst, vec, bup, wt, memt)
    slots = tokens.shape[0]
    rb = 512
    blocks = slots // BQ
    once = pl.Buffered(1)

    def full(a):
        return pl.BlockSpec(a.shape, lambda i: (0,) * len(a.shape), pipeline_mode=once)

    def at(i):
        return jnp.minimum(i, blocks - 1)

    later = pl.BlockSpec((rb, 512), lambda i: (jnp.maximum(i - blocks - 1, 0), 0))
    stat = pl.BlockSpec((H, BQ), lambda i: (0, at(i)))
    score = pltpu.VMEM((H, BK, BQ), F32)
    hbm = pl.BlockSpec(memory_space=pl.ANY)
    return pl.pallas_call(
        functools.partial(scatter_kernel, blocks),
        grid=(blocks + 1 + slots // rb,),
        in_specs=[
            pl.BlockSpec((H, HA, BQ), lambda i: (0, 0, at(i))),
            full(ka), full(va), full(kmn), full(km), full(vmn),
            pl.BlockSpec((512, BQ), lambda i: (0, at(i))), stat, stat,
            hbm, later, full(vec), full(bup), hbm, full(memt),
            hbm,
        ],
        out_specs=[later, fixed(ROWS, 512)],
        out_shape=[jax.ShapeDtypeStruct((slots, 512), F32), jax.ShapeDtypeStruct((ROWS, 512), F32)],
        scratch_shapes=[
            pltpu.VMEM((H, HA, BQ), BF16),
            pltpu.VMEM((H, HA, BQ), BF16),
            pltpu.VMEM((H, HD, BQ), F32),
            pltpu.VMEM((H, HD, slots), F32),
            pltpu.VMEM((H, HD, slots), F32),
            pltpu.VMEM((H, HD, 128), F32),
            pltpu.VMEM((H, HD, 128), F32),
            score, score, score, score,
            pltpu.VMEM((512, slots), BF16),
            pltpu.VMEM((512, slots), BF16),
            pltpu.VMEM((512, slots), BF16),
            pltpu.VMEM((512, 128), BF16),
            pltpu.VMEM((512, 128), BF16),
            pltpu.VMEM(tokens.shape, BF16),
            pltpu.VMEM(wt.shape, BF16),
            pltpu.VMEM((1536, 512), F32),
            pltpu.VMEM((512, 128), F32),
            pltpu.VMEM((4, 2, 2, 2, EARLY, 512), BF16),
            pltpu.VMEM((4, 2, 2, ROWS, 512), BF16),
            pltpu.VMEM((4, 2, 2, ROWS, 512), BF16),
            pltpu.SemaphoreType.DMA((SUM_COPIES,)),
            pltpu.SemaphoreType.DMA((SUM_COPIES,)),
            pltpu.SemaphoreType.DMA((len(SUM_EARLY),)),
            pltpu.SemaphoreType.DMA((2,)),
        ]
        + [pltpu.VMEM(shape, BF16) for shape in slot_shapes(SUM_PARTS).values()],
        compiler_params=params(collective_id=1, has_side_effects=True),
        name="backward_scatter",
    )(
        qa, ka, va, kmn, km, vmn, mgrad, lse, delta, tokens, gfirst, vec, bup, wt, memt,
        early.reshape(4, 2, 2, 2, LATE, 512),
    )


def plain_kernel(
    half, tok_ref, dq_ref, dk_ref, dv_ref, dkm_ref, dvm_ref, gfirst_ref, vec_ref, bup_ref, wt_ref, memt_ref,
    gtok_ref, late_ref, acc_ref, sum_ref,
):
    step = pl.program_id(0)

    @pl.when(step < half)
    def _():
        weight_grads(step, tok_ref, dq_ref, dk_ref, dv_ref, dkm_ref, dvm_ref, memt_ref, acc_ref, sum_ref)

    @pl.when(step == half - 1)
    def _():
        def put(rows, lanes, value):
            late_ref[:, rows, lanes] = value.reshape(PARTS, 16, value.shape[1])

        for j in range(3):
            put(slice(16 * j, 16 * j + 16), slice(0, 512), matrix_grad(j, acc_ref))
        small_grads(dkm_ref, dvm_ref, vec_ref, bup_ref, wt_ref, sum_ref, put)

    @pl.when(step >= half)
    def _():
        token_grads(gtok_ref, gfirst_ref, dq_ref, dk_ref, dv_ref, wt_ref)


def tail(tokens, dq, dk, dv, dkm, dvm, gfirst, vec, bup, wt, memt):
    slots = tokens.shape[0]
    rb = 512
    half = slots // rb
    cols = pl.BlockSpec((512, rb), lambda i: (0, i % half))
    later = pl.BlockSpec((rb, 512), lambda i: (jnp.maximum(i - half, 0), 0))
    return pl.pallas_call(
        functools.partial(plain_kernel, half),
        grid=(2 * half,),
        in_specs=[
            pl.BlockSpec((rb, 512), lambda i: (jnp.minimum(i, half - 1), 0)),
            cols, cols, cols, fixed(512, 128), fixed(512, 128), later,
            fixed(8, 512), fixed(1, 2048), fixed(1536, 512), fixed(512, 128),
        ],
        out_specs=[later, fixed(PARTS, EARLY, 512)],
        out_shape=[jax.ShapeDtypeStruct((slots, 512), F32), jax.ShapeDtypeStruct((PARTS, EARLY, 512), BF16)],
        scratch_shapes=[pltpu.VMEM((1536, 512), F32), pltpu.VMEM((512, 128), F32)],
        compiler_params=params(),
        name="tail",
    )(tokens, dq, dk, dv, dkm, dvm, gfirst, vec, bup, wt, memt)


def unpack_kernel(sum_hbm, part_ref, gtok_ref, wo, up, dn, wq, wk, wv, memory, b_up, *rest):
    vectors, (sum_ref, block, ready, arrive, leave) = rest[:8], rest[8:]
    count = arrive.shape[0]
    rows = block.shape[0] // count
    spans = [slice(rows * k, rows * k + rows) for k in range(count)]
    loads = [pltpu.make_async_copy(part_ref.at[s], block.at[s], arrive.at[k]) for k, s in enumerate(spans)]
    stores = [pltpu.make_async_copy(block.at[s], gtok_ref.at[s], leave.at[k]) for k, s in enumerate(spans)]
    sums = pltpu.make_async_copy(sum_hbm, sum_ref, ready)
    sums.start()
    for load in loads:
        load.start()
    me = lax.axis_index("dp")
    sums.wait()
    wo[...] = sum_ref[0:16]
    for c in range(4):
        up[:, 512 * c : 512 * c + 512] = sum_ref[16 + 16 * c : 32 + 16 * c]
    dn[...] = sum_ref[80:144]
    wq[...] = sum_ref[144:160]
    wk[...] = sum_ref[160:176]
    wv[...] = sum_ref[176:192]
    memory[...] = sum_ref[192:208, 0 : memory.shape[1]]
    turned = sum_ref[192:208, 128:256].T
    for index, vector in enumerate(vectors):
        vector[...] = turned[index : index + 1, :]
    row = lax.broadcasted_iota(jnp.int32, (16, 256), 0)
    lane = lax.broadcasted_iota(jnp.int32, (16, 256), 1)
    own = jnp.sum(jnp.where(row * 4 + lane // 64 == me, sum_ref[192:208, 256:512], 0.0), axis=0, keepdims=True)
    b_up[...] = own[:, 0:64] + own[:, 64:128] + own[:, 128:192] + own[:, 192:256]
    for load, store in zip(loads, stores):
        load.wait()
        store.start()
    for store in stores:
        store.wait()


def unpack(sums, part, mem_rows):
    shapes = [(16, 512), (16, 2048), (64, 512), (16, 512), (16, 512), (16, 512), (16, mem_rows), (1, 64)] + [(1, 16)] * 8
    found = pl.pallas_call(
        unpack_kernel,
        in_specs=[pl.BlockSpec(memory_space=pl.ANY)] * 2,
        out_specs=[pl.BlockSpec(memory_space=pl.ANY)] + [pl.BlockSpec(memory_space=pltpu.VMEM)] * len(shapes),
        out_shape=[jax.ShapeDtypeStruct(s, F32) for s in [part.shape] + shapes],
        scratch_shapes=[
            pltpu.VMEM(sums.shape, F32),
            pltpu.VMEM(part.shape, F32),
            pltpu.SemaphoreType.DMA,
            pltpu.SemaphoreType.DMA((4,)),
            pltpu.SemaphoreType.DMA((4,)),
        ],
        compiler_params=params(),
        name="unpack",
    )(sums, part)
    gtok, found = found[0], found[1:]
    out = dict(zip(("w_out", "w_up", "w_down", "w_query", "w_key", "w_value", "memory"), found[:7]))
    out["memory"] = out["memory"].T
    out["b_up"] = found[7].reshape(64)
    for name, value in zip(VECTORS, found[8:]):
        out[name] = value.reshape(16)
    return gtok, out


NAMES = (
    "memory", "w_query", "b_query", "w_key", "w_value", "b_value", "w_out", "b_out", "gain_attn",
    "shift_attn", "w_up", "b_up", "w_down", "b_down", "gain_ffn", "shift_ffn",
)


def pack_whole(p):
    mem_rows = p["memory"].shape[0]
    mats = [p[name].reshape(PARTS, 16, 512) for name in ("w_query", "w_key", "w_value", "w_out")]
    up = p["w_up"].reshape(PARTS, 16, 4, 512).transpose(0, 2, 1, 3).reshape(PARTS, 64, 512)
    memory = jnp.pad(p["memory"].T, ((0, 0), (0, 128 - mem_rows))).reshape(PARTS, 16, 128)
    vectors = jnp.stack([p[name] for name in VECTORS], axis=1)
    vectors = jnp.pad(vectors, ((0, 0), (0, 120))).reshape(PARTS, 16, 128)
    own = jnp.arange(2048)[None] // 64 == jnp.arange(PARTS)[:, None]
    b_up = jnp.where(own, p["b_up"][None], 0).astype(BF16).reshape(PARTS, 8, 256)
    b_up = jnp.pad(b_up, ((0, 0), (0, 8), (0, 0)))
    small = jnp.concatenate([memory, vectors, b_up], axis=2)
    return jnp.concatenate(mats[:3] + [small, up, p["w_down"].reshape(PARTS, 64, 512), mats[3]], axis=1)


def unpack_whole(early, late, mem_rows):
    small = late[:, 48:64]
    vectors = small[:, :, 128:136].reshape(512, 8)
    out = {
        "memory": small[:, :, 0:mem_rows].reshape(512, mem_rows).T,
        "w_query": late[:, 0:16].reshape(512, 512),
        "w_key": late[:, 16:32].reshape(512, 512),
        "w_value": late[:, 32:48].reshape(512, 512),
        "w_out": early[:, 0:16].reshape(512, 512),
        "w_up": early[:, 16:80].reshape(PARTS, 4, 16, 512).transpose(0, 2, 1, 3).reshape(512, 2048),
        "w_down": early[:, 80:144].reshape(2048, 512),
        "b_up": small[0, 0:8, 256:512].reshape(2048),
    }
    for index, name in enumerate(VECTORS):
        out[name] = vectors[:, index]
    return out


def axis_of(name):
    return 1 if name == "memory" else 0


def shards(n, tokens, segment, counts, *rest):
    p = dict(zip(NAMES, rest[:-1]))
    cotangent = rest[-1]
    slots = tokens.shape[0]
    mem_rows = p["memory"].shape[0]
    whole = None
    if n != PARTS:
        whole = pack_whole({k: lax.all_gather(v, "dp", axis=axis_of(k), tiled=True) for k, v in p.items()})
    found = projections(p, whole, tokens, segment, counts, mem_rows)
    late, qa, ka, va, km, kmn, vmn, wt, memt, rows8, rbup, mixt, lse = found
    seg2 = segment.reshape(slots // 128, 128)
    output, gfirst, mgrad, delta, early, vec, bup = middle(late, rows8, rbup, counts, mixt, tokens, cotangent)
    gtok, sums = backward(
        seg2, counts, early, tokens, qa, ka, va, kmn, km, vmn, mgrad, lse, delta, gfirst, vec, bup, wt, memt, n == PARTS
    )
    if n == PARTS:
        gtok, grads = unpack(sums, gtok, mem_rows)
    else:
        full = unpack_whole(early.astype(F32), sums.astype(F32), mem_rows)
        grads = {
            k: lax.psum_scatter(v, "dp", scatter_dimension=axis_of(k), tiled=True) for k, v in full.items()
        }
    return (output, gtok) + tuple(grads[name] for name in NAMES)


def solution(mesh):
    n = mesh.shape["dp"]
    row, mat, mem = P("dp"), P("dp", None), P(None, "dp")
    spec = {name: mat if name.startswith("w_") else row for name in NAMES}
    spec["memory"] = mem
    weights = tuple(spec[name] for name in NAMES)
    return jax.shard_map(
        functools.partial(shards, n),
        mesh=mesh,
        in_specs=(mat, row, row) + weights + (mat,),
        out_specs=(mat, mat) + weights,
        check_vma=False,
    )
```

```python
import functools
import jax
import jax.numpy as jnp
from jax import lax
from jax.experimental import pallas as pl
from jax.experimental.pallas import tpu as pltpu
from jax.sharding import PartitionSpec as P

H = 8
HD = 64
HA = 80
EPS = 1e-05
BIG = 1e30
PARTS = 32
ROWS = 208
BQ = 256
BK = 256
MP = 32
LONGEST = 1024
F32 = jnp.float32
BF16 = jnp.bfloat16
VMEM_LIMIT = 60 << 20

V_BQ, V_BV, V_BO, V_GA, V_SA, V_BD, V_GF, V_SF = range(8)


def dot(left, right, lc, rc):
    return lax.dot_general(left, right, (((lc,), (rc,)), ((), ())), preferred_element_type=F32)


def params(**kw):
    return pltpu.CompilerParams(vmem_limit_bytes=VMEM_LIMIT, **kw)


MESH = pl.DeviceIdType.MESH
AXES = {"z": (8, 4), "y": (4, 2), "x": (2, 2)}
LAYOUT = ("z", "y", "x")


class Place:
    def __init__(self):
        me = lax.axis_index("dp")
        self.me = me
        self.core = me % 2
        self.far = 1 - self.core
        self.partner = me + 1 - 2 * self.core
        self.at = {a: (me // stride) % length for a, (stride, length) in AXES.items()}
        self.mine = tuple(self.at[a] for a in LAYOUT)
        self.others = {}
        for axis, (stride, length) in AXES.items():
            for distance in range(1, length):
                j = (self.at[axis] + distance) % length
                self.others[axis, distance] = j, me + (j - self.at[axis]) * stride
        self.peers = [self.partner] + [device for _, device in self.others.values()]

    def other(self, axis, distance):
        return self.others[axis, distance]

    def greet(self):
        for peer in self.peers:
            pl.semaphore_signal(
                pltpu.get_barrier_semaphore(), inc=1, device_id=(peer,), device_id_type=MESH
            )

    def met(self):
        pl.semaphore_wait(pltpu.get_barrier_semaphore(), len(self.peers))


class Copies:
    def __init__(self, send, recv):
        self.send, self.recv, self.count, self.open = send, recv, 0, []

    def number(self):
        self.count += 1
        return self.count - 1

    def make(self, src, dst, number, device):
        return pltpu.make_async_remote_copy(
            src_ref=src, dst_ref=dst, send_sem=self.send.at[number], recv_sem=self.recv.at[number],
            device_id=(device,), device_id_type=MESH,
        )

    def start(self, src, dst, number, device):
        self.make(src(), dst(), number, device).start()
        self.open.append((src, dst, number, device))

    def landed(self, block, number, device):
        self.make(block, block, number, device).wait_recv()

    def finish(self):
        for src, dst, number, device in self.open:
            self.make(src(), dst(), number, device).wait_send()
        self.open = []


def gather_part(place, copies, own, base, whole, rows, order, arrivals):
    done = ()

    def mine():
        return own.at[slice(base + rows.start, base + rows.stop)]

    def block(axis, j, core):
        index = tuple(j if a == axis else (slice(None) if a in done else place.at[a]) for a in LAYOUT)
        return lambda: whole.at[index + (core, rows)]

    for axis in order:
        length = AXES[axis][1]
        numbers = [copies.number() for _ in range(2 * length - 2)]
        here = block(axis, place.at[axis], place.core)
        for d in range(1, length):
            copies.start(here if done else mine, here, numbers[d - 1], place.other(axis, d)[1])
        if not done:
            number = copies.number()
            copies.start(mine, here, number, place.partner)
            arrivals.append((block(axis, place.at[axis], place.far), number))
        yield
        for d in range(1, length):
            j, device = place.other(axis, length - d)
            there = block(axis, j, place.core)
            copies.landed(there(), numbers[d - 1], device)
            number = numbers[length - 2 + d]
            copies.start(there, there, number, place.partner)
            arrivals.append((block(axis, j, place.far), number))
        done += (axis,)
    yield


def advance(parts):
    for part in parts:
        next(part)


def scatter_part(place, copies, acc, slots, out, rows, order):
    done = ()

    def block(axis, j):
        index = tuple(j if a == axis else (place.at[a] if a in done else slice(None)) for a in LAYOUT)
        return index + (rows,)

    def taken(index):
        return lambda: acc.at[index]

    def landing(axis, d):
        return lambda: slots[axis, d]

    for axis in order:
        length = AXES[axis][1]
        numbers = [copies.number() for _ in range(length - 1)]
        for d in range(1, length):
            j, device = place.other(axis, d)
            copies.start(taken(block(axis, j)), landing(axis, d), numbers[d - 1], device)
        yield
        for d in range(1, length):
            copies.landed(slots[axis, d], numbers[d - 1], place.partner)
        mine = block(axis, place.at[axis])
        total = acc[mine].astype(F32)
        for d in range(1, length):
            total = total + slots[axis, d][...].astype(F32)
        if axis == order[-1]:
            out[rows, :] = total
        else:
            acc[mine] = total.astype(BF16)
        done += (axis,)
    yield


def slot_shapes(parts):
    shapes = {}
    for number, (rows, order) in enumerate(parts):
        left = ["z", "y", "x"]
        for axis in order:
            left.remove(axis)
            shape = tuple(AXES[a][1] for a in LAYOUT if a in left) + (rows.stop - rows.start, 512)
            for d in range(1, AXES[axis][1]):
                shapes[number, axis, d] = shape
    return shapes


def join(place, copies, acc, source, other, rows, number):
    copies.landed(other.at[:, :, :, rows], number, place.partner)

    @pl.loop(0, 4)
    def _(z):
        mine = source(z) if source else acc[z, :, :, rows]
        acc[z, :, :, rows] = (mine.astype(F32) + other[z, :, :, rows].astype(F32)).astype(BF16)


VECTORS = ("b_query", "b_value", "b_out", "gain_attn", "shift_attn", "b_down", "gain_ffn", "shift_ffn")
EARLY = 64
LATE = 144
EARLY_PARTS = ((slice(0, 16), "zxy"), (slice(16, 32), "zyx"), (slice(32, 48), "zxy"), (slice(48, 64), "zyx"))
LATE_PARTS = (
    (slice(0, 48), "zxy"),
    (slice(48, 96), "zyx"),
    (slice(96, 128), "yzx"),
    (slice(128, 144), "xzy"),
)
GATHER_COPIES = 11 * (len(EARLY_PARTS) + len(LATE_PARTS))


def head_block(rows, features):
    block = jnp.concatenate([rows, features], axis=0)
    return block, jnp.concatenate([block, jnp.zeros((128 - HA, rows.shape[1]), BF16)], axis=0).T


def pack(own, place, wq, wk, wv, wo, up, dn, memory, b_up, vectors):
    own[0:16] = wq[...]
    own[16:32] = wk[...]
    own[32:48] = wv[...]
    own[48:64] = jnp.zeros((16, 512), BF16)
    own[48:64, 0 : memory.shape[1]] = memory[...]
    values = jnp.concatenate([vector[...].astype(F32) for vector in vectors], axis=0)
    own[48:64, 128:136] = values.T.astype(BF16)
    value = jnp.concatenate([b_up[...].astype(F32)] * 4, axis=1)
    row = lax.broadcasted_iota(jnp.int32, (16, 256), 0)
    lane = lax.broadcasted_iota(jnp.int32, (16, 256), 1)
    own[48:64, 256:512] = jnp.where(row * 4 + lane // 64 == place.me, value, 0.0).astype(BF16)
    for c in range(4):
        own[64 + 16 * c : 80 + 16 * c] = up[:, 512 * c : 512 * c + 512]
    own[128:192] = dn[...]
    own[192:208] = wo[...]


def prepare(mem_rows, early, wt_ref, memt_ref, rows_ref, rbup_ref, bias_ref, km_ref, vm_ref, kmn_ref, vmn_ref):
    for j in range(3):
        wt_ref[512 * j : 512 * j + 512, :] = early[..., 16 * j : 16 * j + 16, :].reshape(512, 512).T
    small = early[..., 48:64, 0:256].reshape(512, 256)
    memt = small[:, 0:128]
    memt_ref[...] = memt
    vectors = small[:, 128:256].astype(F32)
    bias_ref[...] = vectors
    rows_ref[...] = vectors.T[0:8, :]
    bup = jnp.sum(early[..., 48:64, 256:512].reshape(PARTS, 16, 256).astype(F32), axis=0)
    for v in range(8):
        rbup_ref[0:1, 256 * v : 256 * v + 256] = bup[v : v + 1, :]
    bv = vectors[:, V_BV : V_BV + 1]
    km = dot(wt_ref[512:1024, :], memt, 1, 0).astype(BF16)
    vm = (dot(wt_ref[1024:1536, :], memt, 1, 0) + bv).astype(BF16)
    frow = lax.broadcasted_iota(jnp.int32, (16, 128), 0)
    lane = lax.broadcasted_iota(jnp.int32, (16, 128), 1)
    kf = jnp.where(frow < 3, jnp.where(lane < mem_rows, 0.0, 1.0), jnp.where(frow < 6, 1.0, 0.0)).astype(BF16)
    vf = jnp.where(frow < 3, 1.0, 0.0).astype(BF16)
    for h in range(H):
        km_ref[h], turned = head_block(km[64 * h : 64 * h + 64, :], kf)
        kmn_ref[h] = turned[0:MP]
        vm_ref[h], turned = head_block(vm[64 * h : 64 * h + 64, :], vf)
        vmn_ref[h] = turned[0:MP]


def project(step, tok_ref, seg_ref, cnt_ref, wt_ref, bias_ref, qa_ref, ka_ref, va_ref):
    rows = tok_ref.shape[0]
    tok = tok_ref[...]
    bq = bias_ref[:, V_BQ : V_BQ + 1]
    bv = bias_ref[:, V_BV : V_BV + 1]
    q = (dot(wt_ref[0:512, :], tok, 1, 1) + bq).astype(BF16) * jnp.asarray(HD ** -0.5, BF16)
    k = dot(wt_ref[512:1024, :], tok, 1, 1).astype(BF16)
    v = (dot(wt_ref[1024:1536, :], tok, 1, 1) + bv).astype(BF16)
    frow = lax.broadcasted_iota(jnp.int32, (16, rows), 0)
    seg = jnp.broadcast_to(seg_ref[...], (16, rows))
    pos = lax.broadcasted_iota(jnp.int32, (16, rows), 1) + step * rows
    valid = pos < cnt_ref[0]
    qf = jnp.where((frow < 3) & (frow != seg), -BIG, 0.0).astype(BF16)
    kf = jnp.where(frow < 3, jnp.where(valid & (frow != seg), 0.0, 1.0), jnp.where(frow < 6, 1.0, 0.0)).astype(BF16)
    vf = jnp.where(frow < 3, 1.0, 0.0).astype(BF16)
    for h in range(H):
        s = slice(64 * h, 64 * h + 64)
        qa_ref[h, 0:64, :] = q[s]
        qa_ref[h, 64:80, :] = qf
        ka_ref[h, 0:64, :] = k[s]
        ka_ref[h, 64:80, :] = kf
        va_ref[h, 0:64, :] = v[s]
        va_ref[h, 64:80, :] = vf


def gather_kernel(
    mem_rows, half, wq, wk, wv, wo, up, dn, memory, b_up, v0, v1, v2, v3, v4, v5, v6, v7, tok_ref, seg_ref, cnt_ref,
    late_ref, qa_ref, ka_ref, va_ref, km_ref, kmn_ref, vmn_ref,
    wt_ref, memt_ref, rows_ref, rbup_ref, mix_ref, lse_ref,
    own, early, bias_ref, vm_ref, qa_all, ka_all, va_all, acc_ref, m_ref, sa_ref, sb_ref, send, recv, local,
):
    step = pl.program_id(0)
    slots = ka_all.shape[2]
    place = Place()
    copies = Copies(send, recv)
    arrivals, late_arrivals = [], []
    firsts = [gather_part(place, copies, own, 0, early, *part, arrivals) for part in EARLY_PARTS]
    lasts = [gather_part(place, copies, own, EARLY, late_ref, *part, late_arrivals) for part in LATE_PARTS]

    @pl.when(step == 0)
    def _():
        place.greet()
        pack(own, place, wq, wk, wv, wo, up, dn, memory, b_up, (v0, v1, v2, v3, v4, v5, v6, v7))
        early[place.mine + (place.core,)] = own[0:EARLY]
        place.met()
        advance(firsts)
        keep = pltpu.make_async_copy(own.at[EARLY:ROWS], late_ref.at[place.mine + (place.core,)], local)
        keep.start()
        advance(firsts)
        advance(firsts)
        keep.wait()
        advance(lasts)
        advance(firsts)
        for block, number in arrivals:
            copies.landed(block(), number, place.partner)
        prepare(
            mem_rows, early, wt_ref, memt_ref, rows_ref, rbup_ref, bias_ref, km_ref, vm_ref, kmn_ref, vmn_ref,
        )

    @pl.when(step < half)
    def _():
        project(step, tok_ref, seg_ref, cnt_ref, wt_ref, bias_ref, qa_ref, ka_ref, va_ref)
        here = pl.ds(pl.multiple_of(step * tok_ref.shape[0], 128), tok_ref.shape[0])
        qa_all[:, :, here] = qa_ref[...]
        ka_all[:, :, here] = ka_ref[...]
        va_all[:, :, here] = va_ref[...]

    @pl.when(step == half - 1)
    def _():
        advance(lasts)

    @pl.when(step >= half)
    def _():
        block = step - half
        reach = LONGEST // BQ
        begin = jnp.maximum(block - reach, 0)
        end = jnp.minimum(block + reach + 1, slots // BQ)
        queries = qa_all.at[:, :, pl.ds(pl.multiple_of(block * BQ, BQ), BQ)]
        attend(
            True, begin * (BQ // 128), (end - begin) * (BQ // BK), queries, ka_all, va_all, kmn_ref, vm_ref, mix_ref, lse_ref,
            acc_ref, m_ref, sa_ref, sb_ref,
        )

    @pl.when(step == half + 2)
    def _():
        advance(lasts)

    @pl.when(step == pl.num_programs(0) - 1)
    def _():
        advance(lasts)
        for block, number in late_arrivals:
            copies.landed(block(), number, place.partner)
        copies.finish()


def project_kernel(
    mem_rows, g_ref, tok_ref, seg_ref, cnt_ref, qa_ref, ka_ref, va_ref, km_ref, vm_ref, kmn_ref, vmn_ref,
    wt_ref, memt_ref, rows_ref, rbup_ref, bias_ref,
):
    step = pl.program_id(0)

    @pl.when(step == 0)
    def _():
        prepare(
            mem_rows, g_ref, wt_ref, memt_ref, rows_ref, rbup_ref, bias_ref, km_ref, vm_ref, kmn_ref, vmn_ref
        )

    project(step, tok_ref, seg_ref, cnt_ref, wt_ref, bias_ref, qa_ref, ka_ref, va_ref)


def fixed(*shape):
    return pl.BlockSpec(shape, lambda i: (0,) * len(shape))


def projections(p, whole, tokens, segment, counts, mem_rows):
    slots = tokens.shape[0]
    rb = 512
    half = slots // rb
    wide = (H, HA, slots)
    mwide, mtall = (H, HA, 128), (H, MP, 128)

    def at(i):
        return jnp.minimum(i, half - 1)

    blk = pl.BlockSpec((H, HA, rb), lambda i: (0, 0, at(i)))
    common = [
        pl.BlockSpec((rb, 512), lambda i: (at(i), 0)),
        pl.BlockSpec((1, rb), lambda i: (0, at(i))),
        pl.BlockSpec(memory_space=pltpu.SMEM),
    ]
    args = (tokens, segment.reshape(1, slots), counts)

    def outs(shapes):
        found = [jax.ShapeDtypeStruct(s, BF16) for s in shapes]
        return found + [jax.ShapeDtypeStruct((8, 512), F32), jax.ShapeDtypeStruct((1, 2048), F32)]

    if whole is not None:
        shapes = outs([wide, wide, wide, mwide, mwide, mtall, mtall, (1536, 512), (512, 128)])
        found = pl.pallas_call(
            functools.partial(project_kernel, mem_rows),
            grid=(half,),
            in_specs=[fixed(PARTS, EARLY, 512)] + common,
            out_specs=[blk, blk, blk] + [fixed(*o.shape) for o in shapes[3:]],
            out_shape=shapes,
            scratch_shapes=[pltpu.VMEM((512, 128), F32)],
            compiler_params=params(),
            name="projections",
        )(whole[:, 0:EARLY], *args)
        qa, ka, va, km, vm, kmn, vmn, wt, memt, rows8, rbup = found
        mixt, lse = attend_forward(segment.reshape(slots // 128, 128), counts, qa, ka, va, kmn, vm)
        return whole[:, EARLY:], qa, ka, va, km, kmn, vmn, wt, memt, rows8, rbup, mixt, lse
    weights = [p[name] for name in ("w_query", "w_key", "w_value", "w_out", "w_up", "w_down")]
    weights += [p["memory"].T, p["b_up"].reshape(1, 64)] + [p[name].reshape(1, 16) for name in VECTORS]
    shapes = outs([wide, wide, wide, mwide, mtall, mtall, (1536, 512), (512, 128)])
    found = pl.pallas_call(
        functools.partial(gather_kernel, mem_rows, half),
        grid=(half + slots // BQ,),
        in_specs=[fixed(*w.shape) for w in weights] + common,
        out_specs=[pl.BlockSpec(memory_space=pl.ANY), blk, blk, blk]
        + [fixed(*o.shape) for o in shapes[3:]]
        + [
            pl.BlockSpec((512, BQ), lambda i: (0, jnp.maximum(i - half, 0))),
            pl.BlockSpec((H, BQ), lambda i: (0, jnp.maximum(i - half, 0))),
        ],
        out_shape=[jax.ShapeDtypeStruct((4, 2, 2, 2, LATE, 512), BF16)]
        + shapes
        + [jax.ShapeDtypeStruct((512, slots), BF16), jax.ShapeDtypeStruct((H, slots), F32)],
        scratch_shapes=[
            pltpu.VMEM((ROWS, 512), BF16),
            pltpu.VMEM((4, 2, 2, 2, EARLY, 512), BF16),
            pltpu.VMEM((512, 128), F32),
            pltpu.VMEM(mwide, BF16),
            pltpu.VMEM(wide, BF16),
            pltpu.VMEM(wide, BF16),
            pltpu.VMEM(wide, BF16),
            pltpu.VMEM((H, HA, BQ), F32),
            pltpu.VMEM((H, BQ), F32),
            pltpu.VMEM((H, BK, BQ), F32),
            pltpu.VMEM((H, BK, BQ), F32),
            pltpu.SemaphoreType.DMA((GATHER_COPIES,)),
            pltpu.SemaphoreType.DMA((GATHER_COPIES,)),
            pltpu.SemaphoreType.DMA,
        ],
        compiler_params=params(collective_id=0, has_side_effects=True),
        name="gather_attend",
    )(*weights, *args)
    return (found[0].reshape(PARTS, LATE, 512),) + tuple(found[1:])


def key_ranges(seg, count, slots, out):
    r, c = seg.shape
    pos = lax.broadcasted_iota(jnp.int32, (r, c), 0) * c + lax.broadcasted_iota(jnp.int32, (r, c), 1)
    valid = pos < count
    ends = [jnp.sum(jnp.where(valid & (seg <= s), 1.0, 0.0)).astype(jnp.int32) for s in range(3)]
    for block in range(slots // BQ):
        first = block * BQ
        last = jnp.minimum(first + BQ, count)
        low, high, start = jnp.int32(slots), jnp.int32(0), jnp.int32(0)
        for end in ends:
            hit = (end > first) & (start < last) & (end > start)
            low = jnp.where(hit, jnp.minimum(low, start), low)
            high = jnp.where(hit, jnp.maximum(high, end), high)
            start = end
        begin = low // 128
        blocks = jnp.where(high > low, (high - begin * 128 + BK - 1) // BK, 0)
        out[0, block] = jnp.minimum(begin, slots // 128 - blocks * (BK // 128))
        out[1, block] = blocks


def key_slots(begin, block):
    return pl.ds(pl.multiple_of((begin + block * (BK // 128)) * 128, 128), BK)


def pipelined(blocks, work, first, second, started, finish):
    if not started:

        @pl.when(blocks > 0)
        def _():
            work((0, first), None)

        pl.when(blocks == 0)(finish)

    pairs = jnp.maximum(blocks - 1, 0) // 2

    def two(j):
        work((j + 1, second), (j, first))
        work((j + 2, first), (j + 1, second))

    @pl.loop(0, pairs // 2)
    def _(i):
        two(4 * i)
        two(4 * i + 2)

    @pl.when(pairs % 2 == 1)
    def _():
        two(2 * pairs - 2)

    j = 2 * pairs

    @pl.when(blocks - j == 2)
    def _():
        work((j + 1, second), (j, first))
        work(None, (j + 1, second))
        finish()

    @pl.when(blocks - j == 1)
    def _():
        work(None, (j, first))
        finish()


def attend(
    sure, begin, blocks, qa_ref, ka_ref, va_ref, kmn_ref, vm_ref, mix_ref, lse_ref, acc_ref, m_ref, sa_ref, sb_ref
):
    def weights(h, s):
        old = m_ref[h : h + 1, :]
        top = jnp.maximum(old, jnp.max(s, axis=0, keepdims=True))
        return jnp.exp(s - top).astype(BF16), jnp.exp(old - top), top

    def work(new, old):
        kept = {}
        for h in range(H + 1):
            if h > 0 and old:
                p, fade, top = kept.pop(h - 1)
                acc_ref[h - 1] = acc_ref[h - 1] * fade + dot(va_ref[h - 1, :, key_slots(begin, old[0])], p, 1, 0)
                m_ref[h - 1 : h, :] = top
            if h < H and new:
                new[1][h] = dot(ka_ref[h, :, key_slots(begin, new[0])], qa_ref[h], 0, 0)
            if h < H and old:
                kept[h] = weights(h, old[1][h])

    scores = [dot(kmn_ref[h, :, 0:HA], qa_ref[h], 1, 0) for h in range(H)]
    if sure:
        work((0, sa_ref), None)
    for h in range(H):
        top = jnp.max(scores[h], axis=0, keepdims=True)
        p = jnp.exp(scores[h] - top).astype(BF16)
        acc_ref[h] = dot(vm_ref[h, :, 0:MP], p, 1, 0)
        m_ref[h : h + 1, :] = top

    def finish():
        for h in range(H):
            total = acc_ref[h, 64:65, :]
            mix_ref[64 * h : 64 * h + 64, :] = (acc_ref[h, 0:64, :] * (1.0 / total)).astype(BF16)
            lse_ref[h : h + 1, :] = m_ref[h : h + 1, :] + jnp.log(total)

    pipelined(blocks, work, sa_ref, sb_ref, sure, finish)


def fwd_kernel(
    slots, seg_ref, cnt_ref, qa_ref, ka_ref, va_ref, kmn_ref, vm_ref,
    mix_ref, lse_ref, acc_ref, m_ref, sa_ref, sb_ref, range_ref,
):
    step = pl.program_id(0)

    @pl.when(step == 0)
    def _():
        key_ranges(seg_ref[...], cnt_ref[0], slots, range_ref)

    attend(
        False, range_ref[0, step], range_ref[1, step], qa_ref, ka_ref, va_ref, kmn_ref, vm_ref, mix_ref, lse_ref,
        acc_ref, m_ref, sa_ref, sb_ref,
    )


def attend_forward(seg2, counts, qa, ka, va, kmn, vm):
    slots = qa.shape[2]
    once = pl.Buffered(1)

    def whole(a):
        return pl.BlockSpec(a.shape, lambda i: (0, 0, 0), pipeline_mode=once)

    return pl.pallas_call(
        functools.partial(fwd_kernel, slots),
        grid=(slots // BQ,),
        in_specs=[
            pl.BlockSpec(seg2.shape, lambda i: (0, 0)),
            pl.BlockSpec(memory_space=pltpu.SMEM),
            pl.BlockSpec((H, HA, BQ), lambda i: (0, 0, i)),
            whole(ka), whole(va), whole(kmn), whole(vm),
        ],
        out_specs=[pl.BlockSpec((512, BQ), lambda i: (0, i)), pl.BlockSpec((H, BQ), lambda i: (0, i))],
        out_shape=[jax.ShapeDtypeStruct((512, slots), BF16), jax.ShapeDtypeStruct((H, slots), F32)],
        scratch_shapes=[
            pltpu.VMEM((H, HA, BQ), F32),
            pltpu.VMEM((H, BQ), F32),
            pltpu.VMEM((H, BK, BQ), F32),
            pltpu.VMEM((H, BK, BQ), F32),
            pltpu.SMEM((2, slots // BQ), jnp.int32),
        ],
        compiler_params=params(),
        name="attend_forward",
    )(seg2, counts, qa, ka, va, kmn, vm)


def norm_parts(value):
    mean = jnp.mean(value, axis=-1, keepdims=True)
    centred = value - mean
    rstd = lax.rsqrt(jnp.mean(centred * centred, axis=-1, keepdims=True) + EPS)
    return centred * rstd, rstd


def norm_grad(grad_hat, hat, rstd):
    return rstd * (
        grad_hat
        - jnp.mean(grad_hat, axis=-1, keepdims=True)
        - hat * jnp.mean(grad_hat * hat, axis=-1, keepdims=True)
    )


def colsum(value):
    return jnp.sum(value, axis=0, keepdims=True)


SUB = 512
FC = 512


def mid_kernel(
    rb, cnt_ref, row_ref, rbup_ref, late_ref, mix_ref, tok_ref, cot_ref,
    out_ref, gfirst_ref, mgrad_ref, delta_ref, gw_ref, vec_ref, bup_ref,
    aup_ref, adn_ref, ao_ref, *scratch,
):
    step = pl.program_id(0)
    subs = rb // SUB

    @pl.when(step == 0)
    def _():
        aup_ref[...] = jnp.zeros_like(aup_ref)
        adn_ref[...] = jnp.zeros_like(adn_ref)
        ao_ref[...] = jnp.zeros_like(ao_ref)
        vec_ref[...] = jnp.zeros_like(vec_ref)
        bup_ref[...] = jnp.zeros_like(bup_ref)

    wo = late_ref[:, 128:144, :].reshape(512, 512)

    def w_up(c):
        return late_ref[:, 16 * c : 16 * c + 16, :].reshape(512, 512)

    def w_down(c):
        return late_ref[8 * c : 8 * c + 8, 64:128, :].reshape(512, 512)

    def row(v):
        return row_ref[v : v + 1, :]

    class Block:
        def __init__(self, index):
            self.s = slice(SUB * index, SUB * index + SUB)
            self.first_row = step * rb + SUB * index
            self.active, self.slope, self.hgrad = scratch[3 * (index % 2) : 3 * (index % 2) + 3]
            self.up_part, self.dact_part = {}, {}

        def head(self):
            self.mixt = mix_ref[:, self.s]
            attention = dot(self.mixt, wo, 0, 0) + row(V_BO)
            self.hat1, self.rstd1 = norm_parts(tok_ref[self.s, :].astype(F32) + attention)
            self.first = self.hat1 * row(V_GA) + row(V_SA)
            self.low = self.first.astype(BF16)
            self.branch = self.first + row(V_BD)

        def up(self, c):
            f = slice(FC * c, FC * c + FC)
            self.up_part[c] = dot(self.low, w_up(c), 1, 0) + rbup_ref[:, f]

        def gelu(self, c):
            f = slice(FC * c, FC * c + FC)
            hidden = self.up_part.pop(c)
            cdf = 0.5 + 0.5 * lax.erf(hidden * (2.0 ** -0.5))
            self.active[:, f] = (hidden * cdf).astype(BF16)
            self.slope[:, f] = cdf + hidden * jnp.exp(hidden * hidden * -0.5) * 0.3989422804014327

        def down(self, c):
            f = slice(FC * c, FC * c + FC)
            self.branch = self.branch + dot(self.active[:, f], w_down(c), 1, 0)

        def turn(self):
            hat2, rstd2 = norm_parts(self.branch)
            valid = lax.broadcasted_iota(jnp.int32, (SUB, 1), 0) + self.first_row < cnt_ref[0]
            out_ref[self.s, :] = jnp.where(valid, hat2 * row(V_GF) + row(V_SF), 0.0).astype(BF16)
            seed = jnp.where(valid, cot_ref[self.s, :].astype(F32), 0.0)
            vec_ref[V_GF : V_GF + 1, :] += colsum(seed * hat2)
            vec_ref[V_SF : V_SF + 1, :] += colsum(seed)
            self.total = norm_grad(seed * row(V_GF), hat2, rstd2)
            self.bgrad = self.total.astype(BF16)
            vec_ref[V_BD : V_BD + 1, :] += colsum(self.bgrad.astype(F32))

        def dact(self, c):
            f = slice(FC * c, FC * c + FC)
            self.dact_part[c] = dot(self.bgrad, w_down(c), 1, 1)

        def grad_down(self, c):
            f = slice(FC * c, FC * c + FC)
            adn_ref[f, :] += dot(self.active[:, f], self.bgrad, 0, 0)

        def hidden_grad(self, c):
            f = slice(FC * c, FC * c + FC)
            grad = (self.dact_part.pop(c) * self.slope[:, f]).astype(BF16)
            self.hgrad[:, f] = grad
            bup_ref[:, f] += colsum(grad.astype(F32))

        def grad_up(self, c):
            f = slice(FC * c, FC * c + FC)
            aup_ref[:, f] += dot(self.low, self.hgrad[:, f], 0, 0)

        def first_grad(self, c):
            f = slice(FC * c, FC * c + FC)
            self.total = self.total + dot(self.hgrad[:, f], w_up(c), 1, 1)

        def finish(self):
            vec_ref[V_GA : V_GA + 1, :] += colsum(self.total * self.hat1)
            vec_ref[V_SA : V_SA + 1, :] += colsum(self.total)
            grad_first = norm_grad(self.total * row(V_GA), self.hat1, self.rstd1)
            gfirst_ref[self.s, :] = grad_first
            agrad = grad_first.astype(BF16)
            vec_ref[V_BO : V_BO + 1, :] += colsum(agrad.astype(F32))
            mgrad = dot(wo, agrad, 1, 1).astype(BF16)
            ao_ref[...] += dot(self.mixt, agrad, 1, 0)
            mgrad_ref[:, self.s] = mgrad
            prod = mgrad.astype(F32) * self.mixt.astype(F32)
            for h in range(H):
                delta_ref[h : h + 1, self.s] = jnp.sum(prod[64 * h : 64 * h + 64, :], axis=0, keepdims=True)

    chunks = 2048 // FC

    def both(ahead, behind):
        if ahead:
            ahead.head()
            ahead.up(0)
        for c in range(chunks):
            if behind:
                behind.dact(c)
            if ahead and c + 1 < chunks:
                ahead.up(c + 1)
            if behind:
                behind.grad_down(c)
            if ahead:
                ahead.gelu(c)
            if behind:
                behind.hidden_grad(c)
                behind.grad_up(c)
                behind.first_grad(c)
            if ahead:
                ahead.down(c)
        if behind:
            behind.finish()
        if ahead:
            ahead.turn()

    blocks = [Block(index) for index in range(subs)]
    for ahead, behind in zip(blocks + [None], [None] + blocks):
        both(ahead, behind)

    @pl.when(step == pl.num_programs(0) - 1)
    def _():
        gw_ref[:, 0:16, :] = ao_ref[...].astype(gw_ref.dtype).reshape(PARTS, 16, 512)
        for c in range(4):
            gw_ref[:, 16 + 16 * c : 32 + 16 * c, :] = (
                aup_ref[:, 512 * c : 512 * c + 512].astype(gw_ref.dtype).reshape(PARTS, 16, 512)
            )
        gw_ref[:, 80:144, :] = adn_ref[...].astype(gw_ref.dtype).reshape(PARTS, 64, 512)


def middle(late, rows8, rbup, counts, mixt, tokens, cotangent, rb=512):
    slots = tokens.shape[0]
    rows = pl.BlockSpec((rb, 512), lambda i: (i, 0))
    cols = pl.BlockSpec((512, rb), lambda i: (0, i))
    once = pl.Buffered(1)
    return pl.pallas_call(
        functools.partial(mid_kernel, rb),
        grid=(slots // rb,),
        in_specs=[
            pl.BlockSpec(memory_space=pltpu.SMEM),
            pl.BlockSpec((8, 512), lambda i: (0, 0)),
            pl.BlockSpec((1, 2048), lambda i: (0, 0)),
            pl.BlockSpec((PARTS, LATE, 512), lambda i: (0, 0, 0), pipeline_mode=once),
            cols, rows, rows,
        ],
        out_specs=[
            rows, rows, cols,
            pl.BlockSpec((H, rb), lambda i: (0, i)),
            pl.BlockSpec((PARTS, 144, 512), lambda i: (0, 0, 0), pipeline_mode=once),
            pl.BlockSpec((8, 512), lambda i: (0, 0)),
            pl.BlockSpec((1, 2048), lambda i: (0, 0)),
        ],
        out_shape=[
            jax.ShapeDtypeStruct((slots, 512), BF16),
            jax.ShapeDtypeStruct((slots, 512), F32),
            jax.ShapeDtypeStruct((512, slots), BF16),
            jax.ShapeDtypeStruct((H, slots), F32),
            jax.ShapeDtypeStruct((PARTS, 144, 512), BF16),
            jax.ShapeDtypeStruct((8, 512), F32),
            jax.ShapeDtypeStruct((1, 2048), F32),
        ],
        scratch_shapes=[
            pltpu.VMEM((512, 2048), F32),
            pltpu.VMEM((2048, 512), F32),
            pltpu.VMEM((512, 512), F32),
        ]
        + [pltpu.VMEM((SUB, 2048), BF16), pltpu.VMEM((SUB, 2048), F32), pltpu.VMEM((SUB, 2048), BF16)] * 2,
        compiler_params=params(),
        name="middle",
    )(counts, rows8, rbup, late, mixt, tokens, cotangent)


def split3(value):
    high = value.astype(BF16)
    rest = value - high.astype(F32)
    mid = rest.astype(BF16)
    return high, mid, (rest - mid.astype(F32)).astype(BF16)


def attend_back(
    sure, finish, begin, blocks, qa_ref, ka_ref, va_ref, kmn_ref, km_ref, vmn_ref, do_ref, lse_ref, delta_ref,
    q2_ref, do2_ref, dqa_ref, dka_ref, dva_ref, dkma_ref, dvma_ref, sa_ref, ga_ref, sb_ref, gb_ref,
):
    frow = lax.broadcasted_iota(jnp.int32, (16, BQ), 0)

    def feature(value, at):
        high, mid, low = (jnp.broadcast_to(v.astype(F32), (16, BQ)) for v in split3(value))
        return jnp.where(frow == at, high, jnp.where(frow == at + 1, mid, jnp.where(frow == at + 2, low, 0.0)))

    for h in range(H):
        q2_ref[h, 0:64, :] = qa_ref[h, 0:64, :]
        q2_ref[h, 64:80, :] = (qa_ref[h, 64:80, :].astype(F32) + feature(-lse_ref[h : h + 1, :], 3)).astype(BF16)
        do2_ref[h, 0:64, :] = do_ref[64 * h : 64 * h + 64, :]
        do2_ref[h, 64:80, :] = feature(-delta_ref[h : h + 1, :], 0).astype(BF16)

    def work(new, old):
        kept = {}
        for h in range(H + 1):
            if h > 0 and old:
                ks = key_slots(begin, old[0])
                p, ds = kept.pop(h - 1)
                dva_ref[h - 1, :, ks] += dot(do2_ref[h - 1, 0:64, :], p, 1, 1)
                dka_ref[h - 1, :, ks] += dot(q2_ref[h - 1, 0:64, :], ds, 1, 1)
                dqa_ref[h - 1] += dot(ka_ref[h - 1, 0:64, ks], ds, 1, 0)
            if h < H and new:
                ks = key_slots(begin, new[0])
                new[1][0][h] = dot(ka_ref[h, :, ks], q2_ref[h], 0, 0)
                new[1][1][h] = dot(va_ref[h, :, ks], do2_ref[h], 0, 0)
            if h < H and old:
                p = jnp.exp(old[1][0][h])
                kept[h] = p.astype(BF16), (p * old[1][1][h]).astype(BF16)

    ps = [dot(kmn_ref[h, :, 0:HA], q2_ref[h], 1, 0) for h in range(H)]
    dps = [dot(vmn_ref[h, :, 0:HA], do2_ref[h], 1, 0) for h in range(H)]
    if sure:
        work((0, (sa_ref, ga_ref)), None)
    ps = [jnp.exp(p) for p in ps]
    dss = [(p * dp).astype(BF16) for p, dp in zip(ps, dps)]
    for h in range(H):
        dvma_ref[h, :, 0:MP] += dot(do2_ref[h, 0:64, :], ps[h].astype(BF16), 1, 1)
        dkma_ref[h, :, 0:MP] += dot(q2_ref[h, 0:64, :], dss[h], 1, 1)
        dqa_ref[h] = dot(km_ref[h, 0:64, 0:MP], dss[h], 1, 0)
    pipelined(blocks, work, (sa_ref, ga_ref), (sb_ref, gb_ref), sure, finish)


def bwd_kernel(
    slots, seg_ref, cnt_ref, qa_ref, ka_ref, va_ref, kmn_ref, km_ref, vmn_ref, do_ref, lse_ref, delta_ref,
    dq_ref, dk_ref, dv_ref, dkm_ref, dvm_ref,
    q2_ref, do2_ref, dqa_ref, dka_ref, dva_ref, dkma_ref, dvma_ref, sa_ref, ga_ref, sb_ref, gb_ref, range_ref,
):
    step = pl.program_id(0)

    @pl.when(step == 0)
    def _():
        key_ranges(seg_ref[...], cnt_ref[0], slots, range_ref)
        for ref in (dka_ref, dva_ref, dkma_ref, dvma_ref):
            ref[...] = jnp.zeros_like(ref)

    def finish():
        for h in range(H):
            dq_ref[64 * h : 64 * h + 64, :] = (dqa_ref[h] * HD ** -0.5).astype(BF16)

    attend_back(
        False, finish, range_ref[0, step], range_ref[1, step], qa_ref, ka_ref, va_ref, kmn_ref, km_ref, vmn_ref, do_ref, lse_ref,
        delta_ref, q2_ref, do2_ref, dqa_ref, dka_ref, dva_ref, dkma_ref, dvma_ref, sa_ref, ga_ref, sb_ref, gb_ref,
    )

    @pl.when(step == pl.num_programs(0) - 1)
    def _():
        for h in range(H):
            s = slice(64 * h, 64 * h + 64)
            dk_ref[s, :] = dka_ref[h].astype(BF16)
            dv_ref[s, :] = dva_ref[h].astype(BF16)
            dkm_ref[s, :] = dkma_ref[h].astype(BF16)
            dvm_ref[s, :] = dvma_ref[h].astype(BF16)


def attend_backward(seg2, counts, qa, ka, va, kmn, km, vmn, mgrad, lse, delta):
    slots = qa.shape[2]
    once = pl.Buffered(1)

    def full(a):
        return pl.BlockSpec(a.shape, lambda i: (0, 0, 0), pipeline_mode=once)

    cols = pl.BlockSpec((512, BQ), lambda i: (0, i))
    stat = pl.BlockSpec((H, BQ), lambda i: (0, i))
    whole = pl.BlockSpec((512, slots), lambda i: (0, 0), pipeline_mode=once)
    mwhole = pl.BlockSpec((512, 128), lambda i: (0, 0))
    block = pltpu.VMEM((H, BK, BQ), F32)
    return pl.pallas_call(
        functools.partial(bwd_kernel, slots),
        grid=(slots // BQ,),
        in_specs=[
            pl.BlockSpec(seg2.shape, lambda i: (0, 0)),
            pl.BlockSpec(memory_space=pltpu.SMEM),
            pl.BlockSpec((H, HA, BQ), lambda i: (0, 0, i)),
            full(ka), full(va), full(kmn), full(km), full(vmn), cols, stat, stat,
        ],
        out_specs=[cols, whole, whole, mwhole, mwhole],
        out_shape=[jax.ShapeDtypeStruct((512, slots), BF16)] * 3 + [jax.ShapeDtypeStruct((512, 128), BF16)] * 2,
        scratch_shapes=[
            pltpu.VMEM((H, HA, BQ), BF16),
            pltpu.VMEM((H, HA, BQ), BF16),
            pltpu.VMEM((H, HD, BQ), F32),
            pltpu.VMEM((H, HD, slots), F32),
            pltpu.VMEM((H, HD, slots), F32),
            pltpu.VMEM((H, HD, 128), F32),
            pltpu.VMEM((H, HD, 128), F32),
            block, block, block, block,
            pltpu.SMEM((2, slots // BQ), jnp.int32),
        ],
        compiler_params=params(),
        name="attend_backward",
    )(seg2, counts, qa, ka, va, kmn, km, vmn, mgrad, lse, delta)


SUM_EARLY = (
    (slice(0, 48), "yxz"),
    (slice(48, 96), "xyz"),
    (slice(96, 112), "xzy"),
    (slice(112, 144), "yzx"),
)
SUM_LATE = ((slice(144, 160), "xyz"), (slice(160, 176), "yxz"), (slice(176, 192), "xyz"), (slice(192, 208), "yxz"))
SUM_PARTS = SUM_EARLY + SUM_LATE
SUM_COPIES = 6 * len(SUM_PARTS)


def weight_grads(step, tok_ref, dq_ref, dk_ref, dv_ref, dkm_ref, dvm_ref, memt_ref, acc_ref, sum_ref):
    @pl.when(step == 0)
    def _():
        acc_ref[0:512, :] = jnp.zeros((512, 512), F32)
        acc_ref[512:1024, :] = dot(dkm_ref[...], memt_ref[...], 1, 1)
        acc_ref[1024:1536, :] = dot(dvm_ref[...], memt_ref[...], 1, 1)
        sum_ref[...] = jnp.zeros_like(sum_ref)
        sum_ref[:, 1:2] = jnp.sum(dvm_ref[...].astype(F32), axis=1, keepdims=True)

    tok = tok_ref[...]
    dq, dk, dv = dq_ref[...], dk_ref[...], dv_ref[...]
    acc_ref[0:512, :] += dot(dq, tok, 1, 0)
    acc_ref[512:1024, :] += dot(dk, tok, 1, 0)
    acc_ref[1024:1536, :] += dot(dv, tok, 1, 0)
    sum_ref[:, 0:1] += jnp.sum(dq.astype(F32), axis=1, keepdims=True)
    sum_ref[:, 1:2] += jnp.sum(dv.astype(F32), axis=1, keepdims=True)


def matrix_grad(j, acc_ref):
    return acc_ref[512 * j : 512 * j + 512, :].T.astype(BF16)


def small_grads(dkm_ref, dvm_ref, vec_ref, bup_ref, wt_ref, sum_ref, late):
    gmem = dot(wt_ref[512:1024, :], dkm_ref[...], 0, 0) + dot(wt_ref[1024:1536, :], dvm_ref[...], 0, 0)
    late(slice(48, 64), slice(0, 128), gmem.astype(BF16))
    lane = lax.broadcasted_iota(jnp.int32, (512, 128), 1)
    vecs = jnp.concatenate([vec_ref[...], jnp.zeros((120, 512), F32)], axis=0).T
    late(slice(48, 64), slice(128, 256), jnp.where(lane < 2, sum_ref[...], vecs).astype(BF16))
    rows = [bup_ref[0:1, 256 * v : 256 * v + 256] for v in range(8)] + [jnp.zeros((8, 256), F32)]
    rows = jnp.concatenate(rows, axis=0).astype(BF16)
    late(slice(48, 64), slice(256, 512), jnp.broadcast_to(rows[None], (PARTS, 16, 256)).reshape(512, 256))


def token_grads(gtok_ref, gfirst_ref, dq_ref, dk_ref, dv_ref, wt_ref):
    gtok_ref[...] = (
        gfirst_ref[...]
        + dot(dq_ref[...], wt_ref[0:512, :], 0, 0)
        + dot(dk_ref[...], wt_ref[512:1024, :], 0, 0)
        + dot(dv_ref[...], wt_ref[1024:1536, :], 0, 0)
    )


def scatter_kernel(
    blocks, qa_ref, ka_ref, va_ref, kmn_ref, km_ref, vmn_ref, do_ref, lse_ref, delta_ref,
    tok_hbm, gfirst_ref, vec_ref, bup_ref, wt_hbm, memt_ref, early_ref, gtok_ref, out_ref,
    q2_ref, do2_ref, dqa_ref, dka_ref, dva_ref, dkma_ref, dvma_ref, sa_ref, ga_ref, sb_ref, gb_ref,
    dq_ref, dk_ref, dv_ref, dkm_ref, dvm_ref,
    tok_ref, wt_ref, acc_ref, sum_ref, late, parts_sum, other, send, recv, local, fetch, *landing,
):
    step = pl.program_id(0)
    place = Place()
    copies = Copies(send, recv)
    slots = dict(zip(slot_shapes(SUM_PARTS), landing))
    crossing = [copies.number() for _ in SUM_PARTS]
    parts = []
    for index, (rows, order) in enumerate(SUM_PARTS):
        mine = {key[1:]: slot for key, slot in slots.items() if key[0] == index}
        parts.append(scatter_part(place, copies, parts_sum, mine, out_ref, rows, order))
    firsts, lasts = parts[: len(SUM_EARLY)], parts[len(SUM_EARLY) :]

    def load(index):
        rows = SUM_EARLY[index][0]
        return pltpu.make_async_copy(
            early_ref.at[:, :, :, place.core, rows], parts_sum.at[:, :, :, rows], local.at[index]
        )

    def fetches():
        return (
            pltpu.make_async_copy(tok_hbm, tok_ref, fetch.at[0]),
            pltpu.make_async_copy(wt_hbm, wt_ref, fetch.at[1]),
        )

    def cross(source, base, rows, number):
        old = slice(rows.start - base, rows.stop - base)
        copies.start(
            lambda: source.at[:, :, :, place.far, old], lambda: other.at[:, :, :, rows], number, place.partner
        )

    @pl.when(step == 0)
    def _():
        place.greet()
        for copy in fetches():
            copy.start()
        for index in range(len(SUM_EARLY)):
            load(index).start()
        for ref in (dka_ref, dva_ref, dkma_ref, dvma_ref, sum_ref):
            ref[...] = jnp.zeros_like(ref)

    @pl.when(step < blocks)
    def _():
        reach = LONGEST // BQ
        begin = jnp.maximum(step - reach, 0)
        end = jnp.minimum(step + reach + 1, blocks)
        here = pl.ds(pl.multiple_of(step * BQ, BQ), BQ)

        def finish():
            for h in range(H):
                dq_ref[64 * h : 64 * h + 64, here] = (dqa_ref[h] * HD ** -0.5).astype(BF16)

        attend_back(
            True, finish, begin * (BQ // 128), (end - begin) * (BQ // BK), qa_ref, ka_ref, va_ref, kmn_ref, km_ref, vmn_ref,
            do_ref, lse_ref, delta_ref, q2_ref, do2_ref, dqa_ref, dka_ref, dva_ref, dkma_ref, dvma_ref,
            sa_ref, ga_ref, sb_ref, gb_ref,
        )

    @pl.when(step == 0)
    def _():
        for copy in fetches():
            copy.wait()
        place.met()
        for number, (rows, _) in zip(crossing, SUM_EARLY):
            cross(early_ref, 0, rows, number)

    @pl.when(step == 1)
    def _():
        for index, (rows, _) in enumerate(SUM_EARLY):
            load(index).wait()
            join(place, copies, parts_sum, None, other, rows, crossing[index])
            next(firsts[index])

    @pl.when(step == 3)
    def _():
        advance(firsts)

    @pl.when(step == 5)
    def _():
        advance(firsts)

    @pl.when(step == blocks - 1)
    def _():
        advance(firsts)

    def put(rows, lanes, value):
        late[:, :, :, :, rows, lanes] = value.reshape(4, 2, 2, 2, 16, value.shape[1])

    def depart(index):
        cross(late, LATE, SUM_LATE[index][0], crossing[len(SUM_EARLY) + index])

    def onward(index):
        rows = SUM_LATE[index][0]
        old = slice(rows.start - LATE, rows.stop - LATE)
        join(
            place, copies, parts_sum, lambda z: late[z, :, :, place.core, old], other, rows,
            crossing[len(SUM_EARLY) + index],
        )
        next(lasts[index])

    @pl.when(step == blocks)
    def _():
        tok = tok_ref[...]
        acc_ref[0:512, :] = dot(dq_ref[...], tok, 1, 0)
        put(slice(0, 16), slice(0, 512), matrix_grad(0, acc_ref))
        depart(0)
        for j, whole, part, memory, memory_part in (
            (1, dka_ref, dk_ref, dkma_ref, dkm_ref),
            (2, dva_ref, dv_ref, dvma_ref, dvm_ref),
        ):
            for h in range(H):
                s = slice(64 * h, 64 * h + 64)
                part[s, :] = whole[h].astype(BF16)
                memory_part[s, :] = memory[h].astype(BF16)
            acc_ref[512 * j : 512 * j + 512, :] = dot(part[...], tok, 1, 0) + dot(
                memory_part[...], memt_ref[...], 1, 1
            )
            put(slice(16 * j, 16 * j + 16), slice(0, 512), matrix_grad(j, acc_ref))
            depart(j)
            onward(j - 1)
        sum_ref[:, 0:1] = jnp.sum(dq_ref[...].astype(F32), axis=1, keepdims=True)
        sum_ref[:, 1:2] = jnp.sum(dv_ref[...].astype(F32), axis=1, keepdims=True) + jnp.sum(
            dvm_ref[...].astype(F32), axis=1, keepdims=True
        )
        small_grads(dkm_ref, dvm_ref, vec_ref, bup_ref, wt_ref, sum_ref, put)
        depart(3)
        onward(2)

    @pl.when(step > blocks)
    def _():
        rows = gtok_ref.shape[0]
        here = pl.ds(pl.multiple_of((step - blocks - 1) * rows, 128), rows)
        token_grads(gtok_ref, gfirst_ref, dq_ref.at[:, here], dk_ref.at[:, here], dv_ref.at[:, here], wt_ref)

    @pl.when(step == blocks + 1)
    def _():
        onward(3)

    @pl.when(step == blocks + 2)
    def _():
        advance(lasts[0:2])

    @pl.when(step == blocks + 3)
    def _():
        advance(lasts[2:4])

    @pl.when(step == pl.num_programs(0) - 1)
    def _():
        advance(lasts)
        advance(lasts)
        copies.finish()


def backward(seg2, counts, early, tokens, qa, ka, va, kmn, km, vmn, mgrad, lse, delta, gfirst, vec, bup, wt, memt, remote):
    if not remote:
        dq, dk, dv, dkm, dvm = attend_backward(seg2, counts, qa, ka, va, kmn, km, vmn, mgrad, lse, delta)
        return tail(tokens, dq, dk, dv, dkm, dvm, gfirst, vec, bup, wt, memt)
    slots = tokens.shape[0]
    rb = 512
    blocks = slots // BQ
    once = pl.Buffered(1)

    def full(a):
        return pl.BlockSpec(a.shape, lambda i: (0,) * len(a.shape), pipeline_mode=once)

    def at(i):
        return jnp.minimum(i, blocks - 1)

    later = pl.BlockSpec((rb, 512), lambda i: (jnp.maximum(i - blocks - 1, 0), 0))
    stat = pl.BlockSpec((H, BQ), lambda i: (0, at(i)))
    score = pltpu.VMEM((H, BK, BQ), F32)
    hbm = pl.BlockSpec(memory_space=pl.ANY)
    return pl.pallas_call(
        functools.partial(scatter_kernel, blocks),
        grid=(blocks + 1 + slots // rb,),
        in_specs=[
            pl.BlockSpec((H, HA, BQ), lambda i: (0, 0, at(i))),
            full(ka), full(va), full(kmn), full(km), full(vmn),
            pl.BlockSpec((512, BQ), lambda i: (0, at(i))), stat, stat,
            hbm, later, full(vec), full(bup), hbm, full(memt),
            hbm,
        ],
        out_specs=[later, fixed(ROWS, 512)],
        out_shape=[jax.ShapeDtypeStruct((slots, 512), F32), jax.ShapeDtypeStruct((ROWS, 512), F32)],
        scratch_shapes=[
            pltpu.VMEM((H, HA, BQ), BF16),
            pltpu.VMEM((H, HA, BQ), BF16),
            pltpu.VMEM((H, HD, BQ), F32),
            pltpu.VMEM((H, HD, slots), F32),
            pltpu.VMEM((H, HD, slots), F32),
            pltpu.VMEM((H, HD, 128), F32),
            pltpu.VMEM((H, HD, 128), F32),
            score, score, score, score,
            pltpu.VMEM((512, slots), BF16),
            pltpu.VMEM((512, slots), BF16),
            pltpu.VMEM((512, slots), BF16),
            pltpu.VMEM((512, 128), BF16),
            pltpu.VMEM((512, 128), BF16),
            pltpu.VMEM(tokens.shape, BF16),
            pltpu.VMEM(wt.shape, BF16),
            pltpu.VMEM((1536, 512), F32),
            pltpu.VMEM((512, 128), F32),
            pltpu.VMEM((4, 2, 2, 2, EARLY, 512), BF16),
            pltpu.VMEM((4, 2, 2, ROWS, 512), BF16),
            pltpu.VMEM((4, 2, 2, ROWS, 512), BF16),
            pltpu.SemaphoreType.DMA((SUM_COPIES,)),
            pltpu.SemaphoreType.DMA((SUM_COPIES,)),
            pltpu.SemaphoreType.DMA((len(SUM_EARLY),)),
            pltpu.SemaphoreType.DMA((2,)),
        ]
        + [pltpu.VMEM(shape, BF16) for shape in slot_shapes(SUM_PARTS).values()],
        compiler_params=params(collective_id=1, has_side_effects=True),
        name="backward_scatter",
    )(
        qa, ka, va, kmn, km, vmn, mgrad, lse, delta, tokens, gfirst, vec, bup, wt, memt,
        early.reshape(4, 2, 2, 2, LATE, 512),
    )


def plain_kernel(
    half, tok_ref, dq_ref, dk_ref, dv_ref, dkm_ref, dvm_ref, gfirst_ref, vec_ref, bup_ref, wt_ref, memt_ref,
    gtok_ref, late_ref, acc_ref, sum_ref,
):
    step = pl.program_id(0)

    @pl.when(step < half)
    def _():
        weight_grads(step, tok_ref, dq_ref, dk_ref, dv_ref, dkm_ref, dvm_ref, memt_ref, acc_ref, sum_ref)

    @pl.when(step == half - 1)
    def _():
        def put(rows, lanes, value):
            late_ref[:, rows, lanes] = value.reshape(PARTS, 16, value.shape[1])

        for j in range(3):
            put(slice(16 * j, 16 * j + 16), slice(0, 512), matrix_grad(j, acc_ref))
        small_grads(dkm_ref, dvm_ref, vec_ref, bup_ref, wt_ref, sum_ref, put)

    @pl.when(step >= half)
    def _():
        token_grads(gtok_ref, gfirst_ref, dq_ref, dk_ref, dv_ref, wt_ref)


def tail(tokens, dq, dk, dv, dkm, dvm, gfirst, vec, bup, wt, memt):
    slots = tokens.shape[0]
    rb = 512
    half = slots // rb
    cols = pl.BlockSpec((512, rb), lambda i: (0, i % half))
    later = pl.BlockSpec((rb, 512), lambda i: (jnp.maximum(i - half, 0), 0))
    return pl.pallas_call(
        functools.partial(plain_kernel, half),
        grid=(2 * half,),
        in_specs=[
            pl.BlockSpec((rb, 512), lambda i: (jnp.minimum(i, half - 1), 0)),
            cols, cols, cols, fixed(512, 128), fixed(512, 128), later,
            fixed(8, 512), fixed(1, 2048), fixed(1536, 512), fixed(512, 128),
        ],
        out_specs=[later, fixed(PARTS, EARLY, 512)],
        out_shape=[jax.ShapeDtypeStruct((slots, 512), F32), jax.ShapeDtypeStruct((PARTS, EARLY, 512), BF16)],
        scratch_shapes=[pltpu.VMEM((1536, 512), F32), pltpu.VMEM((512, 128), F32)],
        compiler_params=params(),
        name="tail",
    )(tokens, dq, dk, dv, dkm, dvm, gfirst, vec, bup, wt, memt)


def unpack_kernel(sum_hbm, part_ref, gtok_ref, wo, up, dn, wq, wk, wv, memory, b_up, *rest):
    vectors, (sum_ref, block, ready, arrive, leave) = rest[:8], rest[8:]
    count = arrive.shape[0]
    rows = block.shape[0] // count
    spans = [slice(rows * k, rows * k + rows) for k in range(count)]
    loads = [pltpu.make_async_copy(part_ref.at[s], block.at[s], arrive.at[k]) for k, s in enumerate(spans)]
    stores = [pltpu.make_async_copy(block.at[s], gtok_ref.at[s], leave.at[k]) for k, s in enumerate(spans)]
    sums = pltpu.make_async_copy(sum_hbm, sum_ref, ready)
    sums.start()
    for load in loads:
        load.start()
    me = lax.axis_index("dp")
    sums.wait()
    wo[...] = sum_ref[0:16]
    for c in range(4):
        up[:, 512 * c : 512 * c + 512] = sum_ref[16 + 16 * c : 32 + 16 * c]
    dn[...] = sum_ref[80:144]
    wq[...] = sum_ref[144:160]
    wk[...] = sum_ref[160:176]
    wv[...] = sum_ref[176:192]
    memory[...] = sum_ref[192:208, 0 : memory.shape[1]]
    turned = sum_ref[192:208, 128:256].T
    for index, vector in enumerate(vectors):
        vector[...] = turned[index : index + 1, :]
    row = lax.broadcasted_iota(jnp.int32, (16, 256), 0)
    lane = lax.broadcasted_iota(jnp.int32, (16, 256), 1)
    own = jnp.sum(jnp.where(row * 4 + lane // 64 == me, sum_ref[192:208, 256:512], 0.0), axis=0, keepdims=True)
    b_up[...] = own[:, 0:64] + own[:, 64:128] + own[:, 128:192] + own[:, 192:256]
    for load, store in zip(loads, stores):
        load.wait()
        store.start()
    for store in stores:
        store.wait()


def unpack(sums, part, mem_rows):
    shapes = [(16, 512), (16, 2048), (64, 512), (16, 512), (16, 512), (16, 512), (16, mem_rows), (1, 64)] + [(1, 16)] * 8
    found = pl.pallas_call(
        unpack_kernel,
        in_specs=[pl.BlockSpec(memory_space=pl.ANY)] * 2,
        out_specs=[pl.BlockSpec(memory_space=pl.ANY)] + [pl.BlockSpec(memory_space=pltpu.VMEM)] * len(shapes),
        out_shape=[jax.ShapeDtypeStruct(s, F32) for s in [part.shape] + shapes],
        scratch_shapes=[
            pltpu.VMEM(sums.shape, F32),
            pltpu.VMEM(part.shape, F32),
            pltpu.SemaphoreType.DMA,
            pltpu.SemaphoreType.DMA((4,)),
            pltpu.SemaphoreType.DMA((4,)),
        ],
        compiler_params=params(),
        name="unpack",
    )(sums, part)
    gtok, found = found[0], found[1:]
    out = dict(zip(("w_out", "w_up", "w_down", "w_query", "w_key", "w_value", "memory"), found[:7]))
    out["memory"] = out["memory"].T
    out["b_up"] = found[7].reshape(64)
    for name, value in zip(VECTORS, found[8:]):
        out[name] = value.reshape(16)
    return gtok, out


NAMES = (
    "memory", "w_query", "b_query", "w_key", "w_value", "b_value", "w_out", "b_out", "gain_attn",
    "shift_attn", "w_up", "b_up", "w_down", "b_down", "gain_ffn", "shift_ffn",
)


def pack_whole(p):
    mem_rows = p["memory"].shape[0]
    mats = [p[name].reshape(PARTS, 16, 512) for name in ("w_query", "w_key", "w_value", "w_out")]
    up = p["w_up"].reshape(PARTS, 16, 4, 512).transpose(0, 2, 1, 3).reshape(PARTS, 64, 512)
    memory = jnp.pad(p["memory"].T, ((0, 0), (0, 128 - mem_rows))).reshape(PARTS, 16, 128)
    vectors = jnp.stack([p[name] for name in VECTORS], axis=1)
    vectors = jnp.pad(vectors, ((0, 0), (0, 120))).reshape(PARTS, 16, 128)
    own = jnp.arange(2048)[None] // 64 == jnp.arange(PARTS)[:, None]
    b_up = jnp.where(own, p["b_up"][None], 0).astype(BF16).reshape(PARTS, 8, 256)
    b_up = jnp.pad(b_up, ((0, 0), (0, 8), (0, 0)))
    small = jnp.concatenate([memory, vectors, b_up], axis=2)
    return jnp.concatenate(mats[:3] + [small, up, p["w_down"].reshape(PARTS, 64, 512), mats[3]], axis=1)


def unpack_whole(early, late, mem_rows):
    small = late[:, 48:64]
    vectors = small[:, :, 128:136].reshape(512, 8)
    out = {
        "memory": small[:, :, 0:mem_rows].reshape(512, mem_rows).T,
        "w_query": late[:, 0:16].reshape(512, 512),
        "w_key": late[:, 16:32].reshape(512, 512),
        "w_value": late[:, 32:48].reshape(512, 512),
        "w_out": early[:, 0:16].reshape(512, 512),
        "w_up": early[:, 16:80].reshape(PARTS, 4, 16, 512).transpose(0, 2, 1, 3).reshape(512, 2048),
        "w_down": early[:, 80:144].reshape(2048, 512),
        "b_up": small[0, 0:8, 256:512].reshape(2048),
    }
    for index, name in enumerate(VECTORS):
        out[name] = vectors[:, index]
    return out


def axis_of(name):
    return 1 if name == "memory" else 0


def shards(n, tokens, segment, counts, *rest):
    p = dict(zip(NAMES, rest[:-1]))
    cotangent = rest[-1]
    slots = tokens.shape[0]
    mem_rows = p["memory"].shape[0]
    whole = None
    if n != PARTS:
        whole = pack_whole({k: lax.all_gather(v, "dp", axis=axis_of(k), tiled=True) for k, v in p.items()})
    found = projections(p, whole, tokens, segment, counts, mem_rows)
    late, qa, ka, va, km, kmn, vmn, wt, memt, rows8, rbup, mixt, lse = found
    seg2 = segment.reshape(slots // 128, 128)
    output, gfirst, mgrad, delta, early, vec, bup = middle(late, rows8, rbup, counts, mixt, tokens, cotangent)
    gtok, sums = backward(
        seg2, counts, early, tokens, qa, ka, va, kmn, km, vmn, mgrad, lse, delta, gfirst, vec, bup, wt, memt, n == PARTS
    )
    if n == PARTS:
        gtok, grads = unpack(sums, gtok, mem_rows)
    else:
        full = unpack_whole(early.astype(F32), sums.astype(F32), mem_rows)
        grads = {
            k: lax.psum_scatter(v, "dp", scatter_dimension=axis_of(k), tiled=True) for k, v in full.items()
        }
    return (output, gtok) + tuple(grads[name] for name in NAMES)


def solution(mesh):
    n = mesh.shape["dp"]
    row, mat, mem = P("dp"), P("dp", None), P(None, "dp")
    spec = {name: mat if name.startswith("w_") else row for name in NAMES}
    spec["memory"] = mem
    weights = tuple(spec[name] for name in NAMES)
    return jax.shard_map(
        functools.partial(shards, n),
        mesh=mesh,
        in_specs=(mat, row, row) + weights + (mat,),
        out_specs=(mat, mat) + weights,
        check_vma=False,
    )
```
